32 devices in a mesh: seq: 4 (over y, x), exp: 8 (over z, core).
Axes of the slice: x: 2, y: 2, z: 4, core: 2. Of those that a mesh axis runs over, the one named last changes fastest.
Arguments:
- tokens: bfloat16 [2, 4, 1024, 1280], P(None, 'seq', 'exp'), may hold values from -6 to 6
- cotangent: bfloat16 [2, 4, 1024, 1280], P(None, 'seq', 'exp'), may hold values from -6 to 6
- expert_ids: int32 [2, 4, 1024, 7], P(None, 'seq', 'exp'), may hold values from 0 to 15, all different within a row; in each aligned block of 128 rows (0 to 127, 128 to 255, ..., all dimensions but the last counted through in order) at most 112 rows name the same one
- owner_table: int32 [16], replicated, may hold values from 0 to 15, each once
- w_query: bfloat16 [1280, 1280], replicated, may hold values from -0.25 to 0.25
- w_key: bfloat16 [1280, 1280], replicated, may hold values from -0.25 to 0.25
- w_value: bfloat16 [1280, 1280], replicated, may hold values from -0.15625 to 0.15625
- w_out: bfloat16 [1280, 1280], replicated, may hold values from -1.25 to 1.25
- gain_one: float32 [1280], replicated, may hold values from 0.5 to 1.5
- gain_two: float32 [1280], replicated, may hold values from 0.5 to 1.5
- w_router: bfloat16 [1280, 16], replicated, may hold values from -0.083984375 to 0.083984375
- shared_gate: bfloat16 [1280, 896], replicated, may hold values from -0.15625 to 0.15625
- shared_up: bfloat16 [1280, 896], replicated, may hold values from -0.15625 to 0.15625
- shared_down: bfloat16 [1280, 896], replicated, may hold values from -0.1875 to 0.1875
- routed_gate: bfloat16 [16, 1280, 896], P('exp'), may hold values from -0.15625 to 0.15625
- routed_up: bfloat16 [16, 1280, 896], P('exp'), may hold values from -0.15625 to 0.15625
- routed_down: bfloat16 [16, 1280, 896], P('exp'), may hold values from -0.1875 to 0.1875
Outputs:
- layer_out: bfloat16 [2, 4, 1024, 1280], P(None, 'seq', 'exp')
- grad_tokens: bfloat16 [2, 4, 1024, 1280], P(None, 'seq', 'exp')
- grad_query: float32 [1280, 1280], P('exp')
- grad_key: float32 [1280, 1280], P('exp')
- grad_value: float32 [1280, 1280], P('exp')
- grad_out_proj: float32 [1280, 1280], P('exp')
- grad_gain_one: float32 [1280], P('exp')
- grad_gain_two: float32 [1280], P('exp')
- grad_router: float32 [1280, 16], P('exp')
- grad_shared_gate: float32 [1280, 896], P('exp')
- grad_shared_up: float32 [1280, 896], P('exp')
- grad_shared_down: float32 [1280, 896], P('exp')
- grad_routed_gate: float32 [16, 1280, 896], P('exp', 'seq')
- grad_routed_up: float32 [16, 1280, 896], P('exp', 'seq')
- grad_routed_down: float32 [16, 1280, 896], P('exp', 'seq')
The draws below stay inside these ranges and needn't reach their ends.
Inputs may be any that keep to these rules, and one draw needn't show every extreme that they name: `expert_ids`: each token names 7 different experts. In each aligned block of 128 positions of a sequence (the tokens of one index of exp), no expert is named by more than 112 tokens; some block has an expert named by exactly 112. A permutation: expert e's weights are row owner_table[e] of routed_gate, routed_up and routed_down.
All inputs are finite; a program needn't handle non-finite values.
Results may differ from the reference program's by a relative error of at most 0.024.
Values may be sent and summed in bfloat16 or wider, within the bound.
A program may use at most 448 MiB of HBM per device.

```python
import math
from functools import partial
import jax
import jax.numpy as jnp
import numpy as np
from jax import lax

D = 1280
HEADS = 10
HD = 128
FF = 896
TOP = 7
MB = 2
SEQ_DEV = 128
EXPERTS = 16
GROUPS = 4
LENGTH = 1024
MOST = 112
N_SEQ = 4
N_EXP = 8


def shard_levels(rng, shape, shards, smallest, high):
    factor_of, own = 1.0, jax.random.fold_in(rng, 6)
    for dim, parts in shards:
        draws = jnp.exp(jax.random.uniform(jax.random.fold_in(own, dim), (parts,), jnp.float32, smallest / len(shards), high / len(shards)))
        factor_of = factor_of * jnp.repeat(draws, shape[dim] // parts).reshape([-1 if axis == dim else 1 for axis in range(len(shape))])
    return factor_of


def assign_block(own_key, own, number, rows, amount, top, most, skew):
    sequence = jax.random.permutation(own_key, amount)
    crowded, usual = load_shares(amount, rows * top, most, skew, True), load_shares(amount, rows * top, most, skew, False)
    places = jnp.arange(amount)

    def named(sizes, turn):
        used = int((sizes > 0).sum())
        fixed = max(1, used // 4)
        moved = fixed + (places - fixed + turn * (used - fixed)) % max(1, amount - fixed)
        return jnp.zeros((amount,), jnp.int32).at[sequence[jnp.where(places < fixed, places, moved)]].set(jnp.asarray(sizes, jnp.int32))

    sizes = jnp.where(number % 4 == 0, named(crowded, number // 4), named(usual, number - number // 4 - 1))
    mixed = jax.random.permutation(jax.random.fold_in(own, 3), amount)
    source_of, taker = mixed[0:amount // 2 * 2:2], mixed[1:amount // 2 * 2:2]
    margin = jnp.minimum(sizes[source_of] - 1, most - sizes[taker]) // 2
    margin = jnp.where((source_of == sequence[0]) | (taker == sequence[0]) | (sizes[taker] == 0), 0, jnp.maximum(margin, 0))
    moved = jax.random.randint(jax.random.fold_in(own, 4), (amount // 2,), 0, 1 << 20) % (margin + 1)
    sizes = sizes.at[source_of].add(-moved).at[taker].add(moved)
    items = jnp.searchsorted(jnp.cumsum(sizes), jnp.arange(rows * top), side="right").astype(jnp.int32)
    listing = items.reshape(top, rows).T
    listing = listing[jax.random.permutation(jax.random.fold_in(own, 1), rows)]
    turn = jax.random.randint(jax.random.fold_in(own, 2), (rows, 1), 0, top)
    return jnp.take_along_axis(listing, (jnp.arange(top)[None, :] + turn) % top, axis=1)


def load_shares(amount, total, limit, slope, full):
    portions = [(1 << 20) // math.isqrt(grade ** slope) + 1 for grade in range(1, amount + 1)]
    largest = limit if full else min(limit, max(-(-total // amount), total * portions[0] // sum(portions)))
    least = 1 if total - largest >= amount - 1 else 0
    given, spare = [largest] + [least] * (amount - 1), total - largest - least * (amount - 1)
    while spare > 0:
        candidates = [i for i in range(1, amount) if given[i] < largest] or [i for i in range(1, amount) if given[i] < limit]
        pool, budget = sum([portions[i] for i in candidates]), spare
        for i in candidates:
            extra = min(limit - given[i], max(1, budget * portions[i] // pool), spare)
            given[i] = given[i] + extra
            spare = spare - extra
    return np.array(given)


def noise(stream_key, extent, scale, reach, shards=(), held_as=jnp.bfloat16):
    values = scale * jax.random.normal(stream_key, extent, jnp.float32)
    if shards:
        values = values * shard_levels(stream_key, extent, shards, -0.22, 0.18)
    return jnp.clip(values, -reach, reach).astype(held_as)


def setup_inputs(seed: int = 0) -> dict:
    streams_of = jax.random.split(jax.random.key(seed), 18)
    tokens = noise(streams_of[0], (MB, GROUPS, LENGTH, D), 1.0, 6.0, ((1, 4), (2, 8)))
    cotangent = noise(streams_of[1], (MB, GROUPS, LENGTH, D), 1.0, 6.0, ((1, 4), (2, 8)))
    expert_ids_keys = jax.random.split(jax.random.fold_in(streams_of[2], 1), MB * GROUPS * LENGTH // SEQ_DEV)
    expert_ids_turns = jax.random.permutation(jax.random.fold_in(streams_of[2], 3), MB * GROUPS * LENGTH // SEQ_DEV)
    expert_ids = jax.vmap(lambda own, number: assign_block(jax.random.fold_in(streams_of[2], 2), own, number, SEQ_DEV, EXPERTS, TOP, MOST, 1))(expert_ids_keys, expert_ids_turns).reshape((MB, GROUPS, LENGTH, TOP))
    owner_table = jax.random.permutation(streams_of[3], EXPERTS).astype(jnp.int32)
    w_query = noise(streams_of[4], (D, D), (D // 2) ** -0.5, 0.25)
    w_key = noise(streams_of[5], (D, D), (D // 2) ** -0.5, 0.25)
    w_value = noise(streams_of[6], (D, D), D ** -0.5, 0.15625)
    w_out = noise(streams_of[7], (D, D), (D // 64) ** -0.5, 1.25)
    gain_one = jnp.clip(1.0 + 0.1 * jax.random.normal(streams_of[8], (D,), jnp.float32), 0.5, 1.5)
    gain_two = jnp.clip(1.0 + 0.1 * jax.random.normal(streams_of[9], (D,), jnp.float32), 0.5, 1.5)
    w_router = noise(streams_of[10], (D, EXPERTS), 0.014, 0.083984375)
    shared_gate = noise(streams_of[11], (D, FF), D ** -0.5, 0.15625)
    shared_up = noise(streams_of[12], (D, FF), D ** -0.5, 0.15625)
    shared_down = noise(streams_of[13], (D, FF), FF ** -0.5, 0.1875)
    routed_gate = noise(streams_of[14], (EXPERTS, D, FF), D ** -0.5, 0.15625, ((0, 8),))
    routed_up = noise(streams_of[15], (EXPERTS, D, FF), D ** -0.5, 0.15625, ((0, 8),))
    routed_down = noise(streams_of[16], (EXPERTS, D, FF), FF ** -0.5, 0.1875, ((0, 8),))
    return dict(tokens=tokens, cotangent=cotangent, expert_ids=expert_ids, owner_table=owner_table, w_query=w_query, w_key=w_key, w_value=w_value, w_out=w_out, gain_one=gain_one, gain_two=gain_two, w_router=w_router, shared_gate=shared_gate, shared_up=shared_up, shared_down=shared_down, routed_gate=routed_gate, routed_up=routed_up, routed_down=routed_down)


eps = 1e-06
highest = lax.Precision.HIGHEST

@jax.custom_vjp
def low(v):
    return lax.optimization_barrier(v.astype(jnp.bfloat16)).astype(jnp.float32)

@jax.custom_vjp
def low_back(v):
    return v

def low_keep(v):
    return (low(v), None)

def low_pass(kept, grad):
    return (grad,)

def back_keep(v):
    return (v, None)

def back_low(kept, grad):
    return (low(grad),)
low.defvjp(low_keep, low_pass)
low_back.defvjp(back_keep, back_low)

def norm_rows(inputs, gain):
    return inputs * lax.rsqrt(lax.optimization_barrier(jnp.mean(inputs * inputs, axis=-1, keepdims=True)) + eps) * gain

def angle_tables(positions):
    steps_half = jnp.arange(HD // 2).astype(positions.dtype)
    frequency = jnp.exp(steps_half * (-2.0 * math.log(10000.0) / HD))
    angles = positions[:, None] * frequency[None, :]
    angles = jnp.concatenate([angles, angles], axis=-1)
    return (jnp.cos(angles), jnp.sin(angles))

def rotate(inputs, cos_table, sin_table):
    row_count = inputs.shape[0]
    per_head = inputs.reshape(row_count, HEADS, HD)
    first_half = per_head[..., :HD // 2]
    second_half = per_head[..., HD // 2:]
    turned = jnp.concatenate([-second_half, first_half], axis=-1)
    return (per_head * cos_table[:, None, :] + turned * sin_table[:, None, :]).reshape(row_count, HEADS * HD)

def softmax_rows(scores):
    largest = lax.optimization_barrier(jnp.max(scores, axis=-1, keepdims=True))
    powers = jnp.exp(scores - largest)
    return powers / lax.optimization_barrier(jnp.sum(powers, axis=-1, keepdims=True))

def attend_block(key_rows, value_rows, packed):
    query_block, block_start = packed
    scores = jnp.einsum('qhd,khd->hqk', query_block, key_rows, precision=highest) * HD ** (-0.5)
    scores = low_back(scores)
    query_pos = block_start + jnp.arange(query_block.shape[0])
    visible = query_pos[:, None] >= jnp.arange(key_rows.shape[0])[None, :]
    attention = softmax_rows(jnp.where(visible[None], scores, -1e+30))
    mixed_rows = jnp.einsum('hqk,khd->qhd', low(attention), value_rows, precision=highest)
    return low(low_back(mixed_rows))

def routed_experts(normed_two, chosen_ids, owner_table, gate_weights, routed_gate, routed_up, routed_down):
    length = normed_two.shape[0]
    blocks = length // SEQ_DEV
    pair_ids = chosen_ids.reshape(blocks, SEQ_DEV * TOP)
    pair_hot = (pair_ids[..., None] == jnp.arange(EXPERTS).astype(jnp.int32)).astype(jnp.int32)
    ranks = lax.optimization_barrier(jnp.sum((jnp.cumsum(pair_hot, axis=1) - pair_hot) * pair_hot, axis=2)).astype(jnp.int32)
    block_ids = jnp.broadcast_to(jnp.arange(blocks).astype(jnp.int32)[:, None], pair_ids.shape)
    pair_rows = low_back(jnp.repeat(normed_two, TOP, axis=0)).reshape(blocks, SEQ_DEV * TOP, D)
    buffer = jnp.zeros((blocks, EXPERTS, MOST, D), normed_two.dtype).at[block_ids, pair_ids, ranks].set(pair_rows)
    expert_gate = routed_gate[owner_table]
    expert_up = routed_up[owner_table]
    expert_down = routed_down[owner_table]
    gate_part = low_back(jnp.einsum('bemd,edf->bemf', buffer, expert_gate, precision=highest))
    up_part = low_back(jnp.einsum('bemd,edf->bemf', buffer, expert_up, precision=highest))
    inner_rows = low(jax.nn.silu(gate_part) * up_part)
    results = low(low_back(jnp.einsum('bemf,edf->bemd', inner_rows, expert_down, precision=highest)))
    pair_out = results[block_ids, pair_ids, ranks].reshape(length, TOP, D)
    return lax.optimization_barrier(jnp.sum(gate_weights[..., None] * pair_out, axis=1))

def sequence_forward(chosen_ids, owner_table, weights, tokens):
    w_query, w_key, w_value, w_out, gain_one, gain_two, w_router, shared_gate, shared_up, shared_down, routed_gate, routed_up, routed_down = weights
    length = tokens.shape[0]
    cos_table, sin_table = angle_tables(jnp.arange(length).astype(tokens.dtype))
    normed = low(norm_rows(tokens, gain_one))
    queries_low = low(rotate(low_back(jnp.dot(normed, w_query, precision=highest)), cos_table, sin_table))
    rotated_keys = low(rotate(low_back(jnp.dot(normed, w_key, precision=highest)), cos_table, sin_table))
    values_low = low(low_back(jnp.dot(normed, w_value, precision=highest)))
    block_rows = min(512, length)
    blocks = queries_low.reshape(length // block_rows, block_rows, HEADS, HD)
    starts = jnp.arange(length // block_rows) * block_rows
    attend = jax.checkpoint(partial(attend_block, rotated_keys.reshape(length, HEADS, HD), values_low.reshape(length, HEADS, HD)))
    mixed_rows = lax.map(attend, (blocks, starts)).reshape(length, HEADS * HD)
    hidden_one = tokens + low_back(jnp.dot(mixed_rows, w_out, precision=highest))
    normed_two = low(norm_rows(hidden_one, gain_two))
    logits = low_back(jnp.dot(normed_two, w_router, precision=highest))
    gate_weights = softmax_rows(jnp.take_along_axis(logits, chosen_ids, axis=1))
    shared_gate_value = low_back(jnp.dot(normed_two, shared_gate, precision=highest))
    shared_up_value = low_back(jnp.dot(normed_two, shared_up, precision=highest))
    shared_hidden = low(jax.nn.silu(shared_gate_value) * shared_up_value)
    shared_result = low_back(jnp.dot(shared_hidden, shared_down.T, precision=highest))
    routed_result = routed_experts(normed_two, chosen_ids, owner_table, gate_weights, routed_gate, routed_up, routed_down)
    return hidden_one + shared_result + routed_result

def reference(tokens, cotangent, expert_ids, owner_table, w_query, w_key, w_value, w_out, gain_one, gain_two, w_router, shared_gate, shared_up, shared_down, routed_gate, routed_up, routed_down):
    weights = tuple((weight_in.astype(jnp.float32) for weight_in in (w_query, w_key, w_value, w_out, gain_one, gain_two, w_router, shared_gate, shared_up, shared_down, routed_gate, routed_up, routed_down)))
    sequences = MB * N_SEQ
    length = SEQ_DEV * N_EXP
    flat_tokens = tokens.reshape(sequences, length, D).astype(jnp.float32)
    flat_grads = cotangent.reshape(sequences, length, D).astype(jnp.float32)
    flat_ids = expert_ids.reshape(sequences, length, TOP).astype(jnp.int32)

    def one_sequence(totals, packed):
        tokens_one, grad_one, ids_one = packed
        result, pullback = jax.vjp(partial(sequence_forward, ids_one, owner_table), weights, tokens_one)
        weight_grads, token_grad = pullback(grad_one)
        totals = jax.tree.map(jnp.add, totals, weight_grads)
        return (totals, (result.astype(jnp.bfloat16), token_grad.astype(jnp.bfloat16)))
    start_totals = jax.tree.map(jnp.zeros_like, weights)
    totals, outputs = lax.scan(one_sequence, start_totals, (flat_tokens, flat_grads, flat_ids))
    layer_out = outputs[0].reshape(MB, N_SEQ, length, D)
    grad_tokens = outputs[1].reshape(MB, N_SEQ, length, D)
    return (layer_out, grad_tokens, totals[0], totals[1], totals[2], totals[3], totals[4], totals[5], totals[6], totals[7], totals[8], totals[9], totals[10], totals[11], totals[12])
```

```python
import functools
import math

import jax
import jax.numpy as jnp
from jax import lax
from jax.experimental import pallas as pl
from jax.experimental.pallas import tpu as pltpu
from jax.sharding import PartitionSpec as P

D = 1280
HEADS = 10
HD = 128
FF = 896
TOP = 7
EXP_DEV = 2
MB = 2
SEQ_DEV = 128
LANES = 128
BLOCK = 256
VMEM_BYTES = 60 * 2**20

eps = 1e-06
BF = jnp.bfloat16
F32 = jnp.float32


def norm_rows(inputs, gain):
    return inputs * lax.rsqrt(jnp.mean(inputs * inputs, axis=-1, keepdims=True) + eps) * gain


def norm_back(inputs, gain, grad):
    scale = lax.rsqrt(jnp.mean(inputs * inputs, axis=-1, keepdims=True) + eps)
    unit = inputs * scale
    weighted = grad * gain
    back = scale * (weighted - unit * jnp.mean(weighted * unit, axis=-1, keepdims=True))
    return back, grad * unit


def angle_tables(positions):
    steps_half = jnp.arange(HD // 2).astype(positions.dtype)
    frequency = jnp.exp(steps_half * (-2.0 * math.log(10000.0) / HD))
    angles = positions[:, None] * frequency[None, :]
    angles = jnp.concatenate([angles, angles], axis=-1)
    return (jnp.cos(angles), jnp.sin(angles))


def dot(a, b):
    return jnp.dot(a, b, preferred_element_type=F32)


def dot_nt(a, b):
    return lax.dot_general(a, b, (((1,), (1,)), ((), ())), preferred_element_type=F32)


def dot_tn(a, b):
    return lax.dot_general(a, b, (((0,), (0,)), ((), ())), preferred_element_type=F32)


def gather_exp(array):
    return lax.all_gather(array, "exp", axis=0, tiled=True)


def scatter_exp(array):
    return lax.psum_scatter(array.astype(BF), "exp", scatter_dimension=0, tiled=True).astype(F32)


def turn(heads, cos_table, sin_table):
    return heads * cos_table + pltpu.roll(heads, HD // 2, 1) * sin_table


def visible_scores(queries, keys, start):
    scores = dot_nt(queries, keys) * HD ** (-0.5)
    rows = queries.shape[0]
    row = lax.broadcasted_iota(jnp.int32, (rows, rows), 0)
    column = lax.broadcasted_iota(jnp.int32, (rows, rows), 1)
    last = jnp.where(row >= column, scores[:, start:], -1e30)
    return last if start == 0 else jnp.concatenate([scores[:, :start], last], axis=1)


def attend_forward(slots, rows_ref, gain_ref, cos_ref, sin_ref, w_ref, normed_ref, qkv_ref, mixed_ref, lse_ref):
    length = rows_ref.shape[0]
    step = BLOCK if length <= 2048 else BLOCK // 2

    def project(i, carry):
        part = pl.ds(pl.multiple_of(i * step, step), step)
        normed = norm_rows(rows_ref[part, :].astype(F32), gain_ref[...]).astype(BF)
        normed_ref[part, :] = normed
        for slot in range(slots):
            base = 3 * HD * slot
            qkv = dot(normed, w_ref[:, base : base + 3 * HD])
            for j in range(2):
                turned = turn(qkv[:, j * HD : (j + 1) * HD], cos_ref[part, :], sin_ref[part, :])
                qkv_ref[part, base + j * HD : base + (j + 1) * HD] = turned.astype(BF)
            qkv_ref[part, base + 2 * HD : base + 3 * HD] = qkv[:, 2 * HD :].astype(BF)
        return carry

    lax.fori_loop(0, length // step, project, 0)
    for slot in range(slots):
        base = 3 * HD * slot
        for start in range(0, length, step):
            stop = start + step
            scores = visible_scores(
                qkv_ref[start:stop, base : base + HD], qkv_ref[:stop, base + HD : base + 2 * HD], start
            )
            largest = jnp.max(scores, axis=-1, keepdims=True)
            powers = jnp.exp(scores - largest)
            total = jnp.sum(powers, axis=-1, keepdims=True)
            attention = (powers * (1.0 / total)).astype(BF)
            mixed = dot(attention, qkv_ref[:stop, base + 2 * HD : base + 3 * HD])
            mixed_ref[start:stop, slot * HD : (slot + 1) * HD] = mixed.astype(BF)
            lse_ref[slot, start:stop, :] = largest + jnp.log(total)


def attend_backward(
    slots, mix_ref, normed_ref, qkv_ref, mixed_ref, lse_ref, cos_ref, sin_ref, w_ref, w_out_ref, live_ref,
    out_sum_ref, qkv_sum_ref, grad_ref, raw_ref, d_mixed_ref, d_keys_ref, d_values_ref,
):
    length = mix_ref.shape[0]
    step = BLOCK if length <= 2048 else BLOCK // 2
    factor = HD ** (-0.5)

    def project(i, carry):
        part = pl.ds(pl.multiple_of(i * step, step), step)
        d_mixed_ref[part, :] = (dot_nt(mix_ref[part, :], w_out_ref[...]) * live_ref[...]).astype(BF)
        return carry

    lax.fori_loop(0, length // step, project, 0)
    for slot in range(slots):
        base = 3 * HD * slot
        d_keys_ref[...] = jnp.zeros_like(d_keys_ref)
        d_values_ref[...] = jnp.zeros_like(d_values_ref)
        for start in range(0, length, step):
            stop = start + step
            queries = qkv_ref[start:stop, base : base + HD]
            keys = qkv_ref[:stop, base + HD : base + 2 * HD]
            values = qkv_ref[:stop, base + 2 * HD : base + 3 * HD]
            d_mixed = d_mixed_ref[start:stop, slot * HD : (slot + 1) * HD]
            attention = jnp.exp(visible_scores(queries, keys, start) - lse_ref[slot, start:stop, :])
            d_att = dot_nt(d_mixed, values)
            row_term = jnp.sum(attention * d_att, axis=-1, keepdims=True)
            d_scores = (attention * (d_att - row_term)).astype(BF)
            d_queries = dot(d_scores, keys) * factor
            raw = turn(d_queries, cos_ref[start:stop, :], -sin_ref[start:stop, :])
            raw_ref[start:stop, base : base + HD] = raw.astype(BF)
            d_keys_ref[:stop, :] += dot_tn(d_scores, queries)
            d_values_ref[:stop, :] += dot_tn(attention.astype(BF), d_mixed)
        raw = turn(d_keys_ref[...] * factor, cos_ref[...], -sin_ref[...])
        raw_ref[:, base + HD : base + 2 * HD] = raw.astype(BF)
        raw_ref[:, base + 2 * HD : base + 3 * HD] = d_values_ref[...].astype(BF)

    def give(i, carry):
        part = pl.ds(pl.multiple_of(i * step, step), step)
        grad_ref[part, :] = dot_nt(raw_ref[part, :], w_ref[...]).astype(BF)
        return carry

    lax.fori_loop(0, length // step, give, 0)
    out_sum_ref[...] = dot_tn(mixed_ref[...], mix_ref[...])

    def sums(i, carry):
        part = pl.ds(pl.multiple_of(i * 256, 256), 256)
        qkv_sum_ref[part, :] = dot_tn(normed_ref[:, part], raw_ref[...])
        return carry

    lax.fori_loop(0, D // 256, sums, 0)


def on_device(
    tokens,
    cotangent,
    expert_ids,
    owner_table,
    w_query,
    w_key,
    w_value,
    w_out,
    gain_one,
    gain_two,
    w_router,
    shared_gate,
    shared_up,
    shared_down,
    routed_gate,
    routed_up,
    routed_down,
):
    devices = lax.axis_size("exp")
    groups = lax.axis_size("seq")
    me = lax.axis_index("exp")
    experts = owner_table.shape[0]
    length = SEQ_DEV * devices
    rows_out = D // devices
    slots = -(-HEADS // devices)
    wide = slots * HD
    share = FF // devices
    used = EXP_DEV * FF + share
    padded = -(-used // LANES) * LANES

    head_of = [jnp.minimum(me + slot * devices, HEADS - 1) for slot in range(slots)]
    slot_live = jnp.concatenate(
        [
            jnp.full((HD,), jnp.where(me + slot * devices < HEADS, 1.0, 0.0), F32)
            for slot in range(slots)
        ]
    )

    w_qkv = jnp.concatenate(
        [
            lax.dynamic_slice(weight, (0, head * HD), (D, HD))
            for head in head_of
            for weight in (w_query, w_key, w_value)
        ],
        axis=1,
    )
    w_out_heads = jnp.concatenate(
        [lax.dynamic_slice(w_out, (head * HD, 0), (HD, D)) for head in head_of], axis=0
    )
    cos_table, sin_table = angle_tables(jnp.arange(length).astype(F32))
    sin_table = jnp.where(jnp.arange(HD) < HD // 2, -sin_table, sin_table)
    in_vmem = pl.BlockSpec(memory_space=pltpu.VMEM)
    params = pltpu.CompilerParams(vmem_limit_bytes=VMEM_BYTES)

    def like(*shape, dtype=BF):
        return jax.ShapeDtypeStruct(shape, dtype)

    forward = pl.pallas_call(
        functools.partial(attend_forward, slots),
        out_shape=(
            like(length, D),
            like(length, 3 * wide),
            like(length, wide),
            like(slots, length, 1, dtype=F32),
        ),
        in_specs=[in_vmem] * 5,
        out_specs=(in_vmem,) * 4,
        compiler_params=params,
        name="attend_forward",
    )
    backward = pl.pallas_call(
        functools.partial(attend_backward, slots),
        out_shape=(like(wide, D, dtype=F32), like(D, 3 * wide, dtype=F32), like(length, D)),
        in_specs=[in_vmem] * 10,
        out_specs=(in_vmem,) * 3,
        scratch_shapes=[
            pltpu.VMEM((length, 3 * wide), BF),
            pltpu.VMEM((length, wide), BF),
            pltpu.VMEM((length, HD), F32),
            pltpu.VMEM((length, HD), F32),
        ],
        compiler_params=params,
        name="attend_backward",
    )

    def joined(routed, shared):
        own = lax.dynamic_slice(shared, (0, me * share), (D, share))
        blank = jnp.zeros((D, padded - used), BF)
        return jnp.concatenate([routed[i] for i in range(EXP_DEV)] + [own, blank], axis=1)

    gate_all = joined(routed_gate, shared_gate)
    up_all = joined(routed_up, shared_up)
    down_all = joined(routed_down, shared_down)

    expert_at = jnp.sum(
        (owner_table[:, None] == jnp.arange(experts)[None, :]) * jnp.arange(experts)[:, None],
        axis=0,
    )
    router_rows = jnp.take(w_router, expert_at, axis=1)
    ids_all = lax.all_gather(expert_ids[:, 0], "exp", axis=1, tiled=True)

    first = []
    for micro_batch in range(MB):
        rows_all = gather_exp(tokens[micro_batch, 0])
        normed, qkv, mixed, lse = forward(rows_all, gain_one[None], cos_table, sin_table, w_qkv)
        sent = lax.all_to_all(
            mixed.reshape(devices, SEQ_DEV, wide), "exp", split_axis=0, concat_axis=0, tiled=True
        )
        own_mixed = (
            sent.reshape(devices, SEQ_DEV, slots, HD)
            .transpose(1, 2, 0, 3)
            .reshape(SEQ_DEV, slots * devices * HD)[:, :D]
        )
        rows_in = tokens[micro_batch, 0].astype(F32)
        hidden_one = rows_in + dot(own_mixed, w_out)
        two_low = norm_rows(hidden_one, gain_two).astype(BF)
        two_all = gather_exp(two_low)
        grad_all = gather_exp(cotangent[micro_batch, 0])
        first.append(
            (normed, qkv, mixed, lse, rows_in, hidden_one, two_all, grad_all)
        )

    column = jnp.arange(padded)
    second = []
    for micro_batch in range(MB):
        two_all, grad_all = first[micro_batch][6:]
        logits = dot(two_all, router_rows)
        named = jnp.any(ids_all[micro_batch][:, :, None] == expert_at[None, None, :], axis=1)
        chosen = jnp.where(named, logits, -jnp.inf)
        powers = jnp.where(named, jnp.exp(chosen - jnp.max(chosen, axis=-1, keepdims=True)), 0.0)
        gates = powers / jnp.sum(powers, axis=-1, keepdims=True)
        own_gates = lax.dynamic_slice(gates, (0, me * EXP_DEV), (length, EXP_DEV))
        weight = jnp.where(
            column[None, :] < FF,
            own_gates[:, :1],
            jnp.where(column[None, :] < 2 * FF, own_gates[:, 1:], 1.0),
        )
        gate_part = dot(two_all, gate_all)
        up_part = dot(two_all, up_all)
        down_part = dot(grad_all, down_all)
        sigmoid = jax.nn.sigmoid(gate_part)
        act = gate_part * sigmoid
        hidden = act * up_part
        products = hidden * down_part
        own_grads = jnp.stack(
            [jnp.sum(products[:, i * FF : (i + 1) * FF], axis=1) for i in range(EXP_DEV)], axis=1
        )
        hidden_low = (weight * hidden).astype(BF)
        weighted = weight * down_part
        d_gate = (weighted * up_part * (sigmoid + act * (1.0 - sigmoid))).astype(BF)
        d_up = (weighted * act).astype(BF)
        out_part = scatter_exp(dot_nt(hidden_low, down_all))
        back_part = scatter_exp(dot_nt(d_gate, gate_all) + dot_nt(d_up, up_all))
        gate_grads = lax.all_gather(own_grads, "exp", axis=1, tiled=True)
        grad_logits = (
            gates * (gate_grads - jnp.sum(gates * gate_grads, axis=-1, keepdims=True))
        ).astype(BF)
        second.append((hidden_low, d_gate, d_up, out_part, back_part, grad_logits))

    two_both = jnp.concatenate([f[6] for f in first])
    grad_both = jnp.concatenate([f[7] for f in first])
    gate_sum = dot_tn(two_both, jnp.concatenate([s[1] for s in second]))
    up_sum = dot_tn(two_both, jnp.concatenate([s[2] for s in second]))
    down_sum = dot_tn(grad_both, jnp.concatenate([s[0] for s in second]))

    def routed_sum(total):
        parts = jnp.stack([total[:, i * FF : (i + 1) * FF] for i in range(EXP_DEV)])
        return lax.psum_scatter(
            parts.astype(BF), "seq", scatter_dimension=1, tiled=True
        ).astype(F32)

    def shared_part(total):
        return total[:, EXP_DEV * FF : used]

    outputs_list = []
    grads_list = []
    small = jnp.zeros((D, experts + 2), F32)
    qkv_sum = jnp.zeros((D, 3 * wide), F32)
    out_sum = jnp.zeros((wide, D), F32)
    for micro_batch in range(MB):
        normed, qkv, mixed, lse, rows_in, hidden_one, two_all, _ = first[micro_batch]
        _, _, _, out_part, back_part, grad_logits = second[micro_batch]
        outputs_list.append((hidden_one + out_part).astype(BF))
        own_logits = lax.dynamic_slice(grad_logits, (me * SEQ_DEV, 0), (SEQ_DEV, experts))
        grad_two = back_part + dot_nt(own_logits, router_rows)
        back, gain_terms = norm_back(hidden_one, gain_two, grad_two)
        grad_hidden = cotangent[micro_batch, 0].astype(F32) + back
        own_two = lax.dynamic_slice(two_all, (me * SEQ_DEV, 0), (SEQ_DEV, D))
        router_part = dot_tn(own_two, own_logits)
        mix_all = gather_exp(grad_hidden.astype(BF))
        out_one, qkv_one, grad_part = backward(
            mix_all, normed, qkv, mixed, lse, cos_table, sin_table, w_qkv, w_out_heads, slot_live[None]
        )
        out_sum = out_sum + out_one
        qkv_sum = qkv_sum + qkv_one
        grad_normed = scatter_exp(grad_part)
        back_one, gain_one_terms = norm_back(rows_in, gain_one, grad_normed)
        grads_list.append((grad_hidden + back_one).astype(BF))
        small = small + jnp.concatenate(
            [
                router_part,
                jnp.sum(gain_one_terms, axis=0)[:, None],
                jnp.sum(gain_terms, axis=0)[:, None],
            ],
            axis=1,
        )

    def to_rows(columns):
        parts = columns.astype(BF).reshape(devices, rows_out, columns.shape[1])
        parts = lax.psum_scatter(parts, "seq", scatter_dimension=1, tiled=True)
        return lax.all_to_all(parts, "exp", split_axis=0, concat_axis=0, tiled=True)

    def to_all(rows):
        return lax.all_gather(rows, "seq", axis=0, tiled=True).astype(F32)

    piece = rows_out // groups
    shared_cols = jnp.concatenate([shared_part(t) for t in (gate_sum, up_sum, down_sum)], axis=1)
    shared_rows = to_rows(shared_cols).reshape(devices, piece, 3, share)
    shared_full = to_all(shared_rows.transpose(1, 2, 0, 3).reshape(piece, 3 * FF))
    qkv_rows = to_rows(qkv_sum).reshape(devices, piece, slots, 3, HD)
    qkv_rows = qkv_rows.transpose(1, 3, 2, 0, 4).reshape(piece, 3, slots * devices * HD)
    qkv_full = to_all(qkv_rows[:, :, :D].reshape(piece, 3 * D))
    out_part = lax.psum_scatter(out_sum.astype(BF), "seq", scatter_dimension=1, tiled=True)
    spread = jnp.zeros((slots * devices * HD, D // groups), BF)
    for slot in range(slots):
        spread = lax.dynamic_update_slice(
            spread, out_part[slot * HD : (slot + 1) * HD], ((me + slot * devices) * HD, 0)
        )
    out_rows = lax.psum_scatter(spread[:D], "exp", scatter_dimension=0, tiled=True)
    out_full = lax.all_gather(out_rows, "seq", axis=1, tiled=True).astype(F32)
    small_rows = lax.psum_scatter(
        lax.psum(small, "seq"), "exp", scatter_dimension=0, tiled=True
    )
    place_of = jnp.take(small_rows, owner_table, axis=1)
    return (
        jnp.stack(outputs_list)[:, None],
        jnp.stack(grads_list)[:, None],
        qkv_full[:, :D],
        qkv_full[:, D : 2 * D],
        qkv_full[:, 2 * D :],
        out_full,
        small_rows[:, experts],
        small_rows[:, experts + 1],
        place_of,
        shared_full[:, :FF],
        shared_full[:, FF : 2 * FF],
        shared_full[:, 2 * FF :],
        routed_sum(gate_sum),
        routed_sum(up_sum),
        routed_sum(down_sum),
    )


def solution(mesh):
    rows = P(None, "seq", "exp", None)
    placed = (rows,) * 3 + (P(),) * 11 + (P("exp", None, None),) * 3
    wide = P("exp", None)
    return jax.shard_map(
        on_device,
        mesh=mesh,
        in_specs=placed,
        out_specs=(rows, rows, wide, wide, wide, wide, P("exp"), P("exp"))
        + (wide,) * 4
        + (P("exp", "seq", None),) * 3,
        check_vma=False,
    )
```

```python
import functools
import math

import jax
import jax.numpy as jnp
from jax import lax
from jax.experimental import pallas as pl
from jax.experimental.pallas import tpu as pltpu
from jax.sharding import PartitionSpec as P

D = 1280
HEADS = 10
HD = 128
FF = 896
TOP = 7
EXP_DEV = 2
MB = 2
SEQ_DEV = 128
LANES = 128
BLOCK = 256
VMEM_BYTES = 60 * 2**20

eps = 1e-06
BF = jnp.bfloat16
F32 = jnp.float32


def norm_rows(inputs, gain):
    return inputs * lax.rsqrt(jnp.mean(inputs * inputs, axis=-1, keepdims=True) + eps) * gain


def norm_back(inputs, gain, grad):
    scale = lax.rsqrt(jnp.mean(inputs * inputs, axis=-1, keepdims=True) + eps)
    unit = inputs * scale
    weighted = grad * gain
    back = scale * (weighted - unit * jnp.mean(weighted * unit, axis=-1, keepdims=True))
    return back, grad * unit


def angle_tables(positions):
    steps_half = jnp.arange(HD // 2).astype(positions.dtype)
    frequency = jnp.exp(steps_half * (-2.0 * math.log(10000.0) / HD))
    angles = positions[:, None] * frequency[None, :]
    angles = jnp.concatenate([angles, angles], axis=-1)
    return (jnp.cos(angles), jnp.sin(angles))


def dot(a, b):
    return jnp.dot(a, b, preferred_element_type=F32)


def dot_nt(a, b):
    return lax.dot_general(a, b, (((1,), (1,)), ((), ())), preferred_element_type=F32)


def dot_tn(a, b):
    return lax.dot_general(a, b, (((0,), (0,)), ((), ())), preferred_element_type=F32)


def gather_exp(array):
    return lax.all_gather(array, "exp", axis=0, tiled=True)


def scatter_exp(array):
    return lax.psum_scatter(array.astype(BF), "exp", scatter_dimension=0, tiled=True).astype(F32)


def turn(heads, cos_table, sin_table):
    return heads * cos_table + pltpu.roll(heads, HD // 2, 1) * sin_table


def visible_scores(queries, keys, start):
    scores = dot_nt(queries, keys) * HD ** (-0.5)
    rows = queries.shape[0]
    row = lax.broadcasted_iota(jnp.int32, (rows, rows), 0)
    column = lax.broadcasted_iota(jnp.int32, (rows, rows), 1)
    last = jnp.where(row >= column, scores[:, start:], -1e30)
    return last if start == 0 else jnp.concatenate([scores[:, :start], last], axis=1)


def attend_forward(slots, rows_ref, gain_ref, cos_ref, sin_ref, w_ref, normed_ref, qkv_ref, mixed_ref, lse_ref):
    length = rows_ref.shape[0]
    step = BLOCK if length <= 2048 else BLOCK // 2

    def project(i, carry):
        part = pl.ds(pl.multiple_of(i * step, step), step)
        normed = norm_rows(rows_ref[part, :].astype(F32), gain_ref[...]).astype(BF)
        normed_ref[part, :] = normed
        for slot in range(slots):
            base = 3 * HD * slot
            qkv = dot(normed, w_ref[:, base : base + 3 * HD])
            for j in range(2):
                turned = turn(qkv[:, j * HD : (j + 1) * HD], cos_ref[part, :], sin_ref[part, :])
                qkv_ref[part, base + j * HD : base + (j + 1) * HD] = turned.astype(BF)
            qkv_ref[part, base + 2 * HD : base + 3 * HD] = qkv[:, 2 * HD :].astype(BF)
        return carry

    lax.fori_loop(0, length // step, project, 0)
    for slot in range(slots):
        base = 3 * HD * slot
        for start in range(0, length, step):
            stop = start + step
            scores = visible_scores(
                qkv_ref[start:stop, base : base + HD], qkv_ref[:stop, base + HD : base + 2 * HD], start
            )
            largest = jnp.max(scores, axis=-1, keepdims=True)
            powers = jnp.exp(scores - largest)
            total = jnp.sum(powers, axis=-1, keepdims=True)
            attention = (powers * (1.0 / total)).astype(BF)
            mixed = dot(attention, qkv_ref[:stop, base + 2 * HD : base + 3 * HD])
            mixed_ref[start:stop, slot * HD : (slot + 1) * HD] = mixed.astype(BF)
            lse_ref[slot, start:stop, :] = largest + jnp.log(total)


def attend_backward(
    slots, mix_ref, normed_ref, qkv_ref, mixed_ref, lse_ref, cos_ref, sin_ref, w_ref, w_out_ref, live_ref,
    out_sum_ref, qkv_sum_ref, grad_ref, raw_ref, d_mixed_ref, d_keys_ref, d_values_ref,
):
    length = mix_ref.shape[0]
    step = BLOCK if length <= 2048 else BLOCK // 2
    factor = HD ** (-0.5)

    def project(i, carry):
        part = pl.ds(pl.multiple_of(i * step, step), step)
        d_mixed_ref[part, :] = (dot_nt(mix_ref[part, :], w_out_ref[...]) * live_ref[...]).astype(BF)
        return carry

    lax.fori_loop(0, length // step, project, 0)
    for slot in range(slots):
        base = 3 * HD * slot
        d_keys_ref[...] = jnp.zeros_like(d_keys_ref)
        d_values_ref[...] = jnp.zeros_like(d_values_ref)
        for start in range(0, length, step):
            stop = start + step
            queries = qkv_ref[start:stop, base : base + HD]
            keys = qkv_ref[:stop, base + HD : base + 2 * HD]
            values = qkv_ref[:stop, base + 2 * HD : base + 3 * HD]
            d_mixed = d_mixed_ref[start:stop, slot * HD : (slot + 1) * HD]
            attention = jnp.exp(visible_scores(queries, keys, start) - lse_ref[slot, start:stop, :])
            d_att = dot_nt(d_mixed, values)
            row_term = jnp.sum(attention * d_att, axis=-1, keepdims=True)
            d_scores = (attention * (d_att - row_term)).astype(BF)
            d_queries = dot(d_scores, keys) * factor
            raw = turn(d_queries, cos_ref[start:stop, :], -sin_ref[start:stop, :])
            raw_ref[start:stop, base : base + HD] = raw.astype(BF)
            d_keys_ref[:stop, :] += dot_tn(d_scores, queries)
            d_values_ref[:stop, :] += dot_tn(attention.astype(BF), d_mixed)
        raw = turn(d_keys_ref[...] * factor, cos_ref[...], -sin_ref[...])
        raw_ref[:, base + HD : base + 2 * HD] = raw.astype(BF)
        raw_ref[:, base + 2 * HD : base + 3 * HD] = d_values_ref[...].astype(BF)

    def give(i, carry):
        part = pl.ds(pl.multiple_of(i * step, step), step)
        grad_ref[part, :] = dot_nt(raw_ref[part, :], w_ref[...]).astype(BF)
        return carry

    lax.fori_loop(0, length // step, give, 0)
    out_sum_ref[...] = dot_tn(mixed_ref[...], mix_ref[...])

    def sums(i, carry):
        part = pl.ds(pl.multiple_of(i * 256, 256), 256)
        qkv_sum_ref[part, :] = dot_tn(normed_ref[:, part], raw_ref[...])
        return carry

    lax.fori_loop(0, D // 256, sums, 0)


MESH = pl.DeviceIdType.MESH


def place():
    me = lax.axis_index("exp")
    return me // 2, me % 2


def remote(source, target, send_sem, recv_sem, chip, core):
    return pltpu.make_async_remote_copy(
        src_ref=source,
        dst_ref=target,
        send_sem=send_sem,
        recv_sem=recv_sem,
        device_id={"exp": 2 * chip + core},
        device_id_type=MESH,
    )


def meet(chips):
    chip, core = place()
    barrier = pltpu.get_barrier_semaphore()

    def greet(to_chip, to_core):
        pl.semaphore_signal(
            barrier, inc=1, device_id={"exp": 2 * to_chip + to_core}, device_id_type=MESH
        )

    greet(chip, 1 - core)

    @pl.when(chip < chips - 1)
    def _():
        greet(chip + 1, core)

    @pl.when(chip > 0)
    def _():
        greet(chip - 1, core)

    below = (chip + chips - 1) // chips
    above = (2 * chips - 2 - chip) // chips
    pl.semaphore_wait(barrier, 1 + below + above)


def gather_sems(chips):
    return [pltpu.SemaphoreType.DMA((chips,))] * 4 + [pltpu.SemaphoreType.DMA((2 * chips,))] * 2


class Gather:
    def __init__(self, chips, own, blocks, sems):
        self.chips, self.own, self.blocks = chips, own, blocks
        self.up_send, self.up_recv, self.down_send, self.down_recv = sems[:4]
        self.pair_send, self.pair_recv = sems[4:]

    def _source(self, hop, number):
        return self.own if hop == 0 else self.blocks.at[number]

    def _up(self, hop):
        chip, core = place()
        number = 2 * (chip - hop) + core
        return remote(
            self._source(hop, number), self.blocks.at[number],
            self.up_send.at[hop], self.up_recv.at[hop], chip + 1, core,
        )

    def _down(self, hop):
        chip, core = place()
        number = 2 * (chip + hop) + core
        return remote(
            self._source(hop, number), self.blocks.at[number],
            self.down_send.at[hop], self.down_recv.at[hop], chip - 1, core,
        )

    def _pair(self, away):
        chip, core = place()
        number = 2 * (chip + away) + core
        source = self.own if isinstance(away, int) and away == 0 else self.blocks.at[number]
        slot = away + self.chips
        return remote(
            source, self.blocks.at[number], self.pair_send.at[slot], self.pair_recv.at[slot],
            chip, 1 - core,
        )

    def _from_pair(self, away):
        chip, core = place()
        block = self.blocks.at[2 * (chip + away) + 1 - core]
        slot = away + self.chips
        return remote(
            block, block, self.pair_send.at[slot], self.pair_recv.at[slot], chip, 1 - core
        )

    def start(self):
        chip, _ = place()

        @pl.when(chip < self.chips - 1)
        def _():
            self._up(0).start()

        @pl.when(chip > 0)
        def _():
            self._down(0).start()

        self._pair(0).start()

    def hop(self, hop):
        chip, core = place()

        @pl.when(chip >= hop)
        def _():
            block = self.blocks.at[2 * (chip - hop) + core]
            remote(
                block, block, self.up_send.at[hop - 1], self.up_recv.at[hop - 1], chip, 1 - core
            ).wait_recv()

            @pl.when(chip < self.chips - 1)
            def _():
                self._up(hop).start()

            self._pair(-hop).start()

        @pl.when(chip + hop < self.chips)
        def _():
            block = self.blocks.at[2 * (chip + hop) + core]
            remote(
                block, block, self.down_send.at[hop - 1], self.down_recv.at[hop - 1], chip, 1 - core
            ).wait_recv()

            @pl.when(chip > 0)
            def _():
                self._down(hop).start()

            self._pair(hop).start()

    def take_pair(self, away):
        self._from_pair(away).wait_recv()

    def finish(self, pairs):
        chip, _ = place()
        for away in range(-self.chips + 1, self.chips):

            @pl.when(jnp.logical_and(chip + away >= 0, chip + away < self.chips))
            def _():
                if pairs:
                    self._from_pair(away).wait_recv()
                self._pair(away).wait_send()

        for hop in range(self.chips):

            @pl.when(jnp.logical_and(chip >= hop, chip < self.chips - 1))
            def _():
                self._up(hop).wait_send()

            @pl.when(jnp.logical_and(chip + hop < self.chips, chip > 0))
            def _():
                self._down(hop).wait_send()


def scatter_sems(chips):
    return [pltpu.SemaphoreType.DMA((chips,))] * 6


class Scatter:
    def __init__(self, chips, theirs, mine, pair, line, sems):
        self.chips, self.theirs, self.mine, self.pair, self.line = chips, theirs, mine, pair, line
        self.pair_send, self.pair_recv, self.up_send, self.up_recv = sems[:4]
        self.down_send, self.down_recv = sems[4:]

    def _pair(self, to):
        chip, core = place()
        return remote(
            self.theirs(to), self.pair.at[to], self.pair_send.at[to], self.pair_recv.at[to],
            chip, 1 - core,
        )

    def _up(self, chip, to):
        return remote(
            self.mine(to), self.line.at[to - chip - 1], self.up_send.at[to], self.up_recv.at[to],
            chip + 1, place()[1],
        )

    def _down(self, chip, to):
        return remote(
            self.mine(to), self.line.at[self.chips - chip + 1 + to],
            self.down_send.at[to], self.down_recv.at[to], chip - 1, place()[1],
        )

    def _arrived_up(self, to):
        chip, core = place()
        block = self.line.at[to - chip]
        remote(block, block, self.up_send.at[to], self.up_recv.at[to], chip, 1 - core).wait_recv()
        return block[...].astype(F32)

    def _arrived_down(self, to):
        chip, core = place()
        block = self.line.at[self.chips - chip + to]
        remote(
            block, block, self.down_send.at[to], self.down_recv.at[to], chip, 1 - core
        ).wait_recv()
        return block[...].astype(F32)

    def _both(self, to):
        chip, core = place()
        block = self.pair.at[to]
        remote(
            block, block, self.pair_send.at[to], self.pair_recv.at[to], chip, 1 - core
        ).wait_recv()
        return self.mine(to)[...].astype(F32) + block[...].astype(F32)

    def start(self):
        for to in range(self.chips):
            self._pair(to).start()

    def slot(self, turn):
        chip, _ = place()
        last = self.chips - 1

        @pl.when(chip <= turn)
        def _():
            to = last - turn + chip
            total = self._both(to)

            @pl.when(chip == 0)
            def _():
                self.mine(to)[...] = total.astype(BF)

            @pl.when(chip > 0)
            def _():
                self.mine(to)[...] = (total + self._arrived_up(to)).astype(BF)

            self._up(chip, to).start()

        @pl.when(last - chip <= turn)
        def _():
            to = turn - last + chip
            total = self._both(to)

            @pl.when(chip == last)
            def _():
                self.mine(to)[...] = total.astype(BF)

            @pl.when(chip < last)
            def _():
                self.mine(to)[...] = (total + self._arrived_down(to)).astype(BF)

            self._down(chip, to).start()

    def finish(self, result):
        chip, _ = place()
        last = self.chips - 1
        result[...] = self._both(chip)

        @pl.when(chip > 0)
        def _():
            result[...] += self._arrived_up(chip)

        @pl.when(chip < last)
        def _():
            result[...] += self._arrived_down(chip)

        for to in range(self.chips):
            self._pair(to).wait_send()

            @pl.when(to > chip)
            def _():
                self._up(chip, to).wait_send()

            @pl.when(to < chip)
            def _():
                self._down(chip, to).wait_send()


def part_of(array, index):
    return array.at[index]


def block_order(chip, turn, chips):
    number, bit = 0, 1
    while bit < chips:
        number = number + bit * ((chip // bit + turn // bit) % 2)
        bit = 2 * bit
    return number


def expert_rows(
    chips, experts,
    own_ref, grad_ref, named_ref, router_ref, routed_refs, shared_refs,
    rows_ref, hidden_ref, d_gate_ref, d_up_ref, out_b_ref, back_b_ref, out_a_ref, back_a_ref,
    weights, rows, grads, stage, out, back, pairs, lines, weight_sem, local_sem, grad_sem, stage_sem, keep_sem,
    *sems,
):
    chip, core = place()
    me = 2 * chip + core
    blocks = chips
    size = 2 * SEQ_DEV
    gathers = [Gather(chips, own_ref.at[m], rows.at[m], sems[6 * m : 6 * m + 6]) for m in range(MB)]
    parts = (out, back)
    scatters = [
        Scatter(
            chips,
            lambda to, k=k: parts[k].at[0, 2 * to + 1 - core],
            lambda to, k=k: parts[k].at[0, 2 * to + core],
            pairs[k], lines[k], sems[12 + 6 * k : 18 + 6 * k],
        )
        for k in range(2)
    ]
    loads = []
    for k in range(3):
        for e in range(EXP_DEV):
            loads.append(
                pltpu.make_async_copy(
                    routed_refs[k].at[e], weights.at[k, :, e * FF : (e + 1) * FF],
                    weight_sem.at[k, e],
                )
            )
        loads.append(
            pltpu.make_async_copy(
                shared_refs[k], weights.at[k, :, EXP_DEV * FF :], weight_sem.at[k, EXP_DEV]
            )
        )

    def grad_load(step):
        block = block_order(chip, step % blocks, chips)
        start = pl.multiple_of(block * size, size)
        return pltpu.make_async_copy(
            grad_ref.at[step // blocks, pl.ds(start, size), :], grads.at[step % 2],
            grad_sem.at[step % 2],
        )

    def stage_out(step, k):
        block = block_order(chip, step % blocks, chips)
        start = pl.multiple_of((step // blocks * blocks + block) * size, size)
        target = (hidden_ref, d_gate_ref, d_up_ref)[k]
        return pltpu.make_async_copy(
            stage.at[step % 2, k], target.at[pl.ds(start, size), :], stage_sem.at[step % 2, k]
        )

    def keep_out(step, k):
        block = block_order(chip, step % blocks, chips)
        target = (out_b_ref, back_b_ref)[k]
        return pltpu.make_async_copy(
            parts[k].at[1, pl.ds(2 * block, 2)], target.at[pl.ds(2 * block, 2)],
            keep_sem.at[k, step % blocks],
        )

    grad_load(0).start()
    for load in loads:
        load.start()
    own_copies = [
        pltpu.make_async_copy(own_ref.at[m], rows.at[m, me], local_sem.at[m]) for m in range(MB)
    ]
    for copy in own_copies:
        copy.start()
    meet(chips)
    gathers[0].start()
    for copy in own_copies:
        copy.wait()
    for load in loads:
        load.wait()

    def at(step, number, action):
        @pl.when(step == number)
        def _():
            action()

    def body(step, carry):
        micro_batch = step // blocks
        block = block_order(chip, step % blocks, chips)
        for m in range(MB):
            for hop in range(1, chips):
                at(step, m * blocks + hop, lambda m=m, hop=hop: gathers[m].hop(hop))
        at(step, 1, gathers[1].start)
        at(step, blocks, lambda: [s.start() for s in scatters])
        for turn in range(chips - 1):
            at(step, blocks + 1 + turn, lambda turn=turn: scatters[1].slot(turn))
        for m in range(MB):

            @pl.when(micro_batch == m)
            def _():
                gathers[m].take_pair(block - chip)

        grad_load(step).wait()

        @pl.when(step + 1 < MB * blocks)
        def _():
            grad_load(step + 1).start()

        @pl.when(step >= 2)
        def _():
            for k in range(3):
                stage_out(step - 2, k).wait()

        slot = step % 2
        normed = rows[micro_batch, pl.ds(2 * block, 2)].reshape(size, D)
        grad = grads[slot]
        logits = dot(normed, router_ref[...])
        named = named_ref[pl.ds(pl.multiple_of((micro_batch * blocks + block) * size, size), size), :]
        chosen = jnp.where(named > 0.0, logits, -1e30)
        powers = jnp.where(
            named > 0.0, jnp.exp(chosen - jnp.max(chosen, axis=1, keepdims=True)), 0.0
        )
        gates = powers / jnp.sum(powers, axis=1, keepdims=True)
        lane = lax.broadcasted_iota(jnp.int32, (size, LANES), 1)
        own = [
            jnp.sum(jnp.where(lane == EXP_DEV * me + e, gates, 0.0), axis=1, keepdims=True)
            for e in range(EXP_DEV)
        ]
        gate_grads = [jnp.zeros((size, 1), F32) for _ in range(EXP_DEV)]
        wide = weights.shape[2]
        for left in range(0, wide, 512):
            right = min(left + 512, wide)
            gate_part = dot(normed, weights[0, :, left:right])
            up_part = dot(normed, weights[1, :, left:right])
            down_part = dot(grad, weights[2, :, left:right])
            sigmoid = 1.0 / (1.0 + jnp.exp(-gate_part))
            act = gate_part * sigmoid
            hidden = act * up_part
            product = hidden * down_part
            scales = []
            for e in range(EXP_DEV + 1):
                low, high = max(left, e * FF), min(right, (e + 1) * FF)
                if low >= high:
                    continue
                if e < EXP_DEV:
                    gate_grads[e] += jnp.sum(
                        product[:, low - left : high - left], axis=1, keepdims=True
                    )
                    scales.append(jnp.broadcast_to(own[e], (size, high - low)))
                else:
                    scales.append(jnp.ones((size, high - low), F32))
            scale = scales[0] if len(scales) == 1 else jnp.concatenate(scales, axis=1)
            scaled = down_part * scale
            stage[slot, 0, :, left:right] = (hidden * scale).astype(BF)
            stage[slot, 1, :, left:right] = (
                scaled * up_part * (sigmoid + act * (1.0 - sigmoid))
            ).astype(BF)
            stage[slot, 2, :, left:right] = (scaled * act).astype(BF)
        for k in range(3):
            stage_out(step, k).start()
        for turn in range(chips - 1):
            at(step, blocks + turn, lambda turn=turn: scatters[0].slot(turn))
        result = dot_nt(stage[slot, 0], weights[2]).astype(BF)
        out[micro_batch, pl.ds(2 * block, 2)] = result.reshape(2, SEQ_DEV, D)
        result = (dot_nt(stage[slot, 1], weights[0]) + dot_nt(stage[slot, 2], weights[1])).astype(BF)
        back[micro_batch, pl.ds(2 * block, 2), :, :D] = result.reshape(2, SEQ_DEV, D)
        tail = jnp.zeros((size, LANES), F32)
        for e in range(EXP_DEV):
            high = gate_grads[e].astype(BF).astype(F32)
            tail = jnp.where(lane == EXP_DEV * me + e, high, tail)
            tail = jnp.where(lane == experts + EXP_DEV * me + e, gate_grads[e] - high, tail)
        back[micro_batch, pl.ds(2 * block, 2), :, D:] = tail.astype(BF).reshape(2, SEQ_DEV, LANES)

        @pl.when(micro_batch == 1)
        def _():
            for k in range(2):
                keep_out(step, k).start()

        return carry

    lax.fori_loop(0, MB * blocks, body, 0)
    last = MB * blocks
    row_copies = [
        pltpu.make_async_copy(rows.at[m], rows_ref.at[m], local_sem.at[m]) for m in range(MB)
    ]
    for copy in row_copies:
        copy.start()
    scatters[0].finish(out_a_ref)
    scatters[1].finish(back_a_ref)
    for m in range(MB):
        gathers[m].finish(False)
    for copy in row_copies:
        copy.wait()
    for step in (last - 2, last - 1):
        for k in range(3):
            stage_out(step, k).wait()
    for turn in range(blocks):
        for k in range(2):
            keep_out(blocks + turn, k).wait()


def expert_sums(
    chips,
    rows_ref, grads_ref, hidden_ref, d_gate_ref, d_up_ref, shared_h_ref, shared_g_ref, shared_u_ref, out_ref, back_ref,
    gate_ref, up_ref, down_ref, shared_ref, out_b_ref, back_b_ref,
    mine_out, mine_back, pairs, lines, local_sem, *sems,
):
    chip, core = place()
    step = pl.program_id(0) * (D // 256) + pl.program_id(1)
    parts, mine = (out_ref, back_ref), (mine_out, mine_back)
    scatters = [
        Scatter(
            chips,
            lambda to, k=k: parts[k].at[2 * to + 1 - core],
            lambda to, k=k: mine[k].at[to],
            pairs[k], lines[k], sems[6 * k : 6 * k + 6],
        )
        for k in range(2)
    ]

    def at(number, action):
        @pl.when(step == number)
        def _():
            action()

    def begin():
        loads = [
            pltpu.make_async_copy(
                parts[k].at[2 * to + core], mine[k].at[to], local_sem.at[k, to]
            )
            for k in range(2)
            for to in range(chips)
        ]
        for load in loads:
            load.start()
        meet(chips)
        for s in scatters:
            s.start()
        for load in loads:
            load.wait()

    at(0, begin)
    ticks = [(k, turn) for turn in range(chips - 1) for k in range(2)]
    for number, (k, turn) in enumerate(ticks):
        at(min(number + 1, 7), lambda k=k, turn=turn: scatters[k].slot(turn))
    normed, grad = rows_ref[...], grads_ref[...]
    gate_ref[0] = dot_tn(normed, d_gate_ref[...]).astype(BF)
    up_ref[0] = dot_tn(normed, d_up_ref[...]).astype(BF)
    down_ref[0] = dot_tn(grad, hidden_ref[...]).astype(BF)

    @pl.when(pl.program_id(0) == 0)
    def _():
        start = pl.ds(pl.multiple_of(pl.program_id(1) * 256, 256), 256)
        shared_ref[0, start, :] = dot_tn(normed, shared_g_ref[...])
        shared_ref[1, start, :] = dot_tn(normed, shared_u_ref[...])
        shared_ref[2, start, :] = dot_tn(grad, shared_h_ref[...])

    at(8, lambda: scatters[0].finish(out_b_ref))
    at(9, lambda: scatters[1].finish(back_b_ref))


def like(*shape, dtype=BF):
    return jax.ShapeDtypeStruct(shape, dtype)


IN_VMEM = pl.BlockSpec(memory_space=pltpu.VMEM)
ANYWHERE = pl.BlockSpec(memory_space=pl.ANY)


def experts_on_lines(two_own, grad_all, ids_all, expert_at, router_rows, routed, shared, share):
    devices = lax.axis_size("exp")
    me = lax.axis_index("exp")
    experts = expert_at.shape[0]
    chips = devices // 2
    length = SEQ_DEV * devices
    wide = EXP_DEV * FF + LANES
    own_shared = [
        jnp.pad(lax.dynamic_slice(w, (0, me * share), (D, share)), ((0, 0), (0, LANES - share)))
        for w in shared
    ]
    spare = jnp.full((LANES - experts,), -1, jnp.int32)
    columns = jnp.concatenate([expert_at.astype(jnp.int32), spare])
    named = jnp.any(ids_all[..., None] == columns, axis=2).astype(F32).reshape(MB * length, LANES)
    router = jnp.pad(router_rows, ((0, 0), (0, LANES - experts)))
    block_back = (devices, SEQ_DEV, D + LANES)
    block_out = (devices, SEQ_DEV, D)
    sems = [gather_sems(chips) for _ in range(MB)] + [scatter_sems(chips) for _ in range(2)]

    def call_rows(own, grad, names, router_in, *weights):
        def kernel(own_ref, grad_ref, named_ref, router_ref, *refs):
            expert_rows(
                chips, experts, own_ref, grad_ref, named_ref, router_ref, refs[:3], refs[3:6], *refs[6:]
            )

        return pl.pallas_call(
            kernel,
            out_shape=(
                like(MB, devices, SEQ_DEV, D),
                like(MB * length, wide),
                like(MB * length, wide),
                like(MB * length, wide),
                like(*block_out),
                like(*block_back),
                like(SEQ_DEV, D, dtype=F32),
                like(SEQ_DEV, D + LANES, dtype=F32),
            ),
            in_specs=[IN_VMEM, ANYWHERE, IN_VMEM, IN_VMEM] + [ANYWHERE] * 6,
            out_specs=(ANYWHERE,) * 6 + (IN_VMEM,) * 2,
            scratch_shapes=[
                pltpu.VMEM((3, D, wide), BF),
                pltpu.VMEM((MB, devices, SEQ_DEV, D), BF),
                pltpu.VMEM((2, 2 * SEQ_DEV, D), BF),
                pltpu.VMEM((2, 3, 2 * SEQ_DEV, wide), BF),
                pltpu.VMEM((MB, *block_out), BF),
                pltpu.VMEM((MB, *block_back), BF),
                (
                    pltpu.VMEM((chips, SEQ_DEV, D), BF),
                    pltpu.VMEM((chips, SEQ_DEV, D + LANES), BF),
                ),
                (
                    pltpu.VMEM((chips + 1, SEQ_DEV, D), BF),
                    pltpu.VMEM((chips + 1, SEQ_DEV, D + LANES), BF),
                ),
                pltpu.SemaphoreType.DMA((3, EXP_DEV + 1)),
                pltpu.SemaphoreType.DMA((MB,)),
                pltpu.SemaphoreType.DMA((2,)),
                pltpu.SemaphoreType.DMA((2, 3)),
                pltpu.SemaphoreType.DMA((2, chips)),
            ]
            + [sem for group in sems for sem in group],
            compiler_params=pltpu.CompilerParams(
                collective_id=1, has_side_effects=True, vmem_limit_bytes=VMEM_BYTES
            ),
            name="expert_rows",
        )(own, grad, names, router_in, *weights)

    rows, hidden, d_gate, d_up, out_b, back_b, out_sum_a, back_sum_a = call_rows(
        two_own, grad_all, named, router, *routed, *own_shared
    )
    flat = MB * length

    def call_sums(*operands):
        def kernel(*refs):
            expert_sums(chips, *refs)

        by_rows = pl.BlockSpec((flat, 256), lambda e, d: (0, d))
        by_expert = pl.BlockSpec((flat, FF), lambda e, d: (0, e))
        last = pl.BlockSpec((flat, LANES), lambda e, d: (0, EXP_DEV * FF // LANES))
        routed_out = pl.BlockSpec((1, 256, FF), lambda e, d: (e, d, 0))

        def whole(*shape):
            return pl.BlockSpec(shape, lambda e, d: (0,) * len(shape))

        return pl.pallas_call(
            kernel,
            grid=(EXP_DEV, D // 256),
            out_shape=(like(EXP_DEV, D, FF),) * 3
            + (
                like(3, D, LANES, dtype=F32),
                like(SEQ_DEV, D, dtype=F32),
                like(SEQ_DEV, D + LANES, dtype=F32),
            ),
            in_specs=[by_rows] * 2 + [by_expert] * 3 + [last] * 3 + [ANYWHERE] * 2,
            out_specs=(routed_out,) * 3
            + (whole(3, D, LANES), whole(SEQ_DEV, D), whole(SEQ_DEV, D + LANES)),
            scratch_shapes=[
                pltpu.VMEM((chips, SEQ_DEV, D), BF),
                pltpu.VMEM((chips, SEQ_DEV, D + LANES), BF),
                (
                    pltpu.VMEM((chips, SEQ_DEV, D), BF),
                    pltpu.VMEM((chips, SEQ_DEV, D + LANES), BF),
                ),
                (
                    pltpu.VMEM((chips + 1, SEQ_DEV, D), BF),
                    pltpu.VMEM((chips + 1, SEQ_DEV, D + LANES), BF),
                ),
                pltpu.SemaphoreType.DMA((2, chips)),
            ]
            + scatter_sems(chips) * 2,
            compiler_params=pltpu.CompilerParams(
                collective_id=2, has_side_effects=True, vmem_limit_bytes=VMEM_BYTES
            ),
            name="expert_sums",
        )(*operands)

    gate_sum, up_sum, down_sum, shared_sum, out_sum_b, back_sum_b = call_sums(
        rows.reshape(flat, D), grad_all.reshape(flat, D), hidden, d_gate, d_up, hidden, d_gate, d_up,
        out_b, back_b,
    )
    backs = (back_sum_a, back_sum_b)
    tails = [
        b[:, D : D + experts] + b[:, D + experts : D + 2 * experts] for b in backs
    ]
    shared_cols = jnp.concatenate([shared_sum[k, :, :share] for k in range(3)], axis=1)
    return (
        (out_sum_a, out_sum_b),
        [b[:, :D] for b in backs],
        tails,
        (gate_sum, up_sum, down_sum),
        shared_cols,
    )


def experts_plain(two_own, grad_all, ids_all, expert_at, router_rows, routed, shared, share):
    me = lax.axis_index("exp")
    used = EXP_DEV * FF + share
    padded = -(-used // LANES) * LANES
    length = grad_all.shape[1]

    def joined(weight, extra):
        own = lax.dynamic_slice(extra, (0, me * share), (D, share))
        blank = jnp.zeros((D, padded - used), BF)
        return jnp.concatenate([weight[i] for i in range(EXP_DEV)] + [own, blank], axis=1)

    gate_all, up_all, down_all = [joined(r, s) for r, s in zip(routed, shared)]
    column = jnp.arange(padded)
    all_rows, kept, outs, backs, tails = [], [], [], [], []
    for micro_batch in range(MB):
        two_all = gather_exp(two_own[micro_batch])
        all_rows.append(two_all)
        logits = dot(two_all, router_rows)
        named = jnp.any(ids_all[micro_batch][:, :, None] == expert_at[None, None, :], axis=1)
        gates = named_softmax(logits, named)
        own_gates = lax.dynamic_slice(gates, (0, me * EXP_DEV), (length, EXP_DEV))
        weight = jnp.where(
            column[None, :] < FF,
            own_gates[:, :1],
            jnp.where(column[None, :] < 2 * FF, own_gates[:, 1:], 1.0),
        )
        gate_part = dot(two_all, gate_all)
        up_part = dot(two_all, up_all)
        down_part = dot(grad_all[micro_batch], down_all)
        sigmoid = jax.nn.sigmoid(gate_part)
        act = gate_part * sigmoid
        hidden = act * up_part
        products = hidden * down_part
        own_grads = jnp.stack(
            [jnp.sum(products[:, i * FF : (i + 1) * FF], axis=1) for i in range(EXP_DEV)], axis=1
        )
        hidden_low = (weight * hidden).astype(BF)
        weighted = weight * down_part
        d_gate = (weighted * up_part * (sigmoid + act * (1.0 - sigmoid))).astype(BF)
        d_up = (weighted * act).astype(BF)
        kept.append((hidden_low, d_gate, d_up))
        outs.append(scatter_exp(dot_nt(hidden_low, down_all)))
        backs.append(scatter_exp(dot_nt(d_gate, gate_all) + dot_nt(d_up, up_all)))
        gate_grads = lax.all_gather(own_grads, "exp", axis=1, tiled=True)
        tails.append(
            lax.dynamic_slice(
                gate_grads, (me * SEQ_DEV, 0), (SEQ_DEV, gate_grads.shape[1])
            )
        )
    two_both = jnp.concatenate(all_rows)
    hidden_low, d_gate, d_up = [jnp.concatenate([k[i] for k in kept]) for i in range(3)]
    sums = (
        dot_tn(two_both, d_gate),
        dot_tn(two_both, d_up),
        dot_tn(grad_all.reshape(MB * length, D), hidden_low),
    )
    routed_sums = [
        jnp.stack([t[:, i * FF : (i + 1) * FF] for i in range(EXP_DEV)]).astype(BF) for t in sums
    ]
    shared_cols = jnp.concatenate([t[:, EXP_DEV * FF : used] for t in sums], axis=1)
    return outs, backs, tails, routed_sums, shared_cols


def named_softmax(logits, named):
    chosen = jnp.where(named, logits, -jnp.inf)
    powers = jnp.where(named, jnp.exp(chosen - jnp.max(chosen, axis=-1, keepdims=True)), 0.0)
    return powers / jnp.sum(powers, axis=-1, keepdims=True)


def on_device(
    tokens,
    cotangent,
    expert_ids,
    owner_table,
    w_query,
    w_key,
    w_value,
    w_out,
    gain_one,
    gain_two,
    w_router,
    shared_gate,
    shared_up,
    shared_down,
    routed_gate,
    routed_up,
    routed_down,
):
    devices = lax.axis_size("exp")
    groups = lax.axis_size("seq")
    me = lax.axis_index("exp")
    experts = owner_table.shape[0]
    length = SEQ_DEV * devices
    rows_out = D // devices
    slots = -(-HEADS // devices)
    wide = slots * HD
    share = FF // devices

    head_of = [jnp.minimum(me + slot * devices, HEADS - 1) for slot in range(slots)]
    slot_live = jnp.concatenate(
        [
            jnp.full((HD,), jnp.where(me + slot * devices < HEADS, 1.0, 0.0), F32)
            for slot in range(slots)
        ]
    )

    w_qkv = jnp.concatenate(
        [
            lax.dynamic_slice(weight, (0, head * HD), (D, HD))
            for head in head_of
            for weight in (w_query, w_key, w_value)
        ],
        axis=1,
    )
    w_out_heads = jnp.concatenate(
        [lax.dynamic_slice(w_out, (head * HD, 0), (HD, D)) for head in head_of], axis=0
    )
    cos_table, sin_table = angle_tables(jnp.arange(length).astype(F32))
    sin_table = jnp.where(jnp.arange(HD) < HD // 2, -sin_table, sin_table)
    params = pltpu.CompilerParams(vmem_limit_bytes=VMEM_BYTES)
    forward = pl.pallas_call(
        functools.partial(attend_forward, slots),
        out_shape=(
            like(length, D),
            like(length, 3 * wide),
            like(length, wide),
            like(slots, length, 1, dtype=F32),
        ),
        in_specs=[IN_VMEM] * 5,
        out_specs=(IN_VMEM,) * 4,
        compiler_params=params,
        name="attend_forward",
    )
    backward = pl.pallas_call(
        functools.partial(attend_backward, slots),
        out_shape=(like(wide, D, dtype=F32), like(D, 3 * wide, dtype=F32), like(length, D)),
        in_specs=[IN_VMEM] * 10,
        out_specs=(IN_VMEM,) * 3,
        scratch_shapes=[
            pltpu.VMEM((length, 3 * wide), BF),
            pltpu.VMEM((length, wide), BF),
            pltpu.VMEM((length, HD), F32),
            pltpu.VMEM((length, HD), F32),
        ],
        compiler_params=params,
        name="attend_backward",
    )

    expert_at = jnp.sum(
        (owner_table[:, None] == jnp.arange(experts)[None, :]) * jnp.arange(experts)[:, None],
        axis=0,
    )
    router_rows = jnp.take(w_router, expert_at, axis=1)
    ids_all = lax.all_gather(expert_ids[:, 0], "exp", axis=1, tiled=True)
    grad_all = lax.all_gather(cotangent[:, 0], "exp", axis=1, tiled=True)

    first = []
    for micro_batch in range(MB):
        rows_all = gather_exp(tokens[micro_batch, 0])
        normed, qkv, mixed, lse = forward(rows_all, gain_one[None], cos_table, sin_table, w_qkv)
        sent = lax.all_to_all(
            mixed.reshape(devices, SEQ_DEV, wide), "exp", split_axis=0, concat_axis=0, tiled=True
        )
        own_mixed = (
            sent.reshape(devices, SEQ_DEV, slots, HD)
            .transpose(1, 2, 0, 3)
            .reshape(SEQ_DEV, slots * devices * HD)[:, :D]
        )
        rows_in = tokens[micro_batch, 0].astype(F32)
        hidden_one = rows_in + dot(own_mixed, w_out)
        two_low = norm_rows(hidden_one, gain_two).astype(BF)
        logits = dot(two_low, router_rows)
        named = jnp.any(
            expert_ids[micro_batch, 0][:, :, None] == expert_at[None, None, :], axis=1
        )
        gates = named_softmax(logits, named)
        first.append((normed, qkv, mixed, lse, rows_in, hidden_one, two_low, gates))

    experts_of = experts_on_lines if devices <= 8 else experts_plain
    outs, backs, tails, routed_sums, shared_cols = experts_of(
        jnp.stack([f[6] for f in first]),
        grad_all,
        ids_all,
        expert_at,
        router_rows,
        (routed_gate, routed_up, routed_down),
        (shared_gate, shared_up, shared_down),
        share,
    )

    def routed_sum(parts):
        return lax.psum_scatter(parts, "seq", scatter_dimension=1, tiled=True).astype(F32)

    outputs_list = []
    grads_list = []
    small = jnp.zeros((D, experts + 2), F32)
    qkv_sum = jnp.zeros((D, 3 * wide), F32)
    out_sum = jnp.zeros((wide, D), F32)
    for micro_batch in range(MB):
        normed, qkv, mixed, lse, rows_in, hidden_one, two_low, gates = first[micro_batch]
        outputs_list.append((hidden_one + outs[micro_batch]).astype(BF))
        tail = tails[micro_batch]
        own_logits = (gates * (tail - jnp.sum(gates * tail, axis=-1, keepdims=True))).astype(BF)
        grad_two = backs[micro_batch] + dot_nt(own_logits, router_rows)
        back, gain_terms = norm_back(hidden_one, gain_two, grad_two)
        grad_hidden = cotangent[micro_batch, 0].astype(F32) + back
        router_part = dot_tn(two_low, own_logits)
        mix_all = gather_exp(grad_hidden.astype(BF))
        out_one, qkv_one, grad_part = backward(
            mix_all, normed, qkv, mixed, lse, cos_table, sin_table, w_qkv, w_out_heads, slot_live[None]
        )
        out_sum = out_sum + out_one
        qkv_sum = qkv_sum + qkv_one
        grad_normed = scatter_exp(grad_part)
        back_one, gain_one_terms = norm_back(rows_in, gain_one, grad_normed)
        grads_list.append((grad_hidden + back_one).astype(BF))
        small = small + jnp.concatenate(
            [
                router_part,
                jnp.sum(gain_one_terms, axis=0)[:, None],
                jnp.sum(gain_terms, axis=0)[:, None],
            ],
            axis=1,
        )

    def to_rows(columns):
        parts = columns.astype(BF).reshape(devices, rows_out, columns.shape[1])
        parts = lax.psum_scatter(parts, "seq", scatter_dimension=1, tiled=True)
        return lax.all_to_all(parts, "exp", split_axis=0, concat_axis=0, tiled=True)

    def to_all(rows):
        return lax.all_gather(rows, "seq", axis=0, tiled=True).astype(F32)

    piece = rows_out // groups
    shared_rows = to_rows(shared_cols).reshape(devices, piece, 3, share)
    shared_full = to_all(shared_rows.transpose(1, 2, 0, 3).reshape(piece, 3 * FF))
    qkv_rows = to_rows(qkv_sum).reshape(devices, piece, slots, 3, HD)
    qkv_rows = qkv_rows.transpose(1, 3, 2, 0, 4).reshape(piece, 3, slots * devices * HD)
    qkv_full = to_all(qkv_rows[:, :, :D].reshape(piece, 3 * D))
    out_part = lax.psum_scatter(out_sum.astype(BF), "seq", scatter_dimension=1, tiled=True)
    spread = jnp.zeros((slots * devices * HD, D // groups), BF)
    for slot in range(slots):
        spread = lax.dynamic_update_slice(
            spread, out_part[slot * HD : (slot + 1) * HD], ((me + slot * devices) * HD, 0)
        )
    out_rows = lax.psum_scatter(spread[:D], "exp", scatter_dimension=0, tiled=True)
    out_full = lax.all_gather(out_rows, "seq", axis=1, tiled=True).astype(F32)
    small_rows = lax.psum_scatter(
        lax.psum(small, "seq"), "exp", scatter_dimension=0, tiled=True
    )
    place_of = jnp.take(small_rows, owner_table, axis=1)
    return (
        jnp.stack(outputs_list)[:, None],
        jnp.stack(grads_list)[:, None],
        qkv_full[:, :D],
        qkv_full[:, D : 2 * D],
        qkv_full[:, 2 * D :],
        out_full,
        small_rows[:, experts],
        small_rows[:, experts + 1],
        place_of,
        shared_full[:, :FF],
        shared_full[:, FF : 2 * FF],
        shared_full[:, 2 * FF :],
        *(routed_sum(parts) for parts in routed_sums),
    )


def solution(mesh):
    rows = P(None, "seq", "exp", None)
    placed = (rows,) * 3 + (P(),) * 11 + (P("exp", None, None),) * 3
    wide = P("exp", None)
    return jax.shard_map(
        on_device,
        mesh=mesh,
        in_specs=placed,
        out_specs=(rows, rows, wide, wide, wide, wide, P("exp"), P("exp"))
        + (wide,) * 4
        + (P("exp", "seq", None),) * 3,
        check_vma=False,
    )
```

```python
import functools
import math

import jax
import jax.numpy as jnp
from jax import lax
from jax.experimental import pallas as pl
from jax.experimental.pallas import tpu as pltpu
from jax.sharding import PartitionSpec as P

D = 1280
HEADS = 10
HD = 128
FF = 896
TOP = 7
EXP_DEV = 2
MB = 2
SEQ_DEV = 128
LANES = 128
BLOCK = 256
VMEM_BYTES = 60 * 2**20

eps = 1e-06
BF = jnp.bfloat16
F32 = jnp.float32


def norm_rows(inputs, gain):
    return inputs * lax.rsqrt(jnp.mean(inputs * inputs, axis=-1, keepdims=True) + eps) * gain


def norm_back(inputs, gain, grad):
    scale = lax.rsqrt(jnp.mean(inputs * inputs, axis=-1, keepdims=True) + eps)
    unit = inputs * scale
    weighted = grad * gain
    back = scale * (weighted - unit * jnp.mean(weighted * unit, axis=-1, keepdims=True))
    return back, grad * unit


def angle_tables(positions):
    steps_half = jnp.arange(HD // 2).astype(positions.dtype)
    frequency = jnp.exp(steps_half * (-2.0 * math.log(10000.0) / HD))
    angles = positions[:, None] * frequency[None, :]
    angles = jnp.concatenate([angles, angles], axis=-1)
    return (jnp.cos(angles), jnp.sin(angles))


def dot(a, b):
    return jnp.dot(a, b, preferred_element_type=F32)


def dot_nt(a, b):
    return lax.dot_general(a, b, (((1,), (1,)), ((), ())), preferred_element_type=F32)


def dot_tn(a, b):
    return lax.dot_general(a, b, (((0,), (0,)), ((), ())), preferred_element_type=F32)


def gather_exp(array):
    return lax.all_gather(array, "exp", axis=0, tiled=True)


def scatter_exp(array):
    return lax.psum_scatter(array.astype(BF), "exp", scatter_dimension=0, tiled=True).astype(F32)


def turn(heads, cos_table, sin_table):
    return heads * cos_table + pltpu.roll(heads, HD // 2, 1) * sin_table


def visible_scores(queries, keys, start):
    scores = dot_nt(queries, keys) * HD ** (-0.5)
    rows = queries.shape[0]
    row = lax.broadcasted_iota(jnp.int32, (rows, rows), 0)
    column = lax.broadcasted_iota(jnp.int32, (rows, rows), 1)
    last = jnp.where(row >= column, scores[:, start:], -1e30)
    return last if start == 0 else jnp.concatenate([scores[:, :start], last], axis=1)


def attend_forward(slots, rows_ref, gain_ref, cos_ref, sin_ref, w_ref, normed_ref, qkv_ref, mixed_ref, lse_ref):
    length = rows_ref.shape[0]
    step = BLOCK if length <= 2048 else BLOCK // 2

    def project(i, carry):
        part = pl.ds(pl.multiple_of(i * step, step), step)
        normed = norm_rows(rows_ref[part, :].astype(F32), gain_ref[...]).astype(BF)
        normed_ref[part, :] = normed
        for slot in range(slots):
            base = 3 * HD * slot
            qkv = dot(normed, w_ref[:, base : base + 3 * HD])
            for j in range(2):
                turned = turn(qkv[:, j * HD : (j + 1) * HD], cos_ref[part, :], sin_ref[part, :])
                qkv_ref[part, base + j * HD : base + (j + 1) * HD] = turned.astype(BF)
            qkv_ref[part, base + 2 * HD : base + 3 * HD] = qkv[:, 2 * HD :].astype(BF)
        return carry

    lax.fori_loop(0, length // step, project, 0)
    for slot in range(slots):
        base = 3 * HD * slot
        for start in range(0, length, step):
            stop = start + step
            scores = visible_scores(
                qkv_ref[start:stop, base : base + HD], qkv_ref[:stop, base + HD : base + 2 * HD], start
            )
            largest = jnp.max(scores, axis=-1, keepdims=True)
            powers = jnp.exp(scores - largest)
            total = jnp.sum(powers, axis=-1, keepdims=True)
            attention = (powers * (1.0 / total)).astype(BF)
            mixed = dot(attention, qkv_ref[:stop, base + 2 * HD : base + 3 * HD])
            mixed_ref[start:stop, slot * HD : (slot + 1) * HD] = mixed.astype(BF)
            lse_ref[slot, start:stop, :] = largest + jnp.log(total)


def attend_backward(
    slots, mix_ref, normed_ref, qkv_ref, mixed_ref, lse_ref, cos_ref, sin_ref, w_ref, w_out_ref, live_ref,
    out_sum_ref, qkv_sum_ref, grad_ref, raw_ref, d_mixed_ref, d_keys_ref, d_values_ref,
):
    length = mix_ref.shape[0]
    step = BLOCK if length <= 2048 else BLOCK // 2
    factor = HD ** (-0.5)

    def project(i, carry):
        part = pl.ds(pl.multiple_of(i * step, step), step)
        d_mixed_ref[part, :] = (dot_nt(mix_ref[part, :], w_out_ref[...]) * live_ref[...]).astype(BF)
        return carry

    lax.fori_loop(0, length // step, project, 0)
    for slot in range(slots):
        base = 3 * HD * slot
        d_keys_ref[...] = jnp.zeros_like(d_keys_ref)
        d_values_ref[...] = jnp.zeros_like(d_values_ref)
        for start in range(0, length, step):
            stop = start + step
            queries = qkv_ref[start:stop, base : base + HD]
            keys = qkv_ref[:stop, base + HD : base + 2 * HD]
            values = qkv_ref[:stop, base + 2 * HD : base + 3 * HD]
            d_mixed = d_mixed_ref[start:stop, slot * HD : (slot + 1) * HD]
            attention = jnp.exp(visible_scores(queries, keys, start) - lse_ref[slot, start:stop, :])
            d_att = dot_nt(d_mixed, values)
            row_term = jnp.sum(attention * d_att, axis=-1, keepdims=True)
            d_scores = (attention * (d_att - row_term)).astype(BF)
            d_queries = dot(d_scores, keys) * factor
            raw = turn(d_queries, cos_ref[start:stop, :], -sin_ref[start:stop, :])
            raw_ref[start:stop, base : base + HD] = raw.astype(BF)
            d_keys_ref[:stop, :] += dot_tn(d_scores, queries)
            d_values_ref[:stop, :] += dot_tn(attention.astype(BF), d_mixed)
        raw = turn(d_keys_ref[...] * factor, cos_ref[...], -sin_ref[...])
        raw_ref[:, base + HD : base + 2 * HD] = raw.astype(BF)
        raw_ref[:, base + 2 * HD : base + 3 * HD] = d_values_ref[...].astype(BF)

    def give(i, carry):
        part = pl.ds(pl.multiple_of(i * step, step), step)
        grad_ref[part, :] = dot_nt(raw_ref[part, :], w_ref[...]).astype(BF)
        return carry

    lax.fori_loop(0, length // step, give, 0)
    out_sum_ref[...] = dot_tn(mixed_ref[...], mix_ref[...])

    def sums(i, carry):
        part = pl.ds(pl.multiple_of(i * 256, 256), 256)
        qkv_sum_ref[part, :] = dot_tn(normed_ref[:, part], raw_ref[...])
        return carry

    lax.fori_loop(0, D // 256, sums, 0)


MESH = pl.DeviceIdType.MESH


def place():
    me = lax.axis_index("exp")
    return me // 2, me % 2


def remote(source, target, send_sem, recv_sem, chip, core):
    return pltpu.make_async_remote_copy(
        src_ref=source,
        dst_ref=target,
        send_sem=send_sem,
        recv_sem=recv_sem,
        device_id={"exp": 2 * chip + core},
        device_id_type=MESH,
    )


def meet(chips):
    chip, core = place()
    barrier = pltpu.get_barrier_semaphore()

    def greet(to_chip, to_core):
        pl.semaphore_signal(
            barrier, inc=1, device_id={"exp": 2 * to_chip + to_core}, device_id_type=MESH
        )

    greet(chip, 1 - core)

    @pl.when(chip < chips - 1)
    def _():
        greet(chip + 1, core)

    @pl.when(chip > 0)
    def _():
        greet(chip - 1, core)

    below = (chip + chips - 1) // chips
    above = (2 * chips - 2 - chip) // chips
    pl.semaphore_wait(barrier, 1 + below + above)


def gather_sems(chips):
    return [pltpu.SemaphoreType.DMA((chips,))] * 4 + [pltpu.SemaphoreType.DMA((2 * chips,))] * 2


class Gather:
    def __init__(self, chips, own, blocks, sems):
        self.chips, self.own, self.blocks = chips, own, blocks
        self.up_send, self.up_recv, self.down_send, self.down_recv = sems[:4]
        self.pair_send, self.pair_recv = sems[4:]

    def _source(self, hop, number):
        return self.own if hop == 0 else self.blocks.at[number]

    def _up(self, hop):
        chip, core = place()
        number = 2 * (chip - hop) + core
        return remote(
            self._source(hop, number), self.blocks.at[number],
            self.up_send.at[hop], self.up_recv.at[hop], chip + 1, core,
        )

    def _down(self, hop):
        chip, core = place()
        number = 2 * (chip + hop) + core
        return remote(
            self._source(hop, number), self.blocks.at[number],
            self.down_send.at[hop], self.down_recv.at[hop], chip - 1, core,
        )

    def _pair(self, away):
        chip, core = place()
        number = 2 * (chip + away) + core
        source = self.own if isinstance(away, int) and away == 0 else self.blocks.at[number]
        slot = away + self.chips
        return remote(
            source, self.blocks.at[number], self.pair_send.at[slot], self.pair_recv.at[slot],
            chip, 1 - core,
        )

    def _from_pair(self, away):
        chip, core = place()
        block = self.blocks.at[2 * (chip + away) + 1 - core]
        slot = away + self.chips
        return remote(
            block, block, self.pair_send.at[slot], self.pair_recv.at[slot], chip, 1 - core
        )

    def start(self):
        chip, _ = place()

        @pl.when(chip < self.chips - 1)
        def _():
            self._up(0).start()

        @pl.when(chip > 0)
        def _():
            self._down(0).start()

        self._pair(0).start()

    def hop(self, hop):
        chip, core = place()

        @pl.when(chip >= hop)
        def _():
            block = self.blocks.at[2 * (chip - hop) + core]
            remote(
                block, block, self.up_send.at[hop - 1], self.up_recv.at[hop - 1], chip, 1 - core
            ).wait_recv()

            @pl.when(chip < self.chips - 1)
            def _():
                self._up(hop).start()

            self._pair(-hop).start()

        @pl.when(chip + hop < self.chips)
        def _():
            block = self.blocks.at[2 * (chip + hop) + core]
            remote(
                block, block, self.down_send.at[hop - 1], self.down_recv.at[hop - 1], chip, 1 - core
            ).wait_recv()

            @pl.when(chip > 0)
            def _():
                self._down(hop).start()

            self._pair(hop).start()

    def take_pair(self, away):
        self._from_pair(away).wait_recv()

    def finish(self, pairs):
        chip, _ = place()
        for away in range(-self.chips + 1, self.chips):

            @pl.when(jnp.logical_and(chip + away >= 0, chip + away < self.chips))
            def _():
                if pairs:
                    self._from_pair(away).wait_recv()
                self._pair(away).wait_send()

        for hop in range(self.chips):

            @pl.when(jnp.logical_and(chip >= hop, chip < self.chips - 1))
            def _():
                self._up(hop).wait_send()

            @pl.when(jnp.logical_and(chip + hop < self.chips, chip > 0))
            def _():
                self._down(hop).wait_send()


def scatter_sems(chips):
    return [pltpu.SemaphoreType.DMA((chips,))] * 6


class Scatter:
    def __init__(self, chips, theirs, mine, pair, line, sems):
        self.chips, self.theirs, self.mine, self.pair, self.line = chips, theirs, mine, pair, line
        self.pair_send, self.pair_recv, self.up_send, self.up_recv = sems[:4]
        self.down_send, self.down_recv = sems[4:]

    def _pair(self, to):
        chip, core = place()
        return remote(
            self.theirs(to), self.pair.at[to], self.pair_send.at[to], self.pair_recv.at[to],
            chip, 1 - core,
        )

    def _up(self, chip, to):
        return remote(
            self.mine(to), self.line.at[to - chip - 1], self.up_send.at[to], self.up_recv.at[to],
            chip + 1, place()[1],
        )

    def _down(self, chip, to):
        return remote(
            self.mine(to), self.line.at[self.chips - chip + 1 + to],
            self.down_send.at[to], self.down_recv.at[to], chip - 1, place()[1],
        )

    def _arrived_up(self, to):
        chip, core = place()
        block = self.line.at[to - chip]
        remote(block, block, self.up_send.at[to], self.up_recv.at[to], chip, 1 - core).wait_recv()
        return block[...].astype(F32)

    def _arrived_down(self, to):
        chip, core = place()
        block = self.line.at[self.chips - chip + to]
        remote(
            block, block, self.down_send.at[to], self.down_recv.at[to], chip, 1 - core
        ).wait_recv()
        return block[...].astype(F32)

    def _both(self, to):
        chip, core = place()
        block = self.pair.at[to]
        remote(
            block, block, self.pair_send.at[to], self.pair_recv.at[to], chip, 1 - core
        ).wait_recv()
        return self.mine(to)[...].astype(F32) + block[...].astype(F32)

    def start(self):
        for to in range(self.chips):
            self._pair(to).start()

    def slot(self, turn):
        chip, _ = place()
        last = self.chips - 1

        @pl.when(chip <= turn)
        def _():
            to = last - turn + chip
            total = self._both(to)

            @pl.when(chip == 0)
            def _():
                self.mine(to)[...] = total.astype(BF)

            @pl.when(chip > 0)
            def _():
                self.mine(to)[...] = (total + self._arrived_up(to)).astype(BF)

            self._up(chip, to).start()

        @pl.when(last - chip <= turn)
        def _():
            to = turn - last + chip
            total = self._both(to)

            @pl.when(chip == last)
            def _():
                self.mine(to)[...] = total.astype(BF)

            @pl.when(chip < last)
            def _():
                self.mine(to)[...] = (total + self._arrived_down(to)).astype(BF)

            self._down(chip, to).start()

    def finish(self, result):
        chip, _ = place()
        last = self.chips - 1
        result[...] = self._both(chip)

        @pl.when(chip > 0)
        def _():
            result[...] += self._arrived_up(chip)

        @pl.when(chip < last)
        def _():
            result[...] += self._arrived_down(chip)

        for to in range(self.chips):
            self._pair(to).wait_send()

            @pl.when(to > chip)
            def _():
                self._up(chip, to).wait_send()

            @pl.when(to < chip)
            def _():
                self._down(chip, to).wait_send()


def part_of(array, index):
    return array.at[index]


def block_order(chip, turn, chips):
    number, bit = 0, 1
    while bit < chips:
        number = number + bit * ((chip // bit + turn // bit) % 2)
        bit = 2 * bit
    return number


def expert_rows(
    chips, experts,
    own_ref, grad_ref, named_ref, router_ref, routed_refs, shared_refs,
    rows_ref, hidden_ref, d_gate_ref, d_up_ref, out_b_ref, back_b_ref, out_a_ref, back_a_ref,
    weights, rows, grads, stage, out, back, pairs, lines, weight_sem, local_sem, grad_sem, stage_sem, keep_sem,
    *sems,
):
    chip, core = place()
    me = 2 * chip + core
    blocks = chips
    size = 2 * SEQ_DEV
    gathers = [Gather(chips, own_ref.at[m], rows.at[m], sems[6 * m : 6 * m + 6]) for m in range(MB)]
    parts = (out, back)
    scatters = [
        Scatter(
            chips,
            lambda to, k=k: parts[k].at[0, 2 * to + 1 - core],
            lambda to, k=k: parts[k].at[0, 2 * to + core],
            pairs[k], lines[k], sems[12 + 6 * k : 18 + 6 * k],
        )
        for k in range(2)
    ]
    loads = []
    for k in range(3):
        for e in range(EXP_DEV):
            loads.append(
                pltpu.make_async_copy(
                    routed_refs[k].at[e], weights.at[k, :, e * FF : (e + 1) * FF],
                    weight_sem.at[k, e],
                )
            )
        loads.append(
            pltpu.make_async_copy(
                shared_refs[k], weights.at[k, :, EXP_DEV * FF :], weight_sem.at[k, EXP_DEV]
            )
        )

    def grad_load(step):
        block = block_order(chip, step % blocks, chips)
        start = pl.multiple_of(block * size, size)
        return pltpu.make_async_copy(
            grad_ref.at[step // blocks, pl.ds(start, size), :], grads.at[step % 2],
            grad_sem.at[step % 2],
        )

    def stage_out(step, k):
        block = block_order(chip, step % blocks, chips)
        start = pl.multiple_of((step // blocks * blocks + block) * size, size)
        target = (hidden_ref, d_gate_ref, d_up_ref)[k]
        return pltpu.make_async_copy(
            stage.at[step % 2, k], target.at[pl.ds(start, size), :], stage_sem.at[step % 2, k]
        )

    def keep_out(step, k):
        block = block_order(chip, step % blocks, chips)
        target = (out_b_ref, back_b_ref)[k]
        return pltpu.make_async_copy(
            parts[k].at[1, pl.ds(2 * block, 2)], target.at[pl.ds(2 * block, 2)],
            keep_sem.at[k, step % blocks],
        )

    grad_load(0).start()
    for load in loads:
        load.start()
    own_copies = [
        pltpu.make_async_copy(own_ref.at[m], rows.at[m, me], local_sem.at[m]) for m in range(MB)
    ]
    for copy in own_copies:
        copy.start()
    meet(chips)
    gathers[0].start()
    for copy in own_copies:
        copy.wait()
    for load in loads:
        load.wait()

    def at(step, number, action):
        @pl.when(step == number)
        def _():
            action()

    def body(step, carry):
        micro_batch = step // blocks
        block = block_order(chip, step % blocks, chips)
        for m in range(MB):
            for hop in range(1, chips):
                at(step, m * blocks + hop, lambda m=m, hop=hop: gathers[m].hop(hop))
        at(step, 1, gathers[1].start)
        at(step, blocks, lambda: [s.start() for s in scatters])
        for turn in range(chips - 1):
            at(step, blocks + 1 + turn, lambda turn=turn: scatters[1].slot(turn))
        for m in range(MB):

            @pl.when(micro_batch == m)
            def _():
                gathers[m].take_pair(block - chip)

        grad_load(step).wait()

        @pl.when(step + 1 < MB * blocks)
        def _():
            grad_load(step + 1).start()

        @pl.when(step >= 2)
        def _():
            for k in range(3):
                stage_out(step - 2, k).wait()

        slot = step % 2
        normed = rows[micro_batch, pl.ds(2 * block, 2)].reshape(size, D)
        grad = grads[slot]
        logits = dot(normed, router_ref[...])
        named = named_ref[pl.ds(pl.multiple_of((micro_batch * blocks + block) * size, size), size), :]
        chosen = jnp.where(named > 0.0, logits, -1e30)
        powers = jnp.where(
            named > 0.0, jnp.exp(chosen - jnp.max(chosen, axis=1, keepdims=True)), 0.0
        )
        gates = powers / jnp.sum(powers, axis=1, keepdims=True)
        lane = lax.broadcasted_iota(jnp.int32, (size, LANES), 1)
        own = [
            jnp.sum(jnp.where(lane == EXP_DEV * me + e, gates, 0.0), axis=1, keepdims=True)
            for e in range(EXP_DEV)
        ]
        gate_grads = [jnp.zeros((size, 1), F32) for _ in range(EXP_DEV)]
        wide = weights.shape[2]
        for left in range(0, wide, 512):
            right = min(left + 512, wide)
            gate_part = dot(normed, weights[0, :, left:right])
            up_part = dot(normed, weights[1, :, left:right])
            down_part = dot(grad, weights[2, :, left:right])
            sigmoid = 1.0 / (1.0 + jnp.exp(-gate_part))
            act = gate_part * sigmoid
            hidden = act * up_part
            product = hidden * down_part
            scales = []
            for e in range(EXP_DEV + 1):
                low, high = max(left, e * FF), min(right, (e + 1) * FF)
                if low >= high:
                    continue
                if e < EXP_DEV:
                    gate_grads[e] += jnp.sum(
                        product[:, low - left : high - left], axis=1, keepdims=True
                    )
                    scales.append(jnp.broadcast_to(own[e], (size, high - low)))
                else:
                    scales.append(jnp.ones((size, high - low), F32))
            scale = scales[0] if len(scales) == 1 else jnp.concatenate(scales, axis=1)
            scaled = down_part * scale
            stage[slot, 0, :, left:right] = (hidden * scale).astype(BF)
            stage[slot, 1, :, left:right] = (
                scaled * up_part * (sigmoid + act * (1.0 - sigmoid))
            ).astype(BF)
            stage[slot, 2, :, left:right] = (scaled * act).astype(BF)
        for k in range(3):
            stage_out(step, k).start()
        for turn in range(chips - 1):
            at(step, blocks + turn, lambda turn=turn: scatters[0].slot(turn))
        result = dot_nt(stage[slot, 0], weights[2]).astype(BF)
        out[micro_batch, pl.ds(2 * block, 2)] = result.reshape(2, SEQ_DEV, D)
        result = (dot_nt(stage[slot, 1], weights[0]) + dot_nt(stage[slot, 2], weights[1])).astype(BF)
        back[micro_batch, pl.ds(2 * block, 2), :, :D] = result.reshape(2, SEQ_DEV, D)
        tail = jnp.zeros((size, LANES), F32)
        for e in range(EXP_DEV):
            high = gate_grads[e].astype(BF).astype(F32)
            tail = jnp.where(lane == EXP_DEV * me + e, high, tail)
            tail = jnp.where(lane == experts + EXP_DEV * me + e, gate_grads[e] - high, tail)
        back[micro_batch, pl.ds(2 * block, 2), :, D:] = tail.astype(BF).reshape(2, SEQ_DEV, LANES)

        @pl.when(micro_batch == 1)
        def _():
            for k in range(2):
                keep_out(step, k).start()

        return carry

    lax.fori_loop(0, MB * blocks, body, 0)
    last = MB * blocks
    row_copies = [
        pltpu.make_async_copy(rows.at[m], rows_ref.at[m], local_sem.at[m]) for m in range(MB)
    ]
    for copy in row_copies:
        copy.start()
    scatters[0].finish(out_a_ref)
    scatters[1].finish(back_a_ref)
    for m in range(MB):
        gathers[m].finish(False)
    for copy in row_copies:
        copy.wait()
    for step in (last - 2, last - 1):
        for k in range(3):
            stage_out(step, k).wait()
    for turn in range(blocks):
        for k in range(2):
            keep_out(blocks + turn, k).wait()


def expert_sums(
    chips,
    rows_ref, grads_ref, hidden_ref, d_gate_ref, d_up_ref, shared_h_ref, shared_g_ref, shared_u_ref, out_ref, back_ref,
    gate_ref, up_ref, down_ref, shared_ref, out_b_ref, back_b_ref,
    mine_out, mine_back, pairs, lines, local_sem, *sems,
):
    chip, core = place()
    step = pl.program_id(0) * (D // 256) + pl.program_id(1)
    parts, mine = (out_ref, back_ref), (mine_out, mine_back)
    scatters = [
        Scatter(
            chips,
            lambda to, k=k: parts[k].at[2 * to + 1 - core],
            lambda to, k=k: mine[k].at[to],
            pairs[k], lines[k], sems[6 * k : 6 * k + 6],
        )
        for k in range(2)
    ]

    def at(number, action):
        @pl.when(step == number)
        def _():
            action()

    def begin():
        loads = [
            pltpu.make_async_copy(
                parts[k].at[2 * to + core], mine[k].at[to], local_sem.at[k, to]
            )
            for k in range(2)
            for to in range(chips)
        ]
        for load in loads:
            load.start()
        meet(chips)
        for s in scatters:
            s.start()
        for load in loads:
            load.wait()

    at(0, begin)
    ticks = [(k, turn) for turn in range(chips - 1) for k in range(2)]
    for number, (k, turn) in enumerate(ticks):
        at(min(number + 1, 7), lambda k=k, turn=turn: scatters[k].slot(turn))
    normed, grad = rows_ref[...], grads_ref[...]
    gate_ref[0] = dot_tn(normed, d_gate_ref[...]).astype(BF)
    up_ref[0] = dot_tn(normed, d_up_ref[...]).astype(BF)
    down_ref[0] = dot_tn(grad, hidden_ref[...]).astype(BF)

    @pl.when(pl.program_id(0) == 0)
    def _():
        start = pl.ds(pl.multiple_of(pl.program_id(1) * 256, 256), 256)
        shared_ref[0, start, :] = dot_tn(normed, shared_g_ref[...]).astype(BF)
        shared_ref[1, start, :] = dot_tn(normed, shared_u_ref[...]).astype(BF)
        shared_ref[2, start, :] = dot_tn(grad, shared_h_ref[...]).astype(BF)

    at(8, lambda: scatters[0].finish(out_b_ref))
    at(9, lambda: scatters[1].finish(back_b_ref))


def meet_all(axes):
    barrier = pltpu.get_barrier_semaphore()
    count = 0
    for axis in axes:
        size = lax.axis_size(axis)
        for away in range(1, size):
            other = (lax.axis_index(axis) + away) % size
            pl.semaphore_signal(barrier, inc=1, device_id={axis: other}, device_id_type=MESH)
            count += 1
    pl.semaphore_wait(barrier, count)


def heads_backward(
    chips, slots,
    own_ref, qkv_ref, mixed_ref, normed_ref, lse_ref, cos_ref, sin_ref, w_ref,
    sums_ref, grad_a_ref, grad_b_ref,
    d_mixed, probs, raw, parts, d_keys, d_values, pairs, lines, local_sem, send_sem, recv_sem, *sems,
):
    devices = 2 * chips
    me = lax.axis_index("exp")
    core = me % 2
    length = SEQ_DEV * devices
    step = BLOCK
    factor = HD ** (-0.5)
    scatters = [
        Scatter(
            chips,
            lambda to, m=m: parts.at[m, 2 * to + 1 - core],
            lambda to, m=m: parts.at[m, 2 * to + core],
            pairs.at[m], lines.at[m], sems[6 * m : 6 * m + 6],
        )
        for m in range(MB)
    ]

    def block_at(m, device, slot):
        rows = pl.ds(pl.multiple_of(device * SEQ_DEV, SEQ_DEV), SEQ_DEV)
        return d_mixed.at[m, rows, slot * HD : (slot + 1) * HD]

    def columns(m, head):
        return own_ref.at[m, :, pl.ds(pl.multiple_of(head * HD, HD), HD)]

    def exchange(m, away, slot):
        other = (me + away) % devices
        return pltpu.make_async_remote_copy(
            src_ref=columns(m, other + slot * devices),
            dst_ref=block_at(m, me, slot),
            send_sem=send_sem.at[m, away, slot],
            recv_sem=recv_sem.at[m, away, slot],
            device_id={"exp": other},
            device_id_type=MESH,
        )

    def arrival(m, away, slot):
        block = block_at(m, (me + devices - away) % devices, slot)
        return pltpu.make_async_remote_copy(
            src_ref=block,
            dst_ref=block,
            send_sem=send_sem.at[m, away, slot],
            recv_sem=recv_sem.at[m, away, slot],
            device_id={"exp": (me + away) % devices},
            device_id_type=MESH,
        )

    def keep(m, slot):
        return pltpu.make_async_copy(
            columns(m, me + slot * devices), block_at(m, me, slot), local_sem.at[m, slot]
        )

    meet_all(("exp",))
    for m in range(MB):
        for away in range(1, devices):
            for slot in range(slots):

                @pl.when((me + away) % devices + slot * devices < HEADS)
                def _():
                    exchange(m, away, slot).start()

        for slot in range(slots):

            @pl.when(me + slot * devices < HEADS)
            def _():
                keep(m, slot).start()

            @pl.when(me + slot * devices >= HEADS)
            def _():
                d_mixed[m, :, slot * HD : (slot + 1) * HD] = jnp.zeros((length, HD), BF)

    def weigh(m, carry):
        for slot in range(slots):
            base = 3 * HD * slot
            for start in range(0, length, step):
                stop = start + step
                scores = visible_scores(
                    qkv_ref[m, start:stop, base : base + HD],
                    qkv_ref[m, :stop, base + HD : base + 2 * HD],
                    start,
                )
                probs[m, slot, start:stop, :stop] = jnp.exp(
                    scores - lse_ref[m, slot, start:stop, :]
                ).astype(BF)
        return carry

    lax.fori_loop(0, MB, weigh, 0)

    def body(m, carry):
        for number in range(MB):

            @pl.when(m == number)
            def _():
                for slot in range(slots):

                    @pl.when(me + slot * devices < HEADS)
                    def _():
                        keep(number, slot).wait()
                        for away in range(1, devices):
                            arrival(number, away, slot).wait_recv()

        @pl.when(m == 1)
        def _():
            scatters[0].start()

        for slot in range(slots):
            base = 3 * HD * slot
            d_keys[...] = jnp.zeros_like(d_keys)
            d_values[...] = jnp.zeros_like(d_values)
            for start in range(0, length, step):
                stop = start + step
                queries = qkv_ref[m, start:stop, base : base + HD]
                keys = qkv_ref[m, :stop, base + HD : base + 2 * HD]
                values = qkv_ref[m, :stop, base + 2 * HD : base + 3 * HD]
                d_mix = d_mixed[m, start:stop, slot * HD : (slot + 1) * HD]
                mixed = mixed_ref[m, start:stop, slot * HD : (slot + 1) * HD]
                row_term = jnp.sum(d_mix.astype(F32) * mixed.astype(F32), axis=1, keepdims=True)
                attention = probs[m, slot, start:stop, :stop]
                d_scores = (attention.astype(F32) * (dot_nt(d_mix, values) - row_term)).astype(BF)
                turned = turn(dot(d_scores, keys) * factor, cos_ref[start:stop, :], -sin_ref[start:stop, :])
                raw[m, start:stop, base : base + HD] = turned.astype(BF)
                d_keys[:stop, :] += dot_tn(d_scores, queries)
                d_values[:stop, :] += dot_tn(attention, d_mix)
            turned = turn(d_keys[...] * factor, cos_ref[...], -sin_ref[...])
            raw[m, :, base + HD : base + 2 * HD] = turned.astype(BF)
            raw[m, :, base + 2 * HD : base + 3 * HD] = d_values[...].astype(BF)

            @pl.when(m == 1)
            def _():
                scatters[0].slot(min(slot, chips - 2))

        for start in range(0, length, step):
            back = dot_nt(raw[m, start : start + step, :], w_ref[...]).astype(BF)
            first = start // SEQ_DEV
            parts[m, first : first + step // SEQ_DEV] = back.reshape(step // SEQ_DEV, SEQ_DEV, D)
        return carry

    lax.fori_loop(0, MB, body, 0)
    scatters[1].start()
    for turn_ in range(min(slots, chips - 1), chips - 1):
        scatters[0].slot(turn_)
    both = raw.reshape(MB * length, 3 * slots * HD)
    rows = normed_ref.reshape(MB * length, D)
    ticks = [lambda: scatters[0].finish(grad_a_ref)]
    ticks = [lambda t=t: scatters[1].slot(t) for t in range(chips - 1)]
    for number, left in enumerate(range(0, D, 256)):
        total = dot_tn(rows[:, left : left + 256], both[...])
        for unit in range(3 * slots):
            sums_ref[unit, left : left + 256, :] = total[:, unit * HD : (unit + 1) * HD].astype(BF)
        if number < len(ticks):
            ticks[number]()
    scatters[0].finish(grad_a_ref)
    for number in range(D // 256, len(ticks)):
        ticks[number]()
    scatters[1].finish(grad_b_ref)
    for m in range(MB):
        for away in range(1, devices):
            for slot in range(slots):

                @pl.when((me + away) % devices + slot * devices < HEADS)
                def _():
                    exchange(m, away, slot).wait_send()


def spread_sums(
    chips,
    qkv_ref, shared_ref, mixed_ref, mix_ref, small_ref,
    attn_out, shared_out, small_out,
    arrived, summed, held, part, out_low, out_arrived, result, pair, line,
    first_send, first_recv, local_sem, second_send, second_recv, out_send, out_recv, third_send, third_recv,
    *sems,
):
    devices = 2 * chips
    group, me = lax.axis_index("seq"), lax.axis_index("exp")
    core = me % 2
    groups = 4
    rows = D // devices
    kinds = groups - 1
    far = D + LANES

    def row_block(device):
        return pl.ds(pl.multiple_of(device * rows, 32), rows)

    scatter = Scatter(
        chips,
        lambda to: part.at[row_block(2 * to + 1 - core)],
        lambda to: part.at[row_block(2 * to + core)],
        pair, line, sems,
    )

    def unit(owner, k):
        return shared_ref.at[owner] if k == 1 else qkv_ref.at[owner + kinds * (k // 2)]

    def lives(k, device):
        return device + (k // 2) * devices < HEADS

    def seq_copy(source, target, send, recv, away):
        return pltpu.make_async_remote_copy(
            src_ref=source, dst_ref=target, send_sem=send, recv_sem=recv,
            device_id={"seq": (group + away) % groups}, device_id_type=MESH,
        )

    def first(away, k):
        owner = (group + away) % groups
        return seq_copy(
            unit(owner, k), arrived.at[away - 1, k], first_send.at[away - 1, k],
            first_recv.at[away - 1, k], away,
        )

    def first_in(away, k):
        block = arrived.at[away - 1, k]
        return seq_copy(
            block, block, first_send.at[away - 1, k], first_recv.at[away - 1, k], away
        )

    def column_block(device, k):
        return pl.ds(pl.multiple_of((k * devices + device) * HD, HD), HD)

    def second(away, k):
        other = (me + away) % devices
        return pltpu.make_async_remote_copy(
            src_ref=summed.at[k, row_block(other)],
            dst_ref=held.at[0, :, column_block(me, k)],
            send_sem=second_send.at[away, k],
            recv_sem=second_recv.at[away, k],
            device_id={"exp": other},
            device_id_type=MESH,
        )

    def second_in(away, k):
        block = held.at[0, :, column_block((me + devices - away) % devices, k)]
        return pltpu.make_async_remote_copy(
            src_ref=block,
            dst_ref=block,
            send_sem=second_send.at[away, k],
            recv_sem=second_recv.at[away, k],
            device_id={"exp": (me + away) % devices},
            device_id_type=MESH,
        )

    def second_own(k):
        return pltpu.make_async_copy(
            summed.at[k, row_block(me)], held.at[0, :, column_block(me, k)], local_sem.at[k]
        )

    def third(away, short):
        if short:
            source, target = held.at[0, :, :far], held.at[away, :, :far]
        else:
            source, target = held.at[0], held.at[away]
        return seq_copy(source, target, third_send.at[away], third_recv.at[away], away)

    def to_last(source_group):
        return pltpu.make_async_remote_copy(
            src_ref=out_low,
            dst_ref=out_arrived.at[source_group],
            send_sem=out_send,
            recv_sem=out_recv.at[source_group],
            device_id={"seq": kinds},
            device_id_type=MESH,
        )

    meet_all(("seq", "exp"))
    for k in range(3):
        for away in range(1, groups):

            @pl.when(jnp.logical_and((group + away) % groups < kinds, lives(k, me)))
            def _():
                first(away, k).start()

    for left in range(0, D, 256):
        part[left : left + 256, :D] = dot_tn(mixed_ref[:, left : left + 256], mix_ref[...]).astype(BF)
    part[:, D:] = small_ref[...].astype(BF)
    scatter.start()
    scatter.slot(0)

    @pl.when(group < kinds)
    def _():
        for k in range(3):

            @pl.when(lives(k, me))
            def _():
                for away in range(1, groups):
                    first_in(away, k).wait_recv()
                total = unit(group, k)[...].astype(F32)
                for away in range(1, groups):
                    total += arrived[away - 1, k].astype(F32)
                summed[k] = total.astype(BF)
                for away in range(1, devices):
                    second(away, k).start()
                second_own(k).start()

    for turn_ in range(1, chips - 1):
        scatter.slot(turn_)

    @pl.when(group < kinds)
    def _():
        for k in range(3):

            @pl.when(lives(k, me))
            def _():
                second_own(k).wait()

            for away in range(1, devices):

                @pl.when(lives(k, (me + devices - away) % devices))
                def _():
                    second_in(away, k).wait_recv()

        for away in range(1, groups):
            third(away, False).start()

    scatter.finish(result)
    out_low[...] = result[...].astype(BF)

    @pl.when(group < kinds)
    def _():
        to_last(group).start()

    @pl.when(group == kinds)
    def _():
        total = result[...]
        for other in range(kinds):
            pltpu.make_async_remote_copy(
                src_ref=out_low, dst_ref=out_arrived.at[other], send_sem=out_send,
                recv_sem=out_recv.at[other], device_id={"seq": other}, device_id_type=MESH,
            ).wait_recv()
            total += out_arrived[other].astype(F32)
        held[0, :, :far] = total.astype(BF)
        for away in range(1, groups):
            third(away, True).start()

    for away in range(1, groups):
        source = (group + groups - away) % groups

        @pl.when(source == kinds)
        def _():
            third(away, True).wait_recv()

        @pl.when(source < kinds)
        def _():
            third(away, False).wait_recv()

    for kind in range(kinds):
        index = (group + groups - kind) % groups
        attn_out[kind, :, : devices * HD] = held[index, :, : devices * HD].astype(F32)
        attn_out[kind, :, devices * HD :] = held[
            index, :, 2 * devices * HD : 2 * devices * HD + D - devices * HD
        ].astype(F32)
        shared_out[kind] = held[index, :, devices * HD : 2 * devices * HD].astype(F32)
    index = (group + groups - kinds) % groups
    attn_out[kinds] = held[index, :, :D].astype(F32)
    small_out[...] = held[index, :, D:far].astype(F32)

    for k in range(3):
        for away in range(1, groups):

            @pl.when(jnp.logical_and((group + away) % groups < kinds, lives(k, me)))
            def _():
                first(away, k).wait_send()

    @pl.when(group < kinds)
    def _():
        for k in range(3):

            @pl.when(lives(k, me))
            def _():
                for away in range(1, devices):
                    second(away, k).wait_send()

        for away in range(1, groups):
            third(away, False).wait_send()
        to_last(group).wait_send()

    @pl.when(group == kinds)
    def _():
        for away in range(1, groups):
            third(away, True).wait_send()


def taking(us):
    return pl.CostEstimate(flops=int(us * 1.0e9), bytes_accessed=2**20, transcendentals=0)


def like(*shape, dtype=BF):
    return jax.ShapeDtypeStruct(shape, dtype)


IN_VMEM = pl.BlockSpec(memory_space=pltpu.VMEM)
ANYWHERE = pl.BlockSpec(memory_space=pl.ANY)


def experts_on_lines(two_own, grad_all, ids_all, expert_at, router_rows, routed, shared, share):
    devices = lax.axis_size("exp")
    me = lax.axis_index("exp")
    experts = expert_at.shape[0]
    chips = devices // 2
    length = SEQ_DEV * devices
    wide = EXP_DEV * FF + LANES
    own_shared = [
        jnp.pad(lax.dynamic_slice(w, (0, me * share), (D, share)), ((0, 0), (0, LANES - share)))
        for w in shared
    ]
    spare = jnp.full((LANES - experts,), -1, jnp.int32)
    columns = jnp.concatenate([expert_at.astype(jnp.int32), spare])
    named = jnp.any(ids_all[..., None] == columns, axis=2).astype(F32).reshape(MB * length, LANES)
    router = jnp.pad(router_rows, ((0, 0), (0, LANES - experts)))
    block_back = (devices, SEQ_DEV, D + LANES)
    block_out = (devices, SEQ_DEV, D)
    sems = [gather_sems(chips) for _ in range(MB)] + [scatter_sems(chips) for _ in range(2)]

    def call_rows(own, grad, names, router_in, *weights):
        def kernel(own_ref, grad_ref, named_ref, router_ref, *refs):
            expert_rows(
                chips, experts, own_ref, grad_ref, named_ref, router_ref, refs[:3], refs[3:6], *refs[6:]
            )

        return pl.pallas_call(
            kernel,
            out_shape=(
                like(MB, devices, SEQ_DEV, D),
                like(MB * length, wide),
                like(MB * length, wide),
                like(MB * length, wide),
                like(*block_out),
                like(*block_back),
                like(SEQ_DEV, D, dtype=F32),
                like(SEQ_DEV, D + LANES, dtype=F32),
            ),
            in_specs=[IN_VMEM, ANYWHERE, IN_VMEM, IN_VMEM] + [ANYWHERE] * 6,
            out_specs=(ANYWHERE,) * 6 + (IN_VMEM,) * 2,
            scratch_shapes=[
                pltpu.VMEM((3, D, wide), BF),
                pltpu.VMEM((MB, devices, SEQ_DEV, D), BF),
                pltpu.VMEM((2, 2 * SEQ_DEV, D), BF),
                pltpu.VMEM((2, 3, 2 * SEQ_DEV, wide), BF),
                pltpu.VMEM((MB, *block_out), BF),
                pltpu.VMEM((MB, *block_back), BF),
                (
                    pltpu.VMEM((chips, SEQ_DEV, D), BF),
                    pltpu.VMEM((chips, SEQ_DEV, D + LANES), BF),
                ),
                (
                    pltpu.VMEM((chips + 1, SEQ_DEV, D), BF),
                    pltpu.VMEM((chips + 1, SEQ_DEV, D + LANES), BF),
                ),
                pltpu.SemaphoreType.DMA((3, EXP_DEV + 1)),
                pltpu.SemaphoreType.DMA((MB,)),
                pltpu.SemaphoreType.DMA((2,)),
                pltpu.SemaphoreType.DMA((2, 3)),
                pltpu.SemaphoreType.DMA((2, chips)),
            ]
            + [sem for group in sems for sem in group],
            compiler_params=pltpu.CompilerParams(
                collective_id=1, has_side_effects=True, vmem_limit_bytes=VMEM_BYTES
            ),
            cost_estimate=taking(100),
            name="expert_rows",
        )(own, grad, names, router_in, *weights)

    rows, hidden, d_gate, d_up, out_b, back_b, out_sum_a, back_sum_a = call_rows(
        two_own, grad_all, named, router, *routed, *own_shared
    )
    flat = MB * length

    def call_sums(*operands):
        def kernel(*refs):
            expert_sums(chips, *refs)

        by_rows = pl.BlockSpec((flat, 256), lambda e, d: (0, d))
        by_expert = pl.BlockSpec((flat, FF), lambda e, d: (0, e))
        last = pl.BlockSpec((flat, LANES), lambda e, d: (0, EXP_DEV * FF // LANES))
        routed_out = pl.BlockSpec((1, 256, FF), lambda e, d: (e, d, 0))

        def whole(*shape):
            return pl.BlockSpec(shape, lambda e, d: (0,) * len(shape))

        return pl.pallas_call(
            kernel,
            grid=(EXP_DEV, D // 256),
            out_shape=(like(EXP_DEV, D, FF),) * 3
            + (
                like(3, D, LANES),
                like(SEQ_DEV, D, dtype=F32),
                like(SEQ_DEV, D + LANES, dtype=F32),
            ),
            in_specs=[by_rows] * 2 + [by_expert] * 3 + [last] * 3 + [ANYWHERE] * 2,
            out_specs=(routed_out,) * 3
            + (whole(3, D, LANES), whole(SEQ_DEV, D), whole(SEQ_DEV, D + LANES)),
            scratch_shapes=[
                pltpu.VMEM((chips, SEQ_DEV, D), BF),
                pltpu.VMEM((chips, SEQ_DEV, D + LANES), BF),
                (
                    pltpu.VMEM((chips, SEQ_DEV, D), BF),
                    pltpu.VMEM((chips, SEQ_DEV, D + LANES), BF),
                ),
                (
                    pltpu.VMEM((chips + 1, SEQ_DEV, D), BF),
                    pltpu.VMEM((chips + 1, SEQ_DEV, D + LANES), BF),
                ),
                pltpu.SemaphoreType.DMA((2, chips)),
            ]
            + scatter_sems(chips) * 2,
            compiler_params=pltpu.CompilerParams(
                collective_id=2, has_side_effects=True, vmem_limit_bytes=VMEM_BYTES
            ),
            cost_estimate=taking(60),
            name="expert_sums",
        )(*operands)

    gate_sum, up_sum, down_sum, shared_sum, out_sum_b, back_sum_b = call_sums(
        rows.reshape(flat, D), grad_all.reshape(flat, D), hidden, d_gate, d_up, hidden, d_gate, d_up,
        out_b, back_b,
    )
    backs = (back_sum_a, back_sum_b)
    tails = [
        b[:, D : D + experts] + b[:, D + experts : D + 2 * experts] for b in backs
    ]
    return (
        (out_sum_a, out_sum_b),
        [b[:, :D] for b in backs],
        tails,
        (gate_sum, up_sum, down_sum),
        shared_sum,
    )


def named_softmax(logits, named):
    chosen = jnp.where(named, logits, -jnp.inf)
    powers = jnp.where(named, jnp.exp(chosen - jnp.max(chosen, axis=-1, keepdims=True)), 0.0)
    return powers / jnp.sum(powers, axis=-1, keepdims=True)


def on_device_plain(
    tokens,
    cotangent,
    expert_ids,
    owner_table,
    w_query,
    w_key,
    w_value,
    w_out,
    gain_one,
    gain_two,
    w_router,
    shared_gate,
    shared_up,
    shared_down,
    routed_gate,
    routed_up,
    routed_down,
):
    devices = lax.axis_size("exp")
    groups = lax.axis_size("seq")
    me = lax.axis_index("exp")
    experts = owner_table.shape[0]
    length = SEQ_DEV * devices
    rows_out = D // devices
    slots = -(-HEADS // devices)
    wide = slots * HD
    share = FF // devices
    used = EXP_DEV * FF + share
    padded = -(-used // LANES) * LANES

    head_of = [jnp.minimum(me + slot * devices, HEADS - 1) for slot in range(slots)]
    slot_live = jnp.concatenate(
        [
            jnp.full((HD,), jnp.where(me + slot * devices < HEADS, 1.0, 0.0), F32)
            for slot in range(slots)
        ]
    )

    w_qkv = jnp.concatenate(
        [
            lax.dynamic_slice(weight, (0, head * HD), (D, HD))
            for head in head_of
            for weight in (w_query, w_key, w_value)
        ],
        axis=1,
    )
    w_out_heads = jnp.concatenate(
        [lax.dynamic_slice(w_out, (head * HD, 0), (HD, D)) for head in head_of], axis=0
    )
    cos_table, sin_table = angle_tables(jnp.arange(length).astype(F32))
    sin_table = jnp.where(jnp.arange(HD) < HD // 2, -sin_table, sin_table)
    params = pltpu.CompilerParams(vmem_limit_bytes=VMEM_BYTES)

    forward = pl.pallas_call(
        functools.partial(attend_forward, slots),
        out_shape=(
            like(length, D),
            like(length, 3 * wide),
            like(length, wide),
            like(slots, length, 1, dtype=F32),
        ),
        in_specs=[IN_VMEM] * 5,
        out_specs=(IN_VMEM,) * 4,
        compiler_params=params,
        name="attend_forward",
    )
    backward = pl.pallas_call(
        functools.partial(attend_backward, slots),
        out_shape=(like(wide, D, dtype=F32), like(D, 3 * wide, dtype=F32), like(length, D)),
        in_specs=[IN_VMEM] * 10,
        out_specs=(IN_VMEM,) * 3,
        scratch_shapes=[
            pltpu.VMEM((length, 3 * wide), BF),
            pltpu.VMEM((length, wide), BF),
            pltpu.VMEM((length, HD), F32),
            pltpu.VMEM((length, HD), F32),
        ],
        compiler_params=params,
        name="attend_backward",
    )

    def joined(routed, shared):
        own = lax.dynamic_slice(shared, (0, me * share), (D, share))
        blank = jnp.zeros((D, padded - used), BF)
        return jnp.concatenate([routed[i] for i in range(EXP_DEV)] + [own, blank], axis=1)

    gate_all = joined(routed_gate, shared_gate)
    up_all = joined(routed_up, shared_up)
    down_all = joined(routed_down, shared_down)

    expert_at = jnp.sum(
        (owner_table[:, None] == jnp.arange(experts)[None, :]) * jnp.arange(experts)[:, None],
        axis=0,
    )
    router_rows = jnp.take(w_router, expert_at, axis=1)
    ids_all = lax.all_gather(expert_ids[:, 0], "exp", axis=1, tiled=True)

    first = []
    for micro_batch in range(MB):
        rows_all = gather_exp(tokens[micro_batch, 0])
        normed, qkv, mixed, lse = forward(rows_all, gain_one[None], cos_table, sin_table, w_qkv)
        sent = lax.all_to_all(
            mixed.reshape(devices, SEQ_DEV, wide), "exp", split_axis=0, concat_axis=0, tiled=True
        )
        own_mixed = (
            sent.reshape(devices, SEQ_DEV, slots, HD)
            .transpose(1, 2, 0, 3)
            .reshape(SEQ_DEV, slots * devices * HD)[:, :D]
        )
        rows_in = tokens[micro_batch, 0].astype(F32)
        hidden_one = rows_in + dot(own_mixed, w_out)
        two_low = norm_rows(hidden_one, gain_two).astype(BF)
        two_all = gather_exp(two_low)
        grad_all = gather_exp(cotangent[micro_batch, 0])
        first.append(
            (normed, qkv, mixed, lse, rows_in, hidden_one, two_all, grad_all)
        )

    column = jnp.arange(padded)
    second = []
    for micro_batch in range(MB):
        two_all, grad_all = first[micro_batch][6:]
        logits = dot(two_all, router_rows)
        named = jnp.any(ids_all[micro_batch][:, :, None] == expert_at[None, None, :], axis=1)
        chosen = jnp.where(named, logits, -jnp.inf)
        powers = jnp.where(named, jnp.exp(chosen - jnp.max(chosen, axis=-1, keepdims=True)), 0.0)
        gates = powers / jnp.sum(powers, axis=-1, keepdims=True)
        own_gates = lax.dynamic_slice(gates, (0, me * EXP_DEV), (length, EXP_DEV))
        weight = jnp.where(
            column[None, :] < FF,
            own_gates[:, :1],
            jnp.where(column[None, :] < 2 * FF, own_gates[:, 1:], 1.0),
        )
        gate_part = dot(two_all, gate_all)
        up_part = dot(two_all, up_all)
        down_part = dot(grad_all, down_all)
        sigmoid = jax.nn.sigmoid(gate_part)
        act = gate_part * sigmoid
        hidden = act * up_part
        products = hidden * down_part
        own_grads = jnp.stack(
            [jnp.sum(products[:, i * FF : (i + 1) * FF], axis=1) for i in range(EXP_DEV)], axis=1
        )
        hidden_low = (weight * hidden).astype(BF)
        weighted = weight * down_part
        d_gate = (weighted * up_part * (sigmoid + act * (1.0 - sigmoid))).astype(BF)
        d_up = (weighted * act).astype(BF)
        out_part = scatter_exp(dot_nt(hidden_low, down_all))
        back_part = scatter_exp(dot_nt(d_gate, gate_all) + dot_nt(d_up, up_all))
        gate_grads = lax.all_gather(own_grads, "exp", axis=1, tiled=True)
        grad_logits = (
            gates * (gate_grads - jnp.sum(gates * gate_grads, axis=-1, keepdims=True))
        ).astype(BF)
        second.append((hidden_low, d_gate, d_up, out_part, back_part, grad_logits))

    two_both = jnp.concatenate([f[6] for f in first])
    grad_both = jnp.concatenate([f[7] for f in first])
    gate_sum = dot_tn(two_both, jnp.concatenate([s[1] for s in second]))
    up_sum = dot_tn(two_both, jnp.concatenate([s[2] for s in second]))
    down_sum = dot_tn(grad_both, jnp.concatenate([s[0] for s in second]))

    def routed_sum(total):
        parts = jnp.stack([total[:, i * FF : (i + 1) * FF] for i in range(EXP_DEV)])
        return lax.psum_scatter(
            parts.astype(BF), "seq", scatter_dimension=1, tiled=True
        ).astype(F32)

    def shared_part(total):
        return total[:, EXP_DEV * FF : used]

    outputs_list = []
    grads_list = []
    small = jnp.zeros((D, experts + 2), F32)
    qkv_sum = jnp.zeros((D, 3 * wide), F32)
    out_sum = jnp.zeros((wide, D), F32)
    for micro_batch in range(MB):
        normed, qkv, mixed, lse, rows_in, hidden_one, two_all, _ = first[micro_batch]
        _, _, _, out_part, back_part, grad_logits = second[micro_batch]
        outputs_list.append((hidden_one + out_part).astype(BF))
        own_logits = lax.dynamic_slice(grad_logits, (me * SEQ_DEV, 0), (SEQ_DEV, experts))
        grad_two = back_part + dot_nt(own_logits, router_rows)
        back, gain_terms = norm_back(hidden_one, gain_two, grad_two)
        grad_hidden = cotangent[micro_batch, 0].astype(F32) + back
        own_two = lax.dynamic_slice(two_all, (me * SEQ_DEV, 0), (SEQ_DEV, D))
        router_part = dot_tn(own_two, own_logits)
        mix_all = gather_exp(grad_hidden.astype(BF))
        out_one, qkv_one, grad_part = backward(
            mix_all, normed, qkv, mixed, lse, cos_table, sin_table, w_qkv, w_out_heads, slot_live[None]
        )
        out_sum = out_sum + out_one
        qkv_sum = qkv_sum + qkv_one
        grad_normed = scatter_exp(grad_part)
        back_one, gain_one_terms = norm_back(rows_in, gain_one, grad_normed)
        grads_list.append((grad_hidden + back_one).astype(BF))
        small = small + jnp.concatenate(
            [
                router_part,
                jnp.sum(gain_one_terms, axis=0)[:, None],
                jnp.sum(gain_terms, axis=0)[:, None],
            ],
            axis=1,
        )

    def to_rows(columns):
        parts = columns.astype(BF).reshape(devices, rows_out, columns.shape[1])
        parts = lax.psum_scatter(parts, "seq", scatter_dimension=1, tiled=True)
        return lax.all_to_all(parts, "exp", split_axis=0, concat_axis=0, tiled=True)

    def to_all(rows):
        return lax.all_gather(rows, "seq", axis=0, tiled=True).astype(F32)

    piece = rows_out // groups
    shared_cols = jnp.concatenate([shared_part(t) for t in (gate_sum, up_sum, down_sum)], axis=1)
    shared_rows = to_rows(shared_cols).reshape(devices, piece, 3, share)
    shared_full = to_all(shared_rows.transpose(1, 2, 0, 3).reshape(piece, 3 * FF))
    qkv_rows = to_rows(qkv_sum).reshape(devices, piece, slots, 3, HD)
    qkv_rows = qkv_rows.transpose(1, 3, 2, 0, 4).reshape(piece, 3, slots * devices * HD)
    qkv_full = to_all(qkv_rows[:, :, :D].reshape(piece, 3 * D))
    out_part = lax.psum_scatter(out_sum.astype(BF), "seq", scatter_dimension=1, tiled=True)
    spread = jnp.zeros((slots * devices * HD, D // groups), BF)
    for slot in range(slots):
        spread = lax.dynamic_update_slice(
            spread, out_part[slot * HD : (slot + 1) * HD], ((me + slot * devices) * HD, 0)
        )
    out_rows = lax.psum_scatter(spread[:D], "exp", scatter_dimension=0, tiled=True)
    out_full = lax.all_gather(out_rows, "seq", axis=1, tiled=True).astype(F32)
    small_rows = lax.psum_scatter(
        lax.psum(small, "seq"), "exp", scatter_dimension=0, tiled=True
    )
    place_of = jnp.take(small_rows, owner_table, axis=1)
    return (
        jnp.stack(outputs_list)[:, None],
        jnp.stack(grads_list)[:, None],
        qkv_full[:, :D],
        qkv_full[:, D : 2 * D],
        qkv_full[:, 2 * D :],
        out_full,
        small_rows[:, experts],
        small_rows[:, experts + 1],
        place_of,
        shared_full[:, :FF],
        shared_full[:, FF : 2 * FF],
        shared_full[:, 2 * FF :],
        routed_sum(gate_sum),
        routed_sum(up_sum),
        routed_sum(down_sum),
    )


def on_device_lines(
    tokens,
    cotangent,
    expert_ids,
    owner_table,
    w_query,
    w_key,
    w_value,
    w_out,
    gain_one,
    gain_two,
    w_router,
    shared_gate,
    shared_up,
    shared_down,
    routed_gate,
    routed_up,
    routed_down,
):
    devices = lax.axis_size("exp")
    groups = lax.axis_size("seq")
    me = lax.axis_index("exp")
    chips = devices // 2
    experts = owner_table.shape[0]
    length = SEQ_DEV * devices
    rows_out = D // devices
    slots = -(-HEADS // devices)
    wide = slots * HD
    share = FF // devices
    own = MB * SEQ_DEV

    head_of = [jnp.minimum(me + slot * devices, HEADS - 1) for slot in range(slots)]
    w_qkv = jnp.concatenate(
        [
            lax.dynamic_slice(weight, (0, head * HD), (D, HD))
            for head in head_of
            for weight in (w_query, w_key, w_value)
        ],
        axis=1,
    )
    cos_table, sin_table = angle_tables(jnp.arange(length).astype(F32))
    sin_table = jnp.where(jnp.arange(HD) < HD // 2, -sin_table, sin_table)
    forward = pl.pallas_call(
        functools.partial(attend_forward, slots),
        out_shape=(
            like(length, D),
            like(length, 3 * wide),
            like(length, wide),
            like(slots, length, 1, dtype=F32),
        ),
        in_specs=[IN_VMEM] * 5,
        out_specs=(IN_VMEM,) * 4,
        compiler_params=pltpu.CompilerParams(vmem_limit_bytes=VMEM_BYTES),
        cost_estimate=taking(12),
        name="attend_forward",
    )

    expert_at = jnp.sum(
        (owner_table[:, None] == jnp.arange(experts)[None, :]) * jnp.arange(experts)[:, None],
        axis=0,
    )
    router_rows = jnp.take(w_router, expert_at, axis=1)
    ids_all = lax.all_gather(expert_ids[:, 0], "exp", axis=1, tiled=True)
    grad_all = lax.all_gather(cotangent[:, 0], "exp", axis=1, tiled=True)

    kept, mixed_rows = [], []
    for micro_batch in range(MB):
        rows_all = gather_exp(tokens[micro_batch, 0])
        normed, qkv, mixed, lse = forward(rows_all, gain_one[None], cos_table, sin_table, w_qkv)
        kept.append((normed, qkv, mixed, lse))
        sent = lax.all_to_all(
            mixed.reshape(devices, SEQ_DEV, wide), "exp", split_axis=0, concat_axis=0, tiled=True
        )
        mixed_rows.append(
            sent.reshape(devices, SEQ_DEV, slots, HD)
            .transpose(1, 2, 0, 3)
            .reshape(SEQ_DEV, slots * devices * HD)[:, :D]
        )
    normed, qkv, mixed, lse = [jnp.stack([k[i] for k in kept]) for i in range(4)]
    own_mixed = jnp.concatenate(mixed_rows)
    rows_in = tokens.reshape(own, D).astype(F32)
    hidden_one = rows_in + dot(own_mixed, w_out)
    two_low = norm_rows(hidden_one, gain_two).astype(BF)
    named = jnp.any(
        expert_ids.reshape(own, TOP)[:, :, None] == expert_at[None, None, :], axis=1
    )
    gates = named_softmax(dot(two_low, router_rows), named)

    outs, backs, tails, routed_sums, shared_sum = experts_on_lines(
        two_low.reshape(MB, SEQ_DEV, D),
        grad_all,
        ids_all,
        expert_at,
        router_rows,
        (routed_gate, routed_up, routed_down),
        (shared_gate, shared_up, shared_down),
        share,
    )
    routed_full = [
        lax.psum_scatter(parts, "seq", scatter_dimension=1, tiled=True).astype(F32)
        for parts in routed_sums
    ]
    layer_out = (hidden_one + jnp.concatenate(outs)).astype(BF)
    tail = jnp.concatenate(tails)
    grad_logits = (gates * (tail - jnp.sum(gates * tail, axis=-1, keepdims=True))).astype(BF)
    grad_two = jnp.concatenate(backs) + dot_nt(grad_logits, router_rows)
    back, gain_two_terms = norm_back(hidden_one, gain_two, grad_two)
    grad_hidden = cotangent.reshape(own, D).astype(F32) + back
    grad_mix = grad_hidden.astype(BF)
    d_mixed = dot_nt(grad_mix, w_out).astype(BF)

    heads_sum, grad_a, grad_b = pl.pallas_call(
        functools.partial(heads_backward, chips, slots),
        out_shape=(
            like(3 * slots, D, HD),
            like(SEQ_DEV, D, dtype=F32),
            like(SEQ_DEV, D, dtype=F32),
        ),
        in_specs=[IN_VMEM] * 8,
        out_specs=(IN_VMEM,) * 3,
        scratch_shapes=[
            pltpu.VMEM((MB, length, wide), BF),
            pltpu.VMEM((MB, slots, length, length), BF),
            pltpu.VMEM((MB, length, 3 * wide), BF),
            pltpu.VMEM((MB, devices, SEQ_DEV, D), BF),
            pltpu.VMEM((length, HD), F32),
            pltpu.VMEM((length, HD), F32),
            pltpu.VMEM((MB, chips, SEQ_DEV, D), BF),
            pltpu.VMEM((MB, chips + 1, SEQ_DEV, D), BF),
            pltpu.SemaphoreType.DMA((MB, slots)),
            pltpu.SemaphoreType.DMA((MB, devices, slots)),
            pltpu.SemaphoreType.DMA((MB, devices, slots)),
        ]
        + scatter_sems(chips) * MB,
        compiler_params=pltpu.CompilerParams(
            collective_id=3, has_side_effects=True, vmem_limit_bytes=VMEM_BYTES
        ),
        cost_estimate=taking(70),
        name="heads_backward",
    )(
        d_mixed.reshape(MB, SEQ_DEV, D), qkv, mixed, normed, lse, cos_table, sin_table, w_qkv
    )
    grad_normed = jnp.concatenate([grad_a, grad_b])
    back_one, gain_one_terms = norm_back(rows_in, gain_one, grad_normed)
    grad_tokens = (grad_hidden + back_one).astype(BF)
    small = jnp.concatenate(
        [
            dot_tn(two_low, grad_logits),
            jnp.sum(gain_one_terms, axis=0)[:, None],
            jnp.sum(gain_two_terms, axis=0)[:, None],
            jnp.zeros((D, LANES - experts - 2), F32),
        ],
        axis=1,
    )
    far = D + LANES
    attn, shared_full, small_rows = pl.pallas_call(
        functools.partial(spread_sums, chips),
        out_shape=(
            like(groups, rows_out, D, dtype=F32),
            like(groups - 1, rows_out, devices * HD, dtype=F32),
            like(rows_out, LANES, dtype=F32),
        ),
        in_specs=[IN_VMEM] * 5,
        out_specs=(IN_VMEM,) * 3,
        scratch_shapes=[
            pltpu.VMEM((groups - 1, 3, D, HD), BF),
            pltpu.VMEM((3, D, HD), BF),
            pltpu.VMEM((groups, rows_out, 3 * devices * HD), BF),
            pltpu.VMEM((D, far), BF),
            pltpu.VMEM((rows_out, far), BF),
            pltpu.VMEM((groups - 1, rows_out, far), BF),
            pltpu.VMEM((rows_out, far), F32),
            pltpu.VMEM((chips, rows_out, far), BF),
            pltpu.VMEM((chips + 1, rows_out, far), BF),
            pltpu.SemaphoreType.DMA((groups - 1, 3)),
            pltpu.SemaphoreType.DMA((groups - 1, 3)),
            pltpu.SemaphoreType.DMA((3,)),
            pltpu.SemaphoreType.DMA((devices, 3)),
            pltpu.SemaphoreType.DMA((devices, 3)),
            pltpu.SemaphoreType.DMA,
            pltpu.SemaphoreType.DMA((groups - 1,)),
            pltpu.SemaphoreType.DMA((groups,)),
            pltpu.SemaphoreType.DMA((groups,)),
        ]
        + scatter_sems(chips),
        compiler_params=pltpu.CompilerParams(
            collective_id=4, has_side_effects=True, vmem_limit_bytes=VMEM_BYTES
        ),
        cost_estimate=taking(60),
        name="spread_sums",
    )(heads_sum, shared_sum, own_mixed, grad_mix, small)
    shared_grads = shared_full.reshape(groups - 1, rows_out, devices, HD)[..., :share].reshape(
        groups - 1, rows_out, FF
    )
    whole = (MB, 1, SEQ_DEV, D)
    return (
        layer_out.reshape(whole),
        grad_tokens.reshape(whole),
        attn[0],
        attn[1],
        attn[2],
        attn[3],
        small_rows[:, experts],
        small_rows[:, experts + 1],
        jnp.take(small_rows[:, :experts], owner_table, axis=1),
        shared_grads[0],
        shared_grads[1],
        shared_grads[2],
        *routed_full,
    )


def solution(mesh):
    rows = P(None, "seq", "exp", None)
    placed = (rows,) * 3 + (P(),) * 11 + (P("exp", None, None),) * 3
    wide = P("exp", None)
    on_lines = mesh.shape["exp"] == 8 and mesh.shape["seq"] == 4
    on_device = on_device_lines if on_lines else on_device_plain
    return jax.shard_map(
        on_device,
        mesh=mesh,
        in_specs=placed,
        out_specs=(rows, rows, wide, wide, wide, wide, P("exp"), P("exp"))
        + (wide,) * 4
        + (P("exp", "seq", None),) * 3,
        check_vma=False,
    )
```

```python
import functools
import math

import jax
import jax.numpy as jnp
import numpy as np
from jax import lax
from jax.experimental import pallas as pl
from jax.experimental.pallas import tpu as pltpu
from jax.sharding import PartitionSpec as P

D = 1280
HEADS = 10
HD = 128
FF = 896
TOP = 7
EXP_DEV = 2
MB = 2
SEQ_DEV = 128
LANES = 128
BLOCK = 256
VMEM_BYTES = 60 * 2**20

eps = 1e-06
BF = jnp.bfloat16
F32 = jnp.float32


def norm_rows(inputs, gain):
    return inputs * lax.rsqrt(jnp.mean(inputs * inputs, axis=-1, keepdims=True) + eps) * gain


def norm_back(inputs, gain, grad):
    scale = lax.rsqrt(jnp.mean(inputs * inputs, axis=-1, keepdims=True) + eps)
    unit = inputs * scale
    weighted = grad * gain
    back = scale * (weighted - unit * jnp.mean(weighted * unit, axis=-1, keepdims=True))
    return back, grad * unit


def angle_tables(positions):
    steps_half = jnp.arange(HD // 2).astype(positions.dtype)
    frequency = jnp.exp(steps_half * (-2.0 * math.log(10000.0) / HD))
    angles = positions[:, None] * frequency[None, :]
    angles = jnp.concatenate([angles, angles], axis=-1)
    return (jnp.cos(angles), jnp.sin(angles))


def turn_tables(length):
    angles = np.arange(length)[:, None] * 10000.0 ** (-2.0 * np.arange(HD // 2) / HD)
    cos, sin = np.cos(angles), np.sin(angles)
    return (
        jnp.asarray(np.concatenate([cos, cos], axis=1), F32),
        jnp.asarray(np.concatenate([-sin, sin], axis=1), F32),
    )


def dot(a, b):
    return jnp.dot(a, b, preferred_element_type=F32)


def dot_nt(a, b):
    return lax.dot_general(a, b, (((1,), (1,)), ((), ())), preferred_element_type=F32)


def dot_tn(a, b):
    return lax.dot_general(a, b, (((0,), (0,)), ((), ())), preferred_element_type=F32)


def gather_exp(array):
    return lax.all_gather(array, "exp", axis=0, tiled=True)


def scatter_exp(array):
    return lax.psum_scatter(array.astype(BF), "exp", scatter_dimension=0, tiled=True).astype(F32)


def turn(heads, cos_table, sin_table):
    return heads * cos_table + pltpu.roll(heads, HD // 2, 1) * sin_table


def visible_scores(queries, keys, start):
    scores = dot_nt(queries, keys) * HD ** (-0.5)
    rows = queries.shape[0]
    row = lax.broadcasted_iota(jnp.int32, (rows, rows), 0)
    column = lax.broadcasted_iota(jnp.int32, (rows, rows), 1)
    last = jnp.where(row >= column, scores[:, start:], -1e30)
    return last if start == 0 else jnp.concatenate([scores[:, :start], last], axis=1)


def attend_forward(slots, rows_ref, gain_ref, cos_ref, sin_ref, w_ref, normed_ref, qkv_ref, mixed_ref, lse_ref):
    length = rows_ref.shape[0]
    step = BLOCK if length <= 2048 else BLOCK // 2

    def project(i, carry):
        part = pl.ds(pl.multiple_of(i * step, step), step)
        normed = norm_rows(rows_ref[part, :].astype(F32), gain_ref[...]).astype(BF)
        normed_ref[part, :] = normed
        for slot in range(slots):
            base = 3 * HD * slot
            qkv = dot(normed, w_ref[:, base : base + 3 * HD])
            for j in range(2):
                turned = turn(qkv[:, j * HD : (j + 1) * HD], cos_ref[part, :], sin_ref[part, :])
                qkv_ref[part, base + j * HD : base + (j + 1) * HD] = turned.astype(BF)
            qkv_ref[part, base + 2 * HD : base + 3 * HD] = qkv[:, 2 * HD :].astype(BF)
        return carry

    lax.fori_loop(0, length // step, project, 0)
    for slot in range(slots):
        base = 3 * HD * slot
        for start in range(0, length, step):
            stop = start + step
            scores = visible_scores(
                qkv_ref[start:stop, base : base + HD], qkv_ref[:stop, base + HD : base + 2 * HD], start
            )
            largest = jnp.max(scores, axis=-1, keepdims=True)
            powers = jnp.exp(scores - largest)
            total = jnp.sum(powers, axis=-1, keepdims=True)
            attention = (powers * (1.0 / total)).astype(BF)
            mixed = dot(attention, qkv_ref[:stop, base + 2 * HD : base + 3 * HD])
            mixed_ref[start:stop, slot * HD : (slot + 1) * HD] = mixed.astype(BF)
            lse_ref[slot, start:stop, :] = largest + jnp.log(total)


def attend_backward(
    slots, mix_ref, normed_ref, qkv_ref, mixed_ref, lse_ref, cos_ref, sin_ref, w_ref, w_out_ref, live_ref,
    out_sum_ref, qkv_sum_ref, grad_ref, raw_ref, d_mixed_ref, d_keys_ref, d_values_ref,
):
    length = mix_ref.shape[0]
    step = BLOCK if length <= 2048 else BLOCK // 2
    factor = HD ** (-0.5)

    def project(i, carry):
        part = pl.ds(pl.multiple_of(i * step, step), step)
        d_mixed_ref[part, :] = (dot_nt(mix_ref[part, :], w_out_ref[...]) * live_ref[...]).astype(BF)
        return carry

    lax.fori_loop(0, length // step, project, 0)
    for slot in range(slots):
        base = 3 * HD * slot
        d_keys_ref[...] = jnp.zeros_like(d_keys_ref)
        d_values_ref[...] = jnp.zeros_like(d_values_ref)
        for start in range(0, length, step):
            stop = start + step
            queries = qkv_ref[start:stop, base : base + HD]
            keys = qkv_ref[:stop, base + HD : base + 2 * HD]
            values = qkv_ref[:stop, base + 2 * HD : base + 3 * HD]
            d_mixed = d_mixed_ref[start:stop, slot * HD : (slot + 1) * HD]
            attention = jnp.exp(visible_scores(queries, keys, start) - lse_ref[slot, start:stop, :])
            d_att = dot_nt(d_mixed, values)
            row_term = jnp.sum(attention * d_att, axis=-1, keepdims=True)
            d_scores = (attention * (d_att - row_term)).astype(BF)
            d_queries = dot(d_scores, keys) * factor
            raw = turn(d_queries, cos_ref[start:stop, :], -sin_ref[start:stop, :])
            raw_ref[start:stop, base : base + HD] = raw.astype(BF)
            d_keys_ref[:stop, :] += dot_tn(d_scores, queries)
            d_values_ref[:stop, :] += dot_tn(attention.astype(BF), d_mixed)
        raw = turn(d_keys_ref[...] * factor, cos_ref[...], -sin_ref[...])
        raw_ref[:, base + HD : base + 2 * HD] = raw.astype(BF)
        raw_ref[:, base + 2 * HD : base + 3 * HD] = d_values_ref[...].astype(BF)

    def give(i, carry):
        part = pl.ds(pl.multiple_of(i * step, step), step)
        grad_ref[part, :] = dot_nt(raw_ref[part, :], w_ref[...]).astype(BF)
        return carry

    lax.fori_loop(0, length // step, give, 0)
    out_sum_ref[...] = dot_tn(mixed_ref[...], mix_ref[...])

    def sums(i, carry):
        part = pl.ds(pl.multiple_of(i * 256, 256), 256)
        qkv_sum_ref[part, :] = dot_tn(normed_ref[:, part], raw_ref[...])
        return carry

    lax.fori_loop(0, D // 256, sums, 0)


MESH = pl.DeviceIdType.MESH


def place():
    me = lax.axis_index("exp")
    return me // 2, me % 2


def remote(source, target, send_sem, recv_sem, chip, core):
    return pltpu.make_async_remote_copy(
        src_ref=source,
        dst_ref=target,
        send_sem=send_sem,
        recv_sem=recv_sem,
        device_id={"exp": 2 * chip + core},
        device_id_type=MESH,
    )


def meet(chips):
    chip, core = place()
    barrier = pltpu.get_barrier_semaphore()

    def greet(to_chip, to_core):
        pl.semaphore_signal(
            barrier, inc=1, device_id={"exp": 2 * to_chip + to_core}, device_id_type=MESH
        )

    greet(chip, 1 - core)

    @pl.when(chip < chips - 1)
    def _():
        greet(chip + 1, core)

    @pl.when(chip > 0)
    def _():
        greet(chip - 1, core)

    below = (chip + chips - 1) // chips
    above = (2 * chips - 2 - chip) // chips
    pl.semaphore_wait(barrier, 1 + below + above)


def gather_sems(chips):
    return [pltpu.SemaphoreType.DMA((chips,))] * 4 + [pltpu.SemaphoreType.DMA((2 * chips,))] * 2


class Gather:
    def __init__(self, chips, own, blocks, sems):
        self.chips, self.own, self.blocks = chips, own, blocks
        self.up_send, self.up_recv, self.down_send, self.down_recv = sems[:4]
        self.pair_send, self.pair_recv = sems[4:]

    def _source(self, hop, number):
        return self.own if hop == 0 else self.blocks.at[number]

    def _up(self, hop):
        chip, core = place()
        number = 2 * (chip - hop) + core
        return remote(
            self._source(hop, number), self.blocks.at[number],
            self.up_send.at[hop], self.up_recv.at[hop], chip + 1, core,
        )

    def _down(self, hop):
        chip, core = place()
        number = 2 * (chip + hop) + core
        return remote(
            self._source(hop, number), self.blocks.at[number],
            self.down_send.at[hop], self.down_recv.at[hop], chip - 1, core,
        )

    def _pair(self, away):
        chip, core = place()
        number = 2 * (chip + away) + core
        source = self.own if isinstance(away, int) and away == 0 else self.blocks.at[number]
        slot = away + self.chips
        return remote(
            source, self.blocks.at[number], self.pair_send.at[slot], self.pair_recv.at[slot],
            chip, 1 - core,
        )

    def _from_pair(self, away):
        chip, core = place()
        block = self.blocks.at[2 * (chip + away) + 1 - core]
        slot = away + self.chips
        return remote(
            block, block, self.pair_send.at[slot], self.pair_recv.at[slot], chip, 1 - core
        )

    def start(self):
        chip, _ = place()

        @pl.when(chip < self.chips - 1)
        def _():
            self._up(0).start()

        @pl.when(chip > 0)
        def _():
            self._down(0).start()

        self._pair(0).start()

    def hop(self, hop):
        chip, core = place()

        @pl.when(chip >= hop)
        def _():
            block = self.blocks.at[2 * (chip - hop) + core]
            remote(
                block, block, self.up_send.at[hop - 1], self.up_recv.at[hop - 1], chip, 1 - core
            ).wait_recv()

            @pl.when(chip < self.chips - 1)
            def _():
                self._up(hop).start()

            self._pair(-hop).start()

        @pl.when(chip + hop < self.chips)
        def _():
            block = self.blocks.at[2 * (chip + hop) + core]
            remote(
                block, block, self.down_send.at[hop - 1], self.down_recv.at[hop - 1], chip, 1 - core
            ).wait_recv()

            @pl.when(chip > 0)
            def _():
                self._down(hop).start()

            self._pair(hop).start()

    def take_pair(self, away):
        self._from_pair(away).wait_recv()

    def finish(self, pairs):
        chip, _ = place()
        for away in range(-self.chips + 1, self.chips):

            @pl.when(jnp.logical_and(chip + away >= 0, chip + away < self.chips))
            def _():
                if pairs:
                    self._from_pair(away).wait_recv()
                self._pair(away).wait_send()

        for hop in range(self.chips):

            @pl.when(jnp.logical_and(chip >= hop, chip < self.chips - 1))
            def _():
                self._up(hop).wait_send()

            @pl.when(jnp.logical_and(chip + hop < self.chips, chip > 0))
            def _():
                self._down(hop).wait_send()


def scatter_sems(chips):
    return [pltpu.SemaphoreType.DMA((chips,))] * 6


class Scatter:
    def __init__(self, chips, theirs, mine, pair, line, sems):
        self.chips, self.theirs, self.mine, self.pair, self.line = chips, theirs, mine, pair, line
        self.pair_send, self.pair_recv, self.up_send, self.up_recv = sems[:4]
        self.down_send, self.down_recv = sems[4:]

    def _pair(self, to):
        chip, core = place()
        return remote(
            self.theirs(to), self.pair.at[to], self.pair_send.at[to], self.pair_recv.at[to],
            chip, 1 - core,
        )

    def _up(self, chip, to):
        return remote(
            self.mine(to), self.line.at[to - chip - 1], self.up_send.at[to], self.up_recv.at[to],
            chip + 1, place()[1],
        )

    def _down(self, chip, to):
        return remote(
            self.mine(to), self.line.at[self.chips - chip + 1 + to],
            self.down_send.at[to], self.down_recv.at[to], chip - 1, place()[1],
        )

    def _arrived_up(self, to):
        chip, core = place()
        block = self.line.at[to - chip]
        remote(block, block, self.up_send.at[to], self.up_recv.at[to], chip, 1 - core).wait_recv()
        return block[...].astype(F32)

    def _arrived_down(self, to):
        chip, core = place()
        block = self.line.at[self.chips - chip + to]
        remote(
            block, block, self.down_send.at[to], self.down_recv.at[to], chip, 1 - core
        ).wait_recv()
        return block[...].astype(F32)

    def _both(self, to):
        chip, core = place()
        block = self.pair.at[to]
        remote(
            block, block, self.pair_send.at[to], self.pair_recv.at[to], chip, 1 - core
        ).wait_recv()
        return self.mine(to)[...].astype(F32) + block[...].astype(F32)

    def start(self):
        for to in range(self.chips):
            self._pair(to).start()

    def slot(self, turn):
        chip, _ = place()
        last = self.chips - 1

        @pl.when(chip <= turn)
        def _():
            to = last - turn + chip
            total = self._both(to)

            @pl.when(chip == 0)
            def _():
                self.mine(to)[...] = total.astype(BF)

            @pl.when(chip > 0)
            def _():
                self.mine(to)[...] = (total + self._arrived_up(to)).astype(BF)

            self._up(chip, to).start()

        @pl.when(last - chip <= turn)
        def _():
            to = turn - last + chip
            total = self._both(to)

            @pl.when(chip == last)
            def _():
                self.mine(to)[...] = total.astype(BF)

            @pl.when(chip < last)
            def _():
                self.mine(to)[...] = (total + self._arrived_down(to)).astype(BF)

            self._down(chip, to).start()

    def finish(self, result):
        chip, _ = place()
        last = self.chips - 1
        result[...] = self._both(chip)

        @pl.when(chip > 0)
        def _():
            result[...] += self._arrived_up(chip)

        @pl.when(chip < last)
        def _():
            result[...] += self._arrived_down(chip)

        for to in range(self.chips):
            self._pair(to).wait_send()

            @pl.when(to > chip)
            def _():
                self._up(chip, to).wait_send()

            @pl.when(to < chip)
            def _():
                self._down(chip, to).wait_send()


def part_of(array, index):
    return array.at[index]


def block_order(chip, turn, chips):
    number, bit = 0, 1
    while bit < chips:
        number = number + bit * ((chip // bit + turn // bit) % 2)
        bit = 2 * bit
    return number


def expert_rows(
    chips, experts,
    own_ref, grad_own_ref, grad_ref, named_ref, router_ref, routed_refs, shared_refs,
    rows_ref, grads_ref, hidden_ref, d_gate_ref, d_up_ref, out_ref, back_b_ref, back_a_ref,
    weights, rows, grads, stage, out, back, pair, line, weight_sem, local_sem, stage_sem, keep_sem,
    *sems,
):
    chip, core = place()
    me = 2 * chip + core
    blocks = chips
    size = 2 * SEQ_DEV
    gathers = [Gather(chips, own_ref.at[m], rows.at[m], sems[6 * m : 6 * m + 6]) for m in range(MB)]
    grad_gather = Gather(chips, grad_own_ref.at[1], grads.at[1], sems[18:24])
    scatter = Scatter(
        chips,
        lambda to: back.at[0, 2 * to + 1 - core],
        lambda to: back.at[0, 2 * to + core],
        pair, line, sems[12:18],
    )
    loads = []
    for k in range(3):
        for e in range(EXP_DEV):
            loads.append(
                pltpu.make_async_copy(
                    routed_refs[k].at[e], weights.at[k, :, e * FF : (e + 1) * FF],
                    weight_sem.at[k, e],
                )
            )
        loads.append(
            pltpu.make_async_copy(
                shared_refs[k], weights.at[k, :, EXP_DEV * FF :], weight_sem.at[k, EXP_DEV]
            )
        )

    def stage_out(step, k):
        block = block_order(chip, step % blocks, chips)
        start = pl.multiple_of((step // blocks * blocks + block) * size, size)
        target = (hidden_ref, d_gate_ref, d_up_ref)[k]
        return pltpu.make_async_copy(
            stage.at[step % 2, k], target.at[pl.ds(start, size), :], stage_sem.at[step % 2, k]
        )

    def out_copy(step):
        block = block_order(chip, step % blocks, chips)
        return pltpu.make_async_copy(
            out.at[step % 2], out_ref.at[step // blocks, pl.ds(2 * block, 2)], keep_sem.at[0, step % 2]
        )

    def back_copy(step):
        block = block_order(chip, step % blocks, chips)
        return pltpu.make_async_copy(
            back.at[1, pl.ds(2 * block, 2)], back_b_ref.at[pl.ds(2 * block, 2)],
            keep_sem.at[1, step % blocks],
        )

    for load in loads:
        load.start()
    own_copies = [
        pltpu.make_async_copy(own_ref.at[m], rows.at[m, me], local_sem.at[m]) for m in range(MB)
    ] + [
        pltpu.make_async_copy(grad_ref, grads.at[0], local_sem.at[2]),
        pltpu.make_async_copy(grad_own_ref.at[1], grads.at[1, me], local_sem.at[3]),
    ]
    for copy in own_copies:
        copy.start()
    meet(chips)
    gathers[0].start()
    for copy in own_copies:
        copy.wait()
    for load in loads:
        load.wait()

    def at(step, number, action):
        @pl.when(step == number)
        def _():
            action()

    def body(step, carry):
        micro_batch = step // blocks
        block = block_order(chip, step % blocks, chips)
        for m in range(MB):
            for hop in range(1, chips):
                at(step, m * blocks + hop, lambda m=m, hop=hop: gathers[m].hop(hop))
        for hop in range(1, chips):
            at(step, blocks + hop, lambda hop=hop: grad_gather.hop(hop))
        at(step, 1, gathers[1].start)
        at(step, 2, grad_gather.start)
        at(step, blocks, scatter.start)
        for m in range(MB):

            @pl.when(micro_batch == m)
            def _():
                gathers[m].take_pair(block - chip)

        @pl.when(micro_batch == 1)
        def _():
            grad_gather.take_pair(block - chip)

        @pl.when(step >= 2)
        def _():
            for k in range(3):
                stage_out(step - 2, k).wait()
            out_copy(step - 2).wait()

        slot = step % 2
        normed = rows[micro_batch, pl.ds(2 * block, 2)].reshape(size, D)
        grad = grads[micro_batch, pl.ds(2 * block, 2)].reshape(size, D)
        logits = dot(normed, router_ref[...])
        names = pl.ds(pl.multiple_of(micro_batch * SEQ_DEV, SEQ_DEV), SEQ_DEV)
        named = named_ref[pl.ds(2 * block, 2), names, :].reshape(size, LANES).astype(F32)
        chosen = jnp.where(named > 0.0, logits, -1e30)
        powers = jnp.where(
            named > 0.0, jnp.exp(chosen - jnp.max(chosen, axis=1, keepdims=True)), 0.0
        )
        gates = powers / jnp.sum(powers, axis=1, keepdims=True)
        lane = lax.broadcasted_iota(jnp.int32, (size, LANES), 1)
        own = [
            jnp.sum(jnp.where(lane == EXP_DEV * me + e, gates, 0.0), axis=1, keepdims=True)
            for e in range(EXP_DEV)
        ]
        gate_grads = [jnp.zeros((size, 1), F32) for _ in range(EXP_DEV)]
        wide = weights.shape[2]
        for left in range(0, wide, 512):
            right = min(left + 512, wide)
            gate_part = dot(normed, weights[0, :, left:right])
            up_part = dot(normed, weights[1, :, left:right])
            down_part = dot(grad, weights[2, :, left:right])
            sigmoid = 1.0 / (1.0 + jnp.exp(-gate_part))
            act = gate_part * sigmoid
            hidden = act * up_part
            product = hidden * down_part
            scales = []
            for e in range(EXP_DEV + 1):
                low, high = max(left, e * FF), min(right, (e + 1) * FF)
                if low >= high:
                    continue
                if e < EXP_DEV:
                    gate_grads[e] += jnp.sum(
                        product[:, low - left : high - left], axis=1, keepdims=True
                    )
                    scales.append(jnp.broadcast_to(own[e], (size, high - low)))
                else:
                    scales.append(jnp.ones((size, high - low), F32))
            scale = scales[0] if len(scales) == 1 else jnp.concatenate(scales, axis=1)
            scaled = down_part * scale
            stage[slot, 0, :, left:right] = (hidden * scale).astype(BF)
            stage[slot, 1, :, left:right] = (
                scaled * up_part * (sigmoid + act * (1.0 - sigmoid))
            ).astype(BF)
            stage[slot, 2, :, left:right] = (scaled * act).astype(BF)
        for k in range(3):
            stage_out(step, k).start()
        for turn in range(chips - 1):
            at(step, blocks + turn, lambda turn=turn: scatter.slot(turn))
        result = dot_nt(stage[slot, 0], weights[2]).astype(BF)
        out[slot] = result.reshape(2, SEQ_DEV, D)
        out_copy(step).start()
        result = (dot_nt(stage[slot, 1], weights[0]) + dot_nt(stage[slot, 2], weights[1])).astype(BF)
        back[micro_batch, pl.ds(2 * block, 2), :, :D] = result.reshape(2, SEQ_DEV, D)
        tail = jnp.zeros((size, LANES), F32)
        for e in range(EXP_DEV):
            high = gate_grads[e].astype(BF).astype(F32)
            tail = jnp.where(lane == EXP_DEV * me + e, high, tail)
            tail = jnp.where(lane == experts + EXP_DEV * me + e, gate_grads[e] - high, tail)
        back[micro_batch, pl.ds(2 * block, 2), :, D:] = tail.astype(BF).reshape(2, SEQ_DEV, LANES)

        @pl.when(micro_batch == 1)
        def _():
            back_copy(step).start()

        return carry

    lax.fori_loop(0, MB * blocks, body, 0)
    last = MB * blocks
    row_copies = [
        pltpu.make_async_copy(rows.at[m], rows_ref.at[m], local_sem.at[m]) for m in range(MB)
    ] + [
        pltpu.make_async_copy(grads.at[m], grads_ref.at[m], local_sem.at[2 + m]) for m in range(MB)
    ]
    for copy in row_copies:
        copy.start()
    scatter.finish(back_a_ref)
    for m in range(MB):
        gathers[m].finish(False)
    grad_gather.finish(False)
    for copy in row_copies:
        copy.wait()
    for step in (last - 2, last - 1):
        for k in range(3):
            stage_out(step, k).wait()
        out_copy(step).wait()
    for turn in range(blocks):
        back_copy(blocks + turn).wait()


def seq_all_scratch(rows, width):
    groups = 4
    return [
        pltpu.VMEM((rows, groups * width), BF),
        pltpu.VMEM((groups - 1, rows, width), BF),
        pltpu.VMEM((rows, groups * width), BF),
    ] + [pltpu.SemaphoreType.DMA((groups,))] * 4


class SeqAll:
    def __init__(self, scratch):
        self.low, self.arrived, self.whole = scratch[:3]
        self.first_send, self.first_recv, self.last_send, self.last_recv = scratch[3:]
        self.groups = 4
        self.width = self.arrived.shape[2]
        self.group = lax.axis_index("seq")

    def _part(self, ref, device):
        return ref.at[:, pl.ds(pl.multiple_of(device * self.width, LANES), self.width)]

    def _copy(self, source, target, send, recv, away):
        return pltpu.make_async_remote_copy(
            src_ref=source, dst_ref=target, send_sem=send.at[away], recv_sem=recv.at[away],
            device_id={"seq": (self.group + away) % self.groups}, device_id_type=MESH,
        )

    def _first(self, away):
        part = self._part(self.low, (self.group + away) % self.groups)
        return self._copy(part, self.arrived.at[away - 1], self.first_send, self.first_recv, away)

    def _last(self, away):
        part = self._part(self.whole, self.group)
        return self._copy(part, part, self.last_send, self.last_recv, away)

    def start(self):
        for away in range(1, self.groups):
            self._first(away).start()

    def middle(self):
        total = self._part(self.low, self.group)[...].astype(F32)
        for away in range(1, self.groups):
            self._first(away).wait_recv()
            total += self.arrived[away - 1].astype(F32)
        self._part(self.whole, self.group)[...] = total.astype(BF)
        for away in range(1, self.groups):
            self._last(away).start()

    def take(self):
        for away in range(1, self.groups):
            part = self._part(self.whole, (self.group + self.groups - away) % self.groups)
            self._copy(part, part, self.last_send, self.last_recv, away).wait_recv()

    def finish(self):
        for away in range(1, self.groups):
            self._first(away).wait_send()
            self._last(away).wait_send()


def packed(padded, devices):
    share = FF // devices
    return jnp.concatenate(
        [padded[:, device * HD : device * HD + share] for device in range(devices)], axis=1
    )


def expert_sums(
    chips,
    rows_ref, grads_ref, hidden_ref, d_gate_ref, d_up_ref, shared_h_ref, shared_g_ref, shared_u_ref, back_ref,
    gate_ref, up_ref, down_ref, back_b_ref, shared_outs, gate_rows_ref, up_rows_ref,
    mine, pair, line, local_sem, stage, stage_sem, shared, arrived, summed, held, *sems,
):
    chip, core = place()
    devices = 2 * chips
    half = D // 2
    matrix, side = pl.program_id(0), pl.program_id(1)
    step = 2 * matrix + side
    last = 2 * 3 * EXP_DEV - 1
    scatter = Scatter(
        chips,
        lambda to: back_ref.at[2 * to + 1 - core],
        lambda to: mine.at[to],
        pair, line, sems[:6],
    )
    spread = Spread(
        devices, 4, 1,
        lambda owner, k: shared.at[owner],
        lambda k, device: device >= 0,
        lambda device, k: device,
        arrived, summed, held, devices * HD, sems[6:13],
    )
    routed = [
        SeqSum(source.at[0], target, k % 2 == 0, k, sems[13:])
        for k, (source, target) in enumerate(((gate_ref, gate_rows_ref), (up_ref, up_rows_ref)))
    ]
    targets = [(gate_ref, 0), (up_ref, 0), (gate_ref, 1), (up_ref, 1), (down_ref, 0), (down_ref, 1)]

    def write(number):
        target, e = targets[number // 2]
        part = pl.ds(number % 2 * half, half)
        return pltpu.make_async_copy(
            stage.at[number % 2], target.at[e, part], stage_sem.at[number % 2]
        )

    def at(number, action):
        @pl.when(step == number)
        def _():
            action()

    def begin():
        loads = [
            pltpu.make_async_copy(back_ref.at[2 * to + core], mine.at[to], local_sem.at[to])
            for to in range(chips)
        ]
        for load in loads:
            load.start()
        meet_all(("seq", "exp"))
        scatter.start()
        for load in loads:
            load.wait()

    at(0, begin)
    for number in range(2, last + 1):
        at(number, lambda number=number: write(number - 2).wait())
    at(2, lambda: scatter.slot(0))
    at(3, routed[0].start)
    at(5, routed[1].start)
    at(4, lambda: scatter.slot(1))
    at(6, lambda: scatter.slot(2))
    at(7, spread.middle)
    slot = step % 2

    @pl.when(jnp.logical_or(matrix == 0, matrix == 2))
    def _():
        stage[slot] = dot_tn(rows_ref[...], d_gate_ref[...]).astype(BF)

    @pl.when(jnp.logical_or(matrix == 1, matrix == 3))
    def _():
        stage[slot] = dot_tn(rows_ref[...], d_up_ref[...]).astype(BF)

    @pl.when(matrix >= 4)
    def _():
        stage[slot] = dot_tn(grads_ref[...], hidden_ref[...]).astype(BF)

    @pl.when(matrix == 0)
    def _():
        part = pl.ds(pl.multiple_of(side * half, half), half)
        shared[0, part, :] = dot_tn(rows_ref[...], shared_g_ref[...]).astype(BF)
        shared[1, part, :] = dot_tn(rows_ref[...], shared_u_ref[...]).astype(BF)
        shared[2, part, :] = dot_tn(grads_ref[...], shared_h_ref[...]).astype(BF)

    for number in range(last + 1):
        at(number, lambda number=number: write(number).start())
    at(1, spread.start)
    at(8, lambda: scatter.finish(back_b_ref))
    at(9, spread.hand_out)
    at(9, routed[0].middle)

    @pl.when(step == last)
    def _():
        routed[1].middle()
        write(last - 1).wait()
        write(last).wait()
        spread.take()
        for kind, target in enumerate(shared_outs):
            target[...] = packed(spread.of_kind(kind)[...].astype(F32), devices)
        for job in routed:
            job.finish()
        spread.finish()


def meet_all(axes):
    barrier = pltpu.get_barrier_semaphore()
    count = 0
    for axis in axes:
        size = lax.axis_size(axis)
        for away in range(1, size):
            other = (lax.axis_index(axis) + away) % size
            pl.semaphore_signal(barrier, inc=1, device_id={axis: other}, device_id_type=MESH)
            count += 1
    pl.semaphore_wait(barrier, count)


FIRST_EXTRA, EXTRA_APART = 2, 3


def slot_head(slot, device, devices):
    return device if slot == 0 else devices + (device - FIRST_EXTRA) // EXTRA_APART


def slot_lives(slot, device, devices):
    if slot == 0:
        return device >= 0
    past = device - FIRST_EXTRA
    return jnp.logical_and(
        jnp.logical_and(past >= 0, past % EXTRA_APART == 0),
        past < EXTRA_APART * (HEADS - devices),
    )


def spread_sems(devices, groups, units):
    return [
        pltpu.SemaphoreType.DMA((groups - 1, units)),
        pltpu.SemaphoreType.DMA((groups - 1, units)),
        pltpu.SemaphoreType.DMA((units,)),
        pltpu.SemaphoreType.DMA((devices, units)),
        pltpu.SemaphoreType.DMA((devices, units)),
        pltpu.SemaphoreType.DMA((groups,)),
        pltpu.SemaphoreType.DMA((groups,)),
    ]


class Spread:
    def __init__(self, devices, groups, units, unit, lives, column, arrived, summed, held, width, sems):
        self.devices, self.groups, self.units = devices, groups, units
        self.unit, self.lives, self.column = unit, lives, column
        self.arrived, self.summed, self.held, self.width = arrived, summed, held, width
        self.first_send, self.first_recv, self.local_sem = sems[:3]
        self.second_send, self.second_recv, self.third_send, self.third_recv = sems[3:]
        self.kinds = groups - 1
        self.rows = D // devices
        self.group, self.me = lax.axis_index("seq"), lax.axis_index("exp")

    def _rows(self, device):
        return pl.ds(pl.multiple_of(device * self.rows, 32), self.rows)

    def _columns(self, device, k):
        return pl.ds(pl.multiple_of(self.column(device, k) * HD, HD), HD)

    def _along_seq(self, source, target, send, recv, away):
        return pltpu.make_async_remote_copy(
            src_ref=source, dst_ref=target, send_sem=send, recv_sem=recv,
            device_id={"seq": (self.group + away) % self.groups}, device_id_type=MESH,
        )

    def _along_exp(self, source, target, away, k):
        return pltpu.make_async_remote_copy(
            src_ref=source, dst_ref=target,
            send_sem=self.second_send.at[away, k], recv_sem=self.second_recv.at[away, k],
            device_id={"exp": (self.me + away) % self.devices}, device_id_type=MESH,
        )

    def _first(self, away, k):
        owner = (self.group + away) % self.groups
        return self._along_seq(
            self.unit(owner, k), self.arrived.at[away - 1, k],
            self.first_send.at[away - 1, k], self.first_recv.at[away - 1, k], away,
        )

    def _second(self, away, k):
        other = (self.me + away) % self.devices
        return self._along_exp(
            self.summed.at[k, self._rows(other)], self.held.at[0, :, self._columns(self.me, k)], away, k
        )

    def _own(self, k):
        return pltpu.make_async_copy(
            self.summed.at[k, self._rows(self.me)], self.held.at[0, :, self._columns(self.me, k)],
            self.local_sem.at[k],
        )

    def _third(self, away):
        return self._along_seq(
            self.held.at[0, :, : self.width], self.held.at[away, :, : self.width],
            self.third_send.at[away], self.third_recv.at[away], away,
        )

    def _sends_first(self, action):
        for k in range(self.units):
            for away in range(1, self.groups):

                @pl.when(
                    jnp.logical_and(
                        (self.group + away) % self.groups < self.kinds, self.lives(k, self.me)
                    )
                )
                def _():
                    action(self._first(away, k))

    def start(self):
        self._sends_first(lambda copy: copy.start())

    def middle(self):
        @pl.when(self.group < self.kinds)
        def _():
            for k in range(self.units):

                @pl.when(self.lives(k, self.me))
                def _():
                    total = self.unit(self.group, k)[...].astype(F32)
                    for away in range(1, self.groups):
                        block = self.arrived.at[away - 1, k]
                        self._along_seq(
                            block, block, self.first_send.at[away - 1, k],
                            self.first_recv.at[away - 1, k], away,
                        ).wait_recv()
                        total += block[...].astype(F32)
                    self.summed[k] = total.astype(BF)
                    for away in range(1, self.devices):
                        self._second(away, k).start()
                    self._own(k).start()

    def hand_out(self):
        @pl.when(self.group < self.kinds)
        def _():
            for k in range(self.units):

                @pl.when(self.lives(k, self.me))
                def _():
                    self._own(k).wait()

                for away in range(1, self.devices):
                    source = (self.me + self.devices - away) % self.devices

                    @pl.when(self.lives(k, source))
                    def _():
                        block = self.held.at[0, :, self._columns(source, k)]
                        self._along_exp(block, block, away, k).wait_recv()

            for away in range(1, self.groups):
                self._third(away).start()

    def take(self):
        for away in range(1, self.groups):

            @pl.when((self.group + self.groups - away) % self.groups < self.kinds)
            def _():
                self._third(away).wait_recv()

    def of_kind(self, kind):
        return self.held.at[(self.group + self.groups - kind) % self.groups]

    def finish(self):
        self._sends_first(lambda copy: copy.wait_send())

        @pl.when(self.group < self.kinds)
        def _():
            for k in range(self.units):

                @pl.when(self.lives(k, self.me))
                def _():
                    for away in range(1, self.devices):
                        self._second(away, k).wait_send()

            for away in range(1, self.groups):
                self._third(away).wait_send()


def seq_scratch(jobs):
    rows = D // 4
    return [
        pltpu.VMEM((jobs, 2, rows, FF), BF),
        pltpu.VMEM((jobs, 2, rows, FF), BF),
        pltpu.VMEM((jobs, rows, FF), BF),
        pltpu.VMEM((rows, FF), F32),
        pltpu.SemaphoreType.DMA((jobs, 2)),
        pltpu.SemaphoreType.DMA((jobs, 2)),
        pltpu.SemaphoreType.DMA((jobs, 2)),
        pltpu.SemaphoreType.DMA((jobs,)),
        pltpu.SemaphoreType.DMA((jobs,)),
        pltpu.SemaphoreType.DMA((jobs,)),
    ]


class SeqSum:
    def __init__(self, source, out, x_first, job, scratch):
        mine, arrived, last, result = scratch[:4]
        self.source, self.out, self.x_first = source, out, x_first
        self.mine, self.arrived, self.last = mine.at[job], arrived.at[job], last.at[job]
        self.result = result
        self.first_send, self.first_recv, self.load_sem = [sem.at[job] for sem in scratch[4:7]]
        self.last_send, self.last_recv, self.out_sem = [sem.at[job] for sem in scratch[7:]]
        group = lax.axis_index("seq")
        self.x, self.y = group % 2, group // 2
        self.rows = source.shape[0] // 4
        self.own = self.y if x_first else self.x

    def _neighbour(self, along_x):
        return 2 * self.y + 1 - self.x if along_x else 2 * (1 - self.y) + self.x

    def _block(self, i, kept):
        side = self.x if self.x_first else self.y
        side = side if kept else 1 - side
        number = 2 * i + side if self.x_first else 2 * side + i
        return self.source.at[pl.ds(pl.multiple_of(number * self.rows, 32), self.rows)]

    def _copy(self, source, target, send, recv, along_x):
        return pltpu.make_async_remote_copy(
            src_ref=source, dst_ref=target, send_sem=send, recv_sem=recv,
            device_id={"seq": self._neighbour(along_x)}, device_id_type=MESH,
        )

    def _first(self, i):
        return self._copy(
            self._block(i, False), self.arrived.at[i], self.first_send.at[i],
            self.first_recv.at[i], self.x_first,
        )

    def _load(self, i):
        return pltpu.make_async_copy(self._block(i, True), self.mine.at[i], self.load_sem.at[i])

    def _last(self):
        return self._copy(
            self.mine.at[1 - self.own], self.last, self.last_send, self.last_recv,
            not self.x_first,
        )

    def _write(self):
        return pltpu.make_async_copy(self.result, self.out, self.out_sem)

    def start(self):
        for i in range(2):
            self._first(i).start()
            self._load(i).start()

    def middle(self):
        for i in range(2):
            self._first(i).wait_recv()
            self._load(i).wait()
            self.mine[i] = (self.mine[i].astype(F32) + self.arrived[i].astype(F32)).astype(BF)
        self._last().start()

    def finish(self):
        self._last().wait_recv()
        self.result[...] = self.mine[self.own].astype(F32) + self.last[...].astype(F32)
        self._write().start()
        for i in range(2):
            self._first(i).wait_send()
        self._last().wait_send()
        self._write().wait()


def heads_forward(
    chips, slots,
    tokens_ref, grad_own_ref, named_own_ref, gain_one_ref, gain_two_ref, cos_ref, sin_ref, w_refs, w_out_ref,
    normed_ref, qkv_ref, mixed_ref, lse_ref, own_mixed_ref, hidden_ref, two_ref, w_all, grad_ref, named_ref,
    rows, w_sem, local_sem, send_sem, recv_sem, *sems,
):
    devices = 2 * chips
    me = lax.axis_index("exp")
    chip, _ = place()
    length = SEQ_DEV * devices
    size = 2 * SEQ_DEV
    step = BLOCK
    gathers = [Gather(chips, tokens_ref.at[m], rows.at[m], sems[6 * m : 6 * m + 6]) for m in range(MB)]
    later = [
        Gather(chips, named_own_ref, named_ref, sems[12:18]),
        Gather(chips, grad_own_ref.at[0], grad_ref, sems[18:24]),
    ]
    keeps = [
        pltpu.make_async_copy(source, target, local_sem.at[number])
        for number, (source, target) in enumerate(
            [(tokens_ref.at[m], rows.at[m, me]) for m in range(MB)]
            + [(named_own_ref, named_ref.at[me]), (grad_own_ref.at[0], grad_ref.at[me])]
        )
    ]

    def load(slot, j):
        head = jnp.clip(slot_head(slot, me, devices), 0, HEADS - 1)
        unit = 3 * slot + j
        return pltpu.make_async_copy(
            w_refs[j].at[:, pl.ds(pl.multiple_of(head * HD, HD), HD)],
            w_all.at[:, unit * HD : (unit + 1) * HD],
            w_sem.at[unit],
        )

    def head_columns(m, device, slot):
        return own_mixed_ref.at[
            m, :, pl.ds(pl.multiple_of(slot_head(slot, device, devices) * HD, HD), HD)
        ]

    def rows_of(m, device, slot):
        part = pl.ds(pl.multiple_of(device * SEQ_DEV, SEQ_DEV), SEQ_DEV)
        return mixed_ref.at[m, part, slot * HD : (slot + 1) * HD]

    def give(m, away, slot):
        other = (me + away) % devices
        return pltpu.make_async_remote_copy(
            src_ref=rows_of(m, other, slot),
            dst_ref=head_columns(m, me, slot),
            send_sem=send_sem.at[m, away, slot],
            recv_sem=recv_sem.at[m, away, slot],
            device_id={"exp": other},
            device_id_type=MESH,
        )

    def keep_own(m, slot):
        return pltpu.make_async_copy(
            rows_of(m, me, slot), head_columns(m, me, slot), recv_sem.at[m, 0, slot]
        )

    def take(m, away, slot):
        block = head_columns(m, (me + devices - away) % devices, slot)
        return pltpu.make_async_remote_copy(
            src_ref=block,
            dst_ref=block,
            send_sem=send_sem.at[m, away, slot],
            recv_sem=recv_sem.at[m, away, slot],
            device_id={"exp": (me + away) % devices},
            device_id_type=MESH,
        )

    for copy in keeps:
        copy.start()
    for slot in range(slots):
        for j in range(3):
            load(slot, j).start()
    meet_all(("exp",))
    gathers[0].start()
    for copy in keeps:
        copy.wait()
    for slot in range(slots):
        for j in range(3):
            load(slot, j).wait()

    def body(m, carry):
        def at(number, action):
            @pl.when(m == number)
            def _():
                action()

        for turn_ in range(chips):
            block = block_order(chip, turn_, chips)
            for number in range(MB):
                if turn_ > 0:
                    at(number, lambda number=number: gathers[number].hop(turn_))
                at(number, lambda number=number: gathers[number].take_pair(block - chip))
            if turn_ == chips - 2:
                at(0, gathers[1].start)
                at(1, later[0].start)
            if turn_ == chips - 1:
                at(1, later[1].start)
            part = pl.ds(pl.multiple_of(block * size, size), size)
            tokens = rows[m, pl.ds(2 * block, 2)].reshape(size, D).astype(F32)
            normed = norm_rows(tokens, gain_one_ref[...]).astype(BF)
            normed_ref[m, part, :] = normed
            qkv = dot(normed, w_all[...])
            for unit in range(3 * slots):
                values = qkv[:, unit * HD : (unit + 1) * HD]
                if unit % 3 < 2:
                    values = turn(values, cos_ref[part, :], sin_ref[part, :])
                qkv_ref[m, part, unit * HD : (unit + 1) * HD] = values.astype(BF)
        for slot in range(slots):
            base = 3 * HD * slot
            for start in range(0, length, step):
                stop = start + step
                scores = visible_scores(
                    qkv_ref[m, start:stop, base : base + HD],
                    qkv_ref[m, :stop, base + HD : base + 2 * HD],
                    start,
                )
                largest = jnp.max(scores, axis=-1, keepdims=True)
                powers = jnp.exp(scores - largest)
                total = jnp.sum(powers, axis=-1, keepdims=True)
                attention = (powers * (1.0 / total)).astype(BF)
                mixed = dot(attention, qkv_ref[m, :stop, base + 2 * HD : base + 3 * HD])
                mixed_ref[m, start:stop, slot * HD : (slot + 1) * HD] = mixed.astype(BF)
                lse_ref[m, slot, start:stop, :] = largest + jnp.log(total)
            for number in range(MB):

                @pl.when(jnp.logical_and(m == number, slot_lives(slot, me, devices)))
                def _():
                    for away in range(1, devices):
                        give(number, away, slot).start()
                    keep_own(number, slot).start()

            at(1, lambda: later[slot].hop(1)) if slot < 2 else None
        return carry

    lax.fori_loop(0, MB, body, 0)

    def finish_rows(m):
        for slot in range(slots):

            @pl.when(slot_lives(slot, me, devices))
            def _():
                keep_own(m, slot).wait()

            for away in range(1, devices):

                @pl.when(slot_lives(slot, (me + devices - away) % devices, devices))
                def _():
                    take(m, away, slot).wait_recv()

        hidden = tokens_ref[m].astype(F32) + dot(own_mixed_ref[m], w_out_ref[...])
        hidden_ref[m] = hidden
        two_ref[m] = norm_rows(hidden, gain_two_ref[...]).astype(BF)

    finish_rows(0)
    for hop in range(2, chips):
        later[0].hop(hop)
    later[1].hop(2)
    finish_rows(1)
    for hop in range(3, chips):
        later[1].hop(hop)
    for gather in gathers:
        gather.finish(False)
    for gather in later:
        gather.finish(True)
    for m in range(MB):
        for slot in range(slots):

            @pl.when(slot_lives(slot, me, devices))
            def _():
                for away in range(1, devices):
                    give(m, away, slot).wait_send()


def heads_backward(
    chips, slots,
    own_ref, qkv_ref, mixed_ref, lse_ref, cos_ref, sin_ref, w_ref, own_mixed_ref, mix_ref, small_ref,
    normed_ref, gate_ref, up_ref, down_ref,
    sums_ref, grad_a_ref, grad_b_ref, w_out_out, small_out, job_outs,
    d_mixed, probs, raw, parts, d_keys, d_values, pairs, lines,
    part, weight_pair, weight_line, result, normed, normed_sem, local_sem, send_sem, recv_sem, *sems,
):
    devices = 2 * chips
    me = lax.axis_index("exp")
    core = me % 2
    length = SEQ_DEV * devices
    step = BLOCK
    factor = HD ** (-0.5)
    scatters = [
        Scatter(
            chips,
            lambda to, m=m: parts.at[m, 2 * to + 1 - core],
            lambda to, m=m: parts.at[m, 2 * to + core],
            pairs.at[m], lines.at[m], sems[6 * m : 6 * m + 6],
        )
        for m in range(MB)
    ]

    routed = [
        SeqSum(source, target, k % 2 == 0, k, sems[6 * MB + 6 : -7])
        for k, (source, target) in enumerate(
            zip((gate_ref.at[1], up_ref.at[1], down_ref.at[0]), job_outs)
        )
    ]

    rows = D // devices

    def row_block(device):
        return pl.ds(pl.multiple_of(device * rows, 32), rows)

    weight = Scatter(
        chips,
        lambda to: part.at[row_block(2 * to + 1 - core)],
        lambda to: part.at[row_block(2 * to + core)],
        weight_pair, weight_line, sems[6 * MB : 6 * MB + 6],
    )
    weight_all = SeqAll(sems[-7:])
    far = D + LANES

    def load(number):
        return pltpu.make_async_copy(
            normed_ref.at[:, :, 256 * number : 256 * (number + 1)], normed.at[number % 2],
            normed_sem.at[number % 2],
        )

    def block_at(m, device, slot):
        rows = pl.ds(pl.multiple_of(device * SEQ_DEV, SEQ_DEV), SEQ_DEV)
        return d_mixed.at[m, rows, slot * HD : (slot + 1) * HD]

    def columns(m, head):
        return own_ref.at[m, :, pl.ds(pl.multiple_of(head * HD, HD), HD)]

    def exchange(m, away, slot):
        other = (me + away) % devices
        return pltpu.make_async_remote_copy(
            src_ref=columns(m, slot_head(slot, other, devices)),
            dst_ref=block_at(m, me, slot),
            send_sem=send_sem.at[m, away, slot],
            recv_sem=recv_sem.at[m, away, slot],
            device_id={"exp": other},
            device_id_type=MESH,
        )

    def arrival(m, away, slot):
        block = block_at(m, (me + devices - away) % devices, slot)
        return pltpu.make_async_remote_copy(
            src_ref=block,
            dst_ref=block,
            send_sem=send_sem.at[m, away, slot],
            recv_sem=recv_sem.at[m, away, slot],
            device_id={"exp": (me + away) % devices},
            device_id_type=MESH,
        )

    def keep(m, slot):
        return pltpu.make_async_copy(
            columns(m, slot_head(slot, me, devices)), block_at(m, me, slot), local_sem.at[m, slot]
        )

    meet_all(("seq", "exp"))
    for m in range(MB):
        for away in range(1, devices):
            for slot in range(slots):

                @pl.when(slot_lives(slot, (me + away) % devices, devices))
                def _():
                    exchange(m, away, slot).start()

        for slot in range(slots):

            @pl.when(slot_lives(slot, me, devices))
            def _():
                keep(m, slot).start()

            @pl.when(jnp.logical_not(slot_lives(slot, me, devices)))
            def _():
                d_mixed[m, :, slot * HD : (slot + 1) * HD] = jnp.zeros((length, HD), BF)

    routed[0].start()
    routed[1].start()
    for number in range(2):
        load(number).start()
    for left in range(0, D, 256):
        part[left : left + 256, :D] = dot_tn(
            own_mixed_ref[:, left : left + 256], mix_ref[...]
        ).astype(BF)
    part[:, D:] = small_ref[...]
    weight.start()

    def weigh(m):
        for slot in range(slots):
            base = 3 * HD * slot
            for start in range(0, length, step):
                stop = start + step
                scores = visible_scores(
                    qkv_ref[m, start:stop, base : base + HD],
                    qkv_ref[m, :stop, base + HD : base + 2 * HD],
                    start,
                )
                probs[slot, start:stop, :stop] = jnp.exp(
                    scores - lse_ref[m, slot, start:stop, :]
                ).astype(BF)

    def body(m, carry):
        weigh(m)
        for number in range(MB):

            @pl.when(m == number)
            def _():
                for slot in range(slots):

                    @pl.when(slot_lives(slot, me, devices))
                    def _():
                        keep(number, slot).wait()
                        for away in range(1, devices):
                            arrival(number, away, slot).wait_recv()

        @pl.when(m == 1)
        def _():
            scatters[0].start()
            for turn_ in range(min(slots, chips - 1), chips - 1):
                weight.slot(turn_)
            routed[0].middle()
            routed[2].start()

        for slot in range(slots):
            base = 3 * HD * slot
            d_keys[...] = jnp.zeros_like(d_keys)
            d_values[...] = jnp.zeros_like(d_values)
            for start in range(0, length, step):
                stop = start + step
                queries = qkv_ref[m, start:stop, base : base + HD]
                keys = qkv_ref[m, :stop, base + HD : base + 2 * HD]
                values = qkv_ref[m, :stop, base + 2 * HD : base + 3 * HD]
                d_mix = d_mixed[m, start:stop, slot * HD : (slot + 1) * HD]
                mixed = mixed_ref[m, start:stop, slot * HD : (slot + 1) * HD]
                row_term = jnp.sum(d_mix.astype(F32) * mixed.astype(F32), axis=1, keepdims=True)
                attention = probs[slot, start:stop, :stop]
                d_scores = (attention.astype(F32) * (dot_nt(d_mix, values) - row_term)).astype(BF)
                turned = turn(dot(d_scores, keys) * factor, cos_ref[start:stop, :], -sin_ref[start:stop, :])
                raw[m, start:stop, base : base + HD] = turned.astype(BF)
                d_keys[:stop, :] += dot_tn(d_scores, queries)
                d_values[:stop, :] += dot_tn(attention, d_mix)
            turned = turn(d_keys[...] * factor, cos_ref[...], -sin_ref[...])
            raw[m, :, base + HD : base + 2 * HD] = turned.astype(BF)
            raw[m, :, base + 2 * HD : base + 3 * HD] = d_values[...].astype(BF)

            @pl.when(m == 1)
            def _():
                scatters[0].slot(min(slot, chips - 2))
                if slot == 0:
                    routed[1].middle()
                else:
                    weight.finish(result)
                    weight_all.low[:, :far] = result[...].astype(BF)
                    weight_all.low[:, far:] = jnp.zeros((rows, LANES), BF)
                    weight_all.start()

            @pl.when(m == 0)
            def _():
                weight.slot(min(slot, chips - 2))

        for start in range(0, length, step):
            back = dot_nt(raw[m, start : start + step, :], w_ref[...]).astype(BF)
            first = start // SEQ_DEV
            parts[m, first : first + step // SEQ_DEV] = back.reshape(step // SEQ_DEV, SEQ_DEV, D)
        return carry

    lax.fori_loop(0, MB, body, 0)
    scatters[1].start()
    routed[0].finish()
    for turn_ in range(min(slots, chips - 1), chips - 1):
        scatters[0].slot(turn_)
    ticks = [lambda t=t: scatters[1].slot(t) for t in range(chips - 1)]
    for number, left in enumerate(range(0, D, 256)):
        load(number).wait()
        total = dot_tn(normed[number % 2, 0], raw[0]) + dot_tn(normed[number % 2, 1], raw[1])
        if number + 2 < D // 256:
            load(number + 2).start()
        for unit in range(3 * slots):
            sums_ref[unit, left : left + 256, :] = total[:, unit * HD : (unit + 1) * HD].astype(BF)
        if number < len(ticks):
            ticks[number]()
    scatters[0].finish(grad_a_ref)
    weight_all.middle()
    routed[1].finish()
    routed[2].middle()
    for number in range(D // 256, len(ticks)):
        ticks[number]()
    scatters[1].finish(grad_b_ref)
    weight_all.take()
    w_out_out[...] = weight_all.whole[:, :D].astype(F32)
    small_out[...] = weight_all.whole[:, D:far].astype(F32)
    weight_all.finish()
    routed[2].finish()
    for m in range(MB):
        for away in range(1, devices):
            for slot in range(slots):

                @pl.when(slot_lives(slot, (me + away) % devices, devices))
                def _():
                    exchange(m, away, slot).wait_send()


def spread_sums(
    chips, slots,
    qkv_ref, out_ref, hidden_ref, down_ref,
    query_out, key_out, value_out, layer_ref, routed_out,
    arrived, summed, held, layer, mine, pair, line, mine_sem,
    *sems,
):
    devices = 2 * chips
    me = lax.axis_index("exp")
    core = me % 2
    groups = 4
    outs = [
        Scatter(
            chips,
            lambda to, m=m: out_ref.at[m, 2 * to + 1 - core],
            lambda to, m=m: mine.at[m, to],
            pair.at[m], line.at[m], sems[6 * m : 6 * m + 6],
        )
        for m in range(MB)
    ]
    spread = Spread(
        devices, groups, slots,
        lambda owner, k: qkv_ref.at[owner + (groups - 1) * k],
        lambda k, device: slot_lives(k, device, devices),
        lambda device, k: slot_head(k, device, devices),
        arrived, summed, held, D, sems[6 * MB : 6 * MB + 7],
    )
    routed = SeqSum(down_ref.at[1], routed_out, False, 0, sems[6 * MB + 7 :])
    loads = [
        pltpu.make_async_copy(out_ref.at[m, 2 * to + core], mine.at[m, to], mine_sem.at[m, to])
        for m in range(MB)
        for to in range(chips)
    ]
    for load in loads:
        load.start()
    meet_all(("seq", "exp"))
    spread.start()
    outs[0].start()
    outs[1].start()
    for load in loads:
        load.wait()
    outs[0].slot(0)
    spread.middle()
    routed.start()
    spread.hand_out()
    outs[1].slot(0)
    for turn_ in range(1, chips - 1):
        outs[0].slot(turn_)
        outs[1].slot(turn_)
    routed.middle()
    for m in range(MB):
        outs[m].finish(layer)
        layer_ref[m] = (layer[...] + hidden_ref[m]).astype(BF)
    spread.take()
    for kind, target in enumerate((query_out, key_out, value_out)):
        target[...] = spread.of_kind(kind)[...].astype(F32)
    spread.finish()
    routed.finish()


def taking(us):
    return pl.CostEstimate(flops=int(us * 1.0e9), bytes_accessed=2**20, transcendentals=0)


def like(*shape, dtype=BF):
    return jax.ShapeDtypeStruct(shape, dtype)


IN_VMEM = pl.BlockSpec(memory_space=pltpu.VMEM)
ANYWHERE = pl.BlockSpec(memory_space=pl.ANY)


def experts_on_lines(two_own, grad_own, grad_a, named, expert_at, router_rows, routed, shared, share):
    devices = lax.axis_size("exp")
    me = lax.axis_index("exp")
    experts = expert_at.shape[0]
    chips = devices // 2
    length = SEQ_DEV * devices
    wide = EXP_DEV * FF + LANES
    own_shared = [
        jnp.pad(lax.dynamic_slice(w, (0, me * share), (D, share)), ((0, 0), (0, LANES - share)))
        for w in shared
    ]
    router = jnp.pad(router_rows, ((0, 0), (0, LANES - experts)))
    block_back = (devices, SEQ_DEV, D + LANES)
    sems = [gather_sems(chips)] * MB + [scatter_sems(chips), gather_sems(chips)]

    def call_rows(*operands):
        def kernel(own_ref, grad_own_ref, grad_ref, named_ref, router_ref, *refs):
            expert_rows(
                chips, experts, own_ref, grad_own_ref, grad_ref, named_ref, router_ref,
                refs[:3], refs[3:6], *refs[6:],
            )

        return pl.pallas_call(
            kernel,
            out_shape=(
                like(MB, devices, SEQ_DEV, D),
                like(MB, devices, SEQ_DEV, D),
                like(MB * length, wide),
                like(MB * length, wide),
                like(MB * length, wide),
                like(MB, devices, SEQ_DEV, D),
                like(*block_back),
                like(SEQ_DEV, D + LANES, dtype=F32),
            ),
            in_specs=[IN_VMEM, ANYWHERE, ANYWHERE, IN_VMEM, IN_VMEM] + [ANYWHERE] * 6,
            out_specs=(ANYWHERE,) * 7 + (IN_VMEM,),
            scratch_shapes=[
                pltpu.VMEM((3, D, wide), BF),
                pltpu.VMEM((MB, devices, SEQ_DEV, D), BF),
                pltpu.VMEM((MB, devices, SEQ_DEV, D), BF),
                pltpu.VMEM((2, 3, 2 * SEQ_DEV, wide), BF),
                pltpu.VMEM((2, 2, SEQ_DEV, D), BF),
                pltpu.VMEM((MB, *block_back), BF),
                pltpu.VMEM((chips, SEQ_DEV, D + LANES), BF),
                pltpu.VMEM((chips + 1, SEQ_DEV, D + LANES), BF),
                pltpu.SemaphoreType.DMA((3, EXP_DEV + 1)),
                pltpu.SemaphoreType.DMA((4,)),
                pltpu.SemaphoreType.DMA((2, 3)),
                pltpu.SemaphoreType.DMA((2, chips)),
            ]
            + [sem for group in sems for sem in group],
            compiler_params=pltpu.CompilerParams(
                collective_id=1, has_side_effects=True, vmem_limit_bytes=VMEM_BYTES
            ),
            cost_estimate=taking(100),
            name="expert_rows",
        )(*operands)

    rows, grads, hidden, d_gate, d_up, out_parts, back_b, back_sum_a = call_rows(
        two_own, grad_own, grad_a, named, router, *routed, *own_shared
    )
    flat = MB * length


    def call_sums(*operands):
        def kernel(*refs):
            expert_sums(chips, *refs[:13], refs[13:16], *refs[16:])

        half = D // 2
        by_rows = pl.BlockSpec((flat, half), lambda k, d: (0, d))
        by_grads = pl.BlockSpec((flat, half), lambda k, d: (0, d))

        def for_gate(k, d):
            return (0, (k + 2) // 4)

        def for_up(k, d):
            return (0, k // 3)

        def for_down(k, d):
            return (0, k // 5)

        last = pl.BlockSpec(
            (flat, LANES), lambda k, d: (0, EXP_DEV * FF // LANES), pipeline_mode=pl.Buffered(1)
        )

        def whole(*shape):
            return pl.BlockSpec(shape, lambda k, d: (0,) * len(shape))

        return pl.pallas_call(
            kernel,
            grid=(3 * EXP_DEV, 2),
            out_shape=(like(EXP_DEV, D, FF),) * 3
            + (like(SEQ_DEV, D + LANES, dtype=F32),)
            + (like(D // devices, FF, dtype=F32),) * 3
            + (like(D // 4, FF, dtype=F32),) * 2,
            in_specs=[by_rows, by_grads]
            + [pl.BlockSpec((flat, FF), use) for use in (for_down, for_gate, for_up)]
            + [last] * 3
            + [ANYWHERE],
            out_specs=(ANYWHERE,) * 3
            + (whole(SEQ_DEV, D + LANES),)
            + (whole(D // devices, FF),) * 3
            + (ANYWHERE,) * 2,
            scratch_shapes=[
                pltpu.VMEM((chips, SEQ_DEV, D + LANES), BF),
                pltpu.VMEM((chips, SEQ_DEV, D + LANES), BF),
                pltpu.VMEM((chips + 1, SEQ_DEV, D + LANES), BF),
                pltpu.SemaphoreType.DMA((chips,)),
                pltpu.VMEM((2, half, FF), BF),
                pltpu.SemaphoreType.DMA((2,)),
                pltpu.VMEM((3, D, HD), BF),
                pltpu.VMEM((3, 1, D, HD), BF),
                pltpu.VMEM((1, D, HD), BF),
                pltpu.VMEM((4, D // devices, devices * HD), BF),
            ]
            + scatter_sems(chips)
            + spread_sems(devices, 4, 1)
            + seq_scratch(2),
            compiler_params=pltpu.CompilerParams(
                collective_id=2, has_side_effects=True, vmem_limit_bytes=VMEM_BYTES
            ),
            cost_estimate=taking(60),
            name="expert_sums",
        )(*operands)

    gate_sum, up_sum, down_sum, back_sum_b, *shared_grads, gate_rows, up_rows = call_sums(
        rows.reshape(flat, D), grads.reshape(flat, D), hidden, d_gate, d_up, hidden, d_gate, d_up, back_b
    )
    backs = (back_sum_a, back_sum_b)
    tails = [
        b[:, D : D + experts] + b[:, D + experts : D + 2 * experts] for b in backs
    ]
    return (
        out_parts,
        [b[:, :D] for b in backs],
        tails,
        (gate_rows, up_rows),
        (gate_sum, up_sum, down_sum),
        shared_grads,
    )


def named_softmax(logits, named):
    chosen = jnp.where(named, logits, -jnp.inf)
    powers = jnp.where(named, jnp.exp(chosen - jnp.max(chosen, axis=-1, keepdims=True)), 0.0)
    return powers / jnp.sum(powers, axis=-1, keepdims=True)


def on_device_plain(
    tokens,
    cotangent,
    expert_ids,
    owner_table,
    w_query,
    w_key,
    w_value,
    w_out,
    gain_one,
    gain_two,
    w_router,
    shared_gate,
    shared_up,
    shared_down,
    routed_gate,
    routed_up,
    routed_down,
):
    devices = lax.axis_size("exp")
    groups = lax.axis_size("seq")
    me = lax.axis_index("exp")
    experts = owner_table.shape[0]
    length = SEQ_DEV * devices
    rows_out = D // devices
    slots = -(-HEADS // devices)
    wide = slots * HD
    share = FF // devices
    used = EXP_DEV * FF + share
    padded = -(-used // LANES) * LANES

    head_of = [jnp.minimum(me + slot * devices, HEADS - 1) for slot in range(slots)]
    slot_live = jnp.concatenate(
        [
            jnp.full((HD,), jnp.where(me + slot * devices < HEADS, 1.0, 0.0), F32)
            for slot in range(slots)
        ]
    )

    w_qkv = jnp.concatenate(
        [
            lax.dynamic_slice(weight, (0, head * HD), (D, HD))
            for head in head_of
            for weight in (w_query, w_key, w_value)
        ],
        axis=1,
    )
    w_out_heads = jnp.concatenate(
        [lax.dynamic_slice(w_out, (head * HD, 0), (HD, D)) for head in head_of], axis=0
    )
    cos_table, sin_table = angle_tables(jnp.arange(length).astype(F32))
    sin_table = jnp.where(jnp.arange(HD) < HD // 2, -sin_table, sin_table)
    params = pltpu.CompilerParams(vmem_limit_bytes=VMEM_BYTES)

    forward = pl.pallas_call(
        functools.partial(attend_forward, slots),
        out_shape=(
            like(length, D),
            like(length, 3 * wide),
            like(length, wide),
            like(slots, length, 1, dtype=F32),
        ),
        in_specs=[IN_VMEM] * 5,
        out_specs=(IN_VMEM,) * 4,
        compiler_params=params,
        name="attend_forward",
    )
    backward = pl.pallas_call(
        functools.partial(attend_backward, slots),
        out_shape=(like(wide, D, dtype=F32), like(D, 3 * wide, dtype=F32), like(length, D)),
        in_specs=[IN_VMEM] * 10,
        out_specs=(IN_VMEM,) * 3,
        scratch_shapes=[
            pltpu.VMEM((length, 3 * wide), BF),
            pltpu.VMEM((length, wide), BF),
            pltpu.VMEM((length, HD), F32),
            pltpu.VMEM((length, HD), F32),
        ],
        compiler_params=params,
        name="attend_backward",
    )

    def joined(routed, shared):
        own = lax.dynamic_slice(shared, (0, me * share), (D, share))
        blank = jnp.zeros((D, padded - used), BF)
        return jnp.concatenate([routed[i] for i in range(EXP_DEV)] + [own, blank], axis=1)

    gate_all = joined(routed_gate, shared_gate)
    up_all = joined(routed_up, shared_up)
    down_all = joined(routed_down, shared_down)

    expert_at = jnp.sum(
        (owner_table[:, None] == jnp.arange(experts)[None, :]) * jnp.arange(experts)[:, None],
        axis=0,
    )
    router_rows = jnp.take(w_router, expert_at, axis=1)
    ids_all = lax.all_gather(expert_ids[:, 0], "exp", axis=1, tiled=True)

    first = []
    for micro_batch in range(MB):
        rows_all = gather_exp(tokens[micro_batch, 0])
        normed, qkv, mixed, lse = forward(rows_all, gain_one[None], cos_table, sin_table, w_qkv)
        sent = lax.all_to_all(
            mixed.reshape(devices, SEQ_DEV, wide), "exp", split_axis=0, concat_axis=0, tiled=True
        )
        own_mixed = (
            sent.reshape(devices, SEQ_DEV, slots, HD)
            .transpose(1, 2, 0, 3)
            .reshape(SEQ_DEV, slots * devices * HD)[:, :D]
        )
        rows_in = tokens[micro_batch, 0].astype(F32)
        hidden_one = rows_in + dot(own_mixed, w_out)
        two_low = norm_rows(hidden_one, gain_two).astype(BF)
        two_all = gather_exp(two_low)
        grad_all = gather_exp(cotangent[micro_batch, 0])
        first.append(
            (normed, qkv, mixed, lse, rows_in, hidden_one, two_all, grad_all)
        )

    column = jnp.arange(padded)
    second = []
    for micro_batch in range(MB):
        two_all, grad_all = first[micro_batch][6:]
        logits = dot(two_all, router_rows)
        named = jnp.any(ids_all[micro_batch][:, :, None] == expert_at[None, None, :], axis=1)
        chosen = jnp.where(named, logits, -jnp.inf)
        powers = jnp.where(named, jnp.exp(chosen - jnp.max(chosen, axis=-1, keepdims=True)), 0.0)
        gates = powers / jnp.sum(powers, axis=-1, keepdims=True)
        own_gates = lax.dynamic_slice(gates, (0, me * EXP_DEV), (length, EXP_DEV))
        weight = jnp.where(
            column[None, :] < FF,
            own_gates[:, :1],
            jnp.where(column[None, :] < 2 * FF, own_gates[:, 1:], 1.0),
        )
        gate_part = dot(two_all, gate_all)
        up_part = dot(two_all, up_all)
        down_part = dot(grad_all, down_all)
        sigmoid = jax.nn.sigmoid(gate_part)
        act = gate_part * sigmoid
        hidden = act * up_part
        products = hidden * down_part
        own_grads = jnp.stack(
            [jnp.sum(products[:, i * FF : (i + 1) * FF], axis=1) for i in range(EXP_DEV)], axis=1
        )
        hidden_low = (weight * hidden).astype(BF)
        weighted = weight * down_part
        d_gate = (weighted * up_part * (sigmoid + act * (1.0 - sigmoid))).astype(BF)
        d_up = (weighted * act).astype(BF)
        out_part = scatter_exp(dot_nt(hidden_low, down_all))
        back_part = scatter_exp(dot_nt(d_gate, gate_all) + dot_nt(d_up, up_all))
        gate_grads = lax.all_gather(own_grads, "exp", axis=1, tiled=True)
        grad_logits = (
            gates * (gate_grads - jnp.sum(gates * gate_grads, axis=-1, keepdims=True))
        ).astype(BF)
        second.append((hidden_low, d_gate, d_up, out_part, back_part, grad_logits))

    two_both = jnp.concatenate([f[6] for f in first])
    grad_both = jnp.concatenate([f[7] for f in first])
    gate_sum = dot_tn(two_both, jnp.concatenate([s[1] for s in second]))
    up_sum = dot_tn(two_both, jnp.concatenate([s[2] for s in second]))
    down_sum = dot_tn(grad_both, jnp.concatenate([s[0] for s in second]))

    def routed_sum(total):
        parts = jnp.stack([total[:, i * FF : (i + 1) * FF] for i in range(EXP_DEV)])
        return lax.psum_scatter(
            parts.astype(BF), "seq", scatter_dimension=1, tiled=True
        ).astype(F32)

    def shared_part(total):
        return total[:, EXP_DEV * FF : used]

    outputs_list = []
    grads_list = []
    small = jnp.zeros((D, experts + 2), F32)
    qkv_sum = jnp.zeros((D, 3 * wide), F32)
    out_sum = jnp.zeros((wide, D), F32)
    for micro_batch in range(MB):
        normed, qkv, mixed, lse, rows_in, hidden_one, two_all, _ = first[micro_batch]
        _, _, _, out_part, back_part, grad_logits = second[micro_batch]
        outputs_list.append((hidden_one + out_part).astype(BF))
        own_logits = lax.dynamic_slice(grad_logits, (me * SEQ_DEV, 0), (SEQ_DEV, experts))
        grad_two = back_part + dot_nt(own_logits, router_rows)
        back, gain_terms = norm_back(hidden_one, gain_two, grad_two)
        grad_hidden = cotangent[micro_batch, 0].astype(F32) + back
        own_two = lax.dynamic_slice(two_all, (me * SEQ_DEV, 0), (SEQ_DEV, D))
        router_part = dot_tn(own_two, own_logits)
        mix_all = gather_exp(grad_hidden.astype(BF))
        out_one, qkv_one, grad_part = backward(
            mix_all, normed, qkv, mixed, lse, cos_table, sin_table, w_qkv, w_out_heads, slot_live[None]
        )
        out_sum = out_sum + out_one
        qkv_sum = qkv_sum + qkv_one
        grad_normed = scatter_exp(grad_part)
        back_one, gain_one_terms = norm_back(rows_in, gain_one, grad_normed)
        grads_list.append((grad_hidden + back_one).astype(BF))
        small = small + jnp.concatenate(
            [
                router_part,
                jnp.sum(gain_one_terms, axis=0)[:, None],
                jnp.sum(gain_terms, axis=0)[:, None],
            ],
            axis=1,
        )

    def to_rows(columns):
        parts = columns.astype(BF).reshape(devices, rows_out, columns.shape[1])
        parts = lax.psum_scatter(parts, "seq", scatter_dimension=1, tiled=True)
        return lax.all_to_all(parts, "exp", split_axis=0, concat_axis=0, tiled=True)

    def to_all(rows):
        return lax.all_gather(rows, "seq", axis=0, tiled=True).astype(F32)

    piece = rows_out // groups
    shared_cols = jnp.concatenate([shared_part(t) for t in (gate_sum, up_sum, down_sum)], axis=1)
    shared_rows = to_rows(shared_cols).reshape(devices, piece, 3, share)
    shared_full = to_all(shared_rows.transpose(1, 2, 0, 3).reshape(piece, 3 * FF))
    qkv_rows = to_rows(qkv_sum).reshape(devices, piece, slots, 3, HD)
    qkv_rows = qkv_rows.transpose(1, 3, 2, 0, 4).reshape(piece, 3, slots * devices * HD)
    qkv_full = to_all(qkv_rows[:, :, :D].reshape(piece, 3 * D))
    out_part = lax.psum_scatter(out_sum.astype(BF), "seq", scatter_dimension=1, tiled=True)
    spread = jnp.zeros((slots * devices * HD, D // groups), BF)
    for slot in range(slots):
        spread = lax.dynamic_update_slice(
            spread, out_part[slot * HD : (slot + 1) * HD], ((me + slot * devices) * HD, 0)
        )
    out_rows = lax.psum_scatter(spread[:D], "exp", scatter_dimension=0, tiled=True)
    out_full = lax.all_gather(out_rows, "seq", axis=1, tiled=True).astype(F32)
    small_rows = lax.psum_scatter(
        lax.psum(small, "seq"), "exp", scatter_dimension=0, tiled=True
    )
    place_of = jnp.take(small_rows, owner_table, axis=1)
    return (
        jnp.stack(outputs_list)[:, None],
        jnp.stack(grads_list)[:, None],
        qkv_full[:, :D],
        qkv_full[:, D : 2 * D],
        qkv_full[:, 2 * D :],
        out_full,
        small_rows[:, experts],
        small_rows[:, experts + 1],
        place_of,
        shared_full[:, :FF],
        shared_full[:, FF : 2 * FF],
        shared_full[:, 2 * FF :],
        routed_sum(gate_sum),
        routed_sum(up_sum),
        routed_sum(down_sum),
    )


def on_device_lines(
    tokens,
    cotangent,
    expert_ids,
    owner_table,
    w_query,
    w_key,
    w_value,
    w_out,
    gain_one,
    gain_two,
    w_router,
    shared_gate,
    shared_up,
    shared_down,
    routed_gate,
    routed_up,
    routed_down,
):
    devices = lax.axis_size("exp")
    groups = lax.axis_size("seq")
    me = lax.axis_index("exp")
    chips = devices // 2
    experts = owner_table.shape[0]
    length = SEQ_DEV * devices
    rows_out = D // devices
    slots = -(-HEADS // devices)
    wide = slots * HD
    share = FF // devices
    own = MB * SEQ_DEV

    cos_table, sin_table = turn_tables(length)

    expert_at = jnp.sum(
        (owner_table[:, None] == jnp.arange(experts)[None, :]) * jnp.arange(experts)[:, None],
        axis=0,
    )
    router_rows = jnp.take(w_router, expert_at, axis=1)
    names = jnp.concatenate([expert_at, jnp.full((LANES - experts,), -1, jnp.int32)])
    named_own = jnp.any(expert_ids.reshape(own, TOP)[:, :, None] == names, axis=1).astype(BF)
    tokens_own = tokens.reshape(MB, SEQ_DEV, D)
    grad_own = cotangent.reshape(MB, SEQ_DEV, D)

    def call_forward(*operands):
        def kernel(*refs):
            heads_forward(chips, slots, *refs[:7], refs[7:10], *refs[10:])

        return pl.pallas_call(
            kernel,
            out_shape=(
                like(MB, length, D),
                like(MB, length, 3 * wide),
                like(MB, length, wide),
                like(MB, slots, length, 1, dtype=F32),
                like(MB, SEQ_DEV, D),
                like(MB, SEQ_DEV, D, dtype=F32),
                like(MB, SEQ_DEV, D),
                like(D, 3 * wide),
                like(devices, SEQ_DEV, D),
                like(devices, own, LANES),
            ),
            in_specs=[IN_VMEM, ANYWHERE] + [IN_VMEM] * 5 + [ANYWHERE] * 3 + [IN_VMEM],
            out_specs=(IN_VMEM,) * 8 + (ANYWHERE, IN_VMEM),
            scratch_shapes=[
                pltpu.VMEM((MB, devices, SEQ_DEV, D), BF),
                pltpu.SemaphoreType.DMA((3 * slots,)),
                pltpu.SemaphoreType.DMA((4,)),
                pltpu.SemaphoreType.DMA((MB, devices, slots)),
                pltpu.SemaphoreType.DMA((MB, devices, slots)),
            ]
            + gather_sems(chips) * 4,
            compiler_params=pltpu.CompilerParams(
                collective_id=5, has_side_effects=True, vmem_limit_bytes=VMEM_BYTES
            ),
            cost_estimate=taking(70),
            name="heads_forward",
        )(*operands)

    normed, qkv, mixed, lse, own_mixed, hidden_one, two_low, w_qkv, grad_a, named_all = call_forward(
        tokens_own, grad_own, named_own, gain_one[None], gain_two[None], cos_table, sin_table,
        w_query, w_key, w_value, w_out,
    )
    rows_in = tokens.reshape(own, D).astype(F32)
    hidden_rows = hidden_one
    own_mixed, hidden_one = own_mixed.reshape(own, D), hidden_one.reshape(own, D)
    two_low = two_low.reshape(own, D)
    gates = named_softmax(dot(two_low, router_rows), named_own[:, :experts] > 0)

    out_parts, backs, tails, done, routed_sums, shared_grads = experts_on_lines(
        two_low.reshape(MB, SEQ_DEV, D),
        grad_own,
        grad_a,
        named_all.reshape(devices, MB * SEQ_DEV, LANES),
        expert_at,
        router_rows,
        (routed_gate, routed_up, routed_down),
        (shared_gate, shared_up, shared_down),
        share,
    )
    tail = jnp.concatenate(tails)
    grad_logits = (gates * (tail - jnp.sum(gates * tail, axis=-1, keepdims=True))).astype(BF)
    grad_two = jnp.concatenate(backs) + dot_nt(grad_logits, router_rows)
    back, gain_two_terms = norm_back(hidden_one, gain_two, grad_two)
    grad_hidden = cotangent.reshape(own, D).astype(F32) + back
    grad_mix = grad_hidden.astype(BF)
    d_mixed = dot_nt(grad_mix, w_out).astype(BF)

    quarter = like(D // groups, FF, dtype=F32)
    far = D + LANES
    small = jnp.concatenate(
        [
            dot_tn(two_low, grad_logits),
            jnp.sum(gain_two_terms, axis=0)[:, None],
            jnp.zeros((D, LANES - experts - 1), F32),
        ],
        axis=1,
    ).astype(BF)

    def backward_kernel(*refs):
        heads_backward(chips, slots, *refs[:19], refs[19:22], *refs[22:])

    heads_sum, normed_a, normed_b, w_out_rows, small_rows, gate_two, up_two, down_one = pl.pallas_call(
        backward_kernel,
        out_shape=(
            like(3 * slots, D, HD),
            like(SEQ_DEV, D, dtype=F32),
            like(SEQ_DEV, D, dtype=F32),
            like(rows_out, D, dtype=F32),
            like(rows_out, LANES, dtype=F32),
        )
        + (quarter,) * 3,
        in_specs=[IN_VMEM] * 10 + [ANYWHERE] * 4,
        out_specs=(IN_VMEM,) * 5 + (ANYWHERE,) * 3,
        scratch_shapes=[
            pltpu.VMEM((MB, length, wide), BF),
            pltpu.VMEM((slots, length, length), BF),
            pltpu.VMEM((MB, length, 3 * wide), BF),
            pltpu.VMEM((MB, devices, SEQ_DEV, D), BF),
            pltpu.VMEM((length, HD), F32),
            pltpu.VMEM((length, HD), F32),
            pltpu.VMEM((MB, chips, SEQ_DEV, D), BF),
            pltpu.VMEM((MB, chips + 1, SEQ_DEV, D), BF),
            pltpu.VMEM((D, far), BF),
            pltpu.VMEM((chips, rows_out, far), BF),
            pltpu.VMEM((chips + 1, rows_out, far), BF),
            pltpu.VMEM((rows_out, far), F32),
            pltpu.VMEM((2, MB, length, 256), BF),
            pltpu.SemaphoreType.DMA((2,)),
            pltpu.SemaphoreType.DMA((MB, slots)),
            pltpu.SemaphoreType.DMA((MB, devices, slots)),
            pltpu.SemaphoreType.DMA((MB, devices, slots)),
        ]
        + scatter_sems(chips) * (MB + 1)
        + seq_scratch(3)
        + seq_all_scratch(rows_out, (far + LANES) // groups),
        compiler_params=pltpu.CompilerParams(
            collective_id=3, has_side_effects=True, vmem_limit_bytes=VMEM_BYTES
        ),
        cost_estimate=taking(70),
        name="heads_backward",
    )(
        d_mixed.reshape(MB, SEQ_DEV, D), qkv, mixed, lse, cos_table, sin_table, w_qkv, own_mixed,
        grad_mix, small, normed, *routed_sums,
    )
    grad_normed = jnp.concatenate([normed_a, normed_b])
    back_one, _ = norm_back(rows_in, gain_one, grad_normed)
    grad_tokens = (grad_hidden + back_one).astype(BF)
    *attn, layer_out, down_two = pl.pallas_call(
        functools.partial(spread_sums, chips, slots),
        out_shape=(like(rows_out, D, dtype=F32),) * 3 + (like(MB, SEQ_DEV, D), quarter),
        in_specs=[IN_VMEM, ANYWHERE, IN_VMEM, ANYWHERE],
        out_specs=(IN_VMEM,) * 4 + (ANYWHERE,),
        scratch_shapes=[
            pltpu.VMEM((groups - 1, slots, D, HD), BF),
            pltpu.VMEM((slots, D, HD), BF),
            pltpu.VMEM((groups, rows_out, D), BF),
            pltpu.VMEM((SEQ_DEV, D), F32),
            pltpu.VMEM((MB, chips, SEQ_DEV, D), BF),
            pltpu.VMEM((MB, chips, SEQ_DEV, D), BF),
            pltpu.VMEM((MB, chips + 1, SEQ_DEV, D), BF),
            pltpu.SemaphoreType.DMA((MB, chips)),
        ]
        + scatter_sems(chips) * MB
        + spread_sems(devices, groups, slots)
        + seq_scratch(1),
        compiler_params=pltpu.CompilerParams(
            collective_id=4, has_side_effects=True, vmem_limit_bytes=VMEM_BYTES
        ),
        cost_estimate=taking(80),
        name="spread_sums",
    )(heads_sum, out_parts, hidden_rows, routed_sums[2])
    gain_rows = lax.dynamic_slice(gain_one, (me * rows_out,), (rows_out,))
    gain_one_grad = sum(
        jnp.sum(
            lax.dynamic_slice(weight, (me * rows_out, 0), (rows_out, D)).astype(F32) * grad, axis=1
        )
        for weight, grad in zip((w_query, w_key, w_value), attn)
    ) / gain_rows
    whole = (MB, 1, SEQ_DEV, D)
    return (
        layer_out.reshape(whole),
        grad_tokens.reshape(whole),
        attn[0],
        attn[1],
        attn[2],
        w_out_rows,
        gain_one_grad,
        small_rows[:, experts],
        jnp.take(small_rows[:, :experts], owner_table, axis=1),
        shared_grads[0],
        shared_grads[1],
        shared_grads[2],
        jnp.stack([done[0], gate_two]),
        jnp.stack([done[1], up_two]),
        jnp.stack([down_one, down_two]),
    )


def solution(mesh):
    rows = P(None, "seq", "exp", None)
    placed = (rows,) * 3 + (P(),) * 11 + (P("exp", None, None),) * 3
    wide = P("exp", None)
    on_lines = mesh.shape["exp"] == 8 and mesh.shape["seq"] == 4
    on_device = on_device_lines if on_lines else on_device_plain
    return jax.shard_map(
        on_device,
        mesh=mesh,
        in_specs=placed,
        out_specs=(rows, rows, wide, wide, wide, wide, P("exp"), P("exp"))
        + (wide,) * 4
        + (P("exp", "seq", None),) * 3,
        check_vma=False,
    )
```

```python
import functools
import math

import jax
import jax.numpy as jnp
import numpy as np
from jax import lax
from jax.experimental import pallas as pl
from jax.experimental.pallas import tpu as pltpu
from jax.sharding import PartitionSpec as P

D = 1280
HEADS = 10
HD = 128
FF = 896
TOP = 7
EXP_DEV = 2
MB = 2
SEQ_DEV = 128
LANES = 128
BLOCK = 256
VMEM_BYTES = 62 * 2**20

eps = 1e-06
BF = jnp.bfloat16
F32 = jnp.float32


def norm_rows(inputs, gain):
    return inputs * lax.rsqrt(jnp.mean(inputs * inputs, axis=-1, keepdims=True) + eps) * gain


def norm_back(inputs, gain, grad):
    scale = lax.rsqrt(jnp.mean(inputs * inputs, axis=-1, keepdims=True) + eps)
    unit = inputs * scale
    weighted = grad * gain
    back = scale * (weighted - unit * jnp.mean(weighted * unit, axis=-1, keepdims=True))
    return back, grad * unit


def angle_tables(positions):
    steps_half = jnp.arange(HD // 2).astype(positions.dtype)
    frequency = jnp.exp(steps_half * (-2.0 * math.log(10000.0) / HD))
    angles = positions[:, None] * frequency[None, :]
    angles = jnp.concatenate([angles, angles], axis=-1)
    return (jnp.cos(angles), jnp.sin(angles))


def turn_tables(length):
    angles = np.arange(length)[:, None] * 10000.0 ** (-2.0 * np.arange(HD // 2) / HD)
    cos, sin = np.cos(angles), np.sin(angles)
    return (
        jnp.asarray(np.concatenate([cos, cos], axis=1), F32),
        jnp.asarray(np.concatenate([-sin, sin], axis=1), F32),
    )


def dot(a, b):
    return jnp.dot(a, b, preferred_element_type=F32)


def dot_nt(a, b):
    return lax.dot_general(a, b, (((1,), (1,)), ((), ())), preferred_element_type=F32)


def dot_tn(a, b):
    return lax.dot_general(a, b, (((0,), (0,)), ((), ())), preferred_element_type=F32)


def gather_exp(array):
    return lax.all_gather(array, "exp", axis=0, tiled=True)


def scatter_exp(array):
    return lax.psum_scatter(array.astype(BF), "exp", scatter_dimension=0, tiled=True).astype(F32)


def turn(heads, cos_table, sin_table):
    return heads * cos_table + pltpu.roll(heads, HD // 2, 1) * sin_table


def visible_scores(queries, keys, start):
    scores = dot_nt(queries, keys) * HD ** (-0.5)
    rows = queries.shape[0]
    row = lax.broadcasted_iota(jnp.int32, (rows, rows), 0)
    column = lax.broadcasted_iota(jnp.int32, (rows, rows), 1)
    last = jnp.where(row >= column, scores[:, start:], -1e30)
    return last if start == 0 else jnp.concatenate([scores[:, :start], last], axis=1)


def attend_forward(slots, rows_ref, gain_ref, cos_ref, sin_ref, w_ref, normed_ref, qkv_ref, mixed_ref, lse_ref):
    length = rows_ref.shape[0]
    step = BLOCK if length <= 2048 else BLOCK // 2

    def project(i, carry):
        part = pl.ds(pl.multiple_of(i * step, step), step)
        normed = norm_rows(rows_ref[part, :].astype(F32), gain_ref[...]).astype(BF)
        normed_ref[part, :] = normed
        for slot in range(slots):
            base = 3 * HD * slot
            qkv = dot(normed, w_ref[:, base : base + 3 * HD])
            for j in range(2):
                turned = turn(qkv[:, j * HD : (j + 1) * HD], cos_ref[part, :], sin_ref[part, :])
                qkv_ref[part, base + j * HD : base + (j + 1) * HD] = turned.astype(BF)
            qkv_ref[part, base + 2 * HD : base + 3 * HD] = qkv[:, 2 * HD :].astype(BF)
        return carry

    lax.fori_loop(0, length // step, project, 0)
    for slot in range(slots):
        base = 3 * HD * slot
        for start in range(0, length, step):
            stop = start + step
            scores = visible_scores(
                qkv_ref[start:stop, base : base + HD], qkv_ref[:stop, base + HD : base + 2 * HD], start
            )
            largest = jnp.max(scores, axis=-1, keepdims=True)
            powers = jnp.exp(scores - largest)
            total = jnp.sum(powers, axis=-1, keepdims=True)
            attention = (powers * (1.0 / total)).astype(BF)
            mixed = dot(attention, qkv_ref[:stop, base + 2 * HD : base + 3 * HD])
            mixed_ref[start:stop, slot * HD : (slot + 1) * HD] = mixed.astype(BF)
            lse_ref[slot, start:stop, :] = largest + jnp.log(total)


def attend_backward(
    slots, mix_ref, normed_ref, qkv_ref, mixed_ref, lse_ref, cos_ref, sin_ref, w_ref, w_out_ref, live_ref,
    out_sum_ref, qkv_sum_ref, grad_ref, raw_ref, d_mixed_ref, d_keys_ref, d_values_ref,
):
    length = mix_ref.shape[0]
    step = BLOCK if length <= 2048 else BLOCK // 2
    factor = HD ** (-0.5)

    def project(i, carry):
        part = pl.ds(pl.multiple_of(i * step, step), step)
        d_mixed_ref[part, :] = (dot_nt(mix_ref[part, :], w_out_ref[...]) * live_ref[...]).astype(BF)
        return carry

    lax.fori_loop(0, length // step, project, 0)
    for slot in range(slots):
        base = 3 * HD * slot
        d_keys_ref[...] = jnp.zeros_like(d_keys_ref)
        d_values_ref[...] = jnp.zeros_like(d_values_ref)
        for start in range(0, length, step):
            stop = start + step
            queries = qkv_ref[start:stop, base : base + HD]
            keys = qkv_ref[:stop, base + HD : base + 2 * HD]
            values = qkv_ref[:stop, base + 2 * HD : base + 3 * HD]
            d_mixed = d_mixed_ref[start:stop, slot * HD : (slot + 1) * HD]
            attention = jnp.exp(visible_scores(queries, keys, start) - lse_ref[slot, start:stop, :])
            d_att = dot_nt(d_mixed, values)
            row_term = jnp.sum(attention * d_att, axis=-1, keepdims=True)
            d_scores = (attention * (d_att - row_term)).astype(BF)
            d_queries = dot(d_scores, keys) * factor
            raw = turn(d_queries, cos_ref[start:stop, :], -sin_ref[start:stop, :])
            raw_ref[start:stop, base : base + HD] = raw.astype(BF)
            d_keys_ref[:stop, :] += dot_tn(d_scores, queries)
            d_values_ref[:stop, :] += dot_tn(attention.astype(BF), d_mixed)
        raw = turn(d_keys_ref[...] * factor, cos_ref[...], -sin_ref[...])
        raw_ref[:, base + HD : base + 2 * HD] = raw.astype(BF)
        raw_ref[:, base + 2 * HD : base + 3 * HD] = d_values_ref[...].astype(BF)

    def give(i, carry):
        part = pl.ds(pl.multiple_of(i * step, step), step)
        grad_ref[part, :] = dot_nt(raw_ref[part, :], w_ref[...]).astype(BF)
        return carry

    lax.fori_loop(0, length // step, give, 0)
    out_sum_ref[...] = dot_tn(mixed_ref[...], mix_ref[...])

    def sums(i, carry):
        part = pl.ds(pl.multiple_of(i * 256, 256), 256)
        qkv_sum_ref[part, :] = dot_tn(normed_ref[:, part], raw_ref[...])
        return carry

    lax.fori_loop(0, D // 256, sums, 0)


MESH = pl.DeviceIdType.MESH


def place():
    me = lax.axis_index("exp")
    return me // 2, me % 2


def remote(source, target, send_sem, recv_sem, chip, core):
    return pltpu.make_async_remote_copy(
        src_ref=source,
        dst_ref=target,
        send_sem=send_sem,
        recv_sem=recv_sem,
        device_id={"exp": 2 * chip + core},
        device_id_type=MESH,
    )


def meet(chips):
    chip, core = place()
    barrier = pltpu.get_barrier_semaphore()

    def greet(to_chip, to_core):
        pl.semaphore_signal(
            barrier, inc=1, device_id={"exp": 2 * to_chip + to_core}, device_id_type=MESH
        )

    greet(chip, 1 - core)

    @pl.when(chip < chips - 1)
    def _():
        greet(chip + 1, core)

    @pl.when(chip > 0)
    def _():
        greet(chip - 1, core)

    below = (chip + chips - 1) // chips
    above = (2 * chips - 2 - chip) // chips
    pl.semaphore_wait(barrier, 1 + below + above)


def gather_sems(chips):
    return [pltpu.SemaphoreType.DMA((chips,))] * 4 + [pltpu.SemaphoreType.DMA((2 * chips,))] * 2


class Gather:
    def __init__(self, chips, own, blocks, sems):
        self.chips, self.own, self.blocks = chips, own, blocks
        self.up_send, self.up_recv, self.down_send, self.down_recv = sems[:4]
        self.pair_send, self.pair_recv = sems[4:]

    def _source(self, hop, number):
        return self.own if hop == 0 else self.blocks.at[number]

    def _up(self, hop):
        chip, core = place()
        number = 2 * (chip - hop) + core
        return remote(
            self._source(hop, number), self.blocks.at[number],
            self.up_send.at[hop], self.up_recv.at[hop], chip + 1, core,
        )

    def _down(self, hop):
        chip, core = place()
        number = 2 * (chip + hop) + core
        return remote(
            self._source(hop, number), self.blocks.at[number],
            self.down_send.at[hop], self.down_recv.at[hop], chip - 1, core,
        )

    def _pair(self, away):
        chip, core = place()
        number = 2 * (chip + away) + core
        source = self.own if isinstance(away, int) and away == 0 else self.blocks.at[number]
        slot = away + self.chips
        return remote(
            source, self.blocks.at[number], self.pair_send.at[slot], self.pair_recv.at[slot],
            chip, 1 - core,
        )

    def _from_pair(self, away):
        chip, core = place()
        block = self.blocks.at[2 * (chip + away) + 1 - core]
        slot = away + self.chips
        return remote(
            block, block, self.pair_send.at[slot], self.pair_recv.at[slot], chip, 1 - core
        )

    def start(self):
        chip, _ = place()

        @pl.when(chip < self.chips - 1)
        def _():
            self._up(0).start()

        @pl.when(chip > 0)
        def _():
            self._down(0).start()

        self._pair(0).start()

    def hop(self, hop):
        chip, core = place()

        @pl.when(chip >= hop)
        def _():
            block = self.blocks.at[2 * (chip - hop) + core]
            remote(
                block, block, self.up_send.at[hop - 1], self.up_recv.at[hop - 1], chip, 1 - core
            ).wait_recv()

            @pl.when(chip < self.chips - 1)
            def _():
                self._up(hop).start()

            self._pair(-hop).start()

        @pl.when(chip + hop < self.chips)
        def _():
            block = self.blocks.at[2 * (chip + hop) + core]
            remote(
                block, block, self.down_send.at[hop - 1], self.down_recv.at[hop - 1], chip, 1 - core
            ).wait_recv()

            @pl.when(chip > 0)
            def _():
                self._down(hop).start()

            self._pair(hop).start()

    def take_pair(self, away):
        self._from_pair(away).wait_recv()

    def finish(self, pairs):
        chip, _ = place()
        for away in range(-self.chips + 1, self.chips):

            @pl.when(jnp.logical_and(chip + away >= 0, chip + away < self.chips))
            def _():
                if pairs:
                    self._from_pair(away).wait_recv()
                self._pair(away).wait_send()

        for hop in range(self.chips):

            @pl.when(jnp.logical_and(chip >= hop, chip < self.chips - 1))
            def _():
                self._up(hop).wait_send()

            @pl.when(jnp.logical_and(chip + hop < self.chips, chip > 0))
            def _():
                self._down(hop).wait_send()


def scatter_sems(chips):
    return [pltpu.SemaphoreType.DMA((chips,))] * 6


class Scatter:
    def __init__(self, chips, theirs, mine, pair, line, sems):
        self.chips, self.theirs, self.mine, self.pair, self.line = chips, theirs, mine, pair, line
        self.pair_send, self.pair_recv, self.up_send, self.up_recv = sems[:4]
        self.down_send, self.down_recv = sems[4:]

    def _pair(self, to):
        chip, core = place()
        return remote(
            self.theirs(to), self.pair.at[to], self.pair_send.at[to], self.pair_recv.at[to],
            chip, 1 - core,
        )

    def _up(self, chip, to):
        return remote(
            self.mine(to), self.line.at[to - chip - 1], self.up_send.at[to], self.up_recv.at[to],
            chip + 1, place()[1],
        )

    def _down(self, chip, to):
        return remote(
            self.mine(to), self.line.at[self.chips - chip + 1 + to],
            self.down_send.at[to], self.down_recv.at[to], chip - 1, place()[1],
        )

    def _arrived_up(self, to):
        chip, core = place()
        block = self.line.at[to - chip]
        remote(block, block, self.up_send.at[to], self.up_recv.at[to], chip, 1 - core).wait_recv()
        return block[...].astype(F32)

    def _arrived_down(self, to):
        chip, core = place()
        block = self.line.at[self.chips - chip + to]
        remote(
            block, block, self.down_send.at[to], self.down_recv.at[to], chip, 1 - core
        ).wait_recv()
        return block[...].astype(F32)

    def _both(self, to):
        chip, core = place()
        block = self.pair.at[to]
        remote(
            block, block, self.pair_send.at[to], self.pair_recv.at[to], chip, 1 - core
        ).wait_recv()
        return self.mine(to)[...].astype(F32) + block[...].astype(F32)

    def start(self):
        for to in range(self.chips):
            self._pair(to).start()

    def slot(self, turn):
        chip, _ = place()
        last = self.chips - 1

        @pl.when(chip <= turn)
        def _():
            to = last - turn + chip
            total = self._both(to)

            @pl.when(chip == 0)
            def _():
                self.mine(to)[...] = total.astype(BF)

            @pl.when(chip > 0)
            def _():
                self.mine(to)[...] = (total + self._arrived_up(to)).astype(BF)

            self._up(chip, to).start()

        @pl.when(last - chip <= turn)
        def _():
            to = turn - last + chip
            total = self._both(to)

            @pl.when(chip == last)
            def _():
                self.mine(to)[...] = total.astype(BF)

            @pl.when(chip < last)
            def _():
                self.mine(to)[...] = (total + self._arrived_down(to)).astype(BF)

            self._down(chip, to).start()

    def finish(self, result):
        chip, _ = place()
        last = self.chips - 1
        result[...] = self._both(chip)

        @pl.when(chip > 0)
        def _():
            result[...] += self._arrived_up(chip)

        @pl.when(chip < last)
        def _():
            result[...] += self._arrived_down(chip)

        for to in range(self.chips):
            self._pair(to).wait_send()

            @pl.when(to > chip)
            def _():
                self._up(chip, to).wait_send()

            @pl.when(to < chip)
            def _():
                self._down(chip, to).wait_send()


def part_of(array, index):
    return array.at[index]


def block_order(chip, turn, chips):
    number, bit = 0, 1
    while bit < chips:
        number = number + bit * ((chip // bit + turn // bit) % 2)
        bit = 2 * bit
    return number


def expert_rows(
    chips, experts,
    own_ref, grad_own_ref, grad_ref, named_ref, router_ref, owner_ref, routed_refs, shared_refs,
    rows_ref, grads_ref, hidden_ref, d_gate_ref, d_up_ref, out_ref, back_b_ref, back_a_ref,
    weights, rows, grads, stage, out, back, pair, line, weight_sem, local_sem, stage_sem, keep_sem,
    *sems,
):
    chip, core = place()
    me = 2 * chip + core
    blocks = chips
    size = 2 * SEQ_DEV
    gathers = [Gather(chips, own_ref.at[m], rows.at[m], sems[6 * m : 6 * m + 6]) for m in range(MB)]
    grad_gather = Gather(chips, grad_own_ref.at[1], grads.at[1], sems[18:24])
    scatter = Scatter(
        chips,
        lambda to: back.at[0, 2 * to + 1 - core],
        lambda to: back.at[0, 2 * to + core],
        pair, line, sems[12:18],
    )
    loads = []
    for k in range(3):
        for e in range(EXP_DEV):
            loads.append(
                pltpu.make_async_copy(
                    routed_refs[k].at[e], weights.at[k, :, e * FF : (e + 1) * FF],
                    weight_sem.at[k, e],
                )
            )

    def shared_load(k):
        columns = pl.ds(pl.multiple_of(me * HD, HD), HD)
        return pltpu.make_async_copy(
            shared_refs[k].at[:, columns], weights.at[k, :, EXP_DEV * FF :], weight_sem.at[k, EXP_DEV]
        )

    def shared_loads(action):
        @pl.when(me < FF // HD)
        def _():
            for k in range(3):
                action(shared_load(k))

    def stage_out(step, k):
        block = block_order(chip, step % blocks, chips)
        start = pl.multiple_of((step // blocks * blocks + block) * size, size)
        target = (hidden_ref, d_gate_ref, d_up_ref)[k]
        return pltpu.make_async_copy(
            stage.at[step % 2, k], target.at[pl.ds(start, size), :], stage_sem.at[step % 2, k]
        )

    def out_copy(step):
        block = block_order(chip, step % blocks, chips)
        return pltpu.make_async_copy(
            out.at[step % 2], out_ref.at[step // blocks, pl.ds(2 * block, 2)], keep_sem.at[0, step % 2]
        )

    def back_copy(step):
        block = block_order(chip, step % blocks, chips)
        return pltpu.make_async_copy(
            back.at[1, pl.ds(2 * block, 2)], back_b_ref.at[pl.ds(2 * block, 2)],
            keep_sem.at[1, step % blocks],
        )

    for load in loads:
        load.start()
    shared_loads(lambda copy: copy.start())

    @pl.when(me >= FF // HD)
    def _():
        for k in range(3):
            weights[k, :, EXP_DEV * FF :] = jnp.zeros((D, HD), BF)

    own_copies = [
        pltpu.make_async_copy(own_ref.at[m], rows.at[m, me], local_sem.at[m]) for m in range(MB)
    ] + [
        pltpu.make_async_copy(grad_ref, grads.at[0], local_sem.at[2]),
        pltpu.make_async_copy(grad_own_ref.at[1], grads.at[1, me], local_sem.at[3]),
    ]
    for copy in own_copies:
        copy.start()
    meet(chips)
    gathers[0].start()
    for copy in own_copies:
        copy.wait()
    for load in loads:
        load.wait()
    shared_loads(lambda copy: copy.wait())

    def at(step, number, action):
        @pl.when(step == number)
        def _():
            action()

    def body(step, carry):
        micro_batch = step // blocks
        block = block_order(chip, step % blocks, chips)
        for m in range(MB):
            for hop in range(1, chips):
                at(step, m * blocks + hop, lambda m=m, hop=hop: gathers[m].hop(hop))
        for hop in range(1, chips):
            at(step, blocks + hop, lambda hop=hop: grad_gather.hop(hop))
        at(step, 1, gathers[1].start)
        at(step, 2, grad_gather.start)
        at(step, blocks, scatter.start)
        for m in range(MB):

            @pl.when(micro_batch == m)
            def _():
                gathers[m].take_pair(block - chip)

        @pl.when(micro_batch == 1)
        def _():
            grad_gather.take_pair(block - chip)

        @pl.when(step >= 2)
        def _():
            for k in range(3):
                stage_out(step - 2, k).wait()
            out_copy(step - 2).wait()

        slot = step % 2
        normed = rows[micro_batch, pl.ds(2 * block, 2)].reshape(size, D)
        grad = grads[micro_batch, pl.ds(2 * block, 2)].reshape(size, D)
        logits = dot(normed, router_ref[...])
        names = pl.ds(pl.multiple_of(micro_batch * SEQ_DEV, SEQ_DEV), SEQ_DEV)
        named = named_ref[pl.ds(2 * block, 2), names, :].reshape(size, LANES).astype(F32)
        chosen = jnp.where(named > 0.0, logits, -1e30)
        powers = jnp.where(
            named > 0.0, jnp.exp(chosen - jnp.max(chosen, axis=1, keepdims=True)), 0.0
        )
        gates = powers / jnp.sum(powers, axis=1, keepdims=True)
        own = [
            jnp.sum(jnp.where(owner_ref[...] == EXP_DEV * me + e, gates, 0.0), axis=1, keepdims=True)
            for e in range(EXP_DEV)
        ]
        gate_grads = [jnp.zeros((size, 1), F32) for _ in range(EXP_DEV)]
        wide = weights.shape[2]
        for left in range(0, wide, 512):
            right = min(left + 512, wide)
            gate_part = dot(normed, weights[0, :, left:right])
            up_part = dot(normed, weights[1, :, left:right])
            down_part = dot(grad, weights[2, :, left:right])
            sigmoid = 1.0 / (1.0 + jnp.exp(-gate_part))
            act = gate_part * sigmoid
            hidden = act * up_part
            product = hidden * down_part
            scales = []
            for e in range(EXP_DEV + 1):
                low, high = max(left, e * FF), min(right, (e + 1) * FF)
                if low >= high:
                    continue
                if e < EXP_DEV:
                    gate_grads[e] += jnp.sum(
                        product[:, low - left : high - left], axis=1, keepdims=True
                    )
                    scales.append(jnp.broadcast_to(own[e], (size, high - low)))
                else:
                    scales.append(jnp.ones((size, high - low), F32))
            scale = scales[0] if len(scales) == 1 else jnp.concatenate(scales, axis=1)
            scaled = down_part * scale
            stage[slot, 0, :, left:right] = (hidden * scale).astype(BF)
            stage[slot, 1, :, left:right] = (
                scaled * up_part * (sigmoid + act * (1.0 - sigmoid))
            ).astype(BF)
            stage[slot, 2, :, left:right] = (scaled * act).astype(BF)
        for k in range(3):
            stage_out(step, k).start()
        for turn in range(chips - 1):
            at(step, blocks + turn, lambda turn=turn: scatter.slot(turn))
        result = dot_nt(stage[slot, 0], weights[2]).astype(BF)
        out[slot] = result.reshape(2, SEQ_DEV, D)
        out_copy(step).start()
        result = (dot_nt(stage[slot, 1], weights[0]) + dot_nt(stage[slot, 2], weights[1])).astype(BF)
        back[micro_batch, pl.ds(2 * block, 2), :, :D] = result.reshape(2, SEQ_DEV, D)
        high_tail, low_tail = jnp.zeros((size, LANES), F32), jnp.zeros((size, LANES), F32)
        for e in range(EXP_DEV):
            ours = owner_ref[...] == EXP_DEV * me + e
            high = gate_grads[e].astype(BF).astype(F32)
            high_tail = jnp.where(ours, high, high_tail)
            low_tail = jnp.where(ours, gate_grads[e] - high, low_tail)
        tail = high_tail + pltpu.roll(low_tail, experts, 1)
        back[micro_batch, pl.ds(2 * block, 2), :, D:] = tail.astype(BF).reshape(2, SEQ_DEV, LANES)

        @pl.when(micro_batch == 1)
        def _():
            back_copy(step).start()

        return carry

    lax.fori_loop(0, MB * blocks, body, 0)
    last = MB * blocks
    row_copies = [
        pltpu.make_async_copy(rows.at[m], rows_ref.at[m], local_sem.at[m]) for m in range(MB)
    ] + [
        pltpu.make_async_copy(grads.at[m], grads_ref.at[m], local_sem.at[2 + m]) for m in range(MB)
    ]
    for copy in row_copies:
        copy.start()
    scatter.finish(back_a_ref)
    for m in range(MB):
        gathers[m].finish(False)
    grad_gather.finish(False)
    for copy in row_copies:
        copy.wait()
    for step in (last - 2, last - 1):
        for k in range(3):
            stage_out(step, k).wait()
        out_copy(step).wait()
    for turn in range(blocks):
        back_copy(blocks + turn).wait()


def seq_all_scratch(rows, width):
    groups = 4
    return [
        pltpu.VMEM((rows, groups * width), BF),
        pltpu.VMEM((groups - 1, rows, width), BF),
        pltpu.VMEM((rows, groups * width), BF),
    ] + [pltpu.SemaphoreType.DMA((groups,))] * 4


class SeqAll:
    def __init__(self, scratch):
        self.low, self.arrived, self.whole = scratch[:3]
        self.first_send, self.first_recv, self.last_send, self.last_recv = scratch[3:]
        self.groups = 4
        self.width = self.arrived.shape[2]
        self.group = lax.axis_index("seq")

    def _part(self, ref, device):
        return ref.at[:, pl.ds(pl.multiple_of(device * self.width, LANES), self.width)]

    def _copy(self, source, target, send, recv, away):
        return pltpu.make_async_remote_copy(
            src_ref=source, dst_ref=target, send_sem=send.at[away], recv_sem=recv.at[away],
            device_id={"seq": (self.group + away) % self.groups}, device_id_type=MESH,
        )

    def _first(self, away):
        part = self._part(self.low, (self.group + away) % self.groups)
        return self._copy(part, self.arrived.at[away - 1], self.first_send, self.first_recv, away)

    def _last(self, away):
        part = self._part(self.whole, self.group)
        return self._copy(part, part, self.last_send, self.last_recv, away)

    def start(self):
        for away in range(1, self.groups):
            self._first(away).start()

    def middle(self):
        total = self._part(self.low, self.group)[...].astype(F32)
        for away in range(1, self.groups):
            self._first(away).wait_recv()
            total += self.arrived[away - 1].astype(F32)
        self._part(self.whole, self.group)[...] = total.astype(BF)
        for away in range(1, self.groups):
            self._last(away).start()

    def take(self):
        for away in range(1, self.groups):
            part = self._part(self.whole, (self.group + self.groups - away) % self.groups)
            self._copy(part, part, self.last_send, self.last_recv, away).wait_recv()

    def finish(self):
        for away in range(1, self.groups):
            self._first(away).wait_send()
            self._last(away).wait_send()


def expert_sums(
    chips,
    rows_ref, grads_ref, hidden_ref, d_gate_ref, d_up_ref, shared_h_ref, shared_g_ref, shared_u_ref, back_ref, out_ref, hidden_one_ref,
    gate_ref, up_ref, down_ref, back_b_ref, layer_ref, shared_outs, gate_rows_ref,
    mine, pair, line, out_mine, out_pair, out_line, layer, local_sem, stage, stage_sem, shared, arrived, summed, held, *sems,
):
    chip, core = place()
    devices = 2 * chips
    half = D // 2
    matrix, side = pl.program_id(0), pl.program_id(1)
    step = 2 * matrix + side
    last = 2 * 3 * EXP_DEV - 1
    scatter = Scatter(
        chips,
        lambda to: back_ref.at[2 * to + 1 - core],
        lambda to: mine.at[to],
        pair, line, sems[:6],
    )
    spread = Spread(
        devices, 4, 1,
        lambda owner, k: shared.at[owner],
        lambda k, device: device < FF // HD,
        lambda device, k: device,
        arrived, summed, held, FF, sems[6:13],
    )
    results = [
        Scatter(
            chips,
            lambda to, m=m: out_ref.at[m, 2 * to + 1 - core],
            lambda to, m=m: out_mine.at[m, to],
            out_pair.at[m], out_line.at[m], sems[13 + 6 * m : 19 + 6 * m],
        )
        for m in range(MB)
    ]
    routed = [
        SeqSum(gate_ref.at[e], gate_rows_ref.at[e], e == 0, e, sems[13 + 6 * MB :])
        for e in range(EXP_DEV)
    ]
    targets = [(ref, e) for ref in (gate_ref, up_ref, down_ref) for e in range(EXP_DEV)]

    def write(number):
        target, e = targets[number // 2]
        part = pl.ds(number % 2 * half, half)
        return pltpu.make_async_copy(
            stage.at[number % 2], target.at[e, part], stage_sem.at[number % 2]
        )

    def at(number, action):
        @pl.when(step == number)
        def _():
            action()

    def begin():
        loads = [
            pltpu.make_async_copy(source, target, local_sem.at[number, to])
            for to in range(chips)
            for number, (source, target) in enumerate(
                [(back_ref.at[2 * to + core], mine.at[to])]
                + [(out_ref.at[m, 2 * to + core], out_mine.at[m, to]) for m in range(MB)]
            )
        ]
        for load in loads:
            load.start()
        meet_all(("seq", "exp"))
        scatter.start()
        for load in loads:
            load.wait()

    at(0, begin)
    for number in range(2, last + 1):
        at(number, lambda number=number: write(number - 2).wait())
    at(2, lambda: scatter.slot(0))
    at(3, routed[0].start)
    at(5, routed[1].start)
    at(4, lambda: scatter.slot(1))
    at(6, lambda: scatter.slot(2))
    at(7, spread.middle)
    at(4, results[0].start)
    at(5, results[1].start)
    at(7, lambda: results[0].slot(0))
    at(8, lambda: results[1].slot(0))
    at(9, lambda: results[0].slot(1))
    at(10, lambda: results[1].slot(1))
    at(11, lambda: results[0].slot(2))
    slot = step % 2

    @pl.when(matrix < EXP_DEV)
    def _():
        stage[slot] = dot_tn(rows_ref[...], d_gate_ref[...]).astype(BF)

    @pl.when(jnp.logical_and(matrix >= EXP_DEV, matrix < 2 * EXP_DEV))
    def _():
        stage[slot] = dot_tn(rows_ref[...], d_up_ref[...]).astype(BF)

    @pl.when(matrix >= 2 * EXP_DEV)
    def _():
        stage[slot] = dot_tn(grads_ref[...], hidden_ref[...]).astype(BF)

    @pl.when(matrix == 0)
    def _():
        part = pl.ds(pl.multiple_of(side * half, half), half)
        shared[0, part, :] = dot_tn(rows_ref[...], shared_g_ref[...]).astype(BF)
        shared[1, part, :] = dot_tn(rows_ref[...], shared_u_ref[...]).astype(BF)
        shared[2, part, :] = dot_tn(grads_ref[...], shared_h_ref[...]).astype(BF)

    for number in range(last + 1):
        at(number, lambda number=number: write(number).start())
    at(1, spread.start)
    at(8, lambda: scatter.finish(back_b_ref))
    at(9, spread.hand_out)
    at(9, routed[0].middle)

    @pl.when(step == last)
    def _():
        routed[1].middle()
        results[1].slot(2)
        results[0].finish(layer)
        layer_ref[0] = (layer[...] + hidden_one_ref[0]).astype(BF)
        write(last - 1).wait()
        write(last).wait()
        spread.take()
        for kind, target in enumerate(shared_outs):
            target[...] = spread.of_kind(kind)[...]
        results[1].finish(layer)
        layer_ref[1] = (layer[...] + hidden_one_ref[1]).astype(BF)
        for job in routed:
            job.finish()
        spread.finish()


def meet_all(axes):
    barrier = pltpu.get_barrier_semaphore()
    count = 0
    for axis in axes:
        size = lax.axis_size(axis)
        for away in range(1, size):
            other = (lax.axis_index(axis) + away) % size
            pl.semaphore_signal(barrier, inc=1, device_id={axis: other}, device_id_type=MESH)
            count += 1
    pl.semaphore_wait(barrier, count)


FIRST_EXTRA, EXTRA_APART = 2, 3


def slot_head(slot, device, devices):
    return device if slot == 0 else devices + (device - FIRST_EXTRA) // EXTRA_APART


def slot_lives(slot, device, devices):
    if slot == 0:
        return device >= 0
    past = device - FIRST_EXTRA
    return jnp.logical_and(
        jnp.logical_and(past >= 0, past % EXTRA_APART == 0),
        past < EXTRA_APART * (HEADS - devices),
    )


def spread_sems(devices, groups, units):
    return [
        pltpu.SemaphoreType.DMA((groups - 1, units)),
        pltpu.SemaphoreType.DMA((groups - 1, units)),
        pltpu.SemaphoreType.DMA((units,)),
        pltpu.SemaphoreType.DMA((devices, units)),
        pltpu.SemaphoreType.DMA((devices, units)),
        pltpu.SemaphoreType.DMA((groups,)),
        pltpu.SemaphoreType.DMA((groups,)),
    ]


class Spread:
    def __init__(self, devices, groups, units, unit, lives, column, arrived, summed, held, width, sems):
        self.devices, self.groups, self.units = devices, groups, units
        self.unit, self.lives, self.column = unit, lives, column
        self.arrived, self.summed, self.held, self.width = arrived, summed, held, width
        self.first_send, self.first_recv, self.local_sem = sems[:3]
        self.second_send, self.second_recv, self.third_send, self.third_recv = sems[3:]
        self.kinds = groups - 1
        self.rows = D // devices
        self.group, self.me = lax.axis_index("seq"), lax.axis_index("exp")

    def _rows(self, device):
        return pl.ds(pl.multiple_of(device * self.rows, 32), self.rows)

    def _columns(self, device, k):
        return pl.ds(pl.multiple_of(self.column(device, k) * HD, HD), HD)

    def _along_seq(self, source, target, send, recv, away):
        return pltpu.make_async_remote_copy(
            src_ref=source, dst_ref=target, send_sem=send, recv_sem=recv,
            device_id={"seq": (self.group + away) % self.groups}, device_id_type=MESH,
        )

    def _along_exp(self, source, target, away, k):
        return pltpu.make_async_remote_copy(
            src_ref=source, dst_ref=target,
            send_sem=self.second_send.at[away, k], recv_sem=self.second_recv.at[away, k],
            device_id={"exp": (self.me + away) % self.devices}, device_id_type=MESH,
        )

    def _first(self, away, k):
        owner = (self.group + away) % self.groups
        return self._along_seq(
            self.unit(owner, k), self.arrived.at[away - 1, k],
            self.first_send.at[away - 1, k], self.first_recv.at[away - 1, k], away,
        )

    def _second(self, away, k):
        other = (self.me + away) % self.devices
        return self._along_exp(
            self.summed.at[k, self._rows(other)], self.held.at[0, :, self._columns(self.me, k)], away, k
        )

    def _own(self, k):
        return pltpu.make_async_copy(
            self.summed.at[k, self._rows(self.me)], self.held.at[0, :, self._columns(self.me, k)],
            self.local_sem.at[k],
        )

    def _third(self, away):
        return self._along_seq(
            self.held.at[0, :, : self.width], self.held.at[away, :, : self.width],
            self.third_send.at[away], self.third_recv.at[away], away,
        )

    def _sends_first(self, action):
        for k in range(self.units):
            for away in range(1, self.groups):

                @pl.when(
                    jnp.logical_and(
                        (self.group + away) % self.groups < self.kinds, self.lives(k, self.me)
                    )
                )
                def _():
                    action(self._first(away, k))

    def start(self):
        self._sends_first(lambda copy: copy.start())

    def middle(self):
        @pl.when(self.group < self.kinds)
        def _():
            for k in range(self.units):

                @pl.when(self.lives(k, self.me))
                def _():
                    total = self.unit(self.group, k)[...].astype(F32)
                    for away in range(1, self.groups):
                        block = self.arrived.at[away - 1, k]
                        self._along_seq(
                            block, block, self.first_send.at[away - 1, k],
                            self.first_recv.at[away - 1, k], away,
                        ).wait_recv()
                        total += block[...].astype(F32)
                    self.summed[k] = total.astype(BF)
                    for away in range(1, self.devices):
                        self._second(away, k).start()
                    self._own(k).start()

    def hand_out(self):
        @pl.when(self.group < self.kinds)
        def _():
            for k in range(self.units):

                @pl.when(self.lives(k, self.me))
                def _():
                    self._own(k).wait()

                for away in range(1, self.devices):
                    source = (self.me + self.devices - away) % self.devices

                    @pl.when(self.lives(k, source))
                    def _():
                        block = self.held.at[0, :, self._columns(source, k)]
                        self._along_exp(block, block, away, k).wait_recv()

            for away in range(1, self.groups):
                self._third(away).start()

    def take(self):
        for away in range(1, self.groups):

            @pl.when((self.group + self.groups - away) % self.groups < self.kinds)
            def _():
                self._third(away).wait_recv()

    def of_kind(self, kind):
        return self.held.at[(self.group + self.groups - kind) % self.groups]

    def finish(self):
        self._sends_first(lambda copy: copy.wait_send())

        @pl.when(self.group < self.kinds)
        def _():
            for k in range(self.units):

                @pl.when(self.lives(k, self.me))
                def _():
                    for away in range(1, self.devices):
                        self._second(away, k).wait_send()

            for away in range(1, self.groups):
                self._third(away).wait_send()


def seq_scratch(jobs):
    rows = D // 4
    return [
        pltpu.VMEM((jobs, 2, rows, FF), BF),
        pltpu.VMEM((jobs, 2, rows, FF), BF),
        pltpu.VMEM((jobs, rows, FF), BF),
        pltpu.VMEM((rows, FF), BF),
        pltpu.SemaphoreType.DMA((jobs, 2)),
        pltpu.SemaphoreType.DMA((jobs, 2)),
        pltpu.SemaphoreType.DMA((jobs, 2)),
        pltpu.SemaphoreType.DMA((jobs,)),
        pltpu.SemaphoreType.DMA((jobs,)),
        pltpu.SemaphoreType.DMA((jobs,)),
    ]


class SeqSum:
    def __init__(self, source, out, x_first, job, scratch):
        mine, arrived, last, result = scratch[:4]
        self.source, self.out, self.x_first = source, out, x_first
        self.mine, self.arrived, self.last = mine.at[job], arrived.at[job], last.at[job]
        self.result = result
        self.first_send, self.first_recv, self.load_sem = [sem.at[job] for sem in scratch[4:7]]
        self.last_send, self.last_recv, self.out_sem = [sem.at[job] for sem in scratch[7:]]
        group = lax.axis_index("seq")
        self.x, self.y = group % 2, group // 2
        self.rows = source.shape[0] // 4
        self.own = self.y if x_first else self.x

    def _neighbour(self, along_x):
        return 2 * self.y + 1 - self.x if along_x else 2 * (1 - self.y) + self.x

    def _block(self, i, kept):
        side = self.x if self.x_first else self.y
        side = side if kept else 1 - side
        number = 2 * i + side if self.x_first else 2 * side + i
        return self.source.at[pl.ds(pl.multiple_of(number * self.rows, 32), self.rows)]

    def _copy(self, source, target, send, recv, along_x):
        return pltpu.make_async_remote_copy(
            src_ref=source, dst_ref=target, send_sem=send, recv_sem=recv,
            device_id={"seq": self._neighbour(along_x)}, device_id_type=MESH,
        )

    def _first(self, i):
        return self._copy(
            self._block(i, False), self.arrived.at[i], self.first_send.at[i],
            self.first_recv.at[i], self.x_first,
        )

    def _load(self, i):
        return pltpu.make_async_copy(self._block(i, True), self.mine.at[i], self.load_sem.at[i])

    def _last(self):
        return self._copy(
            self.mine.at[1 - self.own], self.last, self.last_send, self.last_recv,
            not self.x_first,
        )

    def _write(self):
        return pltpu.make_async_copy(self.result, self.out, self.out_sem)

    def start(self):
        for i in range(2):
            self._first(i).start()
            self._load(i).start()

    def middle(self):
        for i in range(2):
            self._first(i).wait_recv()
            self._load(i).wait()
            self.mine[i] = (self.mine[i].astype(F32) + self.arrived[i].astype(F32)).astype(BF)
        self._last().start()

    def finish(self):
        self._last().wait_recv()
        total = self.mine[self.own].astype(F32) + self.last[...].astype(F32)
        self.result[...] = total.astype(BF)
        self._write().start()
        for i in range(2):
            self._first(i).wait_send()
        self._last().wait_send()
        self._write().wait()


def far_sum_scratch(jobs):
    rows = D // 4
    return [
        pltpu.VMEM((2, rows, FF), BF),
        pltpu.VMEM((2, rows, FF), BF),
        pltpu.VMEM((rows, FF), BF),
        pltpu.SemaphoreType.DMA((jobs, 2)),
        pltpu.SemaphoreType.DMA((jobs, 2)),
        pltpu.SemaphoreType.DMA((jobs, 2)),
        pltpu.SemaphoreType.DMA((jobs,)),
        pltpu.SemaphoreType.DMA((jobs,)),
        pltpu.SemaphoreType.DMA((jobs,)),
        pltpu.SemaphoreType.DMA((jobs, 2)),
    ]


class FarSeqSum(SeqSum):
    def __init__(self, source, out, x_first, job, slots, scratch):
        mine, arrived, last = slots
        self.ours, self.theirs, result = scratch[:3]
        self.more_sem = scratch[9].at[job]
        super().__init__(source, out, x_first, job, [mine, arrived, last, result] + list(scratch[3:9]))

    def _fetch(self, i):
        return pltpu.make_async_copy(self.arrived.at[i], self.theirs.at[i], self.more_sem.at[i])

    def _load(self, i):
        return pltpu.make_async_copy(self._block(i, True), self.ours.at[i], self.load_sem.at[i])

    def _store(self, i):
        return pltpu.make_async_copy(self.ours.at[i], self.mine.at[i], self.load_sem.at[i])

    def start(self):
        for i in range(2):
            self._first(i).start()

    def middle(self):
        for i in range(2):
            self._load(i).start()
        for i in range(2):
            self._first(i).wait_recv()
            self._fetch(i).start()
        for i in range(2):
            self._load(i).wait()
            self._fetch(i).wait()
            self.ours[i] = (self.ours[i].astype(F32) + self.theirs[i].astype(F32)).astype(BF)
            self._store(i).start()
        for i in range(2):
            self._store(i).wait()
        self._last().start()

    def finish(self):
        ours = pltpu.make_async_copy(self.mine.at[self.own], self.ours.at[0], self.load_sem.at[0])
        ours.start()
        self._last().wait_recv()
        theirs = pltpu.make_async_copy(self.last, self.theirs.at[0], self.more_sem.at[0])
        theirs.start()
        ours.wait()
        theirs.wait()
        total = self.ours[0].astype(F32) + self.theirs[0].astype(F32)
        self.result[...] = total.astype(BF)
        self._write().start()
        for i in range(2):
            self._first(i).wait_send()
        self._last().wait_send()
        self._write().wait()


def softmax_low(scores):
    powers = jnp.exp(scores - jnp.max(scores, axis=-1, keepdims=True))
    return (powers * (1.0 / jnp.sum(powers, axis=-1, keepdims=True))).astype(BF)


def heads_forward(
    chips, slots,
    tokens_ref, grad_own_ref, named_own_ref, gain_ref, cos_ref, sin_ref, w_refs, w_out_ref,
    normed_ref, qkv_ref, mixed_ref, own_mixed_ref, hidden_ref, two_ref, w_all, grad_ref, named_ref,
    rows, w_sem, local_sem, send_sem, recv_sem, *sems,
):
    devices = 2 * chips
    me = lax.axis_index("exp")
    chip, _ = place()
    length = SEQ_DEV * devices
    size = 2 * SEQ_DEV
    step = BLOCK
    gathers = [Gather(chips, tokens_ref.at[m], rows.at[m], sems[6 * m : 6 * m + 6]) for m in range(MB)]
    later = [
        Gather(chips, named_own_ref, named_ref, sems[12:18]),
        Gather(chips, grad_own_ref.at[0], grad_ref, sems[18:24]),
    ]
    keeps = [
        pltpu.make_async_copy(source, target, local_sem.at[number])
        for number, (source, target) in enumerate(
            [(tokens_ref.at[m], rows.at[m, me]) for m in range(MB)]
            + [(named_own_ref, named_ref.at[me]), (grad_own_ref.at[0], grad_ref.at[me])]
        )
    ]

    def load(slot, j):
        head = jnp.clip(slot_head(slot, me, devices), 0, HEADS - 1)
        unit = 3 * slot + j
        return pltpu.make_async_copy(
            w_refs[j].at[:, pl.ds(pl.multiple_of(head * HD, HD), HD)],
            w_all.at[:, unit * HD : (unit + 1) * HD],
            w_sem.at[unit],
        )

    def head_columns(m, device, slot):
        return own_mixed_ref.at[
            m, :, pl.ds(pl.multiple_of(slot_head(slot, device, devices) * HD, HD), HD)
        ]

    def rows_of(m, device, slot):
        part = pl.ds(pl.multiple_of(device * SEQ_DEV, SEQ_DEV), SEQ_DEV)
        return mixed_ref.at[m, part, slot * HD : (slot + 1) * HD]

    def give(m, away, slot):
        other = (me + away) % devices
        return pltpu.make_async_remote_copy(
            src_ref=rows_of(m, other, slot),
            dst_ref=head_columns(m, me, slot),
            send_sem=send_sem.at[m, away, slot],
            recv_sem=recv_sem.at[m, away, slot],
            device_id={"exp": other},
            device_id_type=MESH,
        )

    def keep_own(m, slot):
        return pltpu.make_async_copy(
            rows_of(m, me, slot), head_columns(m, me, slot), recv_sem.at[m, 0, slot]
        )

    def take(m, away, slot):
        block = head_columns(m, (me + devices - away) % devices, slot)
        return pltpu.make_async_remote_copy(
            src_ref=block,
            dst_ref=block,
            send_sem=send_sem.at[m, away, slot],
            recv_sem=recv_sem.at[m, away, slot],
            device_id={"exp": (me + away) % devices},
            device_id_type=MESH,
        )

    for copy in keeps:
        copy.start()
    for slot in range(slots):
        for j in range(3):
            load(slot, j).start()
    meet_all(("exp",))
    gathers[0].start()
    for copy in keeps:
        copy.wait()
    for slot in range(slots):
        for j in range(3):
            load(slot, j).wait()

    def body(m, carry):
        def at(number, action):
            @pl.when(m == number)
            def _():
                action()

        for turn_ in range(chips):
            block = block_order(chip, turn_, chips)
            for number in range(MB):
                if turn_ > 0:
                    at(number, lambda number=number: gathers[number].hop(turn_))
                at(number, lambda number=number: gathers[number].take_pair(block - chip))
            if turn_ == chips - 2:
                at(0, gathers[1].start)
                at(1, later[0].start)
            if turn_ == chips - 1:
                at(1, later[1].start)
            part = pl.ds(pl.multiple_of(block * size, size), size)
            tokens = rows[m, pl.ds(2 * block, 2)].reshape(size, D).astype(F32)
            normed = norm_rows(tokens, gain_ref[0:1, :]).astype(BF)
            normed_ref[m, part, :] = normed
            qkv = dot(normed, w_all[...])
            for unit in range(3 * slots):
                values = qkv[:, unit * HD : (unit + 1) * HD]
                if unit % 3 < 2:
                    values = turn(values, cos_ref[part, :], sin_ref[part, :])
                qkv_ref[m, part, unit * HD : (unit + 1) * HD] = values.astype(BF)
        for slot in range(slots):
            base = 3 * HD * slot
            for start in range(0, length, step):
                stop = start + step
                scores = visible_scores(
                    qkv_ref[m, start:stop, base : base + HD],
                    qkv_ref[m, :stop, base + HD : base + 2 * HD],
                    start,
                )
                attention = softmax_low(scores)
                mixed = dot(attention, qkv_ref[m, :stop, base + 2 * HD : base + 3 * HD])
                mixed_ref[m, start:stop, slot * HD : (slot + 1) * HD] = mixed.astype(BF)
            for number in range(MB):

                @pl.when(jnp.logical_and(m == number, slot_lives(slot, me, devices)))
                def _():
                    for away in range(1, devices):
                        give(number, away, slot).start()
                    keep_own(number, slot).start()

            at(1, lambda: later[slot].hop(1)) if slot < 2 else None
        return carry

    lax.fori_loop(0, MB, body, 0)

    def finish_rows(m):
        for slot in range(slots):

            @pl.when(slot_lives(slot, me, devices))
            def _():
                keep_own(m, slot).wait()

            for away in range(1, devices):

                @pl.when(slot_lives(slot, (me + devices - away) % devices, devices))
                def _():
                    take(m, away, slot).wait_recv()

        hidden = tokens_ref[m].astype(F32) + dot(own_mixed_ref[m], w_out_ref[...])
        hidden_ref[m] = hidden
        two_ref[m] = norm_rows(hidden, gain_ref[1:2, :]).astype(BF)

    finish_rows(0)
    for hop in range(2, chips):
        later[0].hop(hop)
    later[1].hop(2)
    finish_rows(1)
    for hop in range(3, chips):
        later[1].hop(hop)
    for gather in gathers:
        gather.finish(False)
    for gather in later:
        gather.finish(True)
    for m in range(MB):
        for slot in range(slots):

            @pl.when(slot_lives(slot, me, devices))
            def _():
                for away in range(1, devices):
                    give(m, away, slot).wait_send()


def heads_backward(
    chips, slots,
    own_ref, qkv_ref, mixed_ref, cos_ref, sin_ref, w_ref, own_mixed_ref, mix_ref, small_ref,
    normed_ref, up_ref, down_ref,
    grad_a_ref, grad_b_ref, weight_outs, w_out_out, small_out, up_out, down_out, job_slots,
    sums_ref, arrived, summed, held, d_mixed, probs, raw, parts, d_keys, d_values, pairs, lines,
    part, weight_pair, weight_line, result, normed, normed_sem, local_sem, send_sem, recv_sem, *sems,
):
    devices = 2 * chips
    me = lax.axis_index("exp")
    core = me % 2
    length = SEQ_DEV * devices
    step = BLOCK
    factor = HD ** (-0.5)
    scatters = [
        Scatter(
            chips,
            lambda to, m=m: parts.at[m, 2 * to + 1 - core],
            lambda to, m=m: parts.at[m, 2 * to + core],
            pairs.at[m], lines.at[m], sems[6 * m : 6 * m + 6],
        )
        for m in range(MB)
    ]

    spread = Spread(
        devices, 4, slots,
        lambda owner, k: sums_ref.at[owner + 3 * k],
        lambda k, device: slot_lives(k, device, devices),
        lambda device, k: slot_head(k, device, devices),
        arrived, summed, held, D, sems[6 * MB + 6 : 6 * MB + 13],
    )
    routed = [
        FarSeqSum(source, target, k % 2 == 0, k, job_slots, sems[6 * MB + 13 : -7])
        for k, (source, target) in enumerate(
            (ref.at[e], out.at[e])
            for ref, out in ((up_ref, up_out), (down_ref, down_out))
            for e in range(EXP_DEV)
        )
    ]
    rows = D // devices

    def row_block(device):
        return pl.ds(pl.multiple_of(device * rows, 32), rows)

    weight = Scatter(
        chips,
        lambda to: part.at[row_block(2 * to + 1 - core)],
        lambda to: part.at[row_block(2 * to + core)],
        weight_pair, weight_line, sems[6 * MB : 6 * MB + 6],
    )
    weight_all = SeqAll(sems[-7:])
    far = D + LANES

    def load(number):
        return pltpu.make_async_copy(
            normed_ref.at[:, :, 256 * number : 256 * (number + 1)], normed.at[number % 2],
            normed_sem.at[number % 2],
        )

    def block_at(m, device, slot):
        rows = pl.ds(pl.multiple_of(device * SEQ_DEV, SEQ_DEV), SEQ_DEV)
        return d_mixed.at[m, rows, slot * HD : (slot + 1) * HD]

    def columns(m, head):
        return own_ref.at[m, :, pl.ds(pl.multiple_of(head * HD, HD), HD)]

    def exchange(m, away, slot):
        other = (me + away) % devices
        return pltpu.make_async_remote_copy(
            src_ref=columns(m, slot_head(slot, other, devices)),
            dst_ref=block_at(m, me, slot),
            send_sem=send_sem.at[m, away, slot],
            recv_sem=recv_sem.at[m, away, slot],
            device_id={"exp": other},
            device_id_type=MESH,
        )

    def arrival(m, away, slot):
        block = block_at(m, (me + devices - away) % devices, slot)
        return pltpu.make_async_remote_copy(
            src_ref=block,
            dst_ref=block,
            send_sem=send_sem.at[m, away, slot],
            recv_sem=recv_sem.at[m, away, slot],
            device_id={"exp": (me + away) % devices},
            device_id_type=MESH,
        )

    def keep(m, slot):
        return pltpu.make_async_copy(
            columns(m, slot_head(slot, me, devices)), block_at(m, me, slot), local_sem.at[m, slot]
        )

    meet_all(("seq", "exp"))
    for m in range(MB):
        for away in range(1, devices):
            for slot in range(slots):

                @pl.when(slot_lives(slot, (me + away) % devices, devices))
                def _():
                    exchange(m, away, slot).start()

        for slot in range(slots):

            @pl.when(slot_lives(slot, me, devices))
            def _():
                keep(m, slot).start()

            @pl.when(jnp.logical_not(slot_lives(slot, me, devices)))
            def _():
                d_mixed[m, :, slot * HD : (slot + 1) * HD] = jnp.zeros((length, HD), BF)

    routed[0].start()
    routed[1].start()
    for number in range(2):
        load(number).start()
    for left in range(0, D, 256):
        part[left : left + 256, :D] = dot_tn(
            own_mixed_ref[:, left : left + 256], mix_ref[...]
        ).astype(BF)
    part[:, D:] = small_ref[...]
    weight.start()

    def weigh(m):
        for slot in range(slots):
            base = 3 * HD * slot
            for start in range(0, length, step):
                stop = start + step
                scores = visible_scores(
                    qkv_ref[m, start:stop, base : base + HD],
                    qkv_ref[m, :stop, base + HD : base + 2 * HD],
                    start,
                )
                probs[start // step][slot] = softmax_low(scores)

    def body(m, carry):
        weigh(m)
        for number in range(MB):

            @pl.when(m == number)
            def _():
                for slot in range(slots):

                    @pl.when(slot_lives(slot, me, devices))
                    def _():
                        keep(number, slot).wait()
                        for away in range(1, devices):
                            arrival(number, away, slot).wait_recv()

        @pl.when(m == 1)
        def _():
            scatters[0].start()
            for turn_ in range(min(slots, chips - 1), chips - 1):
                weight.slot(turn_)
            routed[0].middle()

        for slot in range(slots):
            base = 3 * HD * slot
            d_keys[...] = jnp.zeros_like(d_keys)
            d_values[...] = jnp.zeros_like(d_values)
            for start in range(0, length, step):
                stop = start + step
                queries = qkv_ref[m, start:stop, base : base + HD]
                keys = qkv_ref[m, :stop, base + HD : base + 2 * HD]
                values = qkv_ref[m, :stop, base + 2 * HD : base + 3 * HD]
                d_mix = d_mixed[m, start:stop, slot * HD : (slot + 1) * HD]
                mixed = mixed_ref[m, start:stop, slot * HD : (slot + 1) * HD]
                row_term = jnp.sum(d_mix.astype(F32) * mixed.astype(F32), axis=1, keepdims=True)
                attention = probs[start // step][slot]
                d_scores = (attention.astype(F32) * (dot_nt(d_mix, values) - row_term)).astype(BF)
                turned = turn(dot(d_scores, keys) * factor, cos_ref[start:stop, :], -sin_ref[start:stop, :])
                raw[m, start:stop, base : base + HD] = turned.astype(BF)
                d_keys[:stop, :] += dot_tn(d_scores, queries)
                d_values[:stop, :] += dot_tn(attention, d_mix)
            turned = turn(d_keys[...] * factor, cos_ref[...], -sin_ref[...])
            raw[m, :, base + HD : base + 2 * HD] = turned.astype(BF)
            raw[m, :, base + 2 * HD : base + 3 * HD] = d_values[...].astype(BF)

            @pl.when(m == 1)
            def _():
                scatters[0].slot(min(slot, chips - 2))
                if slot == 0:
                    routed[1].middle()
                else:
                    weight.finish(result)
                    weight_all.low[:, :far] = result[...].astype(BF)
                    weight_all.low[:, far:] = jnp.zeros((rows, LANES), BF)
                    weight_all.start()

            @pl.when(m == 0)
            def _():
                weight.slot(min(slot, chips - 2))

        for start in range(0, length, step):
            back = dot_nt(raw[m, start : start + step, :], w_ref[...]).astype(BF)
            first = start // SEQ_DEV
            parts[m, first : first + step // SEQ_DEV] = back.reshape(step // SEQ_DEV, SEQ_DEV, D)
        return carry

    lax.fori_loop(0, MB, body, 0)
    scatters[1].start()
    for turn_ in range(min(slots, chips - 1), chips - 1):
        scatters[0].slot(turn_)
    ticks = [lambda t=t: scatters[1].slot(t) for t in range(chips - 1)]
    for number, left in enumerate(range(0, D, 256)):
        load(number).wait()
        total = dot_tn(normed[number % 2, 0], raw[0]) + dot_tn(normed[number % 2, 1], raw[1])
        if number + 2 < D // 256:
            load(number + 2).start()
        for unit in range(3 * slots):
            sums_ref[unit, left : left + 256, :] = total[:, unit * HD : (unit + 1) * HD].astype(BF)
        if number == 1:
            ticks[0]()
    spread.start()
    routed[2].start()
    routed[3].start()
    ticks[1]()
    weight_all.middle()
    scatters[0].finish(grad_a_ref)
    routed[0].finish()
    ticks[2]()
    routed[1].finish()
    spread.middle()
    scatters[1].finish(grad_b_ref)
    weight_all.take()
    w_out_out[...] = weight_all.whole[:, :D]
    small_out[...] = weight_all.whole[:, D:far]
    spread.hand_out()
    routed[2].middle()
    routed[3].middle()
    spread.take()
    for kind, target in enumerate(weight_outs):
        target[...] = spread.of_kind(kind)[...]
    routed[2].finish()
    routed[3].finish()
    weight_all.finish()
    spread.finish()
    for m in range(MB):
        for away in range(1, devices):
            for slot in range(slots):

                @pl.when(slot_lives(slot, (me + away) % devices, devices))
                def _():
                    exchange(m, away, slot).wait_send()


def middle_rows(
    back_a_ref, back_b_ref, named_ref, hidden_ref, grad_ref, two_ref, router_ref, gain_ref, w_out_ref,
    grad_hidden_ref, mix_ref, d_mixed_ref, small_ref,
    experts,
):
    size = SEQ_DEV
    lane = lax.broadcasted_iota(jnp.int32, (MB * size, LANES), 1)
    named = named_ref[...].astype(F32)
    logits = jnp.where(named > 0.0, dot(two_ref[...], router_ref[...]), -1e30)
    powers = jnp.where(named > 0.0, jnp.exp(logits - jnp.max(logits, axis=1, keepdims=True)), 0.0)
    gates = powers / jnp.sum(powers, axis=1, keepdims=True)
    tail = jnp.concatenate([back_a_ref[:, D:], back_b_ref[:, D:]], axis=0)
    tail = jnp.where(lane < experts, tail + pltpu.roll(tail, LANES - experts, 1), 0.0)
    grad_logits = gates * (tail - jnp.sum(gates * tail, axis=1, keepdims=True))
    grad_logits = grad_logits.astype(BF)
    grad_two = jnp.concatenate([back_a_ref[:, :D], back_b_ref[:, :D]], axis=0)
    grad_two += dot_nt(grad_logits, router_ref[...])
    back, terms = norm_back(hidden_ref[...], gain_ref[1:2, :], grad_two)
    grad_hidden = grad_ref[...].astype(F32) + back
    grad_hidden_ref[...] = grad_hidden
    mix_ref[...] = grad_hidden.astype(BF)
    d_mixed_ref[...] = dot_nt(mix_ref[...], w_out_ref[...]).astype(BF)
    high = terms.astype(BF)
    low = (terms - high.astype(F32)).astype(BF)
    chosen = jnp.where(lane == experts, 1.0, 0.0).astype(BF)
    total = dot_tn(two_ref[...], grad_logits) + dot_tn(high, chosen) + dot_tn(low, chosen)
    small_ref[...] = total.astype(BF)


def last_rows(
    tokens_ref, normed_a_ref, normed_b_ref, grad_hidden_ref, gain_ref, gain_rows_ref, weight_lows, small_ref, layer_ref,
    far_lows, w_refs,
    grad_tokens_ref, weight_outs, router_ref, gain_one_ref, gain_two_ref, layer_out, far_outs,
    w_rows, w_sem,
    experts,
):
    rows = D // lax.axis_size("exp")
    start = pl.ds(pl.multiple_of(lax.axis_index("exp") * rows, 32), rows)
    loads = [
        pltpu.make_async_copy(w_refs[k].at[start], w_rows.at[k], w_sem.at[k]) for k in range(3)
    ]
    for copy in loads:
        copy.start()
    for low, out in zip(far_lows, far_outs):
        out[...] = low[...].astype(F32)
    layer_out[...] = layer_ref[...]
    for m, normed_ref in enumerate((normed_a_ref, normed_b_ref)):
        part = slice(m * SEQ_DEV, (m + 1) * SEQ_DEV)
        back, _ = norm_back(tokens_ref[part, :].astype(F32), gain_ref[0:1, :], normed_ref[...])
        grad_tokens_ref[part, :] = (grad_hidden_ref[part, :] + back).astype(BF)
    product = jnp.zeros((rows, D), F32)
    for k, (low, out) in enumerate(zip(weight_lows, weight_outs)):
        grad = low[...].astype(F32)
        out[...] = grad
        if k < 3:
            loads[k].wait()
            product += w_rows[k].astype(F32) * grad
    ones = jnp.ones((8, D), BF)
    high = product.astype(BF)
    low = (product - high.astype(F32)).astype(BF)
    gain_one_ref[...] = (dot_nt(ones, high) + dot_nt(ones, low))[0:1, :] / gain_rows_ref[...]
    small = small_ref[...]
    router_ref[...] = small[:, :experts].astype(F32)
    column = lax.broadcasted_iota(jnp.int32, (8, LANES), 1)
    gain_two_ref[...] = dot_nt(jnp.where(column == experts, 1.0, 0.0).astype(BF), small)[0:1, :]


def taking(us):
    return pl.CostEstimate(flops=int(us * 1.0e9), bytes_accessed=2**20, transcendentals=0)


def like(*shape, dtype=BF):
    return jax.ShapeDtypeStruct(shape, dtype)


IN_VMEM = pl.BlockSpec(memory_space=pltpu.VMEM)
ANYWHERE = pl.BlockSpec(memory_space=pl.ANY)


def experts_on_lines(two_own, hidden_one, grad_own, grad_a, named, experts, router, owners, routed, shared):
    devices = lax.axis_size("exp")
    chips = devices // 2
    length = SEQ_DEV * devices
    wide = EXP_DEV * FF + LANES
    block_back = (devices, SEQ_DEV, D + LANES)
    sems = [gather_sems(chips)] * MB + [scatter_sems(chips), gather_sems(chips)]

    def call_rows(*operands):
        def kernel(own_ref, grad_own_ref, grad_ref, named_ref, router_ref, owner_ref, *refs):
            expert_rows(
                chips, experts, own_ref, grad_own_ref, grad_ref, named_ref, router_ref, owner_ref,
                refs[:3], refs[3:6], *refs[6:],
            )

        return pl.pallas_call(
            kernel,
            out_shape=(
                like(MB, devices, SEQ_DEV, D),
                like(MB, devices, SEQ_DEV, D),
                like(MB * length, wide),
                like(MB * length, wide),
                like(MB * length, wide),
                like(MB, devices, SEQ_DEV, D),
                like(*block_back),
                like(SEQ_DEV, D + LANES, dtype=F32),
            ),
            in_specs=[IN_VMEM, ANYWHERE, ANYWHERE] + [IN_VMEM] * 3 + [ANYWHERE] * 6,
            out_specs=(ANYWHERE,) * 7 + (IN_VMEM,),
            scratch_shapes=[
                pltpu.VMEM((3, D, wide), BF),
                pltpu.VMEM((MB, devices, SEQ_DEV, D), BF),
                pltpu.VMEM((MB, devices, SEQ_DEV, D), BF),
                pltpu.VMEM((2, 3, 2 * SEQ_DEV, wide), BF),
                pltpu.VMEM((2, 2, SEQ_DEV, D), BF),
                pltpu.VMEM((MB, *block_back), BF),
                pltpu.VMEM((chips, SEQ_DEV, D + LANES), BF),
                pltpu.VMEM((chips + 1, SEQ_DEV, D + LANES), BF),
                pltpu.SemaphoreType.DMA((3, EXP_DEV + 1)),
                pltpu.SemaphoreType.DMA((4,)),
                pltpu.SemaphoreType.DMA((2, 3)),
                pltpu.SemaphoreType.DMA((2, chips)),
            ]
            + [sem for group in sems for sem in group],
            compiler_params=pltpu.CompilerParams(
                collective_id=1, has_side_effects=True, vmem_limit_bytes=VMEM_BYTES
            ),
            cost_estimate=taking(100),
            name="expert_rows",
        )(*operands)

    rows, grads, hidden, d_gate, d_up, out_parts, back_b, back_sum_a = call_rows(
        two_own, grad_own, grad_a, named, router, owners, *routed, *shared
    )
    flat = MB * length


    def call_sums(*operands):
        def kernel(*refs):
            expert_sums(chips, *refs[:16], refs[16:19], *refs[19:])

        half = D // 2
        by_rows = pl.BlockSpec((flat, half), lambda k, d: (0, d))
        by_grads = pl.BlockSpec((flat, half), lambda k, d: (0, d))

        def for_gate(k, d):
            return (0, (k + 4) // 5)

        def for_up(k, d):
            return (0, k // 3)

        def for_down(k, d):
            return (0, k // 5)

        last = pl.BlockSpec(
            (flat, LANES), lambda k, d: (0, EXP_DEV * FF // LANES), pipeline_mode=pl.Buffered(1)
        )

        def whole(*shape):
            return pl.BlockSpec(shape, lambda k, d: (0,) * len(shape))

        return pl.pallas_call(
            kernel,
            grid=(3 * EXP_DEV, 2),
            out_shape=(like(EXP_DEV, D, FF),) * 3
            + (like(SEQ_DEV, D + LANES, dtype=F32), like(MB, SEQ_DEV, D))
            + (like(D // devices, FF),) * 3
            + (like(EXP_DEV, D // 4, FF),),
            in_specs=[by_rows, by_grads]
            + [pl.BlockSpec((flat, FF), for_down, pipeline_mode=pl.Buffered(1))]
            + [pl.BlockSpec((flat, FF), use) for use in (for_gate, for_up)]
            + [last] * 3
            + [ANYWHERE] * 2
            + [pl.BlockSpec((MB, SEQ_DEV, D), lambda k, d: (0, 0, 0), pipeline_mode=pl.Buffered(1))],
            out_specs=(ANYWHERE,) * 3
            + (whole(SEQ_DEV, D + LANES), whole(MB, SEQ_DEV, D))
            + (whole(D // devices, FF),) * 3
            + (ANYWHERE,),
            scratch_shapes=[
                pltpu.VMEM((chips, SEQ_DEV, D + LANES), BF),
                pltpu.VMEM((chips, SEQ_DEV, D + LANES), BF),
                pltpu.VMEM((chips + 1, SEQ_DEV, D + LANES), BF),
                pltpu.VMEM((MB, chips, SEQ_DEV, D), BF),
                pltpu.VMEM((MB, chips, SEQ_DEV, D), BF),
                pltpu.VMEM((MB, chips + 1, SEQ_DEV, D), BF),
                pltpu.VMEM((SEQ_DEV, D), F32),
                pltpu.SemaphoreType.DMA((1 + MB, chips)),
                pltpu.VMEM((2, half, FF), BF),
                pltpu.SemaphoreType.DMA((2,)),
                pltpu.VMEM((3, D, HD), BF),
                pltpu.VMEM((3, 1, D, HD), BF),
                pltpu.VMEM((1, D, HD), BF),
                pltpu.VMEM((4, D // devices, FF), BF),
            ]
            + scatter_sems(chips)
            + spread_sems(devices, 4, 1)
            + scatter_sems(chips) * MB
            + seq_scratch(2),
            compiler_params=pltpu.CompilerParams(
                collective_id=2, has_side_effects=True, vmem_limit_bytes=VMEM_BYTES
            ),
            cost_estimate=taking(60),
            name="expert_sums",
        )(*operands)

    gate_sum, up_sum, down_sum, back_sum_b, layer_out, *shared_grads, gate_rows = call_sums(
        rows.reshape(flat, D), grads.reshape(flat, D), hidden, d_gate, d_up, hidden, d_gate, d_up, back_b,
        out_parts, hidden_one,
    )
    backs = (back_sum_a, back_sum_b)
    return (
        layer_out,
        backs,
        gate_rows,
        (gate_sum, up_sum, down_sum),
        shared_grads,
    )


def named_softmax(logits, named):
    chosen = jnp.where(named, logits, -jnp.inf)
    powers = jnp.where(named, jnp.exp(chosen - jnp.max(chosen, axis=-1, keepdims=True)), 0.0)
    return powers / jnp.sum(powers, axis=-1, keepdims=True)


def on_device_plain(
    tokens,
    cotangent,
    expert_ids,
    owner_table,
    w_query,
    w_key,
    w_value,
    w_out,
    gain_one,
    gain_two,
    w_router,
    shared_gate,
    shared_up,
    shared_down,
    routed_gate,
    routed_up,
    routed_down,
):
    devices = lax.axis_size("exp")
    groups = lax.axis_size("seq")
    me = lax.axis_index("exp")
    experts = owner_table.shape[0]
    length = SEQ_DEV * devices
    rows_out = D // devices
    slots = -(-HEADS // devices)
    wide = slots * HD
    share = FF // devices
    used = EXP_DEV * FF + share
    padded = -(-used // LANES) * LANES

    head_of = [jnp.minimum(me + slot * devices, HEADS - 1) for slot in range(slots)]
    slot_live = jnp.concatenate(
        [
            jnp.full((HD,), jnp.where(me + slot * devices < HEADS, 1.0, 0.0), F32)
            for slot in range(slots)
        ]
    )

    w_qkv = jnp.concatenate(
        [
            lax.dynamic_slice(weight, (0, head * HD), (D, HD))
            for head in head_of
            for weight in (w_query, w_key, w_value)
        ],
        axis=1,
    )
    w_out_heads = jnp.concatenate(
        [lax.dynamic_slice(w_out, (head * HD, 0), (HD, D)) for head in head_of], axis=0
    )
    cos_table, sin_table = angle_tables(jnp.arange(length).astype(F32))
    sin_table = jnp.where(jnp.arange(HD) < HD // 2, -sin_table, sin_table)
    params = pltpu.CompilerParams(vmem_limit_bytes=VMEM_BYTES)

    forward = pl.pallas_call(
        functools.partial(attend_forward, slots),
        out_shape=(
            like(length, D),
            like(length, 3 * wide),
            like(length, wide),
            like(slots, length, 1, dtype=F32),
        ),
        in_specs=[IN_VMEM] * 5,
        out_specs=(IN_VMEM,) * 4,
        compiler_params=params,
        name="attend_forward",
    )
    backward = pl.pallas_call(
        functools.partial(attend_backward, slots),
        out_shape=(like(wide, D, dtype=F32), like(D, 3 * wide, dtype=F32), like(length, D)),
        in_specs=[IN_VMEM] * 10,
        out_specs=(IN_VMEM,) * 3,
        scratch_shapes=[
            pltpu.VMEM((length, 3 * wide), BF),
            pltpu.VMEM((length, wide), BF),
            pltpu.VMEM((length, HD), F32),
            pltpu.VMEM((length, HD), F32),
        ],
        compiler_params=params,
        name="attend_backward",
    )

    def joined(routed, shared):
        own = lax.dynamic_slice(shared, (0, me * share), (D, share))
        blank = jnp.zeros((D, padded - used), BF)
        return jnp.concatenate([routed[i] for i in range(EXP_DEV)] + [own, blank], axis=1)

    gate_all = joined(routed_gate, shared_gate)
    up_all = joined(routed_up, shared_up)
    down_all = joined(routed_down, shared_down)

    expert_at = jnp.sum(
        (owner_table[:, None] == jnp.arange(experts)[None, :]) * jnp.arange(experts)[:, None],
        axis=0,
    )
    router_rows = jnp.take(w_router, expert_at, axis=1)
    ids_all = lax.all_gather(expert_ids[:, 0], "exp", axis=1, tiled=True)

    first = []
    for micro_batch in range(MB):
        rows_all = gather_exp(tokens[micro_batch, 0])
        normed, qkv, mixed, lse = forward(rows_all, gain_one[None], cos_table, sin_table, w_qkv)
        sent = lax.all_to_all(
            mixed.reshape(devices, SEQ_DEV, wide), "exp", split_axis=0, concat_axis=0, tiled=True
        )
        own_mixed = (
            sent.reshape(devices, SEQ_DEV, slots, HD)
            .transpose(1, 2, 0, 3)
            .reshape(SEQ_DEV, slots * devices * HD)[:, :D]
        )
        rows_in = tokens[micro_batch, 0].astype(F32)
        hidden_one = rows_in + dot(own_mixed, w_out)
        two_low = norm_rows(hidden_one, gain_two).astype(BF)
        two_all = gather_exp(two_low)
        grad_all = gather_exp(cotangent[micro_batch, 0])
        first.append(
            (normed, qkv, mixed, lse, rows_in, hidden_one, two_all, grad_all)
        )

    column = jnp.arange(padded)
    second = []
    for micro_batch in range(MB):
        two_all, grad_all = first[micro_batch][6:]
        logits = dot(two_all, router_rows)
        named = jnp.any(ids_all[micro_batch][:, :, None] == expert_at[None, None, :], axis=1)
        chosen = jnp.where(named, logits, -jnp.inf)
        powers = jnp.where(named, jnp.exp(chosen - jnp.max(chosen, axis=-1, keepdims=True)), 0.0)
        gates = powers / jnp.sum(powers, axis=-1, keepdims=True)
        own_gates = lax.dynamic_slice(gates, (0, me * EXP_DEV), (length, EXP_DEV))
        weight = jnp.where(
            column[None, :] < FF,
            own_gates[:, :1],
            jnp.where(column[None, :] < 2 * FF, own_gates[:, 1:], 1.0),
        )
        gate_part = dot(two_all, gate_all)
        up_part = dot(two_all, up_all)
        down_part = dot(grad_all, down_all)
        sigmoid = jax.nn.sigmoid(gate_part)
        act = gate_part * sigmoid
        hidden = act * up_part
        products = hidden * down_part
        own_grads = jnp.stack(
            [jnp.sum(products[:, i * FF : (i + 1) * FF], axis=1) for i in range(EXP_DEV)], axis=1
        )
        hidden_low = (weight * hidden).astype(BF)
        weighted = weight * down_part
        d_gate = (weighted * up_part * (sigmoid + act * (1.0 - sigmoid))).astype(BF)
        d_up = (weighted * act).astype(BF)
        out_part = scatter_exp(dot_nt(hidden_low, down_all))
        back_part = scatter_exp(dot_nt(d_gate, gate_all) + dot_nt(d_up, up_all))
        gate_grads = lax.all_gather(own_grads, "exp", axis=1, tiled=True)
        grad_logits = (
            gates * (gate_grads - jnp.sum(gates * gate_grads, axis=-1, keepdims=True))
        ).astype(BF)
        second.append((hidden_low, d_gate, d_up, out_part, back_part, grad_logits))

    two_both = jnp.concatenate([f[6] for f in first])
    grad_both = jnp.concatenate([f[7] for f in first])
    gate_sum = dot_tn(two_both, jnp.concatenate([s[1] for s in second]))
    up_sum = dot_tn(two_both, jnp.concatenate([s[2] for s in second]))
    down_sum = dot_tn(grad_both, jnp.concatenate([s[0] for s in second]))

    def routed_sum(total):
        parts = jnp.stack([total[:, i * FF : (i + 1) * FF] for i in range(EXP_DEV)])
        return lax.psum_scatter(
            parts.astype(BF), "seq", scatter_dimension=1, tiled=True
        ).astype(F32)

    def shared_part(total):
        return total[:, EXP_DEV * FF : used]

    outputs_list = []
    grads_list = []
    small = jnp.zeros((D, experts + 2), F32)
    qkv_sum = jnp.zeros((D, 3 * wide), F32)
    out_sum = jnp.zeros((wide, D), F32)
    for micro_batch in range(MB):
        normed, qkv, mixed, lse, rows_in, hidden_one, two_all, _ = first[micro_batch]
        _, _, _, out_part, back_part, grad_logits = second[micro_batch]
        outputs_list.append((hidden_one + out_part).astype(BF))
        own_logits = lax.dynamic_slice(grad_logits, (me * SEQ_DEV, 0), (SEQ_DEV, experts))
        grad_two = back_part + dot_nt(own_logits, router_rows)
        back, gain_terms = norm_back(hidden_one, gain_two, grad_two)
        grad_hidden = cotangent[micro_batch, 0].astype(F32) + back
        own_two = lax.dynamic_slice(two_all, (me * SEQ_DEV, 0), (SEQ_DEV, D))
        router_part = dot_tn(own_two, own_logits)
        mix_all = gather_exp(grad_hidden.astype(BF))
        out_one, qkv_one, grad_part = backward(
            mix_all, normed, qkv, mixed, lse, cos_table, sin_table, w_qkv, w_out_heads, slot_live[None]
        )
        out_sum = out_sum + out_one
        qkv_sum = qkv_sum + qkv_one
        grad_normed = scatter_exp(grad_part)
        back_one, gain_one_terms = norm_back(rows_in, gain_one, grad_normed)
        grads_list.append((grad_hidden + back_one).astype(BF))
        small = small + jnp.concatenate(
            [
                router_part,
                jnp.sum(gain_one_terms, axis=0)[:, None],
                jnp.sum(gain_terms, axis=0)[:, None],
            ],
            axis=1,
        )

    def to_rows(columns):
        parts = columns.astype(BF).reshape(devices, rows_out, columns.shape[1])
        parts = lax.psum_scatter(parts, "seq", scatter_dimension=1, tiled=True)
        return lax.all_to_all(parts, "exp", split_axis=0, concat_axis=0, tiled=True)

    def to_all(rows):
        return lax.all_gather(rows, "seq", axis=0, tiled=True).astype(F32)

    piece = rows_out // groups
    shared_cols = jnp.concatenate([shared_part(t) for t in (gate_sum, up_sum, down_sum)], axis=1)
    shared_rows = to_rows(shared_cols).reshape(devices, piece, 3, share)
    shared_full = to_all(shared_rows.transpose(1, 2, 0, 3).reshape(piece, 3 * FF))
    qkv_rows = to_rows(qkv_sum).reshape(devices, piece, slots, 3, HD)
    qkv_rows = qkv_rows.transpose(1, 3, 2, 0, 4).reshape(piece, 3, slots * devices * HD)
    qkv_full = to_all(qkv_rows[:, :, :D].reshape(piece, 3 * D))
    out_part = lax.psum_scatter(out_sum.astype(BF), "seq", scatter_dimension=1, tiled=True)
    spread = jnp.zeros((slots * devices * HD, D // groups), BF)
    for slot in range(slots):
        spread = lax.dynamic_update_slice(
            spread, out_part[slot * HD : (slot + 1) * HD], ((me + slot * devices) * HD, 0)
        )
    out_rows = lax.psum_scatter(spread[:D], "exp", scatter_dimension=0, tiled=True)
    out_full = lax.all_gather(out_rows, "seq", axis=1, tiled=True).astype(F32)
    small_rows = lax.psum_scatter(
        lax.psum(small, "seq"), "exp", scatter_dimension=0, tiled=True
    )
    place_of = jnp.take(small_rows, owner_table, axis=1)
    return (
        jnp.stack(outputs_list)[:, None],
        jnp.stack(grads_list)[:, None],
        qkv_full[:, :D],
        qkv_full[:, D : 2 * D],
        qkv_full[:, 2 * D :],
        out_full,
        small_rows[:, experts],
        small_rows[:, experts + 1],
        place_of,
        shared_full[:, :FF],
        shared_full[:, FF : 2 * FF],
        shared_full[:, 2 * FF :],
        routed_sum(gate_sum),
        routed_sum(up_sum),
        routed_sum(down_sum),
    )


def on_device_lines(
    tokens,
    cotangent,
    expert_ids,
    owner_table,
    w_query,
    w_key,
    w_value,
    w_out,
    gain_one,
    gain_two,
    w_router,
    shared_gate,
    shared_up,
    shared_down,
    routed_gate,
    routed_up,
    routed_down,
):
    devices = lax.axis_size("exp")
    groups = lax.axis_size("seq")
    me = lax.axis_index("exp")
    chips = devices // 2
    experts = owner_table.shape[0]
    length = SEQ_DEV * devices
    rows_out = D // devices
    slots = -(-HEADS // devices)
    wide = slots * HD
    own = MB * SEQ_DEV

    cos_table, sin_table = turn_tables(length)

    router = jnp.pad(w_router, ((0, 0), (0, LANES - experts)))
    owners = jnp.pad(owner_table, (0, LANES - experts), constant_values=-1)[None]
    gains = jnp.stack([gain_one, gain_two])
    named_own = jnp.any(
        expert_ids.reshape(own, TOP)[:, :, None] == jnp.arange(LANES)[None, None, :], axis=1
    ).astype(BF)
    tokens_own = tokens.reshape(MB, SEQ_DEV, D)
    grad_own = cotangent.reshape(MB, SEQ_DEV, D)

    def call_forward(*operands):
        def kernel(*refs):
            heads_forward(chips, slots, *refs[:6], refs[6:9], *refs[9:])

        return pl.pallas_call(
            kernel,
            out_shape=(
                like(MB, length, D),
                like(MB, length, 3 * wide),
                like(MB, length, wide),
                like(MB, SEQ_DEV, D),
                like(MB, SEQ_DEV, D, dtype=F32),
                like(MB, SEQ_DEV, D),
                like(D, 3 * wide),
                like(devices, SEQ_DEV, D),
                like(devices, own, LANES),
            ),
            in_specs=[IN_VMEM, ANYWHERE] + [IN_VMEM] * 4 + [ANYWHERE] * 3 + [IN_VMEM],
            out_specs=(IN_VMEM,) * 7 + (ANYWHERE, IN_VMEM),
            scratch_shapes=[
                pltpu.VMEM((MB, devices, SEQ_DEV, D), BF),
                pltpu.SemaphoreType.DMA((3 * slots,)),
                pltpu.SemaphoreType.DMA((4,)),
                pltpu.SemaphoreType.DMA((MB, devices, slots)),
                pltpu.SemaphoreType.DMA((MB, devices, slots)),
            ]
            + gather_sems(chips) * 4,
            compiler_params=pltpu.CompilerParams(
                collective_id=5, has_side_effects=True, vmem_limit_bytes=VMEM_BYTES
            ),
            cost_estimate=taking(70),
            name="heads_forward",
        )(*operands)

    normed, qkv, mixed, own_mixed, hidden_one, two_low, w_qkv, grad_a, named_all = call_forward(
        tokens_own, grad_own, named_own, gains, cos_table, sin_table,
        w_query, w_key, w_value, w_out,
    )
    hidden_rows = hidden_one
    own_mixed, hidden_one = own_mixed.reshape(own, D), hidden_one.reshape(own, D)
    two_low = two_low.reshape(own, D)

    layer_out, backs, gate_full, routed_sums, shared_lows = experts_on_lines(
        two_low.reshape(MB, SEQ_DEV, D),
        hidden_rows,
        grad_own,
        grad_a,
        named_all.reshape(devices, MB * SEQ_DEV, LANES),
        experts,
        router,
        owners,
        (routed_gate, routed_up, routed_down),
        (shared_gate, shared_up, shared_down),
    )
    def call_middle(*operands):
        def kernel(*refs):
            middle_rows(*refs, experts)

        return pl.pallas_call(
            kernel,
            out_shape=(like(own, D, dtype=F32), like(own, D), like(own, D), like(D, LANES)),
            in_specs=[IN_VMEM] * 9,
            out_specs=(IN_VMEM,) * 4,
            compiler_params=pltpu.CompilerParams(vmem_limit_bytes=VMEM_BYTES),
            cost_estimate=taking(5),
            name="middle_rows",
        )(*operands)

    grad_hidden, grad_mix, d_mixed, small = call_middle(
        *backs, named_own, hidden_one, cotangent.reshape(own, D), two_low, router, gains, w_out
    )
    quarter = like(EXP_DEV, D // groups, FF)
    far = D + LANES
    jobs = 4
    slot_shape = (jobs, 2, D // groups, FF)

    def backward_kernel(*refs):
        heads_backward(
            chips, slots, *refs[:14], refs[14:17], *refs[17:21], refs[21:24], *refs[24:29],
            refs[29 : 29 + length // BLOCK], *refs[29 + length // BLOCK :],
        )

    normed_a, normed_b, *backward_out = pl.pallas_call(
        backward_kernel,
        out_shape=(like(SEQ_DEV, D, dtype=F32),) * 2
        + (like(rows_out, D),) * 4
        + (like(rows_out, LANES),)
        + (quarter,) * 2
        + (like(*slot_shape), like(*slot_shape), like(jobs, D // groups, FF)),
        in_specs=[IN_VMEM] * 9 + [ANYWHERE] * 3,
        out_specs=(IN_VMEM,) * 7 + (ANYWHERE,) * 5,
        scratch_shapes=[
            pltpu.VMEM((3 * slots, D, HD), BF),
            pltpu.VMEM((groups - 1, slots, D, HD), BF),
            pltpu.VMEM((slots, D, HD), BF),
            pltpu.VMEM((groups, rows_out, D), BF),
            pltpu.VMEM((MB, length, wide), BF),
        ]
        + [pltpu.VMEM((slots, BLOCK, stop), BF) for stop in range(BLOCK, length + 1, BLOCK)]
        + [
            pltpu.VMEM((MB, length, 3 * wide), BF),
            pltpu.VMEM((MB, devices, SEQ_DEV, D), BF),
            pltpu.VMEM((length, HD), F32),
            pltpu.VMEM((length, HD), F32),
            pltpu.VMEM((MB, chips, SEQ_DEV, D), BF),
            pltpu.VMEM((MB, chips + 1, SEQ_DEV, D), BF),
            pltpu.VMEM((D, far), BF),
            pltpu.VMEM((chips, rows_out, far), BF),
            pltpu.VMEM((chips + 1, rows_out, far), BF),
            pltpu.VMEM((rows_out, far), F32),
            pltpu.VMEM((2, MB, length, 256), BF),
            pltpu.SemaphoreType.DMA((2,)),
            pltpu.SemaphoreType.DMA((MB, slots)),
            pltpu.SemaphoreType.DMA((MB, devices, slots)),
            pltpu.SemaphoreType.DMA((MB, devices, slots)),
        ]
        + scatter_sems(chips) * (MB + 1)
        + spread_sems(devices, groups, slots)
        + far_sum_scratch(jobs)
        + seq_all_scratch(rows_out, (far + LANES) // groups),
        compiler_params=pltpu.CompilerParams(
            collective_id=3, has_side_effects=True, vmem_limit_bytes=VMEM_BYTES
        ),
        cost_estimate=taking(140),
        name="heads_backward",
    )(
        d_mixed.reshape(MB, SEQ_DEV, D), qkv, mixed, cos_table, sin_table, w_qkv, own_mixed,
        grad_mix, small, normed, *routed_sums[1:],
    )
    gain_rows = lax.dynamic_slice(gain_one, (me * rows_out,), (rows_out,))[None]

    def call_last(*operands):
        def kernel(*refs):
            last_rows(
                *refs[:6], refs[6:10], *refs[10:12], refs[12:18], refs[18:21], refs[21], refs[22:26],
                *refs[26:30], refs[30:36], *refs[36:], experts,
            )

        full = like(EXP_DEV, D // groups, FF, dtype=F32)
        return pl.pallas_call(
            kernel,
            out_shape=(like(own, D),)
            + (like(rows_out, D, dtype=F32),) * 4
            + (like(rows_out, experts, dtype=F32),)
            + (like(1, rows_out, dtype=F32),) * 2
            + (like(MB, SEQ_DEV, D),)
            + (like(rows_out, FF, dtype=F32),) * 3
            + (full,) * 3,
            in_specs=[IN_VMEM] * 18 + [ANYWHERE] * 3,
            out_specs=(IN_VMEM,) * 15,
            scratch_shapes=[pltpu.VMEM((3, rows_out, D), BF), pltpu.SemaphoreType.DMA((3,))],
            compiler_params=pltpu.CompilerParams(vmem_limit_bytes=VMEM_BYTES),
            cost_estimate=taking(6),
            name="last_rows",
        )(*operands)

    last_out = call_last(
        tokens.reshape(own, D), normed_a, normed_b, grad_hidden, gains, gain_rows,
        *backward_out[:5], layer_out, *shared_lows, gate_full, *backward_out[5:7],
        w_query, w_key, w_value,
    )
    grad_tokens, attn, router_grad = last_out[0], last_out[1:5], last_out[5]
    gain_one_grad, gain_two_grad, layer_out = last_out[6:9]
    far_grads = last_out[9:]
    whole = (MB, 1, SEQ_DEV, D)
    return (
        layer_out.reshape(whole),
        grad_tokens.reshape(whole),
        *attn,
        gain_one_grad[0],
        gain_two_grad[0],
        router_grad,
        *far_grads,
    )


def solution(mesh):
    rows = P(None, "seq", "exp", None)
    placed = (rows,) * 3 + (P(),) * 11 + (P("exp", None, None),) * 3
    wide = P("exp", None)
    on_lines = mesh.shape["exp"] == 8 and mesh.shape["seq"] == 4
    on_device = on_device_lines if on_lines else on_device_plain
    return jax.shard_map(
        on_device,
        mesh=mesh,
        in_specs=placed,
        out_specs=(rows, rows, wide, wide, wide, wide, P("exp"), P("exp"))
        + (wide,) * 4
        + (P("exp", "seq", None),) * 3,
        check_vma=False,
    )
```

```python
import functools
import math

import jax
import jax.numpy as jnp
import numpy as np
from jax import lax
from jax.experimental import pallas as pl
from jax.experimental.pallas import tpu as pltpu
from jax.sharding import PartitionSpec as P

D = 1280
HEADS = 10
HD = 128
FF = 896
TOP = 7
EXP_DEV = 2
MB = 2
SEQ_DEV = 128
LANES = 128
BLOCK = 256
VMEM_BYTES = 62 * 2**20

eps = 1e-06
BF = jnp.bfloat16
F32 = jnp.float32


def norm_rows(inputs, gain):
    return inputs * lax.rsqrt(jnp.mean(inputs * inputs, axis=-1, keepdims=True) + eps) * gain


def norm_back(inputs, gain, grad):
    scale = lax.rsqrt(jnp.mean(inputs * inputs, axis=-1, keepdims=True) + eps)
    unit = inputs * scale
    weighted = grad * gain
    back = scale * (weighted - unit * jnp.mean(weighted * unit, axis=-1, keepdims=True))
    return back, grad * unit


def angle_tables(positions):
    steps_half = jnp.arange(HD // 2).astype(positions.dtype)
    frequency = jnp.exp(steps_half * (-2.0 * math.log(10000.0) / HD))
    angles = positions[:, None] * frequency[None, :]
    angles = jnp.concatenate([angles, angles], axis=-1)
    return (jnp.cos(angles), jnp.sin(angles))


def turn_tables(length):
    angles = np.arange(length)[:, None] * 10000.0 ** (-2.0 * np.arange(HD // 2) / HD)
    cos, sin = np.cos(angles), np.sin(angles)
    return (
        jnp.asarray(np.concatenate([cos, cos], axis=1), F32),
        jnp.asarray(np.concatenate([-sin, sin], axis=1), F32),
    )


def dot(a, b):
    return jnp.dot(a, b, preferred_element_type=F32)


def dot_nt(a, b):
    return lax.dot_general(a, b, (((1,), (1,)), ((), ())), preferred_element_type=F32)


def dot_tn(a, b):
    return lax.dot_general(a, b, (((0,), (0,)), ((), ())), preferred_element_type=F32)


def gather_exp(array):
    return lax.all_gather(array, "exp", axis=0, tiled=True)


def scatter_exp(array):
    return lax.psum_scatter(array.astype(BF), "exp", scatter_dimension=0, tiled=True).astype(F32)


def turn(heads, cos_table, sin_table):
    return heads * cos_table + pltpu.roll(heads, HD // 2, 1) * sin_table


def visible_scores(queries, keys, start):
    scores = dot_nt(queries, keys) * HD ** (-0.5)
    rows = queries.shape[0]
    row = lax.broadcasted_iota(jnp.int32, (rows, rows), 0)
    column = lax.broadcasted_iota(jnp.int32, (rows, rows), 1)
    last = jnp.where(row >= column, scores[:, start:], -1e30)
    return last if start == 0 else jnp.concatenate([scores[:, :start], last], axis=1)


def attend_forward(slots, rows_ref, gain_ref, cos_ref, sin_ref, w_ref, normed_ref, qkv_ref, mixed_ref, lse_ref):
    length = rows_ref.shape[0]
    step = BLOCK if length <= 2048 else BLOCK // 2

    def project(i, carry):
        part = pl.ds(pl.multiple_of(i * step, step), step)
        normed = norm_rows(rows_ref[part, :].astype(F32), gain_ref[...]).astype(BF)
        normed_ref[part, :] = normed
        for slot in range(slots):
            base = 3 * HD * slot
            qkv = dot(normed, w_ref[:, base : base + 3 * HD])
            for j in range(2):
                turned = turn(qkv[:, j * HD : (j + 1) * HD], cos_ref[part, :], sin_ref[part, :])
                qkv_ref[part, base + j * HD : base + (j + 1) * HD] = turned.astype(BF)
            qkv_ref[part, base + 2 * HD : base + 3 * HD] = qkv[:, 2 * HD :].astype(BF)
        return carry

    lax.fori_loop(0, length // step, project, 0)
    for slot in range(slots):
        base = 3 * HD * slot
        for start in range(0, length, step):
            stop = start + step
            scores = visible_scores(
                qkv_ref[start:stop, base : base + HD], qkv_ref[:stop, base + HD : base + 2 * HD], start
            )
            largest = jnp.max(scores, axis=-1, keepdims=True)
            powers = jnp.exp(scores - largest)
            total = jnp.sum(powers, axis=-1, keepdims=True)
            attention = (powers * (1.0 / total)).astype(BF)
            mixed = dot(attention, qkv_ref[:stop, base + 2 * HD : base + 3 * HD])
            mixed_ref[start:stop, slot * HD : (slot + 1) * HD] = mixed.astype(BF)
            lse_ref[slot, start:stop, :] = largest + jnp.log(total)


def attend_backward(
    slots, mix_ref, normed_ref, qkv_ref, mixed_ref, lse_ref, cos_ref, sin_ref, w_ref, w_out_ref, live_ref,
    out_sum_ref, qkv_sum_ref, grad_ref, raw_ref, d_mixed_ref, d_keys_ref, d_values_ref,
):
    length = mix_ref.shape[0]
    step = BLOCK if length <= 2048 else BLOCK // 2
    factor = HD ** (-0.5)

    def project(i, carry):
        part = pl.ds(pl.multiple_of(i * step, step), step)
        d_mixed_ref[part, :] = (dot_nt(mix_ref[part, :], w_out_ref[...]) * live_ref[...]).astype(BF)
        return carry

    lax.fori_loop(0, length // step, project, 0)
    for slot in range(slots):
        base = 3 * HD * slot
        d_keys_ref[...] = jnp.zeros_like(d_keys_ref)
        d_values_ref[...] = jnp.zeros_like(d_values_ref)
        for start in range(0, length, step):
            stop = start + step
            queries = qkv_ref[start:stop, base : base + HD]
            keys = qkv_ref[:stop, base + HD : base + 2 * HD]
            values = qkv_ref[:stop, base + 2 * HD : base + 3 * HD]
            d_mixed = d_mixed_ref[start:stop, slot * HD : (slot + 1) * HD]
            attention = jnp.exp(visible_scores(queries, keys, start) - lse_ref[slot, start:stop, :])
            d_att = dot_nt(d_mixed, values)
            row_term = jnp.sum(attention * d_att, axis=-1, keepdims=True)
            d_scores = (attention * (d_att - row_term)).astype(BF)
            d_queries = dot(d_scores, keys) * factor
            raw = turn(d_queries, cos_ref[start:stop, :], -sin_ref[start:stop, :])
            raw_ref[start:stop, base : base + HD] = raw.astype(BF)
            d_keys_ref[:stop, :] += dot_tn(d_scores, queries)
            d_values_ref[:stop, :] += dot_tn(attention.astype(BF), d_mixed)
        raw = turn(d_keys_ref[...] * factor, cos_ref[...], -sin_ref[...])
        raw_ref[:, base + HD : base + 2 * HD] = raw.astype(BF)
        raw_ref[:, base + 2 * HD : base + 3 * HD] = d_values_ref[...].astype(BF)

    def give(i, carry):
        part = pl.ds(pl.multiple_of(i * step, step), step)
        grad_ref[part, :] = dot_nt(raw_ref[part, :], w_ref[...]).astype(BF)
        return carry

    lax.fori_loop(0, length // step, give, 0)
    out_sum_ref[...] = dot_tn(mixed_ref[...], mix_ref[...])

    def sums(i, carry):
        part = pl.ds(pl.multiple_of(i * 256, 256), 256)
        qkv_sum_ref[part, :] = dot_tn(normed_ref[:, part], raw_ref[...])
        return carry

    lax.fori_loop(0, D // 256, sums, 0)


MESH = pl.DeviceIdType.MESH


def place():
    me = lax.axis_index("exp")
    return me // 2, me % 2


def remote(source, target, send_sem, recv_sem, chip, core):
    return pltpu.make_async_remote_copy(
        src_ref=source,
        dst_ref=target,
        send_sem=send_sem,
        recv_sem=recv_sem,
        device_id={"exp": 2 * chip + core},
        device_id_type=MESH,
    )


def meet(chips):
    chip, core = place()
    barrier = pltpu.get_barrier_semaphore()

    def greet(to_chip, to_core):
        pl.semaphore_signal(
            barrier, inc=1, device_id={"exp": 2 * to_chip + to_core}, device_id_type=MESH
        )

    greet(chip, 1 - core)

    @pl.when(chip < chips - 1)
    def _():
        greet(chip + 1, core)

    @pl.when(chip > 0)
    def _():
        greet(chip - 1, core)

    below = (chip + chips - 1) // chips
    above = (2 * chips - 2 - chip) // chips
    pl.semaphore_wait(barrier, 1 + below + above)


def gather_sems(chips):
    return [pltpu.SemaphoreType.DMA((chips,))] * 4 + [pltpu.SemaphoreType.DMA((2 * chips,))] * 2


class Gather:
    def __init__(self, chips, own, blocks, sems):
        self.chips, self.own, self.blocks = chips, own, blocks
        self.up_send, self.up_recv, self.down_send, self.down_recv = sems[:4]
        self.pair_send, self.pair_recv = sems[4:]

    def _source(self, hop, number):
        return self.own if hop == 0 else self.blocks.at[number]

    def _up(self, hop):
        chip, core = place()
        number = 2 * (chip - hop) + core
        return remote(
            self._source(hop, number), self.blocks.at[number],
            self.up_send.at[hop], self.up_recv.at[hop], chip + 1, core,
        )

    def _down(self, hop):
        chip, core = place()
        number = 2 * (chip + hop) + core
        return remote(
            self._source(hop, number), self.blocks.at[number],
            self.down_send.at[hop], self.down_recv.at[hop], chip - 1, core,
        )

    def _pair(self, away):
        chip, core = place()
        number = 2 * (chip + away) + core
        source = self.own if isinstance(away, int) and away == 0 else self.blocks.at[number]
        slot = away + self.chips
        return remote(
            source, self.blocks.at[number], self.pair_send.at[slot], self.pair_recv.at[slot],
            chip, 1 - core,
        )

    def _from_pair(self, away):
        chip, core = place()
        block = self.blocks.at[2 * (chip + away) + 1 - core]
        slot = away + self.chips
        return remote(
            block, block, self.pair_send.at[slot], self.pair_recv.at[slot], chip, 1 - core
        )

    def start(self):
        chip, _ = place()

        @pl.when(chip < self.chips - 1)
        def _():
            self._up(0).start()

        @pl.when(chip > 0)
        def _():
            self._down(0).start()

        self._pair(0).start()

    def hop(self, hop):
        chip, core = place()

        @pl.when(chip >= hop)
        def _():
            block = self.blocks.at[2 * (chip - hop) + core]
            remote(
                block, block, self.up_send.at[hop - 1], self.up_recv.at[hop - 1], chip, 1 - core
            ).wait_recv()

            @pl.when(chip < self.chips - 1)
            def _():
                self._up(hop).start()

            self._pair(-hop).start()

        @pl.when(chip + hop < self.chips)
        def _():
            block = self.blocks.at[2 * (chip + hop) + core]
            remote(
                block, block, self.down_send.at[hop - 1], self.down_recv.at[hop - 1], chip, 1 - core
            ).wait_recv()

            @pl.when(chip > 0)
            def _():
                self._down(hop).start()

            self._pair(hop).start()

    def take_pair(self, away):
        self._from_pair(away).wait_recv()

    def finish(self, pairs):
        chip, _ = place()
        for away in range(-self.chips + 1, self.chips):

            @pl.when(jnp.logical_and(chip + away >= 0, chip + away < self.chips))
            def _():
                if pairs:
                    self._from_pair(away).wait_recv()
                self._pair(away).wait_send()

        for hop in range(self.chips):

            @pl.when(jnp.logical_and(chip >= hop, chip < self.chips - 1))
            def _():
                self._up(hop).wait_send()

            @pl.when(jnp.logical_and(chip + hop < self.chips, chip > 0))
            def _():
                self._down(hop).wait_send()


def scatter_sems(chips):
    return [pltpu.SemaphoreType.DMA((chips,))] * 6


class Scatter:
    def __init__(self, chips, theirs, mine, pair, line, sems):
        self.chips, self.theirs, self.mine, self.pair, self.line = chips, theirs, mine, pair, line
        self.pair_send, self.pair_recv, self.up_send, self.up_recv = sems[:4]
        self.down_send, self.down_recv = sems[4:]

    def _pair(self, to):
        chip, core = place()
        return remote(
            self.theirs(to), self.pair.at[to], self.pair_send.at[to], self.pair_recv.at[to],
            chip, 1 - core,
        )

    def _up(self, chip, to):
        return remote(
            self.mine(to), self.line.at[to - chip - 1], self.up_send.at[to], self.up_recv.at[to],
            chip + 1, place()[1],
        )

    def _down(self, chip, to):
        return remote(
            self.mine(to), self.line.at[self.chips - chip + 1 + to],
            self.down_send.at[to], self.down_recv.at[to], chip - 1, place()[1],
        )

    def _arrived_up(self, to):
        chip, core = place()
        block = self.line.at[to - chip]
        remote(block, block, self.up_send.at[to], self.up_recv.at[to], chip, 1 - core).wait_recv()
        return block[...].astype(F32)

    def _arrived_down(self, to):
        chip, core = place()
        block = self.line.at[self.chips - chip + to]
        remote(
            block, block, self.down_send.at[to], self.down_recv.at[to], chip, 1 - core
        ).wait_recv()
        return block[...].astype(F32)

    def _both(self, to):
        chip, core = place()
        block = self.pair.at[to]
        remote(
            block, block, self.pair_send.at[to], self.pair_recv.at[to], chip, 1 - core
        ).wait_recv()
        return self.mine(to)[...].astype(F32) + block[...].astype(F32)

    def start(self):
        for to in range(self.chips):
            self._pair(to).start()

    def slot(self, turn):
        chip, _ = place()
        last = self.chips - 1

        @pl.when(chip <= turn)
        def _():
            to = last - turn + chip
            total = self._both(to)

            @pl.when(chip == 0)
            def _():
                self.mine(to)[...] = total.astype(BF)

            @pl.when(chip > 0)
            def _():
                self.mine(to)[...] = (total + self._arrived_up(to)).astype(BF)

            self._up(chip, to).start()

        @pl.when(last - chip <= turn)
        def _():
            to = turn - last + chip
            total = self._both(to)

            @pl.when(chip == last)
            def _():
                self.mine(to)[...] = total.astype(BF)

            @pl.when(chip < last)
            def _():
                self.mine(to)[...] = (total + self._arrived_down(to)).astype(BF)

            self._down(chip, to).start()

    def finish(self, result):
        chip, _ = place()
        last = self.chips - 1
        result[...] = self._both(chip)

        @pl.when(chip > 0)
        def _():
            result[...] += self._arrived_up(chip)

        @pl.when(chip < last)
        def _():
            result[...] += self._arrived_down(chip)

        for to in range(self.chips):
            self._pair(to).wait_send()

            @pl.when(to > chip)
            def _():
                self._up(chip, to).wait_send()

            @pl.when(to < chip)
            def _():
                self._down(chip, to).wait_send()


def part_of(array, index):
    return array.at[index]


def block_order(chip, turn, chips):
    number, bit = 0, 1
    while bit < chips:
        number = number + bit * ((chip // bit + turn // bit) % 2)
        bit = 2 * bit
    return number


def expert_rows(
    chips, experts,
    own_ref, grad_own_ref, grad_ref, named_ref, router_ref, owner_ref, routed_refs, shared_refs,
    rows_ref, grads_ref, hidden_ref, d_gate_ref, d_up_ref, out_ref, back_b_ref, back_a_ref,
    weights, rows, grads, stage, out, back, pair, line, weight_sem, local_sem, stage_sem, keep_sem,
    *sems,
):
    chip, core = place()
    me = 2 * chip + core
    blocks = chips
    size = 2 * SEQ_DEV
    gathers = [Gather(chips, own_ref.at[m], rows.at[m], sems[6 * m : 6 * m + 6]) for m in range(MB)]
    grad_gather = Gather(chips, grad_own_ref.at[1], grads.at[1], sems[18:24])
    scatter = Scatter(
        chips,
        lambda to: back.at[0, 2 * to + 1 - core],
        lambda to: back.at[0, 2 * to + core],
        pair, line, sems[12:18],
    )
    loads = []
    for k in range(3):
        for e in range(EXP_DEV):
            loads.append(
                pltpu.make_async_copy(
                    routed_refs[k].at[e], weights.at[k, :, e * FF : (e + 1) * FF],
                    weight_sem.at[k, e],
                )
            )

    def shared_load(k):
        columns = pl.ds(pl.multiple_of(me * HD, HD), HD)
        return pltpu.make_async_copy(
            shared_refs[k].at[:, columns], weights.at[k, :, EXP_DEV * FF :], weight_sem.at[k, EXP_DEV]
        )

    def shared_loads(action):
        @pl.when(me < FF // HD)
        def _():
            for k in range(3):
                action(shared_load(k))

    def stage_out(step, k):
        block = block_order(chip, step % blocks, chips)
        start = pl.multiple_of((step // blocks * blocks + block) * size, size)
        target = (hidden_ref, d_gate_ref, d_up_ref)[k]
        return pltpu.make_async_copy(
            stage.at[step % 2, k], target.at[pl.ds(start, size), :], stage_sem.at[step % 2, k]
        )

    def out_copy(step):
        block = block_order(chip, step % blocks, chips)
        return pltpu.make_async_copy(
            out.at[step % 2], out_ref.at[step // blocks, pl.ds(2 * block, 2)], keep_sem.at[0, step % 2]
        )

    def back_copy(step):
        block = block_order(chip, step % blocks, chips)
        return pltpu.make_async_copy(
            back.at[1, pl.ds(2 * block, 2)], back_b_ref.at[pl.ds(2 * block, 2)],
            keep_sem.at[1, step % blocks],
        )

    for load in loads:
        load.start()
    shared_loads(lambda copy: copy.start())

    @pl.when(me >= FF // HD)
    def _():
        for k in range(3):
            weights[k, :, EXP_DEV * FF :] = jnp.zeros((D, HD), BF)

    own_copies = [
        pltpu.make_async_copy(own_ref.at[m], rows.at[m, me], local_sem.at[m]) for m in range(MB)
    ] + [
        pltpu.make_async_copy(grad_ref, grads.at[0], local_sem.at[2]),
        pltpu.make_async_copy(grad_own_ref.at[1], grads.at[1, me], local_sem.at[3]),
    ]
    for copy in own_copies:
        copy.start()
    meet(chips)
    gathers[0].start()
    for copy in own_copies:
        copy.wait()
    for load in loads:
        load.wait()
    shared_loads(lambda copy: copy.wait())

    def at(step, number, action):
        @pl.when(step == number)
        def _():
            action()

    row_copies = [
        pltpu.make_async_copy(source.at[m], target.at[m], keep_sem.at[2 + k, m])
        for m in range(MB)
        for k, (source, target) in enumerate(((rows, rows_ref), (grads, grads_ref)))
    ]

    def body(step, carry):
        micro_batch = step // blocks
        block = block_order(chip, step % blocks, chips)
        for m in range(MB):
            for hop in range(1, chips):
                at(step, m * blocks + hop, lambda m=m, hop=hop: gathers[m].hop(hop))
        for hop in range(1, chips):
            at(step, blocks + hop, lambda hop=hop: grad_gather.hop(hop))
        at(step, 1, gathers[1].start)
        at(step, 2, grad_gather.start)
        at(step, blocks, scatter.start)
        at(step, blocks, lambda: [copy.start() for copy in row_copies[:2]])
        for m in range(MB):

            @pl.when(micro_batch == m)
            def _():
                gathers[m].take_pair(block - chip)

        @pl.when(micro_batch == 1)
        def _():
            grad_gather.take_pair(block - chip)

        @pl.when(step >= 2)
        def _():
            for k in range(3):
                stage_out(step - 2, k).wait()
            out_copy(step - 2).wait()

        at(step, 2 * blocks - 1, lambda: [copy.start() for copy in row_copies[2:]])
        slot = step % 2
        normed = rows[micro_batch, pl.ds(2 * block, 2)].reshape(size, D)
        grad = grads[micro_batch, pl.ds(2 * block, 2)].reshape(size, D)
        logits = dot(normed, router_ref[...])
        names = pl.ds(pl.multiple_of(micro_batch * SEQ_DEV, SEQ_DEV), SEQ_DEV)
        named = named_ref[pl.ds(2 * block, 2), names, :].reshape(size, LANES).astype(F32)
        chosen = jnp.where(named > 0.0, logits, -1e30)
        powers = jnp.where(
            named > 0.0, jnp.exp(chosen - jnp.max(chosen, axis=1, keepdims=True)), 0.0
        )
        gates = powers / jnp.sum(powers, axis=1, keepdims=True)
        own = [
            jnp.sum(jnp.where(owner_ref[...] == EXP_DEV * me + e, gates, 0.0), axis=1, keepdims=True)
            for e in range(EXP_DEV)
        ]
        gate_grads = [jnp.zeros((size, 1), F32) for _ in range(EXP_DEV)]
        wide = weights.shape[2]
        for left in range(0, wide, 512):
            right = min(left + 512, wide)
            gate_part = dot(normed, weights[0, :, left:right])
            up_part = dot(normed, weights[1, :, left:right])
            down_part = dot(grad, weights[2, :, left:right])
            sigmoid = 0.5 * jnp.tanh(0.5 * gate_part) + 0.5
            act = gate_part * sigmoid
            hidden = act * up_part
            product = hidden * down_part
            scales = []
            for e in range(EXP_DEV + 1):
                low, high = max(left, e * FF), min(right, (e + 1) * FF)
                if low >= high:
                    continue
                if e < EXP_DEV:
                    gate_grads[e] += jnp.sum(
                        product[:, low - left : high - left], axis=1, keepdims=True
                    )
                    scales.append(jnp.broadcast_to(own[e], (size, high - low)))
                else:
                    scales.append(jnp.ones((size, high - low), F32))
            scale = scales[0] if len(scales) == 1 else jnp.concatenate(scales, axis=1)
            scaled = down_part * scale
            stage[slot, 0, :, left:right] = (hidden * scale).astype(BF)
            stage[slot, 1, :, left:right] = (
                scaled * up_part * (sigmoid + act * (1.0 - sigmoid))
            ).astype(BF)
            stage[slot, 2, :, left:right] = (scaled * act).astype(BF)
        for k in range(3):
            stage_out(step, k).start()
        for turn in range(chips - 1):
            at(step, blocks + turn, lambda turn=turn: scatter.slot(turn))
        result = dot_nt(stage[slot, 0], weights[2]).astype(BF)
        out[slot] = result.reshape(2, SEQ_DEV, D)
        out_copy(step).start()
        result = (dot_nt(stage[slot, 1], weights[0]) + dot_nt(stage[slot, 2], weights[1])).astype(BF)
        back[micro_batch, pl.ds(2 * block, 2), :, :D] = result.reshape(2, SEQ_DEV, D)
        high_tail, low_tail = jnp.zeros((size, LANES), F32), jnp.zeros((size, LANES), F32)
        for e in range(EXP_DEV):
            ours = owner_ref[...] == EXP_DEV * me + e
            high = gate_grads[e].astype(BF).astype(F32)
            high_tail = jnp.where(ours, high, high_tail)
            low_tail = jnp.where(ours, gate_grads[e] - high, low_tail)
        tail = high_tail + pltpu.roll(low_tail, experts, 1)
        back[micro_batch, pl.ds(2 * block, 2), :, D:] = tail.astype(BF).reshape(2, SEQ_DEV, LANES)

        @pl.when(micro_batch == 1)
        def _():
            back_copy(step).start()

        return carry

    lax.fori_loop(0, MB * blocks, body, 0)
    last = MB * blocks
    scatter.finish(back_a_ref)
    for m in range(MB):
        gathers[m].finish(False)
    grad_gather.finish(False)
    for copy in row_copies:
        copy.wait()
    for step in (last - 2, last - 1):
        for k in range(3):
            stage_out(step, k).wait()
        out_copy(step).wait()
    for turn in range(blocks):
        back_copy(blocks + turn).wait()


def seq_all_scratch(rows, width):
    groups = 4
    return [
        pltpu.VMEM((rows, groups * width), BF),
        pltpu.VMEM((groups - 1, rows, width), BF),
        pltpu.VMEM((rows, groups * width), BF),
    ] + [pltpu.SemaphoreType.DMA((groups,))] * 4


class SeqAll:
    def __init__(self, scratch):
        self.low, self.arrived, self.whole = scratch[:3]
        self.first_send, self.first_recv, self.last_send, self.last_recv = scratch[3:]
        self.groups = 4
        self.width = self.arrived.shape[2]
        self.group = lax.axis_index("seq")

    def _part(self, ref, device):
        return ref.at[:, pl.ds(pl.multiple_of(device * self.width, LANES), self.width)]

    def _copy(self, source, target, send, recv, away):
        return pltpu.make_async_remote_copy(
            src_ref=source, dst_ref=target, send_sem=send.at[away], recv_sem=recv.at[away],
            device_id={"seq": (self.group + away) % self.groups}, device_id_type=MESH,
        )

    def _first(self, away):
        part = self._part(self.low, (self.group + away) % self.groups)
        return self._copy(part, self.arrived.at[away - 1], self.first_send, self.first_recv, away)

    def _last(self, away):
        part = self._part(self.whole, self.group)
        return self._copy(part, part, self.last_send, self.last_recv, away)

    def start(self):
        for away in range(1, self.groups):
            self._first(away).start()

    def middle(self):
        total = self._part(self.low, self.group)[...].astype(F32)
        for away in range(1, self.groups):
            self._first(away).wait_recv()
            total += self.arrived[away - 1].astype(F32)
        self._part(self.whole, self.group)[...] = total.astype(BF)
        for away in range(1, self.groups):
            self._last(away).start()

    def take(self):
        for away in range(1, self.groups):
            part = self._part(self.whole, (self.group + self.groups - away) % self.groups)
            self._copy(part, part, self.last_send, self.last_recv, away).wait_recv()

    def finish(self):
        for away in range(1, self.groups):
            self._first(away).wait_send()
            self._last(away).wait_send()


def expert_sums(
    chips,
    rows_ref, grads_ref, hidden_ref, d_gate_ref, d_up_ref, shared_h_ref, shared_g_ref, shared_u_ref, back_ref, out_ref, hidden_one_ref,
    gate_ref, up_ref, down_ref, back_b_ref, layer_ref, shared_outs, gate_rows_ref,
    mine, pair, line, out_mine, out_pair, out_line, layer, local_sem, stage, stage_sem, shared, arrived, summed, held, *sems,
):
    chip, core = place()
    devices = 2 * chips
    half = D // 2
    matrix, side = pl.program_id(0), pl.program_id(1)
    step = 2 * matrix + side
    last = 2 * 3 * EXP_DEV - 1
    scatter = Scatter(
        chips,
        lambda to: back_ref.at[2 * to + 1 - core],
        lambda to: mine.at[to],
        pair, line, sems[:6],
    )
    spread = Spread(
        devices, 4, 1,
        lambda owner, k: shared.at[owner],
        lambda k, device: device < FF // HD,
        lambda device, k: device,
        arrived, summed, held, FF, sems[6:13],
    )
    results = Scatter(
        chips,
        lambda to: out_ref.at[0, 2 * to + 1 - core],
        lambda to: out_mine.at[to],
        out_pair, out_line, sems[13:19],
    )
    routed = [
        SeqSum(gate_ref.at[e], gate_rows_ref.at[e], e == 0, e, sems[19:])
        for e in range(EXP_DEV)
    ]
    targets = [(ref, e) for ref in (gate_ref, up_ref, down_ref) for e in range(EXP_DEV)]

    def write(number):
        target, e = targets[number // 2]
        part = pl.ds(number % 2 * half, half)
        return pltpu.make_async_copy(
            stage.at[number % 2], target.at[e, part], stage_sem.at[number % 2]
        )

    def at(number, action):
        @pl.when(step == number)
        def _():
            action()

    def begin():
        loads = [
            pltpu.make_async_copy(source, target, local_sem.at[number, to])
            for to in range(chips)
            for number, (source, target) in enumerate(
                (
                    (back_ref.at[2 * to + core], mine.at[to]),
                    (out_ref.at[0, 2 * to + core], out_mine.at[to]),
                )
            )
        ]
        for load in loads:
            load.start()
        meet_all(("seq", "exp"))
        scatter.start()
        for load in loads:
            load.wait()

    at(0, begin)
    for number in range(2, last + 1, 2):
        at(number, lambda number=number: [write(number - 2).wait(), write(number - 1).wait()])
    at(2, lambda: scatter.slot(0))
    at(2, routed[0].start)
    at(4, routed[1].start)
    at(4, lambda: scatter.slot(1))
    at(6, lambda: scatter.slot(2))
    at(7, spread.middle)
    at(4, results.start)
    at(7, lambda: results.slot(0))
    at(9, lambda: results.slot(1))
    at(10, lambda: results.slot(2))
    slot = step % 2

    @pl.when(matrix < EXP_DEV)
    def _():
        stage[slot] = dot_tn(rows_ref[...], d_gate_ref[...]).astype(BF)

    @pl.when(jnp.logical_and(matrix >= EXP_DEV, matrix < 2 * EXP_DEV))
    def _():
        stage[slot] = dot_tn(rows_ref[...], d_up_ref[...]).astype(BF)

    @pl.when(matrix >= 2 * EXP_DEV)
    def _():
        stage[slot] = dot_tn(grads_ref[...], hidden_ref[...]).astype(BF)

    @pl.when(matrix == 0)
    def _():
        part = pl.ds(pl.multiple_of(side * half, half), half)
        shared[0, part, :] = dot_tn(rows_ref[...], shared_g_ref[...]).astype(BF)
        shared[1, part, :] = dot_tn(rows_ref[...], shared_u_ref[...]).astype(BF)
        shared[2, part, :] = dot_tn(grads_ref[...], shared_h_ref[...]).astype(BF)

    for number in range(last + 1):
        at(number, lambda number=number: write(number).start())
    at(1, spread.start)
    at(8, lambda: scatter.finish(back_b_ref))
    at(9, spread.hand_out)
    at(9, routed[0].middle)

    @pl.when(step == last)
    def _():
        routed[1].middle()
        results.finish(layer)
        layer_ref[...] = (layer[...] + hidden_one_ref[...]).astype(BF)
        write(last - 1).wait()
        write(last).wait()
        spread.take()
        for kind, target in enumerate(shared_outs):
            target[...] = spread.of_kind(kind)[...]
        for job in routed:
            job.finish()
        spread.finish()


def meet_all(axes):
    barrier = pltpu.get_barrier_semaphore()
    count = 0
    for axis in axes:
        size = lax.axis_size(axis)
        for away in range(1, size):
            other = (lax.axis_index(axis) + away) % size
            pl.semaphore_signal(barrier, inc=1, device_id={axis: other}, device_id_type=MESH)
            count += 1
    pl.semaphore_wait(barrier, count)


FIRST_EXTRA, EXTRA_APART = 2, 3


def slot_head(slot, device, devices):
    return device if slot == 0 else devices + (device - FIRST_EXTRA) // EXTRA_APART


def slot_lives(slot, device, devices):
    if slot == 0:
        return device >= 0
    past = device - FIRST_EXTRA
    return jnp.logical_and(
        jnp.logical_and(past >= 0, past % EXTRA_APART == 0),
        past < EXTRA_APART * (HEADS - devices),
    )


def spread_sems(devices, groups, units):
    return [
        pltpu.SemaphoreType.DMA((groups - 1, units)),
        pltpu.SemaphoreType.DMA((groups - 1, units)),
        pltpu.SemaphoreType.DMA((units,)),
        pltpu.SemaphoreType.DMA((devices, units)),
        pltpu.SemaphoreType.DMA((devices, units)),
        pltpu.SemaphoreType.DMA((groups,)),
        pltpu.SemaphoreType.DMA((groups,)),
    ]


class Spread:
    def __init__(self, devices, groups, units, unit, lives, column, arrived, summed, held, width, sems):
        self.devices, self.groups, self.units = devices, groups, units
        self.unit, self.lives, self.column = unit, lives, column
        self.arrived, self.summed, self.held, self.width = arrived, summed, held, width
        self.first_send, self.first_recv, self.local_sem = sems[:3]
        self.second_send, self.second_recv, self.third_send, self.third_recv = sems[3:]
        self.kinds = groups - 1
        self.rows = D // devices
        self.group, self.me = lax.axis_index("seq"), lax.axis_index("exp")

    def _rows(self, device):
        return pl.ds(pl.multiple_of(device * self.rows, 32), self.rows)

    def _columns(self, device, k):
        return pl.ds(pl.multiple_of(self.column(device, k) * HD, HD), HD)

    def _along_seq(self, source, target, send, recv, away):
        return pltpu.make_async_remote_copy(
            src_ref=source, dst_ref=target, send_sem=send, recv_sem=recv,
            device_id={"seq": (self.group + away) % self.groups}, device_id_type=MESH,
        )

    def _along_exp(self, source, target, away, k):
        return pltpu.make_async_remote_copy(
            src_ref=source, dst_ref=target,
            send_sem=self.second_send.at[away, k], recv_sem=self.second_recv.at[away, k],
            device_id={"exp": (self.me + away) % self.devices}, device_id_type=MESH,
        )

    def _first(self, away, k):
        owner = (self.group + away) % self.groups
        return self._along_seq(
            self.unit(owner, k), self.arrived.at[away - 1, k],
            self.first_send.at[away - 1, k], self.first_recv.at[away - 1, k], away,
        )

    def _second(self, away, k):
        other = (self.me + away) % self.devices
        return self._along_exp(
            self.summed.at[k, self._rows(other)], self.held.at[0, :, self._columns(self.me, k)], away, k
        )

    def _own(self, k):
        return pltpu.make_async_copy(
            self.summed.at[k, self._rows(self.me)], self.held.at[0, :, self._columns(self.me, k)],
            self.local_sem.at[k],
        )

    def _third(self, away):
        return self._along_seq(
            self.held.at[0, :, : self.width], self.held.at[away, :, : self.width],
            self.third_send.at[away], self.third_recv.at[away], away,
        )

    def _sends_first(self, action):
        for k in range(self.units):
            for away in range(1, self.groups):

                @pl.when(
                    jnp.logical_and(
                        (self.group + away) % self.groups < self.kinds, self.lives(k, self.me)
                    )
                )
                def _():
                    action(self._first(away, k))

    def start(self):
        self._sends_first(lambda copy: copy.start())

    def middle(self):
        @pl.when(self.group < self.kinds)
        def _():
            for k in range(self.units):

                @pl.when(self.lives(k, self.me))
                def _():
                    total = self.unit(self.group, k)[...].astype(F32)
                    for away in range(1, self.groups):
                        block = self.arrived.at[away - 1, k]
                        self._along_seq(
                            block, block, self.first_send.at[away - 1, k],
                            self.first_recv.at[away - 1, k], away,
                        ).wait_recv()
                        total += block[...].astype(F32)
                    self.summed[k] = total.astype(BF)
                    for away in range(1, self.devices):
                        self._second(away, k).start()
                    self._own(k).start()

    def hand_out(self):
        @pl.when(self.group < self.kinds)
        def _():
            for k in range(self.units):

                @pl.when(self.lives(k, self.me))
                def _():
                    self._own(k).wait()

                for away in range(1, self.devices):
                    source = (self.me + self.devices - away) % self.devices

                    @pl.when(self.lives(k, source))
                    def _():
                        block = self.held.at[0, :, self._columns(source, k)]
                        self._along_exp(block, block, away, k).wait_recv()

            for away in range(1, self.groups):
                self._third(away).start()

    def take(self):
        for away in range(1, self.groups):

            @pl.when((self.group + self.groups - away) % self.groups < self.kinds)
            def _():
                self._third(away).wait_recv()

    def of_kind(self, kind):
        return self.held.at[(self.group + self.groups - kind) % self.groups]

    def finish(self):
        self._sends_first(lambda copy: copy.wait_send())

        @pl.when(self.group < self.kinds)
        def _():
            for k in range(self.units):

                @pl.when(self.lives(k, self.me))
                def _():
                    for away in range(1, self.devices):
                        self._second(away, k).wait_send()

            for away in range(1, self.groups):
                self._third(away).wait_send()


def seq_scratch(jobs):
    rows = D // 4
    return [
        pltpu.VMEM((jobs, 2, rows, FF), BF),
        pltpu.VMEM((jobs, 2, rows, FF), BF),
        pltpu.VMEM((jobs, rows, FF), BF),
        pltpu.VMEM((rows, FF), BF),
        pltpu.SemaphoreType.DMA((jobs, 2)),
        pltpu.SemaphoreType.DMA((jobs, 2)),
        pltpu.SemaphoreType.DMA((jobs, 2)),
        pltpu.SemaphoreType.DMA((jobs,)),
        pltpu.SemaphoreType.DMA((jobs,)),
        pltpu.SemaphoreType.DMA((jobs,)),
    ]


class SeqSum:
    def __init__(self, source, out, x_first, job, scratch):
        mine, arrived, last, result = scratch[:4]
        self.source, self.out, self.x_first = source, out, x_first
        self.mine, self.arrived, self.last = mine.at[job], arrived.at[job], last.at[job]
        self.result = result
        self.first_send, self.first_recv, self.load_sem = [sem.at[job] for sem in scratch[4:7]]
        self.last_send, self.last_recv, self.out_sem = [sem.at[job] for sem in scratch[7:]]
        group = lax.axis_index("seq")
        self.x, self.y = group % 2, group // 2
        self.rows = source.shape[0] // 4
        self.own = self.y if x_first else self.x

    def _neighbour(self, along_x):
        return 2 * self.y + 1 - self.x if along_x else 2 * (1 - self.y) + self.x

    def _block(self, i, kept):
        side = self.x if self.x_first else self.y
        side = side if kept else 1 - side
        number = 2 * i + side if self.x_first else 2 * side + i
        return self.source.at[pl.ds(pl.multiple_of(number * self.rows, 32), self.rows)]

    def _copy(self, source, target, send, recv, along_x):
        return pltpu.make_async_remote_copy(
            src_ref=source, dst_ref=target, send_sem=send, recv_sem=recv,
            device_id={"seq": self._neighbour(along_x)}, device_id_type=MESH,
        )

    def _first(self, i):
        return self._copy(
            self._block(i, False), self.arrived.at[i], self.first_send.at[i],
            self.first_recv.at[i], self.x_first,
        )

    def _load(self, i):
        return pltpu.make_async_copy(self._block(i, True), self.mine.at[i], self.load_sem.at[i])

    def _last(self):
        return self._copy(
            self.mine.at[1 - self.own], self.last, self.last_send, self.last_recv,
            not self.x_first,
        )

    def _write(self):
        return pltpu.make_async_copy(self.result, self.out, self.out_sem)

    def start(self):
        for i in range(2):
            self._first(i).start()
            self._load(i).start()

    def middle(self):
        for i in range(2):
            self._first(i).wait_recv()
            self._load(i).wait()
            self.mine[i] = (self.mine[i].astype(F32) + self.arrived[i].astype(F32)).astype(BF)
        self._last().start()

    def finish(self):
        self._last().wait_recv()
        total = self.mine[self.own].astype(F32) + self.last[...].astype(F32)
        self.result[...] = total.astype(BF)
        self._write().start()
        for i in range(2):
            self._first(i).wait_send()
        self._last().wait_send()
        self._write().wait()


def far_sum_scratch(jobs):
    rows = D // 4
    return [
        pltpu.VMEM((2, rows, FF), BF),
        pltpu.VMEM((2, rows, FF), BF),
        pltpu.VMEM((rows, FF), BF),
        pltpu.SemaphoreType.DMA((jobs, 2)),
        pltpu.SemaphoreType.DMA((jobs, 2)),
        pltpu.SemaphoreType.DMA((jobs, 2)),
        pltpu.SemaphoreType.DMA((jobs,)),
        pltpu.SemaphoreType.DMA((jobs,)),
        pltpu.SemaphoreType.DMA((jobs,)),
        pltpu.SemaphoreType.DMA((jobs, 2)),
    ]


class FarSeqSum(SeqSum):
    def __init__(self, source, out, x_first, job, slots, scratch):
        mine, arrived, last = slots
        self.ours, self.theirs, result = scratch[:3]
        self.more_sem = scratch[9].at[job]
        super().__init__(source, out, x_first, job, [mine, arrived, last, result] + list(scratch[3:9]))

    def _fetch(self, i):
        return pltpu.make_async_copy(self.arrived.at[i], self.theirs.at[i], self.more_sem.at[i])

    def _load(self, i):
        return pltpu.make_async_copy(self._block(i, True), self.ours.at[i], self.load_sem.at[i])

    def _store(self, i):
        return pltpu.make_async_copy(self.ours.at[i], self.mine.at[i], self.load_sem.at[i])

    def start(self):
        for i in range(2):
            self._first(i).start()

    def middle(self):
        for i in range(2):
            self._load(i).start()
        for i in range(2):
            self._first(i).wait_recv()
            self._fetch(i).start()
        for i in range(2):
            self._load(i).wait()
            self._fetch(i).wait()
            self.ours[i] = (self.ours[i].astype(F32) + self.theirs[i].astype(F32)).astype(BF)
            self._store(i).start()
        for i in range(2):
            self._store(i).wait()
        self._last().start()

    def finish(self):
        ours = pltpu.make_async_copy(self.mine.at[self.own], self.ours.at[0], self.load_sem.at[0])
        ours.start()
        self._last().wait_recv()
        theirs = pltpu.make_async_copy(self.last, self.theirs.at[0], self.more_sem.at[0])
        theirs.start()
        ours.wait()
        theirs.wait()
        total = self.ours[0].astype(F32) + self.theirs[0].astype(F32)
        self.result[...] = total.astype(BF)
        self._write().start()
        for i in range(2):
            self._first(i).wait_send()
        self._last().wait_send()
        self._write().wait()


def softmax_low(scores):
    powers = jnp.exp(scores - jnp.max(scores, axis=-1, keepdims=True))
    return (powers * (1.0 / jnp.sum(powers, axis=-1, keepdims=True))).astype(BF)


def heads_forward(
    chips, slots,
    tokens_ref, grad_own_ref, named_own_ref, gain_ref, cos_ref, sin_ref, w_refs, w_out_ref,
    normed_ref, qkv_ref, mixed_ref, own_mixed_ref, hidden_ref, two_ref, w_all, grad_ref, named_ref,
    rows, w_sem, local_sem, send_sem, recv_sem, *sems,
):
    devices = 2 * chips
    me = lax.axis_index("exp")
    chip, _ = place()
    length = SEQ_DEV * devices
    size = 2 * SEQ_DEV
    step = BLOCK
    gathers = [Gather(chips, tokens_ref.at[m], rows.at[m], sems[6 * m : 6 * m + 6]) for m in range(MB)]
    later = [
        Gather(chips, named_own_ref, named_ref, sems[12:18]),
        Gather(chips, grad_own_ref.at[0], grad_ref, sems[18:24]),
    ]
    keeps = [
        pltpu.make_async_copy(source, target, local_sem.at[number])
        for number, (source, target) in enumerate(
            [(tokens_ref.at[m], rows.at[m, me]) for m in range(MB)]
            + [(named_own_ref, named_ref.at[me]), (grad_own_ref.at[0], grad_ref.at[me])]
        )
    ]

    def load(slot, j):
        head = jnp.clip(slot_head(slot, me, devices), 0, HEADS - 1)
        unit = 3 * slot + j
        return pltpu.make_async_copy(
            w_refs[j].at[:, pl.ds(pl.multiple_of(head * HD, HD), HD)],
            w_all.at[:, unit * HD : (unit + 1) * HD],
            w_sem.at[unit],
        )

    def head_columns(m, device, slot):
        return own_mixed_ref.at[
            m, :, pl.ds(pl.multiple_of(slot_head(slot, device, devices) * HD, HD), HD)
        ]

    def rows_of(m, device, slot):
        part = pl.ds(pl.multiple_of(device * SEQ_DEV, SEQ_DEV), SEQ_DEV)
        return mixed_ref.at[m, part, slot * HD : (slot + 1) * HD]

    def give(m, away, slot):
        other = (me + away) % devices
        return pltpu.make_async_remote_copy(
            src_ref=rows_of(m, other, slot),
            dst_ref=head_columns(m, me, slot),
            send_sem=send_sem.at[m, away, slot],
            recv_sem=recv_sem.at[m, away, slot],
            device_id={"exp": other},
            device_id_type=MESH,
        )

    def keep_own(m, slot):
        return pltpu.make_async_copy(
            rows_of(m, me, slot), head_columns(m, me, slot), recv_sem.at[m, 0, slot]
        )

    def take(m, away, slot):
        block = head_columns(m, (me + devices - away) % devices, slot)
        return pltpu.make_async_remote_copy(
            src_ref=block,
            dst_ref=block,
            send_sem=send_sem.at[m, away, slot],
            recv_sem=recv_sem.at[m, away, slot],
            device_id={"exp": (me + away) % devices},
            device_id_type=MESH,
        )

    for copy in keeps:
        copy.start()
    for slot in range(slots):
        for j in range(3):
            load(slot, j).start()
    meet_all(("exp",))
    gathers[0].start()
    for copy in keeps:
        copy.wait()
    for slot in range(slots):
        for j in range(3):
            load(slot, j).wait()

    def body(m, carry):
        def at(number, action):
            @pl.when(m == number)
            def _():
                action()

        for turn_ in range(chips):
            block = block_order(chip, turn_, chips)
            for number in range(MB):
                if turn_ > 0:
                    at(number, lambda number=number: gathers[number].hop(turn_))
                at(number, lambda number=number: gathers[number].take_pair(block - chip))
            if turn_ == chips - 2:
                at(0, gathers[1].start)
                at(1, later[0].start)
            if turn_ == chips - 1:
                at(1, later[1].start)
            part = pl.ds(pl.multiple_of(block * size, size), size)
            tokens = rows[m, pl.ds(2 * block, 2)].reshape(size, D).astype(F32)
            normed = norm_rows(tokens, gain_ref[0:1, :]).astype(BF)
            normed_ref[m, part, :] = normed
            qkv = dot(normed, w_all[...])
            for unit in range(3 * slots):
                values = qkv[:, unit * HD : (unit + 1) * HD]
                if unit % 3 < 2:
                    values = turn(values, cos_ref[part, :], sin_ref[part, :])
                qkv_ref[m, part, unit * HD : (unit + 1) * HD] = values.astype(BF)
        for slot in range(slots):
            base = 3 * HD * slot
            for start in range(0, length, step):
                stop = start + step
                scores = visible_scores(
                    qkv_ref[m, start:stop, base : base + HD],
                    qkv_ref[m, :stop, base + HD : base + 2 * HD],
                    start,
                )
                attention = softmax_low(scores)
                mixed = dot(attention, qkv_ref[m, :stop, base + 2 * HD : base + 3 * HD])
                mixed_ref[m, start:stop, slot * HD : (slot + 1) * HD] = mixed.astype(BF)
            for number in range(MB):

                @pl.when(jnp.logical_and(m == number, slot_lives(slot, me, devices)))
                def _():
                    for away in range(1, devices):
                        give(number, away, slot).start()
                    keep_own(number, slot).start()

            at(1, lambda: later[slot].hop(1)) if slot < 2 else None
        return carry

    lax.fori_loop(0, MB, body, 0)

    def finish_rows(m):
        for slot in range(slots):

            @pl.when(slot_lives(slot, me, devices))
            def _():
                keep_own(m, slot).wait()

            for away in range(1, devices):

                @pl.when(slot_lives(slot, (me + devices - away) % devices, devices))
                def _():
                    take(m, away, slot).wait_recv()

        hidden = tokens_ref[m].astype(F32) + dot(own_mixed_ref[m], w_out_ref[...])
        hidden_ref[m] = hidden
        two_ref[m] = norm_rows(hidden, gain_ref[1:2, :]).astype(BF)

    finish_rows(0)
    for hop in range(2, chips):
        later[0].hop(hop)
    later[1].hop(2)
    finish_rows(1)
    for hop in range(3, chips):
        later[1].hop(hop)
    for gather in gathers:
        gather.finish(False)
    for gather in later:
        gather.finish(True)
    for m in range(MB):
        for slot in range(slots):

            @pl.when(slot_lives(slot, me, devices))
            def _():
                for away in range(1, devices):
                    give(m, away, slot).wait_send()


def heads_backward(
    chips, slots,
    own_ref, qkv_ref, mixed_ref, cos_ref, sin_ref, w_ref, own_mixed_ref, mix_ref, small_ref, hidden_ref,
    normed_ref, up_ref, down_ref, out_ref,
    grad_a_ref, grad_b_ref, weight_outs, w_out_out, small_out, layer_ref, up_out, down_out, job_slots,
    sums_ref, arrived, summed, held, mine, pair, line, layer, d_mixed, probs, raw, parts, d_keys, d_values, pairs, lines,
    part, weight_pair, weight_line, result, normed, normed_sem, mine_sem, local_sem, send_sem, recv_sem, *sems,
):
    devices = 2 * chips
    me = lax.axis_index("exp")
    core = me % 2
    length = SEQ_DEV * devices
    step = BLOCK
    factor = HD ** (-0.5)
    scatters = [
        Scatter(
            chips,
            lambda to, m=m: parts.at[m, 2 * to + 1 - core],
            lambda to, m=m: parts.at[m, 2 * to + core],
            pairs.at[m], lines.at[m], sems[6 * m : 6 * m + 6],
        )
        for m in range(MB)
    ]

    spread = Spread(
        devices, 4, slots,
        lambda owner, k: sums_ref.at[owner + 3 * k],
        lambda k, device: slot_lives(k, device, devices),
        lambda device, k: slot_head(k, device, devices),
        arrived, summed, held, D, sems[6 * MB + 6 : 6 * MB + 13],
    )
    results = Scatter(
        chips,
        lambda to: out_ref.at[1, 2 * to + 1 - core],
        lambda to: mine.at[to],
        pair, line, sems[6 * MB + 13 : 6 * MB + 19],
    )
    result_loads = [
        pltpu.make_async_copy(out_ref.at[1, 2 * to + core], mine.at[to], mine_sem.at[to])
        for to in range(chips)
    ]
    routed = [
        FarSeqSum(source, target, k % 2 == 0, k, job_slots, sems[6 * MB + 19 : -7])
        for k, (source, target) in enumerate(
            (ref.at[e], out.at[e])
            for ref, out in ((up_ref, up_out), (down_ref, down_out))
            for e in range(EXP_DEV)
        )
    ]
    rows = D // devices

    def row_block(device):
        return pl.ds(pl.multiple_of(device * rows, 32), rows)

    weight = Scatter(
        chips,
        lambda to: part.at[row_block(2 * to + 1 - core)],
        lambda to: part.at[row_block(2 * to + core)],
        weight_pair, weight_line, sems[6 * MB : 6 * MB + 6],
    )
    weight_all = SeqAll(sems[-7:])
    far = D + LANES

    def load(number):
        return pltpu.make_async_copy(
            normed_ref.at[:, :, 256 * number : 256 * (number + 1)], normed.at[number % 2],
            normed_sem.at[number % 2],
        )

    def block_at(m, device, slot):
        rows = pl.ds(pl.multiple_of(device * SEQ_DEV, SEQ_DEV), SEQ_DEV)
        return d_mixed.at[m, rows, slot * HD : (slot + 1) * HD]

    def columns(m, head):
        return own_ref.at[m, :, pl.ds(pl.multiple_of(head * HD, HD), HD)]

    def exchange(m, away, slot):
        other = (me + away) % devices
        return pltpu.make_async_remote_copy(
            src_ref=columns(m, slot_head(slot, other, devices)),
            dst_ref=block_at(m, me, slot),
            send_sem=send_sem.at[m, away, slot],
            recv_sem=recv_sem.at[m, away, slot],
            device_id={"exp": other},
            device_id_type=MESH,
        )

    def arrival(m, away, slot):
        block = block_at(m, (me + devices - away) % devices, slot)
        return pltpu.make_async_remote_copy(
            src_ref=block,
            dst_ref=block,
            send_sem=send_sem.at[m, away, slot],
            recv_sem=recv_sem.at[m, away, slot],
            device_id={"exp": (me + away) % devices},
            device_id_type=MESH,
        )

    def keep(m, slot):
        return pltpu.make_async_copy(
            columns(m, slot_head(slot, me, devices)), block_at(m, me, slot), local_sem.at[m, slot]
        )

    meet_all(("seq", "exp"))
    for m in range(MB):
        for away in range(1, devices):
            for slot in range(slots):

                @pl.when(slot_lives(slot, (me + away) % devices, devices))
                def _():
                    exchange(m, away, slot).start()

        for slot in range(slots):

            @pl.when(slot_lives(slot, me, devices))
            def _():
                keep(m, slot).start()

            @pl.when(jnp.logical_not(slot_lives(slot, me, devices)))
            def _():
                d_mixed[m, :, slot * HD : (slot + 1) * HD] = jnp.zeros((length, HD), BF)

    for job in routed:
        job.start()
    for number in range(2):
        load(number).start()
    for copy in result_loads:
        copy.start()
    for left in range(0, D, 256):
        part[left : left + 256, :D] = dot_tn(
            own_mixed_ref[:, left : left + 256], mix_ref[...]
        ).astype(BF)
    part[:, D:] = small_ref[...]
    weight.start()

    def weigh(m):
        for slot in range(slots):
            base = 3 * HD * slot
            for start in range(0, length, step):
                stop = start + step
                scores = visible_scores(
                    qkv_ref[m, start:stop, base : base + HD],
                    qkv_ref[m, :stop, base + HD : base + 2 * HD],
                    start,
                )
                probs[start // step][slot] = softmax_low(scores)

    def body(m, carry):
        weigh(m)
        for number in range(MB):

            @pl.when(m == number)
            def _():
                for slot in range(slots):

                    @pl.when(slot_lives(slot, me, devices))
                    def _():
                        keep(number, slot).wait()
                        for away in range(1, devices):
                            arrival(number, away, slot).wait_recv()

        @pl.when(m == 1)
        def _():
            scatters[0].start()
            for turn_ in range(min(slots, chips - 1), chips - 1):
                weight.slot(turn_)
            routed[0].middle()

        for slot in range(slots):
            base = 3 * HD * slot
            d_keys[...] = jnp.zeros_like(d_keys)
            d_values[...] = jnp.zeros_like(d_values)
            for start in range(0, length, step):
                stop = start + step
                queries = qkv_ref[m, start:stop, base : base + HD]
                keys = qkv_ref[m, :stop, base + HD : base + 2 * HD]
                values = qkv_ref[m, :stop, base + 2 * HD : base + 3 * HD]
                d_mix = d_mixed[m, start:stop, slot * HD : (slot + 1) * HD]
                mixed = mixed_ref[m, start:stop, slot * HD : (slot + 1) * HD]
                row_term = jnp.sum(d_mix.astype(F32) * mixed.astype(F32), axis=1, keepdims=True)
                attention = probs[start // step][slot]
                d_scores = (attention.astype(F32) * (dot_nt(d_mix, values) - row_term)).astype(BF)
                turned = turn(dot(d_scores, keys) * factor, cos_ref[start:stop, :], -sin_ref[start:stop, :])
                raw[m, start:stop, base : base + HD] = turned.astype(BF)
                d_keys[:stop, :] += dot_tn(d_scores, queries)
                d_values[:stop, :] += dot_tn(attention, d_mix)
            turned = turn(d_keys[...] * factor, cos_ref[...], -sin_ref[...])
            raw[m, :, base + HD : base + 2 * HD] = turned.astype(BF)
            raw[m, :, base + 2 * HD : base + 3 * HD] = d_values[...].astype(BF)

            @pl.when(m == 1)
            def _():
                scatters[0].slot(min(slot, chips - 2))
                if slot == 0:
                    routed[1].middle()
                else:
                    weight.finish(result)
                    weight_all.low[:, :far] = result[...].astype(BF)
                    weight_all.low[:, far:] = jnp.zeros((rows, LANES), BF)
                    weight_all.start()

            @pl.when(m == 0)
            def _():
                weight.slot(min(slot, chips - 2))

        for start in range(0, length, step):
            back = dot_nt(raw[m, start : start + step, :], w_ref[...]).astype(BF)
            first = start // SEQ_DEV
            parts[m, first : first + step // SEQ_DEV] = back.reshape(step // SEQ_DEV, SEQ_DEV, D)
        return carry

    lax.fori_loop(0, MB, body, 0)
    scatters[1].start()
    for turn_ in range(min(slots, chips - 1), chips - 1):
        scatters[0].slot(turn_)
    ticks = [lambda t=t: scatters[1].slot(t) for t in range(chips - 1)]
    for number, left in enumerate(range(0, D, 256)):
        load(number).wait()
        total = dot_tn(normed[number % 2, 0], raw[0]) + dot_tn(normed[number % 2, 1], raw[1])
        if number + 2 < D // 256:
            load(number + 2).start()
        for unit in range(3 * slots):
            sums_ref[unit, left : left + 256, :] = total[:, unit * HD : (unit + 1) * HD].astype(BF)
        if number == 1:
            ticks[0]()
    spread.start()
    results.start()
    ticks[1]()
    scatters[0].finish(grad_a_ref)
    weight_all.middle()
    routed[0].finish()
    for copy in result_loads:
        copy.wait()
    ticks[2]()
    routed[1].finish()
    spread.middle()
    results.slot(0)
    routed[2].middle()
    spread.hand_out()
    routed[3].middle()
    results.slot(1)
    scatters[1].finish(grad_b_ref)
    weight_all.take()
    w_out_out[...] = weight_all.whole[:, :D]
    small_out[...] = weight_all.whole[:, D:far]
    results.slot(2)
    routed[2].finish()
    spread.take()
    for kind, target in enumerate(weight_outs):
        target[...] = spread.of_kind(kind)[...]
    routed[3].finish()
    results.finish(layer)
    layer_ref[...] = (layer[...] + hidden_ref[...]).astype(BF)
    weight_all.finish()
    spread.finish()
    for m in range(MB):
        for away in range(1, devices):
            for slot in range(slots):

                @pl.when(slot_lives(slot, (me + away) % devices, devices))
                def _():
                    exchange(m, away, slot).wait_send()


def middle_rows(
    back_a_ref, back_b_ref, named_ref, hidden_ref, grad_ref, two_ref, router_ref, gain_ref, w_out_ref,
    grad_hidden_ref, mix_ref, d_mixed_ref, small_ref,
    experts,
):
    size = SEQ_DEV
    lane = lax.broadcasted_iota(jnp.int32, (MB * size, LANES), 1)
    named = named_ref[...].astype(F32)
    logits = jnp.where(named > 0.0, dot(two_ref[...], router_ref[...]), -1e30)
    powers = jnp.where(named > 0.0, jnp.exp(logits - jnp.max(logits, axis=1, keepdims=True)), 0.0)
    gates = powers / jnp.sum(powers, axis=1, keepdims=True)
    tail = jnp.concatenate([back_a_ref[:, D:], back_b_ref[:, D:]], axis=0)
    tail = jnp.where(lane < experts, tail + pltpu.roll(tail, LANES - experts, 1), 0.0)
    grad_logits = gates * (tail - jnp.sum(gates * tail, axis=1, keepdims=True))
    grad_logits = grad_logits.astype(BF)
    grad_two = jnp.concatenate([back_a_ref[:, :D], back_b_ref[:, :D]], axis=0)
    grad_two += dot_nt(grad_logits, router_ref[...])
    back, terms = norm_back(hidden_ref[...], gain_ref[1:2, :], grad_two)
    grad_hidden = grad_ref[...].astype(F32) + back
    grad_hidden_ref[...] = grad_hidden
    mix_ref[...] = grad_hidden.astype(BF)
    d_mixed_ref[...] = dot_nt(mix_ref[...], w_out_ref[...]).astype(BF)
    high = terms.astype(BF)
    low = (terms - high.astype(F32)).astype(BF)
    chosen = jnp.where(lane == experts, 1.0, 0.0).astype(BF)
    total = dot_tn(two_ref[...], grad_logits) + dot_tn(high, chosen) + dot_tn(low, chosen)
    small_ref[...] = total.astype(BF)


def last_rows(
    tokens_ref, normed_a_ref, normed_b_ref, grad_hidden_ref, gain_ref, gain_rows_ref, weight_lows, small_ref, layer_refs,
    shared_lows, gate_ref, up_ref, down_ref, w_refs,
    grad_tokens_ref, weight_outs, router_ref, gain_one_ref, gain_two_ref, layer_out, shared_outs, gate_out, up_out, down_out,
    w_rows, w_sem,
    experts,
):
    rows = D // lax.axis_size("exp")
    start = pl.ds(pl.multiple_of(lax.axis_index("exp") * rows, 32), rows)
    loads = [
        pltpu.make_async_copy(w_refs[k].at[start], w_rows.at[k], w_sem.at[k]) for k in range(3)
    ]
    for copy in loads:
        copy.start()
    for low, out in zip(shared_lows, shared_outs):
        out[...] = low[...].astype(F32)
    gate_out[...] = gate_ref[...].astype(F32)
    down_out[...] = down_ref[...].astype(F32)
    up_out[...] = up_ref[...].astype(F32)
    for m in range(MB):
        layer_out[m] = layer_refs[m][...]
    for m, normed_ref in enumerate((normed_a_ref, normed_b_ref)):
        part = slice(m * SEQ_DEV, (m + 1) * SEQ_DEV)
        back, _ = norm_back(tokens_ref[part, :].astype(F32), gain_ref[0:1, :], normed_ref[...])
        grad_tokens_ref[part, :] = (grad_hidden_ref[part, :] + back).astype(BF)
    product = jnp.zeros((rows, D), F32)
    for k, (low, out) in enumerate(zip(weight_lows, weight_outs)):
        grad = low[...].astype(F32)
        out[...] = grad
        if k < 3:
            loads[k].wait()
            product += w_rows[k].astype(F32) * grad
    ones = jnp.ones((8, D), BF)
    high = product.astype(BF)
    low = (product - high.astype(F32)).astype(BF)
    gain_one_ref[...] = (dot_nt(ones, high) + dot_nt(ones, low))[0:1, :] / gain_rows_ref[...]
    small = small_ref[...]
    router_ref[...] = small[:, :experts].astype(F32)
    column = lax.broadcasted_iota(jnp.int32, (8, LANES), 1)
    gain_two_ref[...] = dot_nt(jnp.where(column == experts, 1.0, 0.0).astype(BF), small)[0:1, :]


def taking(us):
    return pl.CostEstimate(flops=int(us * 1.0e9), bytes_accessed=2**20, transcendentals=0)


def like(*shape, dtype=BF):
    return jax.ShapeDtypeStruct(shape, dtype)


IN_VMEM = pl.BlockSpec(memory_space=pltpu.VMEM)
ANYWHERE = pl.BlockSpec(memory_space=pl.ANY)


def experts_on_lines(two_own, hidden_one, grad_own, grad_a, named, experts, router, owners, routed, shared):
    devices = lax.axis_size("exp")
    chips = devices // 2
    length = SEQ_DEV * devices
    wide = EXP_DEV * FF + LANES
    block_back = (devices, SEQ_DEV, D + LANES)
    sems = [gather_sems(chips)] * MB + [scatter_sems(chips), gather_sems(chips)]

    def call_rows(*operands):
        def kernel(own_ref, grad_own_ref, grad_ref, named_ref, router_ref, owner_ref, *refs):
            expert_rows(
                chips, experts, own_ref, grad_own_ref, grad_ref, named_ref, router_ref, owner_ref,
                refs[:3], refs[3:6], *refs[6:],
            )

        return pl.pallas_call(
            kernel,
            out_shape=(
                like(MB, devices, SEQ_DEV, D),
                like(MB, devices, SEQ_DEV, D),
                like(MB * length, wide),
                like(MB * length, wide),
                like(MB * length, wide),
                like(MB, devices, SEQ_DEV, D),
                like(*block_back),
                like(SEQ_DEV, D + LANES, dtype=F32),
            ),
            in_specs=[IN_VMEM, ANYWHERE, ANYWHERE] + [IN_VMEM] * 3 + [ANYWHERE] * 6,
            out_specs=(ANYWHERE,) * 7 + (IN_VMEM,),
            scratch_shapes=[
                pltpu.VMEM((3, D, wide), BF),
                pltpu.VMEM((MB, devices, SEQ_DEV, D), BF),
                pltpu.VMEM((MB, devices, SEQ_DEV, D), BF),
                pltpu.VMEM((2, 3, 2 * SEQ_DEV, wide), BF),
                pltpu.VMEM((2, 2, SEQ_DEV, D), BF),
                pltpu.VMEM((MB, *block_back), BF),
                pltpu.VMEM((chips, SEQ_DEV, D + LANES), BF),
                pltpu.VMEM((chips + 1, SEQ_DEV, D + LANES), BF),
                pltpu.SemaphoreType.DMA((3, EXP_DEV + 1)),
                pltpu.SemaphoreType.DMA((4,)),
                pltpu.SemaphoreType.DMA((2, 3)),
                pltpu.SemaphoreType.DMA((4, chips)),
            ]
            + [sem for group in sems for sem in group],
            compiler_params=pltpu.CompilerParams(
                collective_id=1, has_side_effects=True, vmem_limit_bytes=VMEM_BYTES
            ),
            cost_estimate=taking(100),
            name="expert_rows",
        )(*operands)

    rows, grads, hidden, d_gate, d_up, out_parts, back_b, back_sum_a = call_rows(
        two_own, grad_own, grad_a, named, router, owners, *routed, *shared
    )
    flat = MB * length


    def call_sums(*operands):
        def kernel(*refs):
            expert_sums(chips, *refs[:16], refs[16:19], *refs[19:])

        half = D // 2
        by_rows = pl.BlockSpec((flat, half), lambda k, d: (0, d))
        by_grads = pl.BlockSpec((flat, half), lambda k, d: (0, d))

        def for_gate(k, d):
            return (0, (k + 4) // 5)

        def for_up(k, d):
            return (0, k // 3)

        def for_down(k, d):
            return (0, k // 5)

        last = pl.BlockSpec(
            (flat, LANES), lambda k, d: (0, EXP_DEV * FF // LANES), pipeline_mode=pl.Buffered(1)
        )

        def whole(*shape):
            return pl.BlockSpec(shape, lambda k, d: (0,) * len(shape))

        return pl.pallas_call(
            kernel,
            grid=(3 * EXP_DEV, 2),
            out_shape=(like(EXP_DEV, D, FF),) * 3
            + (like(SEQ_DEV, D + LANES, dtype=F32), like(SEQ_DEV, D))
            + (like(D // devices, FF),) * 3
            + (like(EXP_DEV, D // 4, FF),),
            in_specs=[by_rows, by_grads]
            + [pl.BlockSpec((flat, FF), for_down, pipeline_mode=pl.Buffered(1))]
            + [pl.BlockSpec((flat, FF), use) for use in (for_gate, for_up)]
            + [last] * 3
            + [ANYWHERE] * 2
            + [pl.BlockSpec((SEQ_DEV, D), lambda k, d: (0, 0), pipeline_mode=pl.Buffered(1))],
            out_specs=(ANYWHERE,) * 3
            + (whole(SEQ_DEV, D + LANES), whole(SEQ_DEV, D))
            + (whole(D // devices, FF),) * 3
            + (ANYWHERE,),
            scratch_shapes=[
                pltpu.VMEM((chips, SEQ_DEV, D + LANES), BF),
                pltpu.VMEM((chips, SEQ_DEV, D + LANES), BF),
                pltpu.VMEM((chips + 1, SEQ_DEV, D + LANES), BF),
                pltpu.VMEM((chips, SEQ_DEV, D), BF),
                pltpu.VMEM((chips, SEQ_DEV, D), BF),
                pltpu.VMEM((chips + 1, SEQ_DEV, D), BF),
                pltpu.VMEM((SEQ_DEV, D), F32),
                pltpu.SemaphoreType.DMA((2, chips)),
                pltpu.VMEM((2, half, FF), BF),
                pltpu.SemaphoreType.DMA((2,)),
                pltpu.VMEM((3, D, HD), BF),
                pltpu.VMEM((3, 1, D, HD), BF),
                pltpu.VMEM((1, D, HD), BF),
                pltpu.VMEM((4, D // devices, FF), BF),
            ]
            + scatter_sems(chips)
            + spread_sems(devices, 4, 1)
            + scatter_sems(chips)
            + seq_scratch(2),
            compiler_params=pltpu.CompilerParams(
                collective_id=2, has_side_effects=True, vmem_limit_bytes=VMEM_BYTES
            ),
            cost_estimate=taking(60),
            name="expert_sums",
        )(*operands)

    gate_sum, up_sum, down_sum, back_sum_b, layer_a, *shared_grads, gate_rows = call_sums(
        rows.reshape(flat, D), grads.reshape(flat, D), hidden, d_gate, d_up, hidden, d_gate, d_up, back_b,
        out_parts, hidden_one[0],
    )
    backs = (back_sum_a, back_sum_b)
    return (
        layer_a,
        out_parts,
        backs,
        gate_rows,
        (gate_sum, up_sum, down_sum),
        shared_grads,
    )


def named_softmax(logits, named):
    chosen = jnp.where(named, logits, -jnp.inf)
    powers = jnp.where(named, jnp.exp(chosen - jnp.max(chosen, axis=-1, keepdims=True)), 0.0)
    return powers / jnp.sum(powers, axis=-1, keepdims=True)


def on_device_plain(
    tokens,
    cotangent,
    expert_ids,
    owner_table,
    w_query,
    w_key,
    w_value,
    w_out,
    gain_one,
    gain_two,
    w_router,
    shared_gate,
    shared_up,
    shared_down,
    routed_gate,
    routed_up,
    routed_down,
):
    devices = lax.axis_size("exp")
    groups = lax.axis_size("seq")
    me = lax.axis_index("exp")
    experts = owner_table.shape[0]
    length = SEQ_DEV * devices
    rows_out = D // devices
    slots = -(-HEADS // devices)
    wide = slots * HD
    share = FF // devices
    used = EXP_DEV * FF + share
    padded = -(-used // LANES) * LANES

    head_of = [jnp.minimum(me + slot * devices, HEADS - 1) for slot in range(slots)]
    slot_live = jnp.concatenate(
        [
            jnp.full((HD,), jnp.where(me + slot * devices < HEADS, 1.0, 0.0), F32)
            for slot in range(slots)
        ]
    )

    w_qkv = jnp.concatenate(
        [
            lax.dynamic_slice(weight, (0, head * HD), (D, HD))
            for head in head_of
            for weight in (w_query, w_key, w_value)
        ],
        axis=1,
    )
    w_out_heads = jnp.concatenate(
        [lax.dynamic_slice(w_out, (head * HD, 0), (HD, D)) for head in head_of], axis=0
    )
    cos_table, sin_table = angle_tables(jnp.arange(length).astype(F32))
    sin_table = jnp.where(jnp.arange(HD) < HD // 2, -sin_table, sin_table)
    params = pltpu.CompilerParams(vmem_limit_bytes=VMEM_BYTES)

    forward = pl.pallas_call(
        functools.partial(attend_forward, slots),
        out_shape=(
            like(length, D),
            like(length, 3 * wide),
            like(length, wide),
            like(slots, length, 1, dtype=F32),
        ),
        in_specs=[IN_VMEM] * 5,
        out_specs=(IN_VMEM,) * 4,
        compiler_params=params,
        name="attend_forward",
    )
    backward = pl.pallas_call(
        functools.partial(attend_backward, slots),
        out_shape=(like(wide, D, dtype=F32), like(D, 3 * wide, dtype=F32), like(length, D)),
        in_specs=[IN_VMEM] * 10,
        out_specs=(IN_VMEM,) * 3,
        scratch_shapes=[
            pltpu.VMEM((length, 3 * wide), BF),
            pltpu.VMEM((length, wide), BF),
            pltpu.VMEM((length, HD), F32),
            pltpu.VMEM((length, HD), F32),
        ],
        compiler_params=params,
        name="attend_backward",
    )

    def joined(routed, shared):
        own = lax.dynamic_slice(shared, (0, me * share), (D, share))
        blank = jnp.zeros((D, padded - used), BF)
        return jnp.concatenate([routed[i] for i in range(EXP_DEV)] + [own, blank], axis=1)

    gate_all = joined(routed_gate, shared_gate)
    up_all = joined(routed_up, shared_up)
    down_all = joined(routed_down, shared_down)

    expert_at = jnp.sum(
        (owner_table[:, None] == jnp.arange(experts)[None, :]) * jnp.arange(experts)[:, None],
        axis=0,
    )
    router_rows = jnp.take(w_router, expert_at, axis=1)
    ids_all = lax.all_gather(expert_ids[:, 0], "exp", axis=1, tiled=True)

    first = []
    for micro_batch in range(MB):
        rows_all = gather_exp(tokens[micro_batch, 0])
        normed, qkv, mixed, lse = forward(rows_all, gain_one[None], cos_table, sin_table, w_qkv)
        sent = lax.all_to_all(
            mixed.reshape(devices, SEQ_DEV, wide), "exp", split_axis=0, concat_axis=0, tiled=True
        )
        own_mixed = (
            sent.reshape(devices, SEQ_DEV, slots, HD)
            .transpose(1, 2, 0, 3)
            .reshape(SEQ_DEV, slots * devices * HD)[:, :D]
        )
        rows_in = tokens[micro_batch, 0].astype(F32)
        hidden_one = rows_in + dot(own_mixed, w_out)
        two_low = norm_rows(hidden_one, gain_two).astype(BF)
        two_all = gather_exp(two_low)
        grad_all = gather_exp(cotangent[micro_batch, 0])
        first.append(
            (normed, qkv, mixed, lse, rows_in, hidden_one, two_all, grad_all)
        )

    column = jnp.arange(padded)
    second = []
    for micro_batch in range(MB):
        two_all, grad_all = first[micro_batch][6:]
        logits = dot(two_all, router_rows)
        named = jnp.any(ids_all[micro_batch][:, :, None] == expert_at[None, None, :], axis=1)
        chosen = jnp.where(named, logits, -jnp.inf)
        powers = jnp.where(named, jnp.exp(chosen - jnp.max(chosen, axis=-1, keepdims=True)), 0.0)
        gates = powers / jnp.sum(powers, axis=-1, keepdims=True)
        own_gates = lax.dynamic_slice(gates, (0, me * EXP_DEV), (length, EXP_DEV))
        weight = jnp.where(
            column[None, :] < FF,
            own_gates[:, :1],
            jnp.where(column[None, :] < 2 * FF, own_gates[:, 1:], 1.0),
        )
        gate_part = dot(two_all, gate_all)
        up_part = dot(two_all, up_all)
        down_part = dot(grad_all, down_all)
        sigmoid = jax.nn.sigmoid(gate_part)
        act = gate_part * sigmoid
        hidden = act * up_part
        products = hidden * down_part
        own_grads = jnp.stack(
            [jnp.sum(products[:, i * FF : (i + 1) * FF], axis=1) for i in range(EXP_DEV)], axis=1
        )
        hidden_low = (weight * hidden).astype(BF)
        weighted = weight * down_part
        d_gate = (weighted * up_part * (sigmoid + act * (1.0 - sigmoid))).astype(BF)
        d_up = (weighted * act).astype(BF)
        out_part = scatter_exp(dot_nt(hidden_low, down_all))
        back_part = scatter_exp(dot_nt(d_gate, gate_all) + dot_nt(d_up, up_all))
        gate_grads = lax.all_gather(own_grads, "exp", axis=1, tiled=True)
        grad_logits = (
            gates * (gate_grads - jnp.sum(gates * gate_grads, axis=-1, keepdims=True))
        ).astype(BF)
        second.append((hidden_low, d_gate, d_up, out_part, back_part, grad_logits))

    two_both = jnp.concatenate([f[6] for f in first])
    grad_both = jnp.concatenate([f[7] for f in first])
    gate_sum = dot_tn(two_both, jnp.concatenate([s[1] for s in second]))
    up_sum = dot_tn(two_both, jnp.concatenate([s[2] for s in second]))
    down_sum = dot_tn(grad_both, jnp.concatenate([s[0] for s in second]))

    def routed_sum(total):
        parts = jnp.stack([total[:, i * FF : (i + 1) * FF] for i in range(EXP_DEV)])
        return lax.psum_scatter(
            parts.astype(BF), "seq", scatter_dimension=1, tiled=True
        ).astype(F32)

    def shared_part(total):
        return total[:, EXP_DEV * FF : used]

    outputs_list = []
    grads_list = []
    small = jnp.zeros((D, experts + 2), F32)
    qkv_sum = jnp.zeros((D, 3 * wide), F32)
    out_sum = jnp.zeros((wide, D), F32)
    for micro_batch in range(MB):
        normed, qkv, mixed, lse, rows_in, hidden_one, two_all, _ = first[micro_batch]
        _, _, _, out_part, back_part, grad_logits = second[micro_batch]
        outputs_list.append((hidden_one + out_part).astype(BF))
        own_logits = lax.dynamic_slice(grad_logits, (me * SEQ_DEV, 0), (SEQ_DEV, experts))
        grad_two = back_part + dot_nt(own_logits, router_rows)
        back, gain_terms = norm_back(hidden_one, gain_two, grad_two)
        grad_hidden = cotangent[micro_batch, 0].astype(F32) + back
        own_two = lax.dynamic_slice(two_all, (me * SEQ_DEV, 0), (SEQ_DEV, D))
        router_part = dot_tn(own_two, own_logits)
        mix_all = gather_exp(grad_hidden.astype(BF))
        out_one, qkv_one, grad_part = backward(
            mix_all, normed, qkv, mixed, lse, cos_table, sin_table, w_qkv, w_out_heads, slot_live[None]
        )
        out_sum = out_sum + out_one
        qkv_sum = qkv_sum + qkv_one
        grad_normed = scatter_exp(grad_part)
        back_one, gain_one_terms = norm_back(rows_in, gain_one, grad_normed)
        grads_list.append((grad_hidden + back_one).astype(BF))
        small = small + jnp.concatenate(
            [
                router_part,
                jnp.sum(gain_one_terms, axis=0)[:, None],
                jnp.sum(gain_terms, axis=0)[:, None],
            ],
            axis=1,
        )

    def to_rows(columns):
        parts = columns.astype(BF).reshape(devices, rows_out, columns.shape[1])
        parts = lax.psum_scatter(parts, "seq", scatter_dimension=1, tiled=True)
        return lax.all_to_all(parts, "exp", split_axis=0, concat_axis=0, tiled=True)

    def to_all(rows):
        return lax.all_gather(rows, "seq", axis=0, tiled=True).astype(F32)

    piece = rows_out // groups
    shared_cols = jnp.concatenate([shared_part(t) for t in (gate_sum, up_sum, down_sum)], axis=1)
    shared_rows = to_rows(shared_cols).reshape(devices, piece, 3, share)
    shared_full = to_all(shared_rows.transpose(1, 2, 0, 3).reshape(piece, 3 * FF))
    qkv_rows = to_rows(qkv_sum).reshape(devices, piece, slots, 3, HD)
    qkv_rows = qkv_rows.transpose(1, 3, 2, 0, 4).reshape(piece, 3, slots * devices * HD)
    qkv_full = to_all(qkv_rows[:, :, :D].reshape(piece, 3 * D))
    out_part = lax.psum_scatter(out_sum.astype(BF), "seq", scatter_dimension=1, tiled=True)
    spread = jnp.zeros((slots * devices * HD, D // groups), BF)
    for slot in range(slots):
        spread = lax.dynamic_update_slice(
            spread, out_part[slot * HD : (slot + 1) * HD], ((me + slot * devices) * HD, 0)
        )
    out_rows = lax.psum_scatter(spread[:D], "exp", scatter_dimension=0, tiled=True)
    out_full = lax.all_gather(out_rows, "seq", axis=1, tiled=True).astype(F32)
    small_rows = lax.psum_scatter(
        lax.psum(small, "seq"), "exp", scatter_dimension=0, tiled=True
    )
    place_of = jnp.take(small_rows, owner_table, axis=1)
    return (
        jnp.stack(outputs_list)[:, None],
        jnp.stack(grads_list)[:, None],
        qkv_full[:, :D],
        qkv_full[:, D : 2 * D],
        qkv_full[:, 2 * D :],
        out_full,
        small_rows[:, experts],
        small_rows[:, experts + 1],
        place_of,
        shared_full[:, :FF],
        shared_full[:, FF : 2 * FF],
        shared_full[:, 2 * FF :],
        routed_sum(gate_sum),
        routed_sum(up_sum),
        routed_sum(down_sum),
    )


def on_device_lines(
    tokens,
    cotangent,
    expert_ids,
    owner_table,
    w_query,
    w_key,
    w_value,
    w_out,
    gain_one,
    gain_two,
    w_router,
    shared_gate,
    shared_up,
    shared_down,
    routed_gate,
    routed_up,
    routed_down,
):
    devices = lax.axis_size("exp")
    groups = lax.axis_size("seq")
    me = lax.axis_index("exp")
    chips = devices // 2
    experts = owner_table.shape[0]
    length = SEQ_DEV * devices
    rows_out = D // devices
    slots = -(-HEADS // devices)
    wide = slots * HD
    own = MB * SEQ_DEV

    cos_table, sin_table = turn_tables(length)

    router = jnp.pad(w_router, ((0, 0), (0, LANES - experts)))
    owners = jnp.pad(owner_table, (0, LANES - experts), constant_values=-1)[None]
    gains = jnp.stack([gain_one, gain_two])
    named_own = jnp.any(
        expert_ids.reshape(own, TOP)[:, :, None] == jnp.arange(LANES)[None, None, :], axis=1
    ).astype(BF)
    tokens_own = tokens.reshape(MB, SEQ_DEV, D)
    grad_own = cotangent.reshape(MB, SEQ_DEV, D)

    def call_forward(*operands):
        def kernel(*refs):
            heads_forward(chips, slots, *refs[:6], refs[6:9], *refs[9:])

        return pl.pallas_call(
            kernel,
            out_shape=(
                like(MB, length, D),
                like(MB, length, 3 * wide),
                like(MB, length, wide),
                like(MB, SEQ_DEV, D),
                like(MB, SEQ_DEV, D, dtype=F32),
                like(MB, SEQ_DEV, D),
                like(D, 3 * wide),
                like(devices, SEQ_DEV, D),
                like(devices, own, LANES),
            ),
            in_specs=[IN_VMEM, ANYWHERE] + [IN_VMEM] * 4 + [ANYWHERE] * 3 + [IN_VMEM],
            out_specs=(IN_VMEM,) * 7 + (ANYWHERE, IN_VMEM),
            scratch_shapes=[
                pltpu.VMEM((MB, devices, SEQ_DEV, D), BF),
                pltpu.SemaphoreType.DMA((3 * slots,)),
                pltpu.SemaphoreType.DMA((4,)),
                pltpu.SemaphoreType.DMA((MB, devices, slots)),
                pltpu.SemaphoreType.DMA((MB, devices, slots)),
            ]
            + gather_sems(chips) * 4,
            compiler_params=pltpu.CompilerParams(
                collective_id=5, has_side_effects=True, vmem_limit_bytes=VMEM_BYTES
            ),
            cost_estimate=taking(70),
            name="heads_forward",
        )(*operands)

    normed, qkv, mixed, own_mixed, hidden_one, two_low, w_qkv, grad_a, named_all = call_forward(
        tokens_own, grad_own, named_own, gains, cos_table, sin_table,
        w_query, w_key, w_value, w_out,
    )
    hidden_rows = hidden_one
    own_mixed, hidden_one = own_mixed.reshape(own, D), hidden_one.reshape(own, D)
    two_low = two_low.reshape(own, D)

    layer_a, out_parts, backs, gate_full, routed_sums, shared_lows = experts_on_lines(
        two_low.reshape(MB, SEQ_DEV, D),
        hidden_rows,
        grad_own,
        grad_a,
        named_all.reshape(devices, MB * SEQ_DEV, LANES),
        experts,
        router,
        owners,
        (routed_gate, routed_up, routed_down),
        (shared_gate, shared_up, shared_down),
    )
    def call_middle(*operands):
        def kernel(*refs):
            middle_rows(*refs, experts)

        return pl.pallas_call(
            kernel,
            out_shape=(like(own, D, dtype=F32), like(own, D), like(own, D), like(D, LANES)),
            in_specs=[IN_VMEM] * 9,
            out_specs=(IN_VMEM,) * 4,
            compiler_params=pltpu.CompilerParams(vmem_limit_bytes=VMEM_BYTES),
            cost_estimate=taking(5),
            name="middle_rows",
        )(*operands)

    grad_hidden, grad_mix, d_mixed, small = call_middle(
        *backs, named_own, hidden_one, cotangent.reshape(own, D), two_low, router, gains, w_out
    )
    quarter = like(EXP_DEV, D // groups, FF)
    far = D + LANES
    jobs = 4
    slot_shape = (jobs, 2, D // groups, FF)

    def backward_kernel(*refs):
        heads_backward(
            chips, slots, *refs[:16], refs[16:19], *refs[19:24], refs[24:27], *refs[27:36],
            refs[36 : 36 + length // BLOCK], *refs[36 + length // BLOCK :],
        )

    normed_a, normed_b, *backward_out = pl.pallas_call(
        backward_kernel,
        out_shape=(like(SEQ_DEV, D, dtype=F32),) * 2
        + (like(rows_out, D),) * 4
        + (like(rows_out, LANES), like(SEQ_DEV, D), quarter, quarter)
        + (like(*slot_shape), like(*slot_shape), like(jobs, D // groups, FF)),
        in_specs=[IN_VMEM] * 10 + [ANYWHERE] * 4,
        out_specs=(IN_VMEM,) * 8 + (ANYWHERE,) * 5,
        scratch_shapes=[
            pltpu.VMEM((3 * slots, D, HD), BF),
            pltpu.VMEM((groups - 1, slots, D, HD), BF),
            pltpu.VMEM((slots, D, HD), BF),
            pltpu.VMEM((groups, rows_out, D), BF),
            pltpu.VMEM((chips, SEQ_DEV, D), BF),
            pltpu.VMEM((chips, SEQ_DEV, D), BF),
            pltpu.VMEM((chips + 1, SEQ_DEV, D), BF),
            pltpu.VMEM((SEQ_DEV, D), F32),
            pltpu.VMEM((MB, length, wide), BF),
        ]
        + [pltpu.VMEM((slots, BLOCK, stop), BF) for stop in range(BLOCK, length + 1, BLOCK)]
        + [
            pltpu.VMEM((MB, length, 3 * wide), BF),
            pltpu.VMEM((MB, devices, SEQ_DEV, D), BF),
            pltpu.VMEM((length, HD), F32),
            pltpu.VMEM((length, HD), F32),
            pltpu.VMEM((MB, chips, SEQ_DEV, D), BF),
            pltpu.VMEM((MB, chips + 1, SEQ_DEV, D), BF),
            pltpu.VMEM((D, far), BF),
            pltpu.VMEM((chips, rows_out, far), BF),
            pltpu.VMEM((chips + 1, rows_out, far), BF),
            pltpu.VMEM((rows_out, far), F32),
            pltpu.VMEM((2, MB, length, 256), BF),
            pltpu.SemaphoreType.DMA((2,)),
            pltpu.SemaphoreType.DMA((chips,)),
            pltpu.SemaphoreType.DMA((MB, slots)),
            pltpu.SemaphoreType.DMA((MB, devices, slots)),
            pltpu.SemaphoreType.DMA((MB, devices, slots)),
        ]
        + scatter_sems(chips) * (MB + 1)
        + spread_sems(devices, groups, slots)
        + scatter_sems(chips)
        + far_sum_scratch(jobs)
        + seq_all_scratch(rows_out, (far + LANES) // groups),
        compiler_params=pltpu.CompilerParams(
            collective_id=3, has_side_effects=True, vmem_limit_bytes=VMEM_BYTES
        ),
        cost_estimate=taking(140),
        name="heads_backward",
    )(
        d_mixed.reshape(MB, SEQ_DEV, D), qkv, mixed, cos_table, sin_table, w_qkv, own_mixed,
        grad_mix, small, hidden_rows[1], normed, *routed_sums[1:], out_parts,
    )
    gain_rows = lax.dynamic_slice(gain_one, (me * rows_out,), (rows_out,))[None]

    def call_last(*operands):
        def kernel(*refs):
            last_rows(
                *refs[:6], refs[6:10], refs[10], refs[11:13], refs[13:16], *refs[16:19],
                refs[19:22], refs[22], refs[23:27], *refs[27:31], refs[31:34], *refs[34:], experts,
            )

        full = like(EXP_DEV, D // groups, FF, dtype=F32)
        return pl.pallas_call(
            kernel,
            out_shape=(like(own, D),)
            + (like(rows_out, D, dtype=F32),) * 4
            + (like(rows_out, experts, dtype=F32),)
            + (like(1, rows_out, dtype=F32),) * 2
            + (like(MB, SEQ_DEV, D),)
            + (like(rows_out, FF, dtype=F32),) * 3
            + (full,) * 3,
            in_specs=[IN_VMEM] * 19 + [ANYWHERE] * 3,
            out_specs=(IN_VMEM,) * 15,
            scratch_shapes=[pltpu.VMEM((3, rows_out, D), BF), pltpu.SemaphoreType.DMA((3,))],
            compiler_params=pltpu.CompilerParams(vmem_limit_bytes=VMEM_BYTES),
            cost_estimate=taking(6),
            name="last_rows",
        )(*operands)

    last_out = call_last(
        tokens.reshape(own, D), normed_a, normed_b, grad_hidden, gains, gain_rows,
        *backward_out[:5], layer_a, backward_out[5], *shared_lows, gate_full, *backward_out[6:8],
        w_query, w_key, w_value,
    )
    grad_tokens, attn, router_grad = last_out[0], last_out[1:5], last_out[5]
    gain_one_grad, gain_two_grad, layer_out = last_out[6:9]
    far_grads = last_out[9:]
    whole = (MB, 1, SEQ_DEV, D)
    return (
        layer_out.reshape(whole),
        grad_tokens.reshape(whole),
        *attn,
        gain_one_grad[0],
        gain_two_grad[0],
        router_grad,
        *far_grads,
    )


def solution(mesh):
    rows = P(None, "seq", "exp", None)
    placed = (rows,) * 3 + (P(),) * 11 + (P("exp", None, None),) * 3
    wide = P("exp", None)
    on_lines = mesh.shape["exp"] == 8 and mesh.shape["seq"] == 4
    on_device = on_device_lines if on_lines else on_device_plain
    return jax.shard_map(
        on_device,
        mesh=mesh,
        in_specs=placed,
        out_specs=(rows, rows, wide, wide, wide, wide, P("exp"), P("exp"))
        + (wide,) * 4
        + (P("exp", "seq", None),) * 3,
        check_vma=False,
    )
```

```python
import functools
import math

import jax
import jax.numpy as jnp
import numpy as np
from jax import lax
from jax.experimental import pallas as pl
from jax.experimental.pallas import tpu as pltpu
from jax.sharding import PartitionSpec as P

D = 1280
HEADS = 10
HD = 128
FF = 896
TOP = 7
EXP_DEV = 2
MB = 2
SEQ_DEV = 128
LANES = 128
BLOCK = 256
VMEM_BYTES = 62 * 2**20

eps = 1e-06
BF = jnp.bfloat16
F32 = jnp.float32


def norm_rows(inputs, gain):
    return inputs * lax.rsqrt(jnp.mean(inputs * inputs, axis=-1, keepdims=True) + eps) * gain


def norm_back(inputs, gain, grad):
    scale = lax.rsqrt(jnp.mean(inputs * inputs, axis=-1, keepdims=True) + eps)
    unit = inputs * scale
    weighted = grad * gain
    back = scale * (weighted - unit * jnp.mean(weighted * unit, axis=-1, keepdims=True))
    return back, grad * unit


def angle_tables(positions):
    steps_half = jnp.arange(HD // 2).astype(positions.dtype)
    frequency = jnp.exp(steps_half * (-2.0 * math.log(10000.0) / HD))
    angles = positions[:, None] * frequency[None, :]
    angles = jnp.concatenate([angles, angles], axis=-1)
    return (jnp.cos(angles), jnp.sin(angles))


def turn_tables(length):
    angles = np.arange(length)[:, None] * 10000.0 ** (-2.0 * np.arange(HD // 2) / HD)
    cos, sin = np.cos(angles), np.sin(angles)
    return (
        jnp.asarray(np.concatenate([cos, cos], axis=1), F32),
        jnp.asarray(np.concatenate([-sin, sin], axis=1), F32),
    )


def dot(a, b):
    return jnp.dot(a, b, preferred_element_type=F32)


def dot_nt(a, b):
    return lax.dot_general(a, b, (((1,), (1,)), ((), ())), preferred_element_type=F32)


def dot_tn(a, b):
    return lax.dot_general(a, b, (((0,), (0,)), ((), ())), preferred_element_type=F32)


def gather_exp(array):
    return lax.all_gather(array, "exp", axis=0, tiled=True)


def scatter_exp(array):
    return lax.psum_scatter(array.astype(BF), "exp", scatter_dimension=0, tiled=True).astype(F32)


def turn(heads, cos_table, sin_table):
    return heads * cos_table + pltpu.roll(heads, HD // 2, 1) * sin_table


def visible_scores(queries, keys, start):
    scores = dot_nt(queries, keys) * HD ** (-0.5)
    rows = queries.shape[0]
    row = lax.broadcasted_iota(jnp.int32, (rows, rows), 0)
    column = lax.broadcasted_iota(jnp.int32, (rows, rows), 1)
    last = jnp.where(row >= column, scores[:, start:], -1e30)
    return last if start == 0 else jnp.concatenate([scores[:, :start], last], axis=1)


def attend_forward(slots, rows_ref, gain_ref, cos_ref, sin_ref, w_ref, normed_ref, qkv_ref, mixed_ref, lse_ref):
    length = rows_ref.shape[0]
    step = BLOCK if length <= 2048 else BLOCK // 2

    def project(i, carry):
        part = pl.ds(pl.multiple_of(i * step, step), step)
        normed = norm_rows(rows_ref[part, :].astype(F32), gain_ref[...]).astype(BF)
        normed_ref[part, :] = normed
        for slot in range(slots):
            base = 3 * HD * slot
            qkv = dot(normed, w_ref[:, base : base + 3 * HD])
            for j in range(2):
                turned = turn(qkv[:, j * HD : (j + 1) * HD], cos_ref[part, :], sin_ref[part, :])
                qkv_ref[part, base + j * HD : base + (j + 1) * HD] = turned.astype(BF)
            qkv_ref[part, base + 2 * HD : base + 3 * HD] = qkv[:, 2 * HD :].astype(BF)
        return carry

    lax.fori_loop(0, length // step, project, 0)
    for slot in range(slots):
        base = 3 * HD * slot
        for start in range(0, length, step):
            stop = start + step
            scores = visible_scores(
                qkv_ref[start:stop, base : base + HD], qkv_ref[:stop, base + HD : base + 2 * HD], start
            )
            largest = jnp.max(scores, axis=-1, keepdims=True)
            powers = jnp.exp(scores - largest)
            total = jnp.sum(powers, axis=-1, keepdims=True)
            attention = (powers * (1.0 / total)).astype(BF)
            mixed = dot(attention, qkv_ref[:stop, base + 2 * HD : base + 3 * HD])
            mixed_ref[start:stop, slot * HD : (slot + 1) * HD] = mixed.astype(BF)
            lse_ref[slot, start:stop, :] = largest + jnp.log(total)


def attend_backward(
    slots, mix_ref, normed_ref, qkv_ref, mixed_ref, lse_ref, cos_ref, sin_ref, w_ref, w_out_ref, live_ref,
    out_sum_ref, qkv_sum_ref, grad_ref, raw_ref, d_mixed_ref, d_keys_ref, d_values_ref,
):
    length = mix_ref.shape[0]
    step = BLOCK if length <= 2048 else BLOCK // 2
    factor = HD ** (-0.5)

    def project(i, carry):
        part = pl.ds(pl.multiple_of(i * step, step), step)
        d_mixed_ref[part, :] = (dot_nt(mix_ref[part, :], w_out_ref[...]) * live_ref[...]).astype(BF)
        return carry

    lax.fori_loop(0, length // step, project, 0)
    for slot in range(slots):
        base = 3 * HD * slot
        d_keys_ref[...] = jnp.zeros_like(d_keys_ref)
        d_values_ref[...] = jnp.zeros_like(d_values_ref)
        for start in range(0, length, step):
            stop = start + step
            queries = qkv_ref[start:stop, base : base + HD]
            keys = qkv_ref[:stop, base + HD : base + 2 * HD]
            values = qkv_ref[:stop, base + 2 * HD : base + 3 * HD]
            d_mixed = d_mixed_ref[start:stop, slot * HD : (slot + 1) * HD]
            attention = jnp.exp(visible_scores(queries, keys, start) - lse_ref[slot, start:stop, :])
            d_att = dot_nt(d_mixed, values)
            row_term = jnp.sum(attention * d_att, axis=-1, keepdims=True)
            d_scores = (attention * (d_att - row_term)).astype(BF)
            d_queries = dot(d_scores, keys) * factor
            raw = turn(d_queries, cos_ref[start:stop, :], -sin_ref[start:stop, :])
            raw_ref[start:stop, base : base + HD] = raw.astype(BF)
            d_keys_ref[:stop, :] += dot_tn(d_scores, queries)
            d_values_ref[:stop, :] += dot_tn(attention.astype(BF), d_mixed)
        raw = turn(d_keys_ref[...] * factor, cos_ref[...], -sin_ref[...])
        raw_ref[:, base + HD : base + 2 * HD] = raw.astype(BF)
        raw_ref[:, base + 2 * HD : base + 3 * HD] = d_values_ref[...].astype(BF)

    def give(i, carry):
        part = pl.ds(pl.multiple_of(i * step, step), step)
        grad_ref[part, :] = dot_nt(raw_ref[part, :], w_ref[...]).astype(BF)
        return carry

    lax.fori_loop(0, length // step, give, 0)
    out_sum_ref[...] = dot_tn(mixed_ref[...], mix_ref[...])

    def sums(i, carry):
        part = pl.ds(pl.multiple_of(i * 256, 256), 256)
        qkv_sum_ref[part, :] = dot_tn(normed_ref[:, part], raw_ref[...])
        return carry

    lax.fori_loop(0, D // 256, sums, 0)


MESH = pl.DeviceIdType.MESH


def place():
    me = lax.axis_index("exp")
    return me // 2, me % 2


def remote(source, target, send_sem, recv_sem, chip, core):
    return pltpu.make_async_remote_copy(
        src_ref=source,
        dst_ref=target,
        send_sem=send_sem,
        recv_sem=recv_sem,
        device_id={"exp": 2 * chip + core},
        device_id_type=MESH,
    )


def meet(chips):
    chip, core = place()
    barrier = pltpu.get_barrier_semaphore()

    def greet(to_chip, to_core):
        pl.semaphore_signal(
            barrier, inc=1, device_id={"exp": 2 * to_chip + to_core}, device_id_type=MESH
        )

    greet(chip, 1 - core)

    @pl.when(chip < chips - 1)
    def _():
        greet(chip + 1, core)

    @pl.when(chip > 0)
    def _():
        greet(chip - 1, core)

    below = (chip + chips - 1) // chips
    above = (2 * chips - 2 - chip) // chips
    pl.semaphore_wait(barrier, 1 + below + above)


def gather_sems(chips):
    return [pltpu.SemaphoreType.DMA((chips,))] * 4 + [pltpu.SemaphoreType.DMA((2 * chips,))] * 2


class Gather:
    def __init__(self, chips, own, blocks, sems):
        self.chips, self.own, self.blocks = chips, own, blocks
        self.up_send, self.up_recv, self.down_send, self.down_recv = sems[:4]
        self.pair_send, self.pair_recv = sems[4:]

    def _source(self, hop, number):
        return self.own if hop == 0 else self.blocks.at[number]

    def _up(self, hop):
        chip, core = place()
        number = 2 * (chip - hop) + core
        return remote(
            self._source(hop, number), self.blocks.at[number],
            self.up_send.at[hop], self.up_recv.at[hop], chip + 1, core,
        )

    def _down(self, hop):
        chip, core = place()
        number = 2 * (chip + hop) + core
        return remote(
            self._source(hop, number), self.blocks.at[number],
            self.down_send.at[hop], self.down_recv.at[hop], chip - 1, core,
        )

    def _pair(self, away):
        chip, core = place()
        number = 2 * (chip + away) + core
        source = self.own if isinstance(away, int) and away == 0 else self.blocks.at[number]
        slot = away + self.chips
        return remote(
            source, self.blocks.at[number], self.pair_send.at[slot], self.pair_recv.at[slot],
            chip, 1 - core,
        )

    def _from_pair(self, away):
        chip, core = place()
        block = self.blocks.at[2 * (chip + away) + 1 - core]
        slot = away + self.chips
        return remote(
            block, block, self.pair_send.at[slot], self.pair_recv.at[slot], chip, 1 - core
        )

    def start(self):
        chip, _ = place()

        @pl.when(chip < self.chips - 1)
        def _():
            self._up(0).start()

        @pl.when(chip > 0)
        def _():
            self._down(0).start()

        self._pair(0).start()

    def hop(self, hop):
        chip, core = place()

        @pl.when(chip >= hop)
        def _():
            block = self.blocks.at[2 * (chip - hop) + core]
            remote(
                block, block, self.up_send.at[hop - 1], self.up_recv.at[hop - 1], chip, 1 - core
            ).wait_recv()

            @pl.when(chip < self.chips - 1)
            def _():
                self._up(hop).start()

            self._pair(-hop).start()

        @pl.when(chip + hop < self.chips)
        def _():
            block = self.blocks.at[2 * (chip + hop) + core]
            remote(
                block, block, self.down_send.at[hop - 1], self.down_recv.at[hop - 1], chip, 1 - core
            ).wait_recv()

            @pl.when(chip > 0)
            def _():
                self._down(hop).start()

            self._pair(hop).start()

    def take_pair(self, away):
        self._from_pair(away).wait_recv()

    def finish(self, pairs):
        chip, _ = place()
        for away in range(-self.chips + 1, self.chips):

            @pl.when(jnp.logical_and(chip + away >= 0, chip + away < self.chips))
            def _():
                if pairs:
                    self._from_pair(away).wait_recv()
                self._pair(away).wait_send()

        for hop in range(self.chips):

            @pl.when(jnp.logical_and(chip >= hop, chip < self.chips - 1))
            def _():
                self._up(hop).wait_send()

            @pl.when(jnp.logical_and(chip + hop < self.chips, chip > 0))
            def _():
                self._down(hop).wait_send()


def scatter_sems(chips):
    return [pltpu.SemaphoreType.DMA((chips,))] * 6


class Scatter:
    def __init__(self, chips, theirs, mine, pair, line, sems):
        self.chips, self.theirs, self.mine, self.pair, self.line = chips, theirs, mine, pair, line
        self.pair_send, self.pair_recv, self.up_send, self.up_recv = sems[:4]
        self.down_send, self.down_recv = sems[4:]

    def _pair(self, to):
        chip, core = place()
        return remote(
            self.theirs(to), self.pair.at[to], self.pair_send.at[to], self.pair_recv.at[to],
            chip, 1 - core,
        )

    def _up(self, chip, to):
        return remote(
            self.mine(to), self.line.at[to - chip - 1], self.up_send.at[to], self.up_recv.at[to],
            chip + 1, place()[1],
        )

    def _down(self, chip, to):
        return remote(
            self.mine(to), self.line.at[self.chips - chip + 1 + to],
            self.down_send.at[to], self.down_recv.at[to], chip - 1, place()[1],
        )

    def _arrived_up(self, to):
        chip, core = place()
        block = self.line.at[to - chip]
        remote(block, block, self.up_send.at[to], self.up_recv.at[to], chip, 1 - core).wait_recv()
        return block[...].astype(F32)

    def _arrived_down(self, to):
        chip, core = place()
        block = self.line.at[self.chips - chip + to]
        remote(
            block, block, self.down_send.at[to], self.down_recv.at[to], chip, 1 - core
        ).wait_recv()
        return block[...].astype(F32)

    def _both(self, to):
        chip, core = place()
        block = self.pair.at[to]
        remote(
            block, block, self.pair_send.at[to], self.pair_recv.at[to], chip, 1 - core
        ).wait_recv()
        return self.mine(to)[...].astype(F32) + block[...].astype(F32)

    def start(self):
        for to in range(self.chips):
            self._pair(to).start()

    def slot(self, turn):
        chip, _ = place()
        last = self.chips - 1

        @pl.when(chip <= turn)
        def _():
            to = last - turn + chip
            total = self._both(to)

            @pl.when(chip == 0)
            def _():
                self.mine(to)[...] = total.astype(BF)

            @pl.when(chip > 0)
            def _():
                self.mine(to)[...] = (total + self._arrived_up(to)).astype(BF)

            self._up(chip, to).start()

        @pl.when(last - chip <= turn)
        def _():
            to = turn - last + chip
            total = self._both(to)

            @pl.when(chip == last)
            def _():
                self.mine(to)[...] = total.astype(BF)

            @pl.when(chip < last)
            def _():
                self.mine(to)[...] = (total + self._arrived_down(to)).astype(BF)

            self._down(chip, to).start()

    def finish(self, result):
        chip, _ = place()
        last = self.chips - 1
        result[...] = self._both(chip)

        @pl.when(chip > 0)
        def _():
            result[...] += self._arrived_up(chip)

        @pl.when(chip < last)
        def _():
            result[...] += self._arrived_down(chip)

        for to in range(self.chips):
            self._pair(to).wait_send()

            @pl.when(to > chip)
            def _():
                self._up(chip, to).wait_send()

            @pl.when(to < chip)
            def _():
                self._down(chip, to).wait_send()


def part_of(array, index):
    return array.at[index]


def block_order(chip, turn, chips):
    number, bit = 0, 1
    while bit < chips:
        number = number + bit * ((chip // bit + turn // bit) % 2)
        bit = 2 * bit
    return number


def expert_rows(
    chips, experts,
    own_ref, grad_own_ref, grad_ref, named_ref, router_ref, owner_ref, routed_refs, shared_refs,
    rows_ref, grads_ref, hidden_ref, d_gate_ref, d_up_ref, out_ref, back_b_ref, back_a_ref,
    weights, rows, grads, stage, out, back, pair, line, weight_sem, local_sem, stage_sem, keep_sem,
    *sems,
):
    chip, core = place()
    me = 2 * chip + core
    blocks = chips
    size = 2 * SEQ_DEV
    gathers = [Gather(chips, own_ref.at[m], rows.at[m], sems[6 * m : 6 * m + 6]) for m in range(MB)]
    grad_gather = Gather(chips, grad_own_ref.at[1], grads.at[1], sems[18:24])
    scatter = Scatter(
        chips,
        lambda to: back.at[0, 2 * to + 1 - core],
        lambda to: back.at[0, 2 * to + core],
        pair, line, sems[12:18],
    )
    loads = []
    for k in range(3):
        for e in range(EXP_DEV):
            loads.append(
                pltpu.make_async_copy(
                    routed_refs[k].at[e], weights.at[k, :, e * FF : (e + 1) * FF],
                    weight_sem.at[k, e],
                )
            )

    def shared_load(k):
        columns = pl.ds(pl.multiple_of(me * HD, HD), HD)
        return pltpu.make_async_copy(
            shared_refs[k].at[:, columns], weights.at[k, :, EXP_DEV * FF :], weight_sem.at[k, EXP_DEV]
        )

    def shared_loads(action):
        @pl.when(me < FF // HD)
        def _():
            for k in range(3):
                action(shared_load(k))

    def stage_out(step, k):
        block = block_order(chip, step % blocks, chips)
        start = pl.multiple_of((step // blocks * blocks + block) * size, size)
        target = (hidden_ref, d_gate_ref, d_up_ref)[k]
        return pltpu.make_async_copy(
            stage.at[step % 2, k], target.at[pl.ds(start, size), :], stage_sem.at[step % 2, k]
        )

    def out_copy(step):
        block = block_order(chip, step % blocks, chips)
        return pltpu.make_async_copy(
            out.at[step % 2], out_ref.at[step // blocks, pl.ds(2 * block, 2)], keep_sem.at[0, step % 2]
        )

    def back_copy(step):
        block = block_order(chip, step % blocks, chips)
        return pltpu.make_async_copy(
            back.at[1, pl.ds(2 * block, 2)], back_b_ref.at[pl.ds(2 * block, 2)],
            keep_sem.at[1, step % blocks],
        )

    for load in loads:
        load.start()
    shared_loads(lambda copy: copy.start())

    @pl.when(me >= FF // HD)
    def _():
        for k in range(3):
            weights[k, :, EXP_DEV * FF :] = jnp.zeros((D, HD), BF)

    own_copies = [
        pltpu.make_async_copy(own_ref.at[m], rows.at[m, me], local_sem.at[m]) for m in range(MB)
    ] + [
        pltpu.make_async_copy(grad_ref, grads.at[0], local_sem.at[2]),
        pltpu.make_async_copy(grad_own_ref.at[1], grads.at[1, me], local_sem.at[3]),
    ]
    for copy in own_copies:
        copy.start()
    meet(chips)
    gathers[0].start()
    for copy in own_copies:
        copy.wait()
    for load in loads:
        load.wait()
    shared_loads(lambda copy: copy.wait())

    def at(step, number, action):
        @pl.when(step == number)
        def _():
            action()

    row_copies = [
        pltpu.make_async_copy(source.at[m], target.at[m], keep_sem.at[2 + k, m])
        for m in range(MB)
        for k, (source, target) in enumerate(((rows, rows_ref), (grads, grads_ref)))
    ]

    def body(step, carry):
        micro_batch = step // blocks
        block = block_order(chip, step % blocks, chips)
        for m in range(MB):
            for hop in range(1, chips):
                at(step, m * blocks + hop, lambda m=m, hop=hop: gathers[m].hop(hop))
        for hop in range(1, chips):
            at(step, blocks + hop, lambda hop=hop: grad_gather.hop(hop))
        at(step, 1, gathers[1].start)
        at(step, 2, grad_gather.start)
        at(step, blocks, scatter.start)
        at(step, blocks, lambda: [copy.start() for copy in row_copies[:2]])
        for m in range(MB):

            @pl.when(micro_batch == m)
            def _():
                gathers[m].take_pair(block - chip)

        @pl.when(micro_batch == 1)
        def _():
            grad_gather.take_pair(block - chip)

        @pl.when(step >= 2)
        def _():
            for k in range(3):
                stage_out(step - 2, k).wait()
            out_copy(step - 2).wait()

        at(step, 2 * blocks - 1, lambda: [copy.start() for copy in row_copies[2:]])
        slot = step % 2
        normed = rows[micro_batch, pl.ds(2 * block, 2)].reshape(size, D)
        grad = grads[micro_batch, pl.ds(2 * block, 2)].reshape(size, D)
        logits = dot(normed, router_ref[...])
        names = pl.ds(pl.multiple_of(micro_batch * SEQ_DEV, SEQ_DEV), SEQ_DEV)
        named = named_ref[pl.ds(2 * block, 2), names, :].reshape(size, LANES).astype(F32)
        chosen = jnp.where(named > 0.0, logits, -1e30)
        powers = jnp.where(
            named > 0.0, jnp.exp(chosen - jnp.max(chosen, axis=1, keepdims=True)), 0.0
        )
        gates = powers / jnp.sum(powers, axis=1, keepdims=True)
        own = [
            jnp.sum(jnp.where(owner_ref[...] == EXP_DEV * me + e, gates, 0.0), axis=1, keepdims=True)
            for e in range(EXP_DEV)
        ]
        gate_grads = [jnp.zeros((size, 1), F32) for _ in range(EXP_DEV)]
        wide = weights.shape[2]
        for left in range(0, wide, 512):
            right = min(left + 512, wide)
            gate_part = dot(normed, weights[0, :, left:right])
            up_part = dot(normed, weights[1, :, left:right])
            down_part = dot(grad, weights[2, :, left:right])
            sigmoid = 0.5 * jnp.tanh(0.5 * gate_part) + 0.5
            act = gate_part * sigmoid
            hidden = act * up_part
            product = hidden * down_part
            scales = []
            for e in range(EXP_DEV + 1):
                low, high = max(left, e * FF), min(right, (e + 1) * FF)
                if low >= high:
                    continue
                if e < EXP_DEV:
                    gate_grads[e] += jnp.sum(
                        product[:, low - left : high - left], axis=1, keepdims=True
                    )
                    scales.append(jnp.broadcast_to(own[e], (size, high - low)))
                else:
                    scales.append(jnp.ones((size, high - low), F32))
            scale = scales[0] if len(scales) == 1 else jnp.concatenate(scales, axis=1)
            scaled = down_part * scale
            stage[slot, 0, :, left:right] = (hidden * scale).astype(BF)
            stage[slot, 1, :, left:right] = (
                scaled * up_part * (sigmoid + act * (1.0 - sigmoid))
            ).astype(BF)
            stage[slot, 2, :, left:right] = (scaled * act).astype(BF)
        for k in range(3):
            stage_out(step, k).start()
        for turn in range(chips - 1):
            at(step, blocks + turn, lambda turn=turn: scatter.slot(turn))
        result = dot_nt(stage[slot, 0], weights[2]).astype(BF)
        out[slot] = result.reshape(2, SEQ_DEV, D)
        out_copy(step).start()
        result = (dot_nt(stage[slot, 1], weights[0]) + dot_nt(stage[slot, 2], weights[1])).astype(BF)
        back[micro_batch, pl.ds(2 * block, 2), :, :D] = result.reshape(2, SEQ_DEV, D)
        high_tail, low_tail = jnp.zeros((size, LANES), F32), jnp.zeros((size, LANES), F32)
        for e in range(EXP_DEV):
            ours = owner_ref[...] == EXP_DEV * me + e
            high = gate_grads[e].astype(BF).astype(F32)
            high_tail = jnp.where(ours, high, high_tail)
            low_tail = jnp.where(ours, gate_grads[e] - high, low_tail)
        tail = high_tail + pltpu.roll(low_tail, experts, 1)
        back[micro_batch, pl.ds(2 * block, 2), :, D:] = tail.astype(BF).reshape(2, SEQ_DEV, LANES)

        @pl.when(micro_batch == 1)
        def _():
            back_copy(step).start()

        return carry

    lax.fori_loop(0, MB * blocks, body, 0)
    last = MB * blocks
    scatter.finish(back_a_ref)
    for m in range(MB):
        gathers[m].finish(False)
    grad_gather.finish(False)
    for copy in row_copies:
        copy.wait()
    for step in (last - 2, last - 1):
        for k in range(3):
            stage_out(step, k).wait()
        out_copy(step).wait()
    for turn in range(blocks):
        back_copy(blocks + turn).wait()


def seq_all_scratch(rows, width):
    groups = 4
    return [
        pltpu.VMEM((rows, groups * width), BF),
        pltpu.VMEM((groups - 1, rows, width), BF),
        pltpu.VMEM((rows, groups * width), BF),
    ] + [pltpu.SemaphoreType.DMA((groups,))] * 4


class SeqAll:
    def __init__(self, scratch):
        self.low, self.arrived, self.whole = scratch[:3]
        self.first_send, self.first_recv, self.last_send, self.last_recv = scratch[3:]
        self.groups = 4
        self.width = self.arrived.shape[2]
        self.group = lax.axis_index("seq")

    def _part(self, ref, device):
        return ref.at[:, pl.ds(pl.multiple_of(device * self.width, LANES), self.width)]

    def _copy(self, source, target, send, recv, away):
        return pltpu.make_async_remote_copy(
            src_ref=source, dst_ref=target, send_sem=send.at[away], recv_sem=recv.at[away],
            device_id={"seq": (self.group + away) % self.groups}, device_id_type=MESH,
        )

    def _first(self, away):
        part = self._part(self.low, (self.group + away) % self.groups)
        return self._copy(part, self.arrived.at[away - 1], self.first_send, self.first_recv, away)

    def _last(self, away):
        part = self._part(self.whole, self.group)
        return self._copy(part, part, self.last_send, self.last_recv, away)

    def start(self):
        for away in range(1, self.groups):
            self._first(away).start()

    def middle(self):
        total = self._part(self.low, self.group)[...].astype(F32)
        for away in range(1, self.groups):
            self._first(away).wait_recv()
            total += self.arrived[away - 1].astype(F32)
        self._part(self.whole, self.group)[...] = total.astype(BF)
        for away in range(1, self.groups):
            self._last(away).start()

    def take(self):
        for away in range(1, self.groups):
            part = self._part(self.whole, (self.group + self.groups - away) % self.groups)
            self._copy(part, part, self.last_send, self.last_recv, away).wait_recv()

    def finish(self):
        for away in range(1, self.groups):
            self._first(away).wait_send()
            self._last(away).wait_send()


def expert_sums(
    chips,
    rows_ref, grads_ref, hidden_ref, d_gate_ref, d_up_ref, shared_h_ref, shared_g_ref, shared_u_ref, back_ref, out_ref, hidden_one_ref,
    gate_ref, up_ref, down_ref, back_b_ref, layer_ref, shared_outs, gate_rows_ref,
    mine, pair, line, out_mine, out_pair, out_line, layer, local_sem, stage, stage_sem, shared, arrived, summed, held, *sems,
):
    chip, core = place()
    devices = 2 * chips
    half = D // 2
    matrix, side = pl.program_id(0), pl.program_id(1)
    step = 2 * matrix + side
    last = 2 * 3 * EXP_DEV - 1
    scatter = Scatter(
        chips,
        lambda to: back_ref.at[2 * to + 1 - core],
        lambda to: mine.at[to],
        pair, line, sems[:6],
    )
    spread = Spread(
        devices, 4, 1,
        lambda owner, k: shared.at[owner],
        lambda k, device: device < FF // HD,
        lambda device, k: device,
        arrived, summed, held, FF, sems[6:13],
    )
    results = Scatter(
        chips,
        lambda to: out_ref.at[0, 2 * to + 1 - core],
        lambda to: out_mine.at[to],
        out_pair, out_line, sems[13:19],
    )
    routed = [
        SeqSum(gate_ref.at[e], gate_rows_ref.at[e], e == 0, e, sems[19:])
        for e in range(EXP_DEV)
    ]
    targets = [(ref, e) for ref in (gate_ref, up_ref, down_ref) for e in range(EXP_DEV)]

    def write(number):
        target, e = targets[number // 2]
        part = pl.ds(number % 2 * half, half)
        return pltpu.make_async_copy(
            stage.at[number % 2], target.at[e, part], stage_sem.at[number % 2]
        )

    def at(number, action):
        @pl.when(step == number)
        def _():
            action()

    def begin():
        loads = [
            pltpu.make_async_copy(source, target, local_sem.at[number, to])
            for to in range(chips)
            for number, (source, target) in enumerate(
                (
                    (back_ref.at[2 * to + core], mine.at[to]),
                    (out_ref.at[0, 2 * to + core], out_mine.at[to]),
                )
            )
        ]
        for load in loads:
            load.start()
        meet_all(("seq", "exp"))
        scatter.start()
        for load in loads:
            load.wait()

    at(0, begin)
    for number in range(2, last + 1, 2):
        at(number, lambda number=number: [write(number - 2).wait(), write(number - 1).wait()])
    at(2, lambda: scatter.slot(0))
    at(2, routed[0].start)
    at(4, routed[1].start)
    at(4, lambda: scatter.slot(1))
    at(6, lambda: scatter.slot(2))
    at(7, spread.middle)
    at(4, results.start)
    at(7, lambda: results.slot(0))
    at(9, lambda: results.slot(1))
    at(10, lambda: results.slot(2))
    slot = step % 2

    @pl.when(matrix < EXP_DEV)
    def _():
        stage[slot] = dot_tn(rows_ref[...], d_gate_ref[...]).astype(BF)

    @pl.when(jnp.logical_and(matrix >= EXP_DEV, matrix < 2 * EXP_DEV))
    def _():
        stage[slot] = dot_tn(rows_ref[...], d_up_ref[...]).astype(BF)

    @pl.when(matrix >= 2 * EXP_DEV)
    def _():
        stage[slot] = dot_tn(grads_ref[...], hidden_ref[...]).astype(BF)

    @pl.when(matrix == 0)
    def _():
        part = pl.ds(pl.multiple_of(side * half, half), half)
        shared[0, part, :] = dot_tn(rows_ref[...], shared_g_ref[...]).astype(BF)
        shared[1, part, :] = dot_tn(rows_ref[...], shared_u_ref[...]).astype(BF)
        shared[2, part, :] = dot_tn(grads_ref[...], shared_h_ref[...]).astype(BF)

    for number in range(last + 1):
        at(number, lambda number=number: write(number).start())
    at(1, spread.start)
    at(8, lambda: scatter.finish(back_b_ref))
    at(9, spread.hand_out)
    at(9, routed[0].middle)

    @pl.when(step == last)
    def _():
        routed[1].middle()
        results.finish(layer)
        layer_ref[...] = (layer[...] + hidden_one_ref[...]).astype(BF)
        write(last - 1).wait()
        write(last).wait()
        spread.take()
        for kind, target in enumerate(shared_outs):
            target[...] = spread.of_kind(kind)[...]
        for job in routed:
            job.finish()
        spread.finish()


def meet_all(axes):
    barrier = pltpu.get_barrier_semaphore()
    count = 0
    for axis in axes:
        size = lax.axis_size(axis)
        for away in range(1, size):
            other = (lax.axis_index(axis) + away) % size
            pl.semaphore_signal(barrier, inc=1, device_id={axis: other}, device_id_type=MESH)
            count += 1
    pl.semaphore_wait(barrier, count)


FIRST_EXTRA, EXTRA_APART = 2, 3


def slot_head(slot, device, devices):
    return device if slot == 0 else devices + (device - FIRST_EXTRA) // EXTRA_APART


def slot_lives(slot, device, devices):
    if slot == 0:
        return device >= 0
    past = device - FIRST_EXTRA
    return jnp.logical_and(
        jnp.logical_and(past >= 0, past % EXTRA_APART == 0),
        past < EXTRA_APART * (HEADS - devices),
    )


def spread_sems(devices, groups, units):
    return [
        pltpu.SemaphoreType.DMA((groups - 1, units)),
        pltpu.SemaphoreType.DMA((groups - 1, units)),
        pltpu.SemaphoreType.DMA((units,)),
        pltpu.SemaphoreType.DMA((devices, units)),
        pltpu.SemaphoreType.DMA((devices, units)),
        pltpu.SemaphoreType.DMA((groups,)),
        pltpu.SemaphoreType.DMA((groups,)),
    ]


class Spread:
    def __init__(self, devices, groups, units, unit, lives, column, arrived, summed, held, width, sems):
        self.devices, self.groups, self.units = devices, groups, units
        self.unit, self.lives, self.column = unit, lives, column
        self.arrived, self.summed, self.held, self.width = arrived, summed, held, width
        self.first_send, self.first_recv, self.local_sem = sems[:3]
        self.second_send, self.second_recv, self.third_send, self.third_recv = sems[3:]
        self.kinds = groups - 1
        self.rows = D // devices
        self.group, self.me = lax.axis_index("seq"), lax.axis_index("exp")

    def _rows(self, device):
        return pl.ds(pl.multiple_of(device * self.rows, 32), self.rows)

    def _columns(self, device, k):
        return pl.ds(pl.multiple_of(self.column(device, k) * HD, HD), HD)

    def _along_seq(self, source, target, send, recv, away):
        return pltpu.make_async_remote_copy(
            src_ref=source, dst_ref=target, send_sem=send, recv_sem=recv,
            device_id={"seq": (self.group + away) % self.groups}, device_id_type=MESH,
        )

    def _along_exp(self, source, target, away, k):
        return pltpu.make_async_remote_copy(
            src_ref=source, dst_ref=target,
            send_sem=self.second_send.at[away, k], recv_sem=self.second_recv.at[away, k],
            device_id={"exp": (self.me + away) % self.devices}, device_id_type=MESH,
        )

    def _first(self, away, k):
        owner = (self.group + away) % self.groups
        return self._along_seq(
            self.unit(owner, k), self.arrived.at[away - 1, k],
            self.first_send.at[away - 1, k], self.first_recv.at[away - 1, k], away,
        )

    def _second(self, away, k):
        other = (self.me + away) % self.devices
        return self._along_exp(
            self.summed.at[k, self._rows(other)], self.held.at[0, :, self._columns(self.me, k)], away, k
        )

    def _own(self, k):
        return pltpu.make_async_copy(
            self.summed.at[k, self._rows(self.me)], self.held.at[0, :, self._columns(self.me, k)],
            self.local_sem.at[k],
        )

    def _third(self, away):
        return self._along_seq(
            self.held.at[0, :, : self.width], self.held.at[away, :, : self.width],
            self.third_send.at[away], self.third_recv.at[away], away,
        )

    def _sends_first(self, action):
        for k in range(self.units):
            for away in range(1, self.groups):

                @pl.when(
                    jnp.logical_and(
                        (self.group + away) % self.groups < self.kinds, self.lives(k, self.me)
                    )
                )
                def _():
                    action(self._first(away, k))

    def start(self):
        self._sends_first(lambda copy: copy.start())

    def middle(self):
        @pl.when(self.group < self.kinds)
        def _():
            for k in range(self.units):

                @pl.when(self.lives(k, self.me))
                def _():
                    total = self.unit(self.group, k)[...].astype(F32)
                    for away in range(1, self.groups):
                        block = self.arrived.at[away - 1, k]
                        self._along_seq(
                            block, block, self.first_send.at[away - 1, k],
                            self.first_recv.at[away - 1, k], away,
                        ).wait_recv()
                        total += block[...].astype(F32)
                    self.summed[k] = total.astype(BF)
                    for away in range(1, self.devices):
                        self._second(away, k).start()
                    self._own(k).start()

    def hand_out(self):
        @pl.when(self.group < self.kinds)
        def _():
            for k in range(self.units):

                @pl.when(self.lives(k, self.me))
                def _():
                    self._own(k).wait()

                for away in range(1, self.devices):
                    source = (self.me + self.devices - away) % self.devices

                    @pl.when(self.lives(k, source))
                    def _():
                        block = self.held.at[0, :, self._columns(source, k)]
                        self._along_exp(block, block, away, k).wait_recv()

            for away in range(1, self.groups):
                self._third(away).start()

    def take(self):
        for away in range(1, self.groups):

            @pl.when((self.group + self.groups - away) % self.groups < self.kinds)
            def _():
                self._third(away).wait_recv()

    def of_kind(self, kind):
        return self.held.at[(self.group + self.groups - kind) % self.groups]

    def finish(self):
        self._sends_first(lambda copy: copy.wait_send())

        @pl.when(self.group < self.kinds)
        def _():
            for k in range(self.units):

                @pl.when(self.lives(k, self.me))
                def _():
                    for away in range(1, self.devices):
                        self._second(away, k).wait_send()

            for away in range(1, self.groups):
                self._third(away).wait_send()


def seq_scratch(jobs):
    rows = D // 4
    return [
        pltpu.VMEM((jobs, 2, rows, FF), BF),
        pltpu.VMEM((jobs, 2, rows, FF), BF),
        pltpu.VMEM((jobs, rows, FF), BF),
        pltpu.VMEM((rows, FF), BF),
        pltpu.SemaphoreType.DMA((jobs, 2)),
        pltpu.SemaphoreType.DMA((jobs, 2)),
        pltpu.SemaphoreType.DMA((jobs, 2)),
        pltpu.SemaphoreType.DMA((jobs,)),
        pltpu.SemaphoreType.DMA((jobs,)),
        pltpu.SemaphoreType.DMA((jobs,)),
    ]


class SeqSum:
    def __init__(self, source, out, x_first, job, scratch):
        mine, arrived, last, result = scratch[:4]
        self.source, self.out, self.x_first = source, out, x_first
        self.mine, self.arrived, self.last = mine.at[job], arrived.at[job], last.at[job]
        self.result = result
        self.first_send, self.first_recv, self.load_sem = [sem.at[job] for sem in scratch[4:7]]
        self.last_send, self.last_recv, self.out_sem = [sem.at[job] for sem in scratch[7:]]
        group = lax.axis_index("seq")
        self.x, self.y = group % 2, group // 2
        self.rows = source.shape[0] // 4
        self.own = self.y if x_first else self.x

    def _neighbour(self, along_x):
        return 2 * self.y + 1 - self.x if along_x else 2 * (1 - self.y) + self.x

    def _block(self, i, kept):
        side = self.x if self.x_first else self.y
        side = side if kept else 1 - side
        number = 2 * i + side if self.x_first else 2 * side + i
        return self.source.at[pl.ds(pl.multiple_of(number * self.rows, 32), self.rows)]

    def _copy(self, source, target, send, recv, along_x):
        return pltpu.make_async_remote_copy(
            src_ref=source, dst_ref=target, send_sem=send, recv_sem=recv,
            device_id={"seq": self._neighbour(along_x)}, device_id_type=MESH,
        )

    def _first(self, i):
        return self._copy(
            self._block(i, False), self.arrived.at[i], self.first_send.at[i],
            self.first_recv.at[i], self.x_first,
        )

    def _load(self, i):
        return pltpu.make_async_copy(self._block(i, True), self.mine.at[i], self.load_sem.at[i])

    def _last(self):
        return self._copy(
            self.mine.at[1 - self.own], self.last, self.last_send, self.last_recv,
            not self.x_first,
        )

    def _write(self):
        return pltpu.make_async_copy(self.result, self.out, self.out_sem)

    def start(self):
        for i in range(2):
            self._first(i).start()
            self._load(i).start()

    def middle(self):
        for i in range(2):
            self._first(i).wait_recv()
            self._load(i).wait()
            self.mine[i] = (self.mine[i].astype(F32) + self.arrived[i].astype(F32)).astype(BF)
        self._last().start()

    def finish(self):
        self._last().wait_recv()
        total = self.mine[self.own].astype(F32) + self.last[...].astype(F32)
        self.result[...] = total.astype(BF)
        self._write().start()
        for i in range(2):
            self._first(i).wait_send()
        self._last().wait_send()
        self._write().wait()


def far_sum_scratch(jobs):
    rows = D // 4
    return [
        pltpu.VMEM((2, rows, FF), BF),
        pltpu.VMEM((2, rows, FF), BF),
        pltpu.VMEM((rows, FF), BF),
        pltpu.SemaphoreType.DMA((jobs, 2)),
        pltpu.SemaphoreType.DMA((jobs, 2)),
        pltpu.SemaphoreType.DMA((jobs, 2)),
        pltpu.SemaphoreType.DMA((jobs,)),
        pltpu.SemaphoreType.DMA((jobs,)),
        pltpu.SemaphoreType.DMA((jobs,)),
        pltpu.SemaphoreType.DMA((jobs, 2)),
    ]


class FarSeqSum(SeqSum):
    def __init__(self, source, out, x_first, job, slots, scratch):
        mine, arrived, last = slots
        self.ours, self.theirs, result = scratch[:3]
        self.more_sem = scratch[9].at[job]
        super().__init__(source, out, x_first, job, [mine, arrived, last, result] + list(scratch[3:9]))

    def _fetch(self, i):
        return pltpu.make_async_copy(self.arrived.at[i], self.theirs.at[i], self.more_sem.at[i])

    def _load(self, i):
        return pltpu.make_async_copy(self._block(i, True), self.ours.at[i], self.load_sem.at[i])

    def _store(self, i):
        return pltpu.make_async_copy(self.ours.at[i], self.mine.at[i], self.load_sem.at[i])

    def start(self):
        for i in range(2):
            self._first(i).start()

    def middle(self):
        for i in range(2):
            self._load(i).start()
        for i in range(2):
            self._first(i).wait_recv()
            self._fetch(i).start()
        for i in range(2):
            self._load(i).wait()
            self._fetch(i).wait()
            self.ours[i] = (self.ours[i].astype(F32) + self.theirs[i].astype(F32)).astype(BF)
            self._store(i).start()
        for i in range(2):
            self._store(i).wait()
        self._last().start()

    def finish(self):
        ours = pltpu.make_async_copy(self.mine.at[self.own], self.ours.at[0], self.load_sem.at[0])
        ours.start()
        self._last().wait_recv()
        theirs = pltpu.make_async_copy(self.last, self.theirs.at[0], self.more_sem.at[0])
        theirs.start()
        ours.wait()
        theirs.wait()
        total = self.ours[0].astype(F32) + self.theirs[0].astype(F32)
        self.result[...] = total.astype(BF)
        self._write().start()
        for i in range(2):
            self._first(i).wait_send()
        self._last().wait_send()
        self._write().wait()


def softmax_low(scores):
    powers = jnp.exp(scores - jnp.max(scores, axis=-1, keepdims=True))
    return (powers * (1.0 / jnp.sum(powers, axis=-1, keepdims=True))).astype(BF)


def heads_forward(
    chips, slots,
    tokens_ref, grad_own_ref, named_own_ref, gain_ref, cos_ref, sin_ref, w_refs, w_out_ref,
    normed_ref, qkv_ref, mixed_ref, own_mixed_ref, hidden_ref, two_ref, w_all, grad_ref, named_ref,
    rows, w_sem, local_sem, send_sem, recv_sem, *sems,
):
    devices = 2 * chips
    me = lax.axis_index("exp")
    chip, _ = place()
    length = SEQ_DEV * devices
    size = 2 * SEQ_DEV
    step = BLOCK
    gathers = [Gather(chips, tokens_ref.at[m], rows.at[m], sems[6 * m : 6 * m + 6]) for m in range(MB)]
    later = [
        Gather(chips, named_own_ref, named_ref, sems[12:18]),
        Gather(chips, grad_own_ref.at[0], grad_ref, sems[18:24]),
    ]
    keeps = [
        pltpu.make_async_copy(source, target, local_sem.at[number])
        for number, (source, target) in enumerate(
            [(tokens_ref.at[m], rows.at[m, me]) for m in range(MB)]
            + [(named_own_ref, named_ref.at[me]), (grad_own_ref.at[0], grad_ref.at[me])]
        )
    ]

    def load(slot, j):
        head = jnp.clip(slot_head(slot, me, devices), 0, HEADS - 1)
        unit = 3 * slot + j
        return pltpu.make_async_copy(
            w_refs[j].at[:, pl.ds(pl.multiple_of(head * HD, HD), HD)],
            w_all.at[:, unit * HD : (unit + 1) * HD],
            w_sem.at[unit],
        )

    def head_columns(m, device, slot):
        return own_mixed_ref.at[
            m, :, pl.ds(pl.multiple_of(slot_head(slot, device, devices) * HD, HD), HD)
        ]

    def rows_of(m, device, slot):
        part = pl.ds(pl.multiple_of(device * SEQ_DEV, SEQ_DEV), SEQ_DEV)
        return mixed_ref.at[m, part, slot * HD : (slot + 1) * HD]

    def give(m, away, slot):
        other = (me + away) % devices
        return pltpu.make_async_remote_copy(
            src_ref=rows_of(m, other, slot),
            dst_ref=head_columns(m, me, slot),
            send_sem=send_sem.at[m, away, slot],
            recv_sem=recv_sem.at[m, away, slot],
            device_id={"exp": other},
            device_id_type=MESH,
        )

    def keep_own(m, slot):
        return pltpu.make_async_copy(
            rows_of(m, me, slot), head_columns(m, me, slot), recv_sem.at[m, 0, slot]
        )

    def take(m, away, slot):
        block = head_columns(m, (me + devices - away) % devices, slot)
        return pltpu.make_async_remote_copy(
            src_ref=block,
            dst_ref=block,
            send_sem=send_sem.at[m, away, slot],
            recv_sem=recv_sem.at[m, away, slot],
            device_id={"exp": (me + away) % devices},
            device_id_type=MESH,
        )

    for copy in keeps:
        copy.start()
    for slot in range(slots):
        for j in range(3):
            load(slot, j).start()
    meet_all(("exp",))
    gathers[0].start()
    for copy in keeps:
        copy.wait()
    for slot in range(slots):
        for j in range(3):
            load(slot, j).wait()

    def body(m, carry):
        def at(number, action):
            @pl.when(m == number)
            def _():
                action()

        for turn_ in range(chips):
            block = block_order(chip, turn_, chips)
            for number in range(MB):
                if turn_ > number:
                    at(number, lambda number=number: gathers[number].hop(turn_))
                at(number, lambda number=number: gathers[number].take_pair(block - chip))
            if turn_ == chips - 2:
                at(0, gathers[1].start)
                at(1, later[0].start)
                at(1, later[1].start)
            part = pl.ds(pl.multiple_of(block * size, size), size)
            tokens = rows[m, pl.ds(2 * block, 2)].reshape(size, D).astype(F32)
            normed = norm_rows(tokens, gain_ref[0:1, :]).astype(BF)
            normed_ref[m, part, :] = normed
            qkv = dot(normed, w_all[...])
            for unit in range(3 * slots):
                values = qkv[:, unit * HD : (unit + 1) * HD]
                if unit % 3 < 2:
                    values = turn(values, cos_ref[part, :], sin_ref[part, :])
                qkv_ref[m, part, unit * HD : (unit + 1) * HD] = values.astype(BF)
        for slot in range(slots):
            base = 3 * HD * slot
            for start in range(0, length, step):
                stop = start + step
                scores = visible_scores(
                    qkv_ref[m, start:stop, base : base + HD],
                    qkv_ref[m, :stop, base + HD : base + 2 * HD],
                    start,
                )
                attention = softmax_low(scores)
                mixed = dot(attention, qkv_ref[m, :stop, base + 2 * HD : base + 3 * HD])
                mixed_ref[m, start:stop, slot * HD : (slot + 1) * HD] = mixed.astype(BF)
            for number in range(MB):

                @pl.when(jnp.logical_and(m == number, slot_lives(slot, me, devices)))
                def _():
                    for away in range(1, devices):
                        give(number, away, slot).start()
                    keep_own(number, slot).start()

            if slot == 0:
                at(0, lambda: gathers[1].hop(1))
                at(1, lambda: [gather.hop(1) for gather in later])
            else:
                at(1, lambda: [gather.hop(2) for gather in later])
        return carry

    lax.fori_loop(0, MB, body, 0)

    def finish_rows(m):
        for slot in range(slots):

            @pl.when(slot_lives(slot, me, devices))
            def _():
                keep_own(m, slot).wait()

            for away in range(1, devices):

                @pl.when(slot_lives(slot, (me + devices - away) % devices, devices))
                def _():
                    take(m, away, slot).wait_recv()

        hidden = tokens_ref[m].astype(F32) + dot(own_mixed_ref[m], w_out_ref[...])
        hidden_ref[m] = hidden
        two_ref[m] = norm_rows(hidden, gain_ref[1:2, :]).astype(BF)

    finish_rows(0)
    finish_rows(1)
    for hop in range(3, chips):
        for gather in later:
            gather.hop(hop)
    for gather in gathers:
        gather.finish(False)
    for gather in later:
        gather.finish(True)
    for m in range(MB):
        for slot in range(slots):

            @pl.when(slot_lives(slot, me, devices))
            def _():
                for away in range(1, devices):
                    give(m, away, slot).wait_send()


def heads_backward(
    chips, slots,
    own_ref, qkv_ref, mixed_ref, cos_ref, sin_ref, w_ref, own_mixed_ref, mix_ref, small_ref, hidden_ref,
    normed_ref, up_ref, down_ref, out_ref,
    grad_a_ref, grad_b_ref, weight_outs, w_out_out, small_out, layer_ref, up_out, down_out, job_slots,
    sums_ref, arrived, summed, held, mine, pair, line, layer, d_mixed, probs, raw, parts, d_keys, d_values, pairs, lines,
    part, weight_pair, weight_line, result, normed, normed_sem, mine_sem, local_sem, send_sem, recv_sem, *sems,
):
    devices = 2 * chips
    me = lax.axis_index("exp")
    core = me % 2
    length = SEQ_DEV * devices
    step = BLOCK
    factor = HD ** (-0.5)
    scatters = [
        Scatter(
            chips,
            lambda to, m=m: parts.at[m, 2 * to + 1 - core],
            lambda to, m=m: parts.at[m, 2 * to + core],
            pairs.at[m], lines.at[m], sems[6 * m : 6 * m + 6],
        )
        for m in range(MB)
    ]

    spread = Spread(
        devices, 4, slots,
        lambda owner, k: sums_ref.at[owner + 3 * k],
        lambda k, device: slot_lives(k, device, devices),
        lambda device, k: slot_head(k, device, devices),
        arrived, summed, held, D, sems[6 * MB + 6 : 6 * MB + 13],
    )
    results = Scatter(
        chips,
        lambda to: out_ref.at[1, 2 * to + 1 - core],
        lambda to: mine.at[to],
        pair, line, sems[6 * MB + 13 : 6 * MB + 19],
    )
    result_loads = [
        pltpu.make_async_copy(out_ref.at[1, 2 * to + core], mine.at[to], mine_sem.at[to])
        for to in range(chips)
    ]
    routed = [
        FarSeqSum(source, target, k % 2 == 0, k, job_slots, sems[6 * MB + 19 : -7])
        for k, (source, target) in enumerate(
            (ref.at[e], out.at[e])
            for ref, out in ((up_ref, up_out), (down_ref, down_out))
            for e in range(EXP_DEV)
        )
    ]
    rows = D // devices

    def row_block(device):
        return pl.ds(pl.multiple_of(device * rows, 32), rows)

    weight = Scatter(
        chips,
        lambda to: part.at[row_block(2 * to + 1 - core)],
        lambda to: part.at[row_block(2 * to + core)],
        weight_pair, weight_line, sems[6 * MB : 6 * MB + 6],
    )
    weight_all = SeqAll(sems[-7:])
    far = D + LANES

    def load(number):
        return pltpu.make_async_copy(
            normed_ref.at[:, :, 256 * number : 256 * (number + 1)], normed.at[number % 2],
            normed_sem.at[number % 2],
        )

    def block_at(m, device, slot):
        rows = pl.ds(pl.multiple_of(device * SEQ_DEV, SEQ_DEV), SEQ_DEV)
        return d_mixed.at[m, rows, slot * HD : (slot + 1) * HD]

    def columns(m, head):
        return own_ref.at[m, :, pl.ds(pl.multiple_of(head * HD, HD), HD)]

    def exchange(m, away, slot):
        other = (me + away) % devices
        return pltpu.make_async_remote_copy(
            src_ref=columns(m, slot_head(slot, other, devices)),
            dst_ref=block_at(m, me, slot),
            send_sem=send_sem.at[m, away, slot],
            recv_sem=recv_sem.at[m, away, slot],
            device_id={"exp": other},
            device_id_type=MESH,
        )

    def arrival(m, away, slot):
        block = block_at(m, (me + devices - away) % devices, slot)
        return pltpu.make_async_remote_copy(
            src_ref=block,
            dst_ref=block,
            send_sem=send_sem.at[m, away, slot],
            recv_sem=recv_sem.at[m, away, slot],
            device_id={"exp": (me + away) % devices},
            device_id_type=MESH,
        )

    def keep(m, slot):
        return pltpu.make_async_copy(
            columns(m, slot_head(slot, me, devices)), block_at(m, me, slot), local_sem.at[m, slot]
        )

    meet_all(("seq", "exp"))
    for m in range(MB):
        for away in range(1, devices):
            for slot in range(slots):

                @pl.when(slot_lives(slot, (me + away) % devices, devices))
                def _():
                    exchange(m, away, slot).start()

        for slot in range(slots):

            @pl.when(slot_lives(slot, me, devices))
            def _():
                keep(m, slot).start()

            @pl.when(jnp.logical_not(slot_lives(slot, me, devices)))
            def _():
                d_mixed[m, :, slot * HD : (slot + 1) * HD] = jnp.zeros((length, HD), BF)

    for job in routed:
        job.start()
    for number in range(2):
        load(number).start()
    for copy in result_loads:
        copy.start()
    for left in range(0, D, 256):
        part[left : left + 256, :D] = dot_tn(
            own_mixed_ref[:, left : left + 256], mix_ref[...]
        ).astype(BF)
    part[:, D:] = small_ref[...]
    weight.start()

    def weigh(m):
        for slot in range(slots):
            base = 3 * HD * slot
            for start in range(0, length, step):
                stop = start + step
                scores = visible_scores(
                    qkv_ref[m, start:stop, base : base + HD],
                    qkv_ref[m, :stop, base + HD : base + 2 * HD],
                    start,
                )
                probs[start // step][slot] = softmax_low(scores)

    def body(m, carry):
        weigh(m)
        for number in range(MB):

            @pl.when(m == number)
            def _():
                for slot in range(slots):

                    @pl.when(slot_lives(slot, me, devices))
                    def _():
                        keep(number, slot).wait()
                        for away in range(1, devices):
                            arrival(number, away, slot).wait_recv()

        @pl.when(m == 1)
        def _():
            scatters[0].start()
            weight.slot(0)

        for slot in range(slots):
            base = 3 * HD * slot
            d_keys[...] = jnp.zeros_like(d_keys)
            d_values[...] = jnp.zeros_like(d_values)
            for start in range(0, length, step):
                stop = start + step
                queries = qkv_ref[m, start:stop, base : base + HD]
                keys = qkv_ref[m, :stop, base + HD : base + 2 * HD]
                values = qkv_ref[m, :stop, base + 2 * HD : base + 3 * HD]
                d_mix = d_mixed[m, start:stop, slot * HD : (slot + 1) * HD]
                mixed = mixed_ref[m, start:stop, slot * HD : (slot + 1) * HD]
                row_term = jnp.sum(d_mix.astype(F32) * mixed.astype(F32), axis=1, keepdims=True)
                attention = probs[start // step][slot]
                d_scores = (attention.astype(F32) * (dot_nt(d_mix, values) - row_term)).astype(BF)
                turned = turn(dot(d_scores, keys) * factor, cos_ref[start:stop, :], -sin_ref[start:stop, :])
                raw[m, start:stop, base : base + HD] = turned.astype(BF)
                d_keys[:stop, :] += dot_tn(d_scores, queries)
                d_values[:stop, :] += dot_tn(attention, d_mix)
            turned = turn(d_keys[...] * factor, cos_ref[...], -sin_ref[...])
            raw[m, :, base + HD : base + 2 * HD] = turned.astype(BF)
            raw[m, :, base + 2 * HD : base + 3 * HD] = d_values[...].astype(BF)

            @pl.when(m == 1)
            def _():
                scatters[0].slot(min(slot, chips - 2))
                if slot == 1:
                    routed[0].middle()
                    routed[1].middle()

        for start in range(0, length, step):
            back = dot_nt(raw[m, start : start + step, :], w_ref[...]).astype(BF)
            first = start // SEQ_DEV
            parts[m, first : first + step // SEQ_DEV] = back.reshape(step // SEQ_DEV, SEQ_DEV, D)
        return carry

    lax.fori_loop(0, MB, body, 0)
    scatters[1].start()
    for turn_ in range(min(slots, chips - 1), chips - 1):
        scatters[0].slot(turn_)
    ticks = [lambda t=t: scatters[1].slot(t) for t in range(chips - 1)]
    for number, left in enumerate(range(0, D, 256)):
        load(number).wait()
        total = dot_tn(normed[number % 2, 0], raw[0]) + dot_tn(normed[number % 2, 1], raw[1])
        if number + 2 < D // 256:
            load(number + 2).start()
        for unit in range(3 * slots):
            sums_ref[unit, left : left + 256, :] = total[:, unit * HD : (unit + 1) * HD].astype(BF)
        if number == 1:
            ticks[0]()
    spread.start()
    results.start()
    for turn_ in range(1, chips - 1):
        weight.slot(turn_)
    weight.finish(result)
    weight_all.low[:, :far] = result[...].astype(BF)
    weight_all.low[:, far:] = jnp.zeros((rows, LANES), BF)
    weight_all.start()
    scatters[0].finish(grad_a_ref)
    routed[2].middle()
    routed[3].middle()
    spread.middle()
    ticks[1]()
    weight_all.middle()
    for copy in result_loads:
        copy.wait()
    ticks[2]()
    results.slot(0)
    spread.hand_out()
    routed[0].finish()
    routed[1].finish()
    results.slot(1)
    scatters[1].finish(grad_b_ref)
    results.slot(2)
    routed[2].finish()
    routed[3].finish()
    weight_all.take()
    w_out_out[...] = weight_all.whole[:, :D]
    small_out[...] = weight_all.whole[:, D:far]
    spread.take()
    for kind, target in enumerate(weight_outs):
        target[...] = spread.of_kind(kind)[...]
    results.finish(layer)
    layer_ref[...] = (layer[...] + hidden_ref[...]).astype(BF)
    weight_all.finish()
    spread.finish()
    for m in range(MB):
        for away in range(1, devices):
            for slot in range(slots):

                @pl.when(slot_lives(slot, (me + away) % devices, devices))
                def _():
                    exchange(m, away, slot).wait_send()


def middle_rows(
    back_a_ref, back_b_ref, named_ref, hidden_ref, grad_ref, two_ref, router_ref, gain_ref, w_out_ref,
    grad_hidden_ref, mix_ref, d_mixed_ref, small_ref,
    experts,
):
    size = SEQ_DEV
    lane = lax.broadcasted_iota(jnp.int32, (MB * size, LANES), 1)
    named = named_ref[...].astype(F32)
    logits = jnp.where(named > 0.0, dot(two_ref[...], router_ref[...]), -1e30)
    powers = jnp.where(named > 0.0, jnp.exp(logits - jnp.max(logits, axis=1, keepdims=True)), 0.0)
    gates = powers / jnp.sum(powers, axis=1, keepdims=True)
    tail = jnp.concatenate([back_a_ref[:, D:], back_b_ref[:, D:]], axis=0)
    tail = jnp.where(lane < experts, tail + pltpu.roll(tail, LANES - experts, 1), 0.0)
    grad_logits = gates * (tail - jnp.sum(gates * tail, axis=1, keepdims=True))
    grad_logits = grad_logits.astype(BF)
    grad_two = jnp.concatenate([back_a_ref[:, :D], back_b_ref[:, :D]], axis=0)
    grad_two += dot_nt(grad_logits, router_ref[...])
    back, terms = norm_back(hidden_ref[...], gain_ref[1:2, :], grad_two)
    grad_hidden = grad_ref[...].astype(F32) + back
    grad_hidden_ref[...] = grad_hidden
    mix_ref[...] = grad_hidden.astype(BF)
    d_mixed_ref[...] = dot_nt(mix_ref[...], w_out_ref[...]).astype(BF)
    high = terms.astype(BF)
    low = (terms - high.astype(F32)).astype(BF)
    chosen = jnp.where(lane == experts, 1.0, 0.0).astype(BF)
    total = dot_tn(two_ref[...], grad_logits) + dot_tn(high, chosen) + dot_tn(low, chosen)
    small_ref[...] = total.astype(BF)


def last_rows(
    tokens_ref, normed_a_ref, normed_b_ref, grad_hidden_ref, gain_ref, gain_rows_ref, weight_lows, small_ref, layer_refs,
    shared_lows, gate_ref, up_ref, down_ref, w_refs,
    grad_tokens_ref, weight_outs, router_ref, gain_one_ref, gain_two_ref, layer_out, shared_outs, gate_out, up_out, down_out,
    w_rows, w_sem,
    experts,
):
    rows = D // lax.axis_size("exp")
    start = pl.ds(pl.multiple_of(lax.axis_index("exp") * rows, 32), rows)
    loads = [
        pltpu.make_async_copy(w_refs[k].at[start], w_rows.at[k], w_sem.at[k]) for k in range(3)
    ]
    for copy in loads:
        copy.start()
    for low, out in zip(shared_lows, shared_outs):
        out[...] = low[...].astype(F32)
    gate_out[...] = gate_ref[...].astype(F32)
    down_out[...] = down_ref[...].astype(F32)
    up_out[...] = up_ref[...].astype(F32)
    for m in range(MB):
        layer_out[m] = layer_refs[m][...]
    for m, normed_ref in enumerate((normed_a_ref, normed_b_ref)):
        part = slice(m * SEQ_DEV, (m + 1) * SEQ_DEV)
        back, _ = norm_back(tokens_ref[part, :].astype(F32), gain_ref[0:1, :], normed_ref[...])
        grad_tokens_ref[part, :] = (grad_hidden_ref[part, :] + back).astype(BF)
    product = jnp.zeros((rows, D), F32)
    for k, (low, out) in enumerate(zip(weight_lows, weight_outs)):
        grad = low[...].astype(F32)
        out[...] = grad
        if k < 3:
            loads[k].wait()
            product += w_rows[k].astype(F32) * grad
    ones = jnp.ones((8, D), BF)
    high = product.astype(BF)
    low = (product - high.astype(F32)).astype(BF)
    gain_one_ref[...] = (dot_nt(ones, high) + dot_nt(ones, low))[0:1, :] / gain_rows_ref[...]
    small = small_ref[...]
    router_ref[...] = small[:, :experts].astype(F32)
    column = lax.broadcasted_iota(jnp.int32, (8, LANES), 1)
    gain_two_ref[...] = dot_nt(jnp.where(column == experts, 1.0, 0.0).astype(BF), small)[0:1, :]


def taking(us):
    return pl.CostEstimate(flops=int(us * 1.0e9), bytes_accessed=2**20, transcendentals=0)


def like(*shape, dtype=BF):
    return jax.ShapeDtypeStruct(shape, dtype)


IN_VMEM = pl.BlockSpec(memory_space=pltpu.VMEM)
ANYWHERE = pl.BlockSpec(memory_space=pl.ANY)


def experts_on_lines(two_own, hidden_one, grad_own, grad_a, named, experts, router, owners, routed, shared):
    devices = lax.axis_size("exp")
    chips = devices // 2
    length = SEQ_DEV * devices
    wide = EXP_DEV * FF + LANES
    block_back = (devices, SEQ_DEV, D + LANES)
    sems = [gather_sems(chips)] * MB + [scatter_sems(chips), gather_sems(chips)]

    def call_rows(*operands):
        def kernel(own_ref, grad_own_ref, grad_ref, named_ref, router_ref, owner_ref, *refs):
            expert_rows(
                chips, experts, own_ref, grad_own_ref, grad_ref, named_ref, router_ref, owner_ref,
                refs[:3], refs[3:6], *refs[6:],
            )

        return pl.pallas_call(
            kernel,
            out_shape=(
                like(MB, devices, SEQ_DEV, D),
                like(MB, devices, SEQ_DEV, D),
                like(MB * length, wide),
                like(MB * length, wide),
                like(MB * length, wide),
                like(MB, devices, SEQ_DEV, D),
                like(*block_back),
                like(SEQ_DEV, D + LANES, dtype=F32),
            ),
            in_specs=[IN_VMEM, ANYWHERE, ANYWHERE] + [IN_VMEM] * 3 + [ANYWHERE] * 6,
            out_specs=(ANYWHERE,) * 7 + (IN_VMEM,),
            scratch_shapes=[
                pltpu.VMEM((3, D, wide), BF),
                pltpu.VMEM((MB, devices, SEQ_DEV, D), BF),
                pltpu.VMEM((MB, devices, SEQ_DEV, D), BF),
                pltpu.VMEM((2, 3, 2 * SEQ_DEV, wide), BF),
                pltpu.VMEM((2, 2, SEQ_DEV, D), BF),
                pltpu.VMEM((MB, *block_back), BF),
                pltpu.VMEM((chips, SEQ_DEV, D + LANES), BF),
                pltpu.VMEM((chips + 1, SEQ_DEV, D + LANES), BF),
                pltpu.SemaphoreType.DMA((3, EXP_DEV + 1)),
                pltpu.SemaphoreType.DMA((4,)),
                pltpu.SemaphoreType.DMA((2, 3)),
                pltpu.SemaphoreType.DMA((4, chips)),
            ]
            + [sem for group in sems for sem in group],
            compiler_params=pltpu.CompilerParams(
                collective_id=1, has_side_effects=True, vmem_limit_bytes=VMEM_BYTES
            ),
            cost_estimate=taking(100),
            name="expert_rows",
        )(*operands)

    rows, grads, hidden, d_gate, d_up, out_parts, back_b, back_sum_a = call_rows(
        two_own, grad_own, grad_a, named, router, owners, *routed, *shared
    )
    flat = MB * length


    def call_sums(*operands):
        def kernel(*refs):
            expert_sums(chips, *refs[:16], refs[16:19], *refs[19:])

        half = D // 2
        by_rows = pl.BlockSpec((flat, half), lambda k, d: (0, d))
        by_grads = pl.BlockSpec((flat, half), lambda k, d: (0, d))

        def for_gate(k, d):
            return (0, (k + 4) // 5)

        def for_up(k, d):
            return (0, k // 3)

        def for_down(k, d):
            return (0, k // 5)

        last = pl.BlockSpec(
            (flat, LANES), lambda k, d: (0, EXP_DEV * FF // LANES), pipeline_mode=pl.Buffered(1)
        )

        def whole(*shape):
            return pl.BlockSpec(shape, lambda k, d: (0,) * len(shape))

        return pl.pallas_call(
            kernel,
            grid=(3 * EXP_DEV, 2),
            out_shape=(like(EXP_DEV, D, FF),) * 3
            + (like(SEQ_DEV, D + LANES, dtype=F32), like(SEQ_DEV, D))
            + (like(D // devices, FF),) * 3
            + (like(EXP_DEV, D // 4, FF),),
            in_specs=[by_rows, by_grads]
            + [pl.BlockSpec((flat, FF), for_down, pipeline_mode=pl.Buffered(1))]
            + [pl.BlockSpec((flat, FF), use) for use in (for_gate, for_up)]
            + [last] * 3
            + [ANYWHERE] * 2
            + [pl.BlockSpec((SEQ_DEV, D), lambda k, d: (0, 0), pipeline_mode=pl.Buffered(1))],
            out_specs=(ANYWHERE,) * 3
            + (whole(SEQ_DEV, D + LANES), whole(SEQ_DEV, D))
            + (whole(D // devices, FF),) * 3
            + (ANYWHERE,),
            scratch_shapes=[
                pltpu.VMEM((chips, SEQ_DEV, D + LANES), BF),
                pltpu.VMEM((chips, SEQ_DEV, D + LANES), BF),
                pltpu.VMEM((chips + 1, SEQ_DEV, D + LANES), BF),
                pltpu.VMEM((chips, SEQ_DEV, D), BF),
                pltpu.VMEM((chips, SEQ_DEV, D), BF),
                pltpu.VMEM((chips + 1, SEQ_DEV, D), BF),
                pltpu.VMEM((SEQ_DEV, D), F32),
                pltpu.SemaphoreType.DMA((2, chips)),
                pltpu.VMEM((2, half, FF), BF),
                pltpu.SemaphoreType.DMA((2,)),
                pltpu.VMEM((3, D, HD), BF),
                pltpu.VMEM((3, 1, D, HD), BF),
                pltpu.VMEM((1, D, HD), BF),
                pltpu.VMEM((4, D // devices, FF), BF),
            ]
            + scatter_sems(chips)
            + spread_sems(devices, 4, 1)
            + scatter_sems(chips)
            + seq_scratch(2),
            compiler_params=pltpu.CompilerParams(
                collective_id=2, has_side_effects=True, vmem_limit_bytes=VMEM_BYTES
            ),
            cost_estimate=taking(60),
            name="expert_sums",
        )(*operands)

    gate_sum, up_sum, down_sum, back_sum_b, layer_a, *shared_grads, gate_rows = call_sums(
        rows.reshape(flat, D), grads.reshape(flat, D), hidden, d_gate, d_up, hidden, d_gate, d_up, back_b,
        out_parts, hidden_one[0],
    )
    backs = (back_sum_a, back_sum_b)
    return (
        layer_a,
        out_parts,
        backs,
        gate_rows,
        (gate_sum, up_sum, down_sum),
        shared_grads,
    )


def named_softmax(logits, named):
    chosen = jnp.where(named, logits, -jnp.inf)
    powers = jnp.where(named, jnp.exp(chosen - jnp.max(chosen, axis=-1, keepdims=True)), 0.0)
    return powers / jnp.sum(powers, axis=-1, keepdims=True)


def on_device_plain(
    tokens,
    cotangent,
    expert_ids,
    owner_table,
    w_query,
    w_key,
    w_value,
    w_out,
    gain_one,
    gain_two,
    w_router,
    shared_gate,
    shared_up,
    shared_down,
    routed_gate,
    routed_up,
    routed_down,
):
    devices = lax.axis_size("exp")
    groups = lax.axis_size("seq")
    me = lax.axis_index("exp")
    experts = owner_table.shape[0]
    length = SEQ_DEV * devices
    rows_out = D // devices
    slots = -(-HEADS // devices)
    wide = slots * HD
    share = FF // devices
    used = EXP_DEV * FF + share
    padded = -(-used // LANES) * LANES

    head_of = [jnp.minimum(me + slot * devices, HEADS - 1) for slot in range(slots)]
    slot_live = jnp.concatenate(
        [
            jnp.full((HD,), jnp.where(me + slot * devices < HEADS, 1.0, 0.0), F32)
            for slot in range(slots)
        ]
    )

    w_qkv = jnp.concatenate(
        [
            lax.dynamic_slice(weight, (0, head * HD), (D, HD))
            for head in head_of
            for weight in (w_query, w_key, w_value)
        ],
        axis=1,
    )
    w_out_heads = jnp.concatenate(
        [lax.dynamic_slice(w_out, (head * HD, 0), (HD, D)) for head in head_of], axis=0
    )
    cos_table, sin_table = angle_tables(jnp.arange(length).astype(F32))
    sin_table = jnp.where(jnp.arange(HD) < HD // 2, -sin_table, sin_table)
    params = pltpu.CompilerParams(vmem_limit_bytes=VMEM_BYTES)

    forward = pl.pallas_call(
        functools.partial(attend_forward, slots),
        out_shape=(
            like(length, D),
            like(length, 3 * wide),
            like(length, wide),
            like(slots, length, 1, dtype=F32),
        ),
        in_specs=[IN_VMEM] * 5,
        out_specs=(IN_VMEM,) * 4,
        compiler_params=params,
        name="attend_forward",
    )
    backward = pl.pallas_call(
        functools.partial(attend_backward, slots),
        out_shape=(like(wide, D, dtype=F32), like(D, 3 * wide, dtype=F32), like(length, D)),
        in_specs=[IN_VMEM] * 10,
        out_specs=(IN_VMEM,) * 3,
        scratch_shapes=[
            pltpu.VMEM((length, 3 * wide), BF),
            pltpu.VMEM((length, wide), BF),
            pltpu.VMEM((length, HD), F32),
            pltpu.VMEM((length, HD), F32),
        ],
        compiler_params=params,
        name="attend_backward",
    )

    def joined(routed, shared):
        own = lax.dynamic_slice(shared, (0, me * share), (D, share))
        blank = jnp.zeros((D, padded - used), BF)
        return jnp.concatenate([routed[i] for i in range(EXP_DEV)] + [own, blank], axis=1)

    gate_all = joined(routed_gate, shared_gate)
    up_all = joined(routed_up, shared_up)
    down_all = joined(routed_down, shared_down)

    expert_at = jnp.sum(
        (owner_table[:, None] == jnp.arange(experts)[None, :]) * jnp.arange(experts)[:, None],
        axis=0,
    )
    router_rows = jnp.take(w_router, expert_at, axis=1)
    ids_all = lax.all_gather(expert_ids[:, 0], "exp", axis=1, tiled=True)

    first = []
    for micro_batch in range(MB):
        rows_all = gather_exp(tokens[micro_batch, 0])
        normed, qkv, mixed, lse = forward(rows_all, gain_one[None], cos_table, sin_table, w_qkv)
        sent = lax.all_to_all(
            mixed.reshape(devices, SEQ_DEV, wide), "exp", split_axis=0, concat_axis=0, tiled=True
        )
        own_mixed = (
            sent.reshape(devices, SEQ_DEV, slots, HD)
            .transpose(1, 2, 0, 3)
            .reshape(SEQ_DEV, slots * devices * HD)[:, :D]
        )
        rows_in = tokens[micro_batch, 0].astype(F32)
        hidden_one = rows_in + dot(own_mixed, w_out)
        two_low = norm_rows(hidden_one, gain_two).astype(BF)
        two_all = gather_exp(two_low)
        grad_all = gather_exp(cotangent[micro_batch, 0])
        first.append(
            (normed, qkv, mixed, lse, rows_in, hidden_one, two_all, grad_all)
        )

    column = jnp.arange(padded)
    second = []
    for micro_batch in range(MB):
        two_all, grad_all = first[micro_batch][6:]
        logits = dot(two_all, router_rows)
        named = jnp.any(ids_all[micro_batch][:, :, None] == expert_at[None, None, :], axis=1)
        chosen = jnp.where(named, logits, -jnp.inf)
        powers = jnp.where(named, jnp.exp(chosen - jnp.max(chosen, axis=-1, keepdims=True)), 0.0)
        gates = powers / jnp.sum(powers, axis=-1, keepdims=True)
        own_gates = lax.dynamic_slice(gates, (0, me * EXP_DEV), (length, EXP_DEV))
        weight = jnp.where(
            column[None, :] < FF,
            own_gates[:, :1],
            jnp.where(column[None, :] < 2 * FF, own_gates[:, 1:], 1.0),
        )
        gate_part = dot(two_all, gate_all)
        up_part = dot(two_all, up_all)
        down_part = dot(grad_all, down_all)
        sigmoid = jax.nn.sigmoid(gate_part)
        act = gate_part * sigmoid
        hidden = act * up_part
        products = hidden * down_part
        own_grads = jnp.stack(
            [jnp.sum(products[:, i * FF : (i + 1) * FF], axis=1) for i in range(EXP_DEV)], axis=1
        )
        hidden_low = (weight * hidden).astype(BF)
        weighted = weight * down_part
        d_gate = (weighted * up_part * (sigmoid + act * (1.0 - sigmoid))).astype(BF)
        d_up = (weighted * act).astype(BF)
        out_part = scatter_exp(dot_nt(hidden_low, down_all))
        back_part = scatter_exp(dot_nt(d_gate, gate_all) + dot_nt(d_up, up_all))
        gate_grads = lax.all_gather(own_grads, "exp", axis=1, tiled=True)
        grad_logits = (
            gates * (gate_grads - jnp.sum(gates * gate_grads, axis=-1, keepdims=True))
        ).astype(BF)
        second.append((hidden_low, d_gate, d_up, out_part, back_part, grad_logits))

    two_both = jnp.concatenate([f[6] for f in first])
    grad_both = jnp.concatenate([f[7] for f in first])
    gate_sum = dot_tn(two_both, jnp.concatenate([s[1] for s in second]))
    up_sum = dot_tn(two_both, jnp.concatenate([s[2] for s in second]))
    down_sum = dot_tn(grad_both, jnp.concatenate([s[0] for s in second]))

    def routed_sum(total):
        parts = jnp.stack([total[:, i * FF : (i + 1) * FF] for i in range(EXP_DEV)])
        return lax.psum_scatter(
            parts.astype(BF), "seq", scatter_dimension=1, tiled=True
        ).astype(F32)

    def shared_part(total):
        return total[:, EXP_DEV * FF : used]

    outputs_list = []
    grads_list = []
    small = jnp.zeros((D, experts + 2), F32)
    qkv_sum = jnp.zeros((D, 3 * wide), F32)
    out_sum = jnp.zeros((wide, D), F32)
    for micro_batch in range(MB):
        normed, qkv, mixed, lse, rows_in, hidden_one, two_all, _ = first[micro_batch]
        _, _, _, out_part, back_part, grad_logits = second[micro_batch]
        outputs_list.append((hidden_one + out_part).astype(BF))
        own_logits = lax.dynamic_slice(grad_logits, (me * SEQ_DEV, 0), (SEQ_DEV, experts))
        grad_two = back_part + dot_nt(own_logits, router_rows)
        back, gain_terms = norm_back(hidden_one, gain_two, grad_two)
        grad_hidden = cotangent[micro_batch, 0].astype(F32) + back
        own_two = lax.dynamic_slice(two_all, (me * SEQ_DEV, 0), (SEQ_DEV, D))
        router_part = dot_tn(own_two, own_logits)
        mix_all = gather_exp(grad_hidden.astype(BF))
        out_one, qkv_one, grad_part = backward(
            mix_all, normed, qkv, mixed, lse, cos_table, sin_table, w_qkv, w_out_heads, slot_live[None]
        )
        out_sum = out_sum + out_one
        qkv_sum = qkv_sum + qkv_one
        grad_normed = scatter_exp(grad_part)
        back_one, gain_one_terms = norm_back(rows_in, gain_one, grad_normed)
        grads_list.append((grad_hidden + back_one).astype(BF))
        small = small + jnp.concatenate(
            [
                router_part,
                jnp.sum(gain_one_terms, axis=0)[:, None],
                jnp.sum(gain_terms, axis=0)[:, None],
            ],
            axis=1,
        )

    def to_rows(columns):
        parts = columns.astype(BF).reshape(devices, rows_out, columns.shape[1])
        parts = lax.psum_scatter(parts, "seq", scatter_dimension=1, tiled=True)
        return lax.all_to_all(parts, "exp", split_axis=0, concat_axis=0, tiled=True)

    def to_all(rows):
        return lax.all_gather(rows, "seq", axis=0, tiled=True).astype(F32)

    piece = rows_out // groups
    shared_cols = jnp.concatenate([shared_part(t) for t in (gate_sum, up_sum, down_sum)], axis=1)
    shared_rows = to_rows(shared_cols).reshape(devices, piece, 3, share)
    shared_full = to_all(shared_rows.transpose(1, 2, 0, 3).reshape(piece, 3 * FF))
    qkv_rows = to_rows(qkv_sum).reshape(devices, piece, slots, 3, HD)
    qkv_rows = qkv_rows.transpose(1, 3, 2, 0, 4).reshape(piece, 3, slots * devices * HD)
    qkv_full = to_all(qkv_rows[:, :, :D].reshape(piece, 3 * D))
    out_part = lax.psum_scatter(out_sum.astype(BF), "seq", scatter_dimension=1, tiled=True)
    spread = jnp.zeros((slots * devices * HD, D // groups), BF)
    for slot in range(slots):
        spread = lax.dynamic_update_slice(
            spread, out_part[slot * HD : (slot + 1) * HD], ((me + slot * devices) * HD, 0)
        )
    out_rows = lax.psum_scatter(spread[:D], "exp", scatter_dimension=0, tiled=True)
    out_full = lax.all_gather(out_rows, "seq", axis=1, tiled=True).astype(F32)
    small_rows = lax.psum_scatter(
        lax.psum(small, "seq"), "exp", scatter_dimension=0, tiled=True
    )
    place_of = jnp.take(small_rows, owner_table, axis=1)
    return (
        jnp.stack(outputs_list)[:, None],
        jnp.stack(grads_list)[:, None],
        qkv_full[:, :D],
        qkv_full[:, D : 2 * D],
        qkv_full[:, 2 * D :],
        out_full,
        small_rows[:, experts],
        small_rows[:, experts + 1],
        place_of,
        shared_full[:, :FF],
        shared_full[:, FF : 2 * FF],
        shared_full[:, 2 * FF :],
        routed_sum(gate_sum),
        routed_sum(up_sum),
        routed_sum(down_sum),
    )


def on_device_lines(
    tokens,
    cotangent,
    expert_ids,
    owner_table,
    w_query,
    w_key,
    w_value,
    w_out,
    gain_one,
    gain_two,
    w_router,
    shared_gate,
    shared_up,
    shared_down,
    routed_gate,
    routed_up,
    routed_down,
):
    devices = lax.axis_size("exp")
    groups = lax.axis_size("seq")
    me = lax.axis_index("exp")
    chips = devices // 2
    experts = owner_table.shape[0]
    length = SEQ_DEV * devices
    rows_out = D // devices
    slots = -(-HEADS // devices)
    wide = slots * HD
    own = MB * SEQ_DEV

    cos_table, sin_table = turn_tables(length)

    router = jnp.pad(w_router, ((0, 0), (0, LANES - experts)))
    owners = jnp.pad(owner_table, (0, LANES - experts), constant_values=-1)[None]
    gains = jnp.stack([gain_one, gain_two])
    named_own = jnp.any(
        expert_ids.reshape(own, TOP)[:, :, None] == jnp.arange(LANES)[None, None, :], axis=1
    ).astype(BF)
    tokens_own = tokens.reshape(MB, SEQ_DEV, D)
    grad_own = cotangent.reshape(MB, SEQ_DEV, D)

    def call_forward(*operands):
        def kernel(*refs):
            heads_forward(chips, slots, *refs[:6], refs[6:9], *refs[9:])

        return pl.pallas_call(
            kernel,
            out_shape=(
                like(MB, length, D),
                like(MB, length, 3 * wide),
                like(MB, length, wide),
                like(MB, SEQ_DEV, D),
                like(MB, SEQ_DEV, D, dtype=F32),
                like(MB, SEQ_DEV, D),
                like(D, 3 * wide),
                like(devices, SEQ_DEV, D),
                like(devices, own, LANES),
            ),
            in_specs=[IN_VMEM, ANYWHERE] + [IN_VMEM] * 4 + [ANYWHERE] * 3 + [IN_VMEM],
            out_specs=(IN_VMEM,) * 7 + (ANYWHERE, IN_VMEM),
            scratch_shapes=[
                pltpu.VMEM((MB, devices, SEQ_DEV, D), BF),
                pltpu.SemaphoreType.DMA((3 * slots,)),
                pltpu.SemaphoreType.DMA((4,)),
                pltpu.SemaphoreType.DMA((MB, devices, slots)),
                pltpu.SemaphoreType.DMA((MB, devices, slots)),
            ]
            + gather_sems(chips) * 4,
            compiler_params=pltpu.CompilerParams(
                collective_id=5, has_side_effects=True, vmem_limit_bytes=VMEM_BYTES
            ),
            cost_estimate=taking(70),
            name="heads_forward",
        )(*operands)

    normed, qkv, mixed, own_mixed, hidden_one, two_low, w_qkv, grad_a, named_all = call_forward(
        tokens_own, grad_own, named_own, gains, cos_table, sin_table,
        w_query, w_key, w_value, w_out,
    )
    hidden_rows = hidden_one
    own_mixed, hidden_one = own_mixed.reshape(own, D), hidden_one.reshape(own, D)
    two_low = two_low.reshape(own, D)

    layer_a, out_parts, backs, gate_full, routed_sums, shared_lows = experts_on_lines(
        two_low.reshape(MB, SEQ_DEV, D),
        hidden_rows,
        grad_own,
        grad_a,
        named_all.reshape(devices, MB * SEQ_DEV, LANES),
        experts,
        router,
        owners,
        (routed_gate, routed_up, routed_down),
        (shared_gate, shared_up, shared_down),
    )
    def call_middle(*operands):
        def kernel(*refs):
            middle_rows(*refs, experts)

        return pl.pallas_call(
            kernel,
            out_shape=(like(own, D, dtype=F32), like(own, D), like(own, D), like(D, LANES)),
            in_specs=[IN_VMEM] * 9,
            out_specs=(IN_VMEM,) * 4,
            compiler_params=pltpu.CompilerParams(vmem_limit_bytes=VMEM_BYTES),
            cost_estimate=taking(5),
            name="middle_rows",
        )(*operands)

    grad_hidden, grad_mix, d_mixed, small = call_middle(
        *backs, named_own, hidden_one, cotangent.reshape(own, D), two_low, router, gains, w_out
    )
    quarter = like(EXP_DEV, D // groups, FF)
    far = D + LANES
    jobs = 4
    slot_shape = (jobs, 2, D // groups, FF)

    def backward_kernel(*refs):
        heads_backward(
            chips, slots, *refs[:16], refs[16:19], *refs[19:24], refs[24:27], *refs[27:36],
            refs[36 : 36 + length // BLOCK], *refs[36 + length // BLOCK :],
        )

    normed_a, normed_b, *backward_out = pl.pallas_call(
        backward_kernel,
        out_shape=(like(SEQ_DEV, D, dtype=F32),) * 2
        + (like(rows_out, D),) * 4
        + (like(rows_out, LANES), like(SEQ_DEV, D), quarter, quarter)
        + (like(*slot_shape), like(*slot_shape), like(jobs, D // groups, FF)),
        in_specs=[IN_VMEM] * 10 + [ANYWHERE] * 4,
        out_specs=(IN_VMEM,) * 8 + (ANYWHERE,) * 5,
        scratch_shapes=[
            pltpu.VMEM((3 * slots, D, HD), BF),
            pltpu.VMEM((groups - 1, slots, D, HD), BF),
            pltpu.VMEM((slots, D, HD), BF),
            pltpu.VMEM((groups, rows_out, D), BF),
            pltpu.VMEM((chips, SEQ_DEV, D), BF),
            pltpu.VMEM((chips, SEQ_DEV, D), BF),
            pltpu.VMEM((chips + 1, SEQ_DEV, D), BF),
            pltpu.VMEM((SEQ_DEV, D), F32),
            pltpu.VMEM((MB, length, wide), BF),
        ]
        + [pltpu.VMEM((slots, BLOCK, stop), BF) for stop in range(BLOCK, length + 1, BLOCK)]
        + [
            pltpu.VMEM((MB, length, 3 * wide), BF),
            pltpu.VMEM((MB, devices, SEQ_DEV, D), BF),
            pltpu.VMEM((length, HD), F32),
            pltpu.VMEM((length, HD), F32),
            pltpu.VMEM((MB, chips, SEQ_DEV, D), BF),
            pltpu.VMEM((MB, chips + 1, SEQ_DEV, D), BF),
            pltpu.VMEM((D, far), BF),
            pltpu.VMEM((chips, rows_out, far), BF),
            pltpu.VMEM((chips + 1, rows_out, far), BF),
            pltpu.VMEM((rows_out, far), F32),
            pltpu.VMEM((2, MB, length, 256), BF),
            pltpu.SemaphoreType.DMA((2,)),
            pltpu.SemaphoreType.DMA((chips,)),
            pltpu.SemaphoreType.DMA((MB, slots)),
            pltpu.SemaphoreType.DMA((MB, devices, slots)),
            pltpu.SemaphoreType.DMA((MB, devices, slots)),
        ]
        + scatter_sems(chips) * (MB + 1)
        + spread_sems(devices, groups, slots)
        + scatter_sems(chips)
        + far_sum_scratch(jobs)
        + seq_all_scratch(rows_out, (far + LANES) // groups),
        compiler_params=pltpu.CompilerParams(
            collective_id=3, has_side_effects=True, vmem_limit_bytes=VMEM_BYTES
        ),
        cost_estimate=taking(140),
        name="heads_backward",
    )(
        d_mixed.reshape(MB, SEQ_DEV, D), qkv, mixed, cos_table, sin_table, w_qkv, own_mixed,
        grad_mix, small, hidden_rows[1], normed, *routed_sums[1:], out_parts,
    )
    gain_rows = lax.dynamic_slice(gain_one, (me * rows_out,), (rows_out,))[None]

    def call_last(*operands):
        def kernel(*refs):
            last_rows(
                *refs[:6], refs[6:10], refs[10], refs[11:13], refs[13:16], *refs[16:19],
                refs[19:22], refs[22], refs[23:27], *refs[27:31], refs[31:34], *refs[34:], experts,
            )

        full = like(EXP_DEV, D // groups, FF, dtype=F32)
        return pl.pallas_call(
            kernel,
            out_shape=(like(own, D),)
            + (like(rows_out, D, dtype=F32),) * 4
            + (like(rows_out, experts, dtype=F32),)
            + (like(1, rows_out, dtype=F32),) * 2
            + (like(MB, SEQ_DEV, D),)
            + (like(rows_out, FF, dtype=F32),) * 3
            + (full,) * 3,
            in_specs=[IN_VMEM] * 19 + [ANYWHERE] * 3,
            out_specs=(IN_VMEM,) * 15,
            scratch_shapes=[pltpu.VMEM((3, rows_out, D), BF), pltpu.SemaphoreType.DMA((3,))],
            compiler_params=pltpu.CompilerParams(vmem_limit_bytes=VMEM_BYTES),
            cost_estimate=taking(6),
            name="last_rows",
        )(*operands)

    last_out = call_last(
        tokens.reshape(own, D), normed_a, normed_b, grad_hidden, gains, gain_rows,
        *backward_out[:5], layer_a, backward_out[5], *shared_lows, gate_full, *backward_out[6:8],
        w_query, w_key, w_value,
    )
    grad_tokens, attn, router_grad = last_out[0], last_out[1:5], last_out[5]
    gain_one_grad, gain_two_grad, layer_out = last_out[6:9]
    far_grads = last_out[9:]
    whole = (MB, 1, SEQ_DEV, D)
    return (
        layer_out.reshape(whole),
        grad_tokens.reshape(whole),
        *attn,
        gain_one_grad[0],
        gain_two_grad[0],
        router_grad,
        *far_grads,
    )


def solution(mesh):
    rows = P(None, "seq", "exp", None)
    placed = (rows,) * 3 + (P(),) * 11 + (P("exp", None, None),) * 3
    wide = P("exp", None)
    on_lines = mesh.shape["exp"] == 8 and mesh.shape["seq"] == 4
    on_device = on_device_lines if on_lines else on_device_plain
    return jax.shard_map(
        on_device,
        mesh=mesh,
        in_specs=placed,
        out_specs=(rows, rows, wide, wide, wide, wide, P("exp"), P("exp"))
        + (wide,) * 4
        + (P("exp", "seq", None),) * 3,
        check_vma=False,
    )
```

```python
import functools
import math

import jax
import jax.numpy as jnp
import numpy as np
from jax import lax
from jax.experimental import pallas as pl
from jax.experimental.pallas import tpu as pltpu
from jax.sharding import PartitionSpec as P

D = 1280
HEADS = 10
HD = 128
FF = 896
TOP = 7
EXP_DEV = 2
MB = 2
SEQ_DEV = 128
LANES = 128
BLOCK = 256
VMEM_BYTES = 62 * 2**20

eps = 1e-06
BF = jnp.bfloat16
F32 = jnp.float32


def norm_rows(inputs, gain):
    return inputs * lax.rsqrt(jnp.mean(inputs * inputs, axis=-1, keepdims=True) + eps) * gain


def norm_back(inputs, gain, grad):
    scale = lax.rsqrt(jnp.mean(inputs * inputs, axis=-1, keepdims=True) + eps)
    unit = inputs * scale
    weighted = grad * gain
    back = scale * (weighted - unit * jnp.mean(weighted * unit, axis=-1, keepdims=True))
    return back, grad * unit


def angle_tables(positions):
    steps_half = jnp.arange(HD // 2).astype(positions.dtype)
    frequency = jnp.exp(steps_half * (-2.0 * math.log(10000.0) / HD))
    angles = positions[:, None] * frequency[None, :]
    angles = jnp.concatenate([angles, angles], axis=-1)
    return (jnp.cos(angles), jnp.sin(angles))


def turn_tables(length):
    angles = np.arange(length)[:, None] * 10000.0 ** (-2.0 * np.arange(HD // 2) / HD)
    cos, sin = np.cos(angles), np.sin(angles)
    return (
        jnp.asarray(np.concatenate([cos, cos], axis=1), F32),
        jnp.asarray(np.concatenate([-sin, sin], axis=1), F32),
    )


def dot(a, b):
    return jnp.dot(a, b, preferred_element_type=F32)


def dot_nt(a, b):
    return lax.dot_general(a, b, (((1,), (1,)), ((), ())), preferred_element_type=F32)


def dot_tn(a, b):
    return lax.dot_general(a, b, (((0,), (0,)), ((), ())), preferred_element_type=F32)


def gather_exp(array):
    return lax.all_gather(array, "exp", axis=0, tiled=True)


def scatter_exp(array):
    return lax.psum_scatter(array.astype(BF), "exp", scatter_dimension=0, tiled=True).astype(F32)


def turn(heads, cos_table, sin_table):
    return heads * cos_table + pltpu.roll(heads, HD // 2, 1) * sin_table


def visible_scores(queries, keys, start):
    scores = dot_nt(queries, keys) * HD ** (-0.5)
    rows = queries.shape[0]
    row = lax.broadcasted_iota(jnp.int32, (rows, rows), 0)
    column = lax.broadcasted_iota(jnp.int32, (rows, rows), 1)
    last = jnp.where(row >= column, scores[:, start:], -1e30)
    return last if start == 0 else jnp.concatenate([scores[:, :start], last], axis=1)


def attend_forward(slots, rows_ref, gain_ref, cos_ref, sin_ref, w_ref, normed_ref, qkv_ref, mixed_ref, lse_ref):
    length = rows_ref.shape[0]
    step = BLOCK if length <= 2048 else BLOCK // 2

    def project(i, carry):
        part = pl.ds(pl.multiple_of(i * step, step), step)
        normed = norm_rows(rows_ref[part, :].astype(F32), gain_ref[...]).astype(BF)
        normed_ref[part, :] = normed
        for slot in range(slots):
            base = 3 * HD * slot
            qkv = dot(normed, w_ref[:, base : base + 3 * HD])
            for j in range(2):
                turned = turn(qkv[:, j * HD : (j + 1) * HD], cos_ref[part, :], sin_ref[part, :])
                qkv_ref[part, base + j * HD : base + (j + 1) * HD] = turned.astype(BF)
            qkv_ref[part, base + 2 * HD : base + 3 * HD] = qkv[:, 2 * HD :].astype(BF)
        return carry

    lax.fori_loop(0, length // step, project, 0)
    for slot in range(slots):
        base = 3 * HD * slot
        for start in range(0, length, step):
            stop = start + step
            scores = visible_scores(
                qkv_ref[start:stop, base : base + HD], qkv_ref[:stop, base + HD : base + 2 * HD], start
            )
            largest = jnp.max(scores, axis=-1, keepdims=True)
            powers = jnp.exp(scores - largest)
            total = jnp.sum(powers, axis=-1, keepdims=True)
            attention = (powers * (1.0 / total)).astype(BF)
            mixed = dot(attention, qkv_ref[:stop, base + 2 * HD : base + 3 * HD])
            mixed_ref[start:stop, slot * HD : (slot + 1) * HD] = mixed.astype(BF)
            lse_ref[slot, start:stop, :] = largest + jnp.log(total)


def attend_backward(
    slots, mix_ref, normed_ref, qkv_ref, mixed_ref, lse_ref, cos_ref, sin_ref, w_ref, w_out_ref, live_ref,
    out_sum_ref, qkv_sum_ref, grad_ref, raw_ref, d_mixed_ref, d_keys_ref, d_values_ref,
):
    length = mix_ref.shape[0]
    step = BLOCK if length <= 2048 else BLOCK // 2
    factor = HD ** (-0.5)

    def project(i, carry):
        part = pl.ds(pl.multiple_of(i * step, step), step)
        d_mixed_ref[part, :] = (dot_nt(mix_ref[part, :], w_out_ref[...]) * live_ref[...]).astype(BF)
        return carry

    lax.fori_loop(0, length // step, project, 0)
    for slot in range(slots):
        base = 3 * HD * slot
        d_keys_ref[...] = jnp.zeros_like(d_keys_ref)
        d_values_ref[...] = jnp.zeros_like(d_values_ref)
        for start in range(0, length, step):
            stop = start + step
            queries = qkv_ref[start:stop, base : base + HD]
            keys = qkv_ref[:stop, base + HD : base + 2 * HD]
            values = qkv_ref[:stop, base + 2 * HD : base + 3 * HD]
            d_mixed = d_mixed_ref[start:stop, slot * HD : (slot + 1) * HD]
            attention = jnp.exp(visible_scores(queries, keys, start) - lse_ref[slot, start:stop, :])
            d_att = dot_nt(d_mixed, values)
            row_term = jnp.sum(attention * d_att, axis=-1, keepdims=True)
            d_scores = (attention * (d_att - row_term)).astype(BF)
            d_queries = dot(d_scores, keys) * factor
            raw = turn(d_queries, cos_ref[start:stop, :], -sin_ref[start:stop, :])
            raw_ref[start:stop, base : base + HD] = raw.astype(BF)
            d_keys_ref[:stop, :] += dot_tn(d_scores, queries)
            d_values_ref[:stop, :] += dot_tn(attention.astype(BF), d_mixed)
        raw = turn(d_keys_ref[...] * factor, cos_ref[...], -sin_ref[...])
        raw_ref[:, base + HD : base + 2 * HD] = raw.astype(BF)
        raw_ref[:, base + 2 * HD : base + 3 * HD] = d_values_ref[...].astype(BF)

    def give(i, carry):
        part = pl.ds(pl.multiple_of(i * step, step), step)
        grad_ref[part, :] = dot_nt(raw_ref[part, :], w_ref[...]).astype(BF)
        return carry

    lax.fori_loop(0, length // step, give, 0)
    out_sum_ref[...] = dot_tn(mixed_ref[...], mix_ref[...])

    def sums(i, carry):
        part = pl.ds(pl.multiple_of(i * 256, 256), 256)
        qkv_sum_ref[part, :] = dot_tn(normed_ref[:, part], raw_ref[...])
        return carry

    lax.fori_loop(0, D // 256, sums, 0)


MESH = pl.DeviceIdType.MESH


def place():
    me = lax.axis_index("exp")
    return me // 2, me % 2


def remote(source, target, send_sem, recv_sem, chip, core):
    return pltpu.make_async_remote_copy(
        src_ref=source,
        dst_ref=target,
        send_sem=send_sem,
        recv_sem=recv_sem,
        device_id={"exp": 2 * chip + core},
        device_id_type=MESH,
    )


def meet(chips):
    chip, core = place()
    barrier = pltpu.get_barrier_semaphore()

    def greet(to_chip, to_core):
        pl.semaphore_signal(
            barrier, inc=1, device_id={"exp": 2 * to_chip + to_core}, device_id_type=MESH
        )

    greet(chip, 1 - core)

    @pl.when(chip < chips - 1)
    def _():
        greet(chip + 1, core)

    @pl.when(chip > 0)
    def _():
        greet(chip - 1, core)

    below = (chip + chips - 1) // chips
    above = (2 * chips - 2 - chip) // chips
    pl.semaphore_wait(barrier, 1 + below + above)


def gather_sems(chips):
    return [pltpu.SemaphoreType.DMA((chips,))] * 4 + [pltpu.SemaphoreType.DMA((2 * chips,))] * 2


class Gather:
    def __init__(self, chips, own, blocks, sems):
        self.chips, self.own, self.blocks = chips, own, blocks
        self.up_send, self.up_recv, self.down_send, self.down_recv = sems[:4]
        self.pair_send, self.pair_recv = sems[4:]

    def _source(self, hop, number):
        return self.own if hop == 0 else self.blocks.at[number]

    def _up(self, hop):
        chip, core = place()
        number = 2 * (chip - hop) + core
        return remote(
            self._source(hop, number), self.blocks.at[number],
            self.up_send.at[hop], self.up_recv.at[hop], chip + 1, core,
        )

    def _down(self, hop):
        chip, core = place()
        number = 2 * (chip + hop) + core
        return remote(
            self._source(hop, number), self.blocks.at[number],
            self.down_send.at[hop], self.down_recv.at[hop], chip - 1, core,
        )

    def _pair(self, away):
        chip, core = place()
        number = 2 * (chip + away) + core
        source = self.own if isinstance(away, int) and away == 0 else self.blocks.at[number]
        slot = away + self.chips
        return remote(
            source, self.blocks.at[number], self.pair_send.at[slot], self.pair_recv.at[slot],
            chip, 1 - core,
        )

    def _from_pair(self, away):
        chip, core = place()
        block = self.blocks.at[2 * (chip + away) + 1 - core]
        slot = away + self.chips
        return remote(
            block, block, self.pair_send.at[slot], self.pair_recv.at[slot], chip, 1 - core
        )

    def start(self):
        chip, _ = place()

        @pl.when(chip < self.chips - 1)
        def _():
            self._up(0).start()

        @pl.when(chip > 0)
        def _():
            self._down(0).start()

        self._pair(0).start()

    def hop(self, hop):
        chip, core = place()

        @pl.when(chip >= hop)
        def _():
            block = self.blocks.at[2 * (chip - hop) + core]
            remote(
                block, block, self.up_send.at[hop - 1], self.up_recv.at[hop - 1], chip, 1 - core
            ).wait_recv()

            @pl.when(chip < self.chips - 1)
            def _():
                self._up(hop).start()

            self._pair(-hop).start()

        @pl.when(chip + hop < self.chips)
        def _():
            block = self.blocks.at[2 * (chip + hop) + core]
            remote(
                block, block, self.down_send.at[hop - 1], self.down_recv.at[hop - 1], chip, 1 - core
            ).wait_recv()

            @pl.when(chip > 0)
            def _():
                self._down(hop).start()

            self._pair(hop).start()

    def take_pair(self, away):
        self._from_pair(away).wait_recv()

    def finish(self, pairs):
        chip, _ = place()
        for away in range(-self.chips + 1, self.chips):

            @pl.when(jnp.logical_and(chip + away >= 0, chip + away < self.chips))
            def _():
                if pairs:
                    self._from_pair(away).wait_recv()
                self._pair(away).wait_send()

        for hop in range(self.chips):

            @pl.when(jnp.logical_and(chip >= hop, chip < self.chips - 1))
            def _():
                self._up(hop).wait_send()

            @pl.when(jnp.logical_and(chip + hop < self.chips, chip > 0))
            def _():
                self._down(hop).wait_send()


def scatter_sems(chips):
    return [pltpu.SemaphoreType.DMA((chips,))] * 6


class Scatter:
    def __init__(self, chips, theirs, mine, pair, line, sems):
        self.chips, self.theirs, self.mine, self.pair, self.line = chips, theirs, mine, pair, line
        self.pair_send, self.pair_recv, self.up_send, self.up_recv = sems[:4]
        self.down_send, self.down_recv = sems[4:]

    def _pair(self, to):
        chip, core = place()
        return remote(
            self.theirs(to), self.pair.at[to], self.pair_send.at[to], self.pair_recv.at[to],
            chip, 1 - core,
        )

    def _up(self, chip, to):
        return remote(
            self.mine(to), self.line.at[to - chip - 1], self.up_send.at[to], self.up_recv.at[to],
            chip + 1, place()[1],
        )

    def _down(self, chip, to):
        return remote(
            self.mine(to), self.line.at[self.chips - chip + 1 + to],
            self.down_send.at[to], self.down_recv.at[to], chip - 1, place()[1],
        )

    def _arrived_up(self, to):
        chip, core = place()
        block = self.line.at[to - chip]
        remote(block, block, self.up_send.at[to], self.up_recv.at[to], chip, 1 - core).wait_recv()
        return block[...].astype(F32)

    def _arrived_down(self, to):
        chip, core = place()
        block = self.line.at[self.chips - chip + to]
        remote(
            block, block, self.down_send.at[to], self.down_recv.at[to], chip, 1 - core
        ).wait_recv()
        return block[...].astype(F32)

    def _both(self, to):
        chip, core = place()
        block = self.pair.at[to]
        remote(
            block, block, self.pair_send.at[to], self.pair_recv.at[to], chip, 1 - core
        ).wait_recv()
        return self.mine(to)[...].astype(F32) + block[...].astype(F32)

    def start(self):
        for to in range(self.chips):
            self._pair(to).start()

    def slot(self, turn):
        chip, _ = place()
        last = self.chips - 1

        @pl.when(chip <= turn)
        def _():
            to = last - turn + chip
            total = self._both(to)

            @pl.when(chip == 0)
            def _():
                self.mine(to)[...] = total.astype(BF)

            @pl.when(chip > 0)
            def _():
                self.mine(to)[...] = (total + self._arrived_up(to)).astype(BF)

            self._up(chip, to).start()

        @pl.when(last - chip <= turn)
        def _():
            to = turn - last + chip
            total = self._both(to)

            @pl.when(chip == last)
            def _():
                self.mine(to)[...] = total.astype(BF)

            @pl.when(chip < last)
            def _():
                self.mine(to)[...] = (total + self._arrived_down(to)).astype(BF)

            self._down(chip, to).start()

    def finish(self, result):
        chip, _ = place()
        last = self.chips - 1
        result[...] = self._both(chip)

        @pl.when(chip > 0)
        def _():
            result[...] += self._arrived_up(chip)

        @pl.when(chip < last)
        def _():
            result[...] += self._arrived_down(chip)

        for to in range(self.chips):
            self._pair(to).wait_send()

            @pl.when(to > chip)
            def _():
                self._up(chip, to).wait_send()

            @pl.when(to < chip)
            def _():
                self._down(chip, to).wait_send()


def part_of(array, index):
    return array.at[index]


def block_order(chip, turn, chips):
    number, bit = 0, 1
    while bit < chips:
        number = number + bit * ((chip // bit + turn // bit) % 2)
        bit = 2 * bit
    return number


def expert_rows(
    chips, experts,
    own_ref, grad_own_ref, grad_ref, named_ref, router_ref, owner_ref, routed_refs, shared_refs,
    rows_ref, grads_ref, hidden_ref, d_gate_ref, d_up_ref, out_ref, back_b_ref, back_a_ref,
    weights, rows, grads, stage, out, back, pair, line, weight_sem, local_sem, stage_sem, keep_sem,
    *sems,
):
    chip, core = place()
    me = 2 * chip + core
    blocks = chips
    size = 2 * SEQ_DEV
    gathers = [Gather(chips, own_ref.at[m], rows.at[m], sems[6 * m : 6 * m + 6]) for m in range(MB)]
    grad_gather = Gather(chips, grad_own_ref.at[1], grads.at[1], sems[18:24])
    scatter = Scatter(
        chips,
        lambda to: back.at[0, 2 * to + 1 - core],
        lambda to: back.at[0, 2 * to + core],
        pair, line, sems[12:18],
    )
    loads = []
    for k in range(3):
        for e in range(EXP_DEV):
            loads.append(
                pltpu.make_async_copy(
                    routed_refs[k].at[e], weights.at[k, :, e * FF : (e + 1) * FF],
                    weight_sem.at[k, e],
                )
            )

    def shared_load(k):
        columns = pl.ds(pl.multiple_of(me * HD, HD), HD)
        return pltpu.make_async_copy(
            shared_refs[k].at[:, columns], weights.at[k, :, EXP_DEV * FF :], weight_sem.at[k, EXP_DEV]
        )

    def shared_loads(action):
        @pl.when(me < FF // HD)
        def _():
            for k in range(3):
                action(shared_load(k))

    def stage_out(step, k):
        block = block_order(chip, step % blocks, chips)
        start = pl.multiple_of((step // blocks * blocks + block) * size, size)
        target = (hidden_ref, d_gate_ref, d_up_ref)[k]
        return pltpu.make_async_copy(
            stage.at[step % 2, k], target.at[pl.ds(start, size), :], stage_sem.at[step % 2, k]
        )

    def out_copy(step):
        block = block_order(chip, step % blocks, chips)
        return pltpu.make_async_copy(
            out.at[step % 2], out_ref.at[step // blocks, pl.ds(2 * block, 2)], keep_sem.at[0, step % 2]
        )

    def back_copy(step):
        block = block_order(chip, step % blocks, chips)
        return pltpu.make_async_copy(
            back.at[1, pl.ds(2 * block, 2)], back_b_ref.at[pl.ds(2 * block, 2)],
            keep_sem.at[1, step % blocks],
        )

    for load in loads:
        load.start()
    shared_loads(lambda copy: copy.start())

    @pl.when(me >= FF // HD)
    def _():
        for k in range(3):
            weights[k, :, EXP_DEV * FF :] = jnp.zeros((D, HD), BF)

    own_copies = [
        pltpu.make_async_copy(own_ref.at[m], rows.at[m, me], local_sem.at[m]) for m in range(MB)
    ] + [
        pltpu.make_async_copy(grad_ref, grads.at[0], local_sem.at[2]),
        pltpu.make_async_copy(grad_own_ref.at[1], grads.at[1, me], local_sem.at[3]),
    ]
    for copy in own_copies:
        copy.start()
    meet(chips)
    gathers[0].start()
    for copy in own_copies:
        copy.wait()
    for load in loads:
        load.wait()
    shared_loads(lambda copy: copy.wait())

    def at(step, number, action):
        @pl.when(step == number)
        def _():
            action()

    row_copies = [
        pltpu.make_async_copy(source.at[m], target.at[m], keep_sem.at[2 + k, m])
        for m in range(MB)
        for k, (source, target) in enumerate(((rows, rows_ref), (grads, grads_ref)))
    ]

    def body(step, carry):
        micro_batch = step // blocks
        block = block_order(chip, step % blocks, chips)
        for m in range(MB):
            for hop in range(1, chips):
                at(step, m * blocks + hop, lambda m=m, hop=hop: gathers[m].hop(hop))
        for hop in range(1, chips):
            at(step, blocks + hop, lambda hop=hop: grad_gather.hop(hop))
        at(step, 1, gathers[1].start)
        at(step, 2, grad_gather.start)
        at(step, blocks, scatter.start)
        at(step, blocks, lambda: [copy.start() for copy in row_copies[:2]])
        for m in range(MB):

            @pl.when(micro_batch == m)
            def _():
                gathers[m].take_pair(block - chip)

        @pl.when(micro_batch == 1)
        def _():
            grad_gather.take_pair(block - chip)

        @pl.when(step >= 2)
        def _():
            for k in range(3):
                stage_out(step - 2, k).wait()
            out_copy(step - 2).wait()

        at(step, 2 * blocks - 1, lambda: [copy.start() for copy in row_copies[2:]])
        slot = step % 2
        normed = rows[micro_batch, pl.ds(2 * block, 2)].reshape(size, D)
        grad = grads[micro_batch, pl.ds(2 * block, 2)].reshape(size, D)
        logits = dot(normed, router_ref[...])
        names = pl.ds(pl.multiple_of(micro_batch * SEQ_DEV, SEQ_DEV), SEQ_DEV)
        named = named_ref[pl.ds(2 * block, 2), names, :].reshape(size, LANES).astype(F32)
        chosen = jnp.where(named > 0.0, logits, -1e30)
        powers = jnp.where(
            named > 0.0, jnp.exp(chosen - jnp.max(chosen, axis=1, keepdims=True)), 0.0
        )
        gates = powers / jnp.sum(powers, axis=1, keepdims=True)
        own = [
            jnp.sum(jnp.where(owner_ref[...] == EXP_DEV * me + e, gates, 0.0), axis=1, keepdims=True)
            for e in range(EXP_DEV)
        ]
        gate_grads = [jnp.zeros((size, 1), F32) for _ in range(EXP_DEV)]
        wide = weights.shape[2]
        for left in range(0, wide, 512):
            right = min(left + 512, wide)
            gate_part = dot(normed, weights[0, :, left:right])
            up_part = dot(normed, weights[1, :, left:right])
            down_part = dot(grad, weights[2, :, left:right])
            sigmoid = 0.5 * jnp.tanh(0.5 * gate_part) + 0.5
            act = gate_part * sigmoid
            hidden = act * up_part
            product = hidden * down_part
            scales = []
            for e in range(EXP_DEV + 1):
                low, high = max(left, e * FF), min(right, (e + 1) * FF)
                if low >= high:
                    continue
                if e < EXP_DEV:
                    gate_grads[e] += jnp.sum(
                        product[:, low - left : high - left], axis=1, keepdims=True
                    )
                    scales.append(jnp.broadcast_to(own[e], (size, high - low)))
                else:
                    scales.append(jnp.ones((size, high - low), F32))
            scale = scales[0] if len(scales) == 1 else jnp.concatenate(scales, axis=1)
            scaled = down_part * scale
            stage[slot, 0, :, left:right] = (hidden * scale).astype(BF)
            stage[slot, 1, :, left:right] = (
                scaled * up_part * (sigmoid + act * (1.0 - sigmoid))
            ).astype(BF)
            stage[slot, 2, :, left:right] = (scaled * act).astype(BF)
        for k in range(3):
            stage_out(step, k).start()
        for turn in range(chips - 1):
            at(step, blocks + turn, lambda turn=turn: scatter.slot(turn))
        result = dot_nt(stage[slot, 0], weights[2]).astype(BF)
        out[slot] = result.reshape(2, SEQ_DEV, D)
        out_copy(step).start()
        result = (dot_nt(stage[slot, 1], weights[0]) + dot_nt(stage[slot, 2], weights[1])).astype(BF)
        back[micro_batch, pl.ds(2 * block, 2), :, :D] = result.reshape(2, SEQ_DEV, D)
        high_tail, low_tail = jnp.zeros((size, LANES), F32), jnp.zeros((size, LANES), F32)
        for e in range(EXP_DEV):
            ours = owner_ref[...] == EXP_DEV * me + e
            high = gate_grads[e].astype(BF).astype(F32)
            high_tail = jnp.where(ours, high, high_tail)
            low_tail = jnp.where(ours, gate_grads[e] - high, low_tail)
        tail = high_tail + pltpu.roll(low_tail, experts, 1)
        back[micro_batch, pl.ds(2 * block, 2), :, D:] = tail.astype(BF).reshape(2, SEQ_DEV, LANES)

        @pl.when(micro_batch == 1)
        def _():
            back_copy(step).start()

        return carry

    lax.fori_loop(0, MB * blocks, body, 0)
    last = MB * blocks
    scatter.finish(back_a_ref)
    for m in range(MB):
        gathers[m].finish(False)
    grad_gather.finish(False)
    for copy in row_copies:
        copy.wait()
    for step in (last - 2, last - 1):
        for k in range(3):
            stage_out(step, k).wait()
        out_copy(step).wait()
    for turn in range(blocks):
        back_copy(blocks + turn).wait()


def seq_all_scratch(rows, width):
    groups = 4
    return [
        pltpu.VMEM((rows, groups * width), BF),
        pltpu.VMEM((groups - 1, rows, width), BF),
        pltpu.VMEM((rows, groups * width), BF),
    ] + [pltpu.SemaphoreType.DMA((groups,))] * 4


class SeqAll:
    def __init__(self, scratch):
        self.low, self.arrived, self.whole = scratch[:3]
        self.first_send, self.first_recv, self.last_send, self.last_recv = scratch[3:]
        self.groups = 4
        self.width = self.arrived.shape[2]
        self.group = lax.axis_index("seq")

    def _part(self, ref, device):
        return ref.at[:, pl.ds(pl.multiple_of(device * self.width, LANES), self.width)]

    def _copy(self, source, target, send, recv, away):
        return pltpu.make_async_remote_copy(
            src_ref=source, dst_ref=target, send_sem=send.at[away], recv_sem=recv.at[away],
            device_id={"seq": (self.group + away) % self.groups}, device_id_type=MESH,
        )

    def _first(self, away):
        part = self._part(self.low, (self.group + away) % self.groups)
        return self._copy(part, self.arrived.at[away - 1], self.first_send, self.first_recv, away)

    def _last(self, away):
        part = self._part(self.whole, self.group)
        return self._copy(part, part, self.last_send, self.last_recv, away)

    def start(self):
        for away in range(1, self.groups):
            self._first(away).start()

    def middle(self):
        total = self._part(self.low, self.group)[...].astype(F32)
        for away in range(1, self.groups):
            self._first(away).wait_recv()
            total += self.arrived[away - 1].astype(F32)
        self._part(self.whole, self.group)[...] = total.astype(BF)
        for away in range(1, self.groups):
            self._last(away).start()

    def take(self):
        for away in range(1, self.groups):
            part = self._part(self.whole, (self.group + self.groups - away) % self.groups)
            self._copy(part, part, self.last_send, self.last_recv, away).wait_recv()

    def finish(self):
        for away in range(1, self.groups):
            self._first(away).wait_send()
            self._last(away).wait_send()


def expert_sums(
    chips,
    rows_ref, grads_ref, hidden_ref, d_gate_ref, d_up_ref, shared_h_ref, shared_g_ref, shared_u_ref, back_ref, out_ref, hidden_one_ref,
    gate_ref, up_ref, down_ref, back_b_ref, layer_ref, shared_outs, gate_rows_ref,
    mine, pair, line, out_mine, out_pair, out_line, layer, local_sem, stage, stage_sem, shared, arrived, summed, held, *sems,
):
    chip, core = place()
    devices = 2 * chips
    half = D // 2
    matrix, side = pl.program_id(0), pl.program_id(1)
    step = 2 * matrix + side
    last = 2 * 3 * EXP_DEV - 1
    scatter = Scatter(
        chips,
        lambda to: back_ref.at[2 * to + 1 - core],
        lambda to: mine.at[to],
        pair, line, sems[:6],
    )
    spread = Spread(
        devices, 4, 1,
        lambda owner, k: shared.at[owner],
        lambda k, device: device < FF // HD,
        lambda device, k: device,
        arrived, summed, held, FF, sems[6:13],
    )
    results = Scatter(
        chips,
        lambda to: out_ref.at[0, 2 * to + 1 - core],
        lambda to: out_mine.at[to],
        out_pair, out_line, sems[13:19],
    )
    routed = [
        SeqSum(gate_ref.at[e], gate_rows_ref.at[e], e == 0, e, sems[19:])
        for e in range(EXP_DEV)
    ]
    targets = [(ref, e) for ref in (gate_ref, up_ref, down_ref) for e in range(EXP_DEV)]

    def write(number):
        target, e = targets[number // 2]
        part = pl.ds(number % 2 * half, half)
        return pltpu.make_async_copy(
            stage.at[number % 2], target.at[e, part], stage_sem.at[number % 2]
        )

    def at(number, action):
        @pl.when(step == number)
        def _():
            action()

    def begin():
        loads = [
            pltpu.make_async_copy(source, target, local_sem.at[number, to])
            for to in range(chips)
            for number, (source, target) in enumerate(
                (
                    (back_ref.at[2 * to + core], mine.at[to]),
                    (out_ref.at[0, 2 * to + core], out_mine.at[to]),
                )
            )
        ]
        for load in loads:
            load.start()
        meet_all(("seq", "exp"))
        scatter.start()
        for load in loads:
            load.wait()

    at(0, begin)
    for number in range(2, last + 1, 2):
        at(number, lambda number=number: [write(number - 2).wait(), write(number - 1).wait()])
    at(2, lambda: scatter.slot(0))
    at(2, routed[0].start)
    at(4, routed[1].start)
    at(4, lambda: scatter.slot(1))
    at(6, lambda: scatter.slot(2))
    at(7, spread.middle)
    at(4, results.start)
    at(7, lambda: results.slot(0))
    at(9, lambda: results.slot(1))
    at(10, lambda: results.slot(2))
    slot = step % 2

    @pl.when(matrix < EXP_DEV)
    def _():
        stage[slot] = dot_tn(rows_ref[...], d_gate_ref[...]).astype(BF)

    @pl.when(jnp.logical_and(matrix >= EXP_DEV, matrix < 2 * EXP_DEV))
    def _():
        stage[slot] = dot_tn(rows_ref[...], d_up_ref[...]).astype(BF)

    @pl.when(matrix >= 2 * EXP_DEV)
    def _():
        stage[slot] = dot_tn(grads_ref[...], hidden_ref[...]).astype(BF)

    @pl.when(matrix == 0)
    def _():
        part = pl.ds(pl.multiple_of(side * half, half), half)
        shared[0, part, :] = dot_tn(rows_ref[...], shared_g_ref[...]).astype(BF)
        shared[1, part, :] = dot_tn(rows_ref[...], shared_u_ref[...]).astype(BF)
        shared[2, part, :] = dot_tn(grads_ref[...], shared_h_ref[...]).astype(BF)

    for number in range(last + 1):
        at(number, lambda number=number: write(number).start())
    at(1, spread.start)
    at(8, lambda: scatter.finish(back_b_ref))
    at(9, spread.hand_out)
    at(9, routed[0].middle)

    @pl.when(step == last)
    def _():
        routed[1].middle()
        results.finish(layer)
        layer_ref[...] = (layer[...] + hidden_one_ref[...]).astype(BF)
        write(last - 1).wait()
        write(last).wait()
        spread.take()
        for kind, target in enumerate(shared_outs):
            target[...] = spread.of_kind(kind)[...]
        for job in routed:
            job.finish()
        spread.finish()


def meet_all(axes):
    barrier = pltpu.get_barrier_semaphore()
    count = 0
    for axis in axes:
        size = lax.axis_size(axis)
        for away in range(1, size):
            other = (lax.axis_index(axis) + away) % size
            pl.semaphore_signal(barrier, inc=1, device_id={axis: other}, device_id_type=MESH)
            count += 1
    pl.semaphore_wait(barrier, count)


FIRST_EXTRA, EXTRA_APART = 2, 3


def slot_head(slot, device, devices):
    return device if slot == 0 else devices + (device - FIRST_EXTRA) // EXTRA_APART


def slot_lives(slot, device, devices):
    if slot == 0:
        return device >= 0
    past = device - FIRST_EXTRA
    return jnp.logical_and(
        jnp.logical_and(past >= 0, past % EXTRA_APART == 0),
        past < EXTRA_APART * (HEADS - devices),
    )


def spread_sems(devices, groups, units):
    return [
        pltpu.SemaphoreType.DMA((groups - 1, units)),
        pltpu.SemaphoreType.DMA((groups - 1, units)),
        pltpu.SemaphoreType.DMA((units,)),
        pltpu.SemaphoreType.DMA((devices, units)),
        pltpu.SemaphoreType.DMA((devices, units)),
        pltpu.SemaphoreType.DMA((groups,)),
        pltpu.SemaphoreType.DMA((groups,)),
    ]


class Spread:
    def __init__(self, devices, groups, units, unit, lives, column, arrived, summed, held, width, sems):
        self.devices, self.groups, self.units = devices, groups, units
        self.unit, self.lives, self.column = unit, lives, column
        self.arrived, self.summed, self.held, self.width = arrived, summed, held, width
        self.first_send, self.first_recv, self.local_sem = sems[:3]
        self.second_send, self.second_recv, self.third_send, self.third_recv = sems[3:]
        self.kinds = groups - 1
        self.rows = D // devices
        self.group, self.me = lax.axis_index("seq"), lax.axis_index("exp")

    def _rows(self, device):
        return pl.ds(pl.multiple_of(device * self.rows, 32), self.rows)

    def _columns(self, device, k):
        return pl.ds(pl.multiple_of(self.column(device, k) * HD, HD), HD)

    def _along_seq(self, source, target, send, recv, away):
        return pltpu.make_async_remote_copy(
            src_ref=source, dst_ref=target, send_sem=send, recv_sem=recv,
            device_id={"seq": (self.group + away) % self.groups}, device_id_type=MESH,
        )

    def _along_exp(self, source, target, away, k):
        return pltpu.make_async_remote_copy(
            src_ref=source, dst_ref=target,
            send_sem=self.second_send.at[away, k], recv_sem=self.second_recv.at[away, k],
            device_id={"exp": (self.me + away) % self.devices}, device_id_type=MESH,
        )

    def _first(self, away, k):
        owner = (self.group + away) % self.groups
        return self._along_seq(
            self.unit(owner, k), self.arrived.at[away - 1, k],
            self.first_send.at[away - 1, k], self.first_recv.at[away - 1, k], away,
        )

    def _second(self, away, k):
        other = (self.me + away) % self.devices
        return self._along_exp(
            self.summed.at[k, self._rows(other)], self.held.at[0, :, self._columns(self.me, k)], away, k
        )

    def _own(self, k):
        return pltpu.make_async_copy(
            self.summed.at[k, self._rows(self.me)], self.held.at[0, :, self._columns(self.me, k)],
            self.local_sem.at[k],
        )

    def _third(self, away):
        return self._along_seq(
            self.held.at[0, :, : self.width], self.held.at[away, :, : self.width],
            self.third_send.at[away], self.third_recv.at[away], away,
        )

    def _sends_first(self, action):
        for k in range(self.units):
            for away in range(1, self.groups):

                @pl.when(
                    jnp.logical_and(
                        (self.group + away) % self.groups < self.kinds, self.lives(k, self.me)
                    )
                )
                def _():
                    action(self._first(away, k))

    def start(self):
        self._sends_first(lambda copy: copy.start())

    def middle(self):
        @pl.when(self.group < self.kinds)
        def _():
            for k in range(self.units):

                @pl.when(self.lives(k, self.me))
                def _():
                    total = self.unit(self.group, k)[...].astype(F32)
                    for away in range(1, self.groups):
                        block = self.arrived.at[away - 1, k]
                        self._along_seq(
                            block, block, self.first_send.at[away - 1, k],
                            self.first_recv.at[away - 1, k], away,
                        ).wait_recv()
                        total += block[...].astype(F32)
                    self.summed[k] = total.astype(BF)
                    for away in range(1, self.devices):
                        self._second(away, k).start()
                    self._own(k).start()

    def hand_out(self):
        @pl.when(self.group < self.kinds)
        def _():
            for k in range(self.units):

                @pl.when(self.lives(k, self.me))
                def _():
                    self._own(k).wait()

                for away in range(1, self.devices):
                    source = (self.me + self.devices - away) % self.devices

                    @pl.when(self.lives(k, source))
                    def _():
                        block = self.held.at[0, :, self._columns(source, k)]
                        self._along_exp(block, block, away, k).wait_recv()

            for away in range(1, self.groups):
                self._third(away).start()

    def take(self):
        for away in range(1, self.groups):

            @pl.when((self.group + self.groups - away) % self.groups < self.kinds)
            def _():
                self._third(away).wait_recv()

    def of_kind(self, kind):
        return self.held.at[(self.group + self.groups - kind) % self.groups]

    def finish(self):
        self._sends_first(lambda copy: copy.wait_send())

        @pl.when(self.group < self.kinds)
        def _():
            for k in range(self.units):

                @pl.when(self.lives(k, self.me))
                def _():
                    for away in range(1, self.devices):
                        self._second(away, k).wait_send()

            for away in range(1, self.groups):
                self._third(away).wait_send()


def seq_scratch(jobs):
    rows = D // 4
    return [
        pltpu.VMEM((jobs, 2, rows, FF), BF),
        pltpu.VMEM((jobs, 2, rows, FF), BF),
        pltpu.VMEM((jobs, rows, FF), BF),
        pltpu.VMEM((rows, FF), BF),
        pltpu.SemaphoreType.DMA((jobs, 2)),
        pltpu.SemaphoreType.DMA((jobs, 2)),
        pltpu.SemaphoreType.DMA((jobs, 2)),
        pltpu.SemaphoreType.DMA((jobs,)),
        pltpu.SemaphoreType.DMA((jobs,)),
        pltpu.SemaphoreType.DMA((jobs,)),
    ]


class SeqSum:
    def __init__(self, source, out, x_first, job, scratch):
        mine, arrived, last, result = scratch[:4]
        self.source, self.out, self.x_first = source, out, x_first
        self.mine, self.arrived, self.last = mine.at[job], arrived.at[job], last.at[job]
        self.result = result
        self.first_send, self.first_recv, self.load_sem = [sem.at[job] for sem in scratch[4:7]]
        self.last_send, self.last_recv, self.out_sem = [sem.at[job] for sem in scratch[7:]]
        group = lax.axis_index("seq")
        self.x, self.y = group % 2, group // 2
        self.rows = source.shape[0] // 4
        self.own = self.y if x_first else self.x

    def _neighbour(self, along_x):
        return 2 * self.y + 1 - self.x if along_x else 2 * (1 - self.y) + self.x

    def _block(self, i, kept):
        side = self.x if self.x_first else self.y
        side = side if kept else 1 - side
        number = 2 * i + side if self.x_first else 2 * side + i
        return self.source.at[pl.ds(pl.multiple_of(number * self.rows, 32), self.rows)]

    def _copy(self, source, target, send, recv, along_x):
        return pltpu.make_async_remote_copy(
            src_ref=source, dst_ref=target, send_sem=send, recv_sem=recv,
            device_id={"seq": self._neighbour(along_x)}, device_id_type=MESH,
        )

    def _first(self, i):
        return self._copy(
            self._block(i, False), self.arrived.at[i], self.first_send.at[i],
            self.first_recv.at[i], self.x_first,
        )

    def _load(self, i):
        return pltpu.make_async_copy(self._block(i, True), self.mine.at[i], self.load_sem.at[i])

    def _last(self):
        return self._copy(
            self.mine.at[1 - self.own], self.last, self.last_send, self.last_recv,
            not self.x_first,
        )

    def _write(self):
        return pltpu.make_async_copy(self.result, self.out, self.out_sem)

    def start(self):
        for i in range(2):
            self._first(i).start()
            self._load(i).start()

    def middle(self):
        for i in range(2):
            self._first(i).wait_recv()
            self._load(i).wait()
            self.mine[i] = (self.mine[i].astype(F32) + self.arrived[i].astype(F32)).astype(BF)
        self._last().start()

    def finish(self):
        self._last().wait_recv()
        total = self.mine[self.own].astype(F32) + self.last[...].astype(F32)
        self.result[...] = total.astype(BF)
        self._write().start()
        for i in range(2):
            self._first(i).wait_send()
        self._last().wait_send()
        self._write().wait()


def far_sum_scratch(jobs):
    rows = D // 4
    return [
        pltpu.VMEM((2, rows, FF), BF),
        pltpu.VMEM((2, rows, FF), BF),
        pltpu.VMEM((rows, FF), BF),
        pltpu.SemaphoreType.DMA((jobs, 2)),
        pltpu.SemaphoreType.DMA((jobs, 2)),
        pltpu.SemaphoreType.DMA((jobs, 2)),
        pltpu.SemaphoreType.DMA((jobs,)),
        pltpu.SemaphoreType.DMA((jobs,)),
        pltpu.SemaphoreType.DMA((jobs,)),
        pltpu.SemaphoreType.DMA((jobs, 2)),
    ]


class FarSeqSum(SeqSum):
    def __init__(self, source, out, x_first, job, slots, scratch):
        mine, arrived, last = slots
        self.ours, self.theirs, result = scratch[:3]
        self.more_sem = scratch[9].at[job]
        super().__init__(source, out, x_first, job, [mine, arrived, last, result] + list(scratch[3:9]))

    def _fetch(self, i):
        return pltpu.make_async_copy(self.arrived.at[i], self.theirs.at[i], self.more_sem.at[i])

    def _load(self, i):
        return pltpu.make_async_copy(self._block(i, True), self.ours.at[i], self.load_sem.at[i])

    def _store(self, i):
        return pltpu.make_async_copy(self.ours.at[i], self.mine.at[i], self.load_sem.at[i])

    def start(self):
        for i in range(2):
            self._first(i).start()

    def middle(self):
        for i in range(2):
            self._load(i).start()
        for i in range(2):
            self._first(i).wait_recv()
            self._fetch(i).start()
        for i in range(2):
            self._load(i).wait()
            self._fetch(i).wait()
            self.ours[i] = (self.ours[i].astype(F32) + self.theirs[i].astype(F32)).astype(BF)
            self._store(i).start()
        for i in range(2):
            self._store(i).wait()
        self._last().start()

    def finish(self):
        ours = pltpu.make_async_copy(self.mine.at[self.own], self.ours.at[0], self.load_sem.at[0])
        ours.start()
        self._last().wait_recv()
        theirs = pltpu.make_async_copy(self.last, self.theirs.at[0], self.more_sem.at[0])
        theirs.start()
        ours.wait()
        theirs.wait()
        total = self.ours[0].astype(F32) + self.theirs[0].astype(F32)
        self.result[...] = total.astype(BF)
        self._write().start()
        for i in range(2):
            self._first(i).wait_send()
        self._last().wait_send()
        self._write().wait()


def softmax_low(scores):
    powers = jnp.exp(scores - jnp.max(scores, axis=-1, keepdims=True))
    return (powers * (1.0 / jnp.sum(powers, axis=-1, keepdims=True))).astype(BF)


def heads_forward(
    chips, slots,
    tokens_ref, grad_own_ref, named_own_ref, gain_ref, cos_ref, sin_ref, w_refs, w_out_ref,
    normed_ref, qkv_ref, mixed_ref, own_mixed_ref, hidden_ref, two_ref, w_all, grad_ref, named_ref,
    rows, w_sem, local_sem, send_sem, recv_sem, *sems,
):
    devices = 2 * chips
    me = lax.axis_index("exp")
    chip, _ = place()
    length = SEQ_DEV * devices
    size = 2 * SEQ_DEV
    step = BLOCK
    gathers = [Gather(chips, tokens_ref.at[m], rows.at[m], sems[6 * m : 6 * m + 6]) for m in range(MB)]
    later = [
        Gather(chips, named_own_ref, named_ref, sems[12:18]),
        Gather(chips, grad_own_ref.at[0], grad_ref, sems[18:24]),
    ]
    keeps = [
        pltpu.make_async_copy(source, target, local_sem.at[number])
        for number, (source, target) in enumerate(
            [(tokens_ref.at[m], rows.at[m, me]) for m in range(MB)]
            + [(named_own_ref, named_ref.at[me]), (grad_own_ref.at[0], grad_ref.at[me])]
        )
    ]

    def load(slot, j):
        head = jnp.clip(slot_head(slot, me, devices), 0, HEADS - 1)
        unit = 3 * slot + j
        return pltpu.make_async_copy(
            w_refs[j].at[:, pl.ds(pl.multiple_of(head * HD, HD), HD)],
            w_all.at[:, unit * HD : (unit + 1) * HD],
            w_sem.at[unit],
        )

    def head_columns(m, device, slot):
        return own_mixed_ref.at[
            m, :, pl.ds(pl.multiple_of(slot_head(slot, device, devices) * HD, HD), HD)
        ]

    def rows_of(m, device, slot):
        part = pl.ds(pl.multiple_of(device * SEQ_DEV, SEQ_DEV), SEQ_DEV)
        return mixed_ref.at[m, part, slot * HD : (slot + 1) * HD]

    def give(m, away, slot):
        other = (me + away) % devices
        return pltpu.make_async_remote_copy(
            src_ref=rows_of(m, other, slot),
            dst_ref=head_columns(m, me, slot),
            send_sem=send_sem.at[m, away, slot],
            recv_sem=recv_sem.at[m, away, slot],
            device_id={"exp": other},
            device_id_type=MESH,
        )

    def keep_own(m, slot):
        return pltpu.make_async_copy(
            rows_of(m, me, slot), head_columns(m, me, slot), recv_sem.at[m, 0, slot]
        )

    def take(m, away, slot):
        block = head_columns(m, (me + devices - away) % devices, slot)
        return pltpu.make_async_remote_copy(
            src_ref=block,
            dst_ref=block,
            send_sem=send_sem.at[m, away, slot],
            recv_sem=recv_sem.at[m, away, slot],
            device_id={"exp": (me + away) % devices},
            device_id_type=MESH,
        )

    for copy in keeps:
        copy.start()
    for slot in range(slots):
        for j in range(3):
            load(slot, j).start()
    meet_all(("exp",))
    gathers[0].start()
    for copy in keeps:
        copy.wait()
    for slot in range(slots):
        for j in range(3):
            load(slot, j).wait()

    def body(m, carry):
        def at(number, action):
            @pl.when(m == number)
            def _():
                action()

        for turn_ in range(chips):
            block = block_order(chip, turn_, chips)
            for number in range(MB):
                if turn_ > number:
                    at(number, lambda number=number: gathers[number].hop(turn_))
                at(number, lambda number=number: gathers[number].take_pair(block - chip))
            if turn_ == 1:
                at(0, gathers[1].start)
            if turn_ == chips - 2:
                at(1, later[0].start)
                at(1, later[1].start)
            part = pl.ds(pl.multiple_of(block * size, size), size)
            tokens = rows[m, pl.ds(2 * block, 2)].reshape(size, D).astype(F32)
            normed = norm_rows(tokens, gain_ref[0:1, :]).astype(BF)
            normed_ref[m, part, :] = normed
            qkv = dot(normed, w_all[...])
            for unit in range(3 * slots):
                values = qkv[:, unit * HD : (unit + 1) * HD]
                if unit % 3 < 2:
                    values = turn(values, cos_ref[part, :], sin_ref[part, :])
                qkv_ref[m, part, unit * HD : (unit + 1) * HD] = values.astype(BF)
        for slot in range(slots):
            base = 3 * HD * slot
            for start in range(0, length, step):
                stop = start + step
                scores = visible_scores(
                    qkv_ref[m, start:stop, base : base + HD],
                    qkv_ref[m, :stop, base + HD : base + 2 * HD],
                    start,
                )
                attention = softmax_low(scores)
                mixed = dot(attention, qkv_ref[m, :stop, base + 2 * HD : base + 3 * HD])
                mixed_ref[m, start:stop, slot * HD : (slot + 1) * HD] = mixed.astype(BF)
            for number in range(MB):

                @pl.when(jnp.logical_and(m == number, slot_lives(slot, me, devices)))
                def _():
                    for away in range(1, devices):
                        give(number, away, slot).start()
                    keep_own(number, slot).start()

            if slot == 0:
                at(0, lambda: gathers[1].hop(1))
                at(1, lambda: [gather.hop(1) for gather in later])
            else:
                at(1, lambda: [gather.hop(2) for gather in later])
        return carry

    lax.fori_loop(0, MB, body, 0)

    def finish_rows(m):
        for slot in range(slots):

            @pl.when(slot_lives(slot, me, devices))
            def _():
                keep_own(m, slot).wait()

            for away in range(1, devices):

                @pl.when(slot_lives(slot, (me + devices - away) % devices, devices))
                def _():
                    take(m, away, slot).wait_recv()

        hidden = tokens_ref[m].astype(F32) + dot(own_mixed_ref[m], w_out_ref[...])
        hidden_ref[m] = hidden
        two_ref[m] = norm_rows(hidden, gain_ref[1:2, :]).astype(BF)

    finish_rows(0)
    finish_rows(1)
    for hop in range(3, chips):
        for gather in later:
            gather.hop(hop)
    for gather in gathers:
        gather.finish(False)
    for gather in later:
        gather.finish(True)
    for m in range(MB):
        for slot in range(slots):

            @pl.when(slot_lives(slot, me, devices))
            def _():
                for away in range(1, devices):
                    give(m, away, slot).wait_send()


def heads_backward(
    chips, slots,
    own_ref, qkv_ref, mixed_ref, cos_ref, sin_ref, w_ref, own_mixed_ref, mix_ref, small_ref, hidden_ref,
    normed_ref, up_ref, down_ref, out_ref,
    grad_a_ref, grad_b_ref, weight_outs, w_out_out, small_out, layer_ref, up_out, down_out, job_slots,
    sums_ref, arrived, summed, held, mine, pair, line, layer, d_mixed, probs, raw, parts, d_keys, d_values, pairs, lines,
    part, weight_pair, weight_line, result, normed, normed_sem, mine_sem, local_sem, send_sem, recv_sem, *sems,
):
    devices = 2 * chips
    me = lax.axis_index("exp")
    core = me % 2
    length = SEQ_DEV * devices
    step = BLOCK
    factor = HD ** (-0.5)
    scatters = [
        Scatter(
            chips,
            lambda to, m=m: parts.at[m, 2 * to + 1 - core],
            lambda to, m=m: parts.at[m, 2 * to + core],
            pairs.at[m], lines.at[m], sems[6 * m : 6 * m + 6],
        )
        for m in range(MB)
    ]

    spread = Spread(
        devices, 4, slots,
        lambda owner, k: sums_ref.at[owner + 3 * k],
        lambda k, device: slot_lives(k, device, devices),
        lambda device, k: slot_head(k, device, devices),
        arrived, summed, held, D, sems[6 * MB + 6 : 6 * MB + 13],
    )
    results = Scatter(
        chips,
        lambda to: out_ref.at[1, 2 * to + 1 - core],
        lambda to: mine.at[to],
        pair, line, sems[6 * MB + 13 : 6 * MB + 19],
    )
    result_loads = [
        pltpu.make_async_copy(out_ref.at[1, 2 * to + core], mine.at[to], mine_sem.at[to])
        for to in range(chips)
    ]
    routed = [
        FarSeqSum(source, target, k % 2 == 0, k, job_slots, sems[6 * MB + 19 : -7])
        for k, (source, target) in enumerate(
            (ref.at[e], out.at[e])
            for ref, out in ((up_ref, up_out), (down_ref, down_out))
            for e in range(EXP_DEV)
        )
    ]
    rows = D // devices

    def row_block(device):
        return pl.ds(pl.multiple_of(device * rows, 32), rows)

    weight = Scatter(
        chips,
        lambda to: part.at[row_block(2 * to + 1 - core)],
        lambda to: part.at[row_block(2 * to + core)],
        weight_pair, weight_line, sems[6 * MB : 6 * MB + 6],
    )
    weight_all = SeqAll(sems[-7:])
    far = D + LANES

    def load(number):
        return pltpu.make_async_copy(
            normed_ref.at[:, :, 256 * number : 256 * (number + 1)], normed.at[number % 2],
            normed_sem.at[number % 2],
        )

    def block_at(m, device, slot):
        rows = pl.ds(pl.multiple_of(device * SEQ_DEV, SEQ_DEV), SEQ_DEV)
        return d_mixed.at[m, rows, slot * HD : (slot + 1) * HD]

    def columns(m, head):
        return own_ref.at[m, :, pl.ds(pl.multiple_of(head * HD, HD), HD)]

    def exchange(m, away, slot):
        other = (me + away) % devices
        return pltpu.make_async_remote_copy(
            src_ref=columns(m, slot_head(slot, other, devices)),
            dst_ref=block_at(m, me, slot),
            send_sem=send_sem.at[m, away, slot],
            recv_sem=recv_sem.at[m, away, slot],
            device_id={"exp": other},
            device_id_type=MESH,
        )

    def arrival(m, away, slot):
        block = block_at(m, (me + devices - away) % devices, slot)
        return pltpu.make_async_remote_copy(
            src_ref=block,
            dst_ref=block,
            send_sem=send_sem.at[m, away, slot],
            recv_sem=recv_sem.at[m, away, slot],
            device_id={"exp": (me + away) % devices},
            device_id_type=MESH,
        )

    def keep(m, slot):
        return pltpu.make_async_copy(
            columns(m, slot_head(slot, me, devices)), block_at(m, me, slot), local_sem.at[m, slot]
        )

    meet_all(("seq", "exp"))
    for m in range(MB):
        for away in range(1, devices):
            for slot in range(slots):

                @pl.when(slot_lives(slot, (me + away) % devices, devices))
                def _():
                    exchange(m, away, slot).start()

        for slot in range(slots):

            @pl.when(slot_lives(slot, me, devices))
            def _():
                keep(m, slot).start()

            @pl.when(jnp.logical_not(slot_lives(slot, me, devices)))
            def _():
                d_mixed[m, :, slot * HD : (slot + 1) * HD] = jnp.zeros((length, HD), BF)

    for job in routed:
        job.start()
    for number in range(2):
        load(number).start()
    for copy in result_loads:
        copy.start()
    for left in range(0, D, 256):
        part[left : left + 256, :D] = dot_tn(
            own_mixed_ref[:, left : left + 256], mix_ref[...]
        ).astype(BF)
    part[:, D:] = small_ref[...]
    weight.start()

    def weigh(m):
        for slot in range(slots):
            base = 3 * HD * slot
            for start in range(0, length, step):
                stop = start + step
                scores = visible_scores(
                    qkv_ref[m, start:stop, base : base + HD],
                    qkv_ref[m, :stop, base + HD : base + 2 * HD],
                    start,
                )
                probs[start // step][slot] = softmax_low(scores)

    def body(m, carry):
        weigh(m)
        for number in range(MB):

            @pl.when(m == number)
            def _():
                for slot in range(slots):

                    @pl.when(slot_lives(slot, me, devices))
                    def _():
                        keep(number, slot).wait()
                        for away in range(1, devices):
                            arrival(number, away, slot).wait_recv()

        @pl.when(m == 1)
        def _():
            scatters[0].start()
            weight.slot(0)

        for slot in range(slots):
            base = 3 * HD * slot
            d_keys[...] = jnp.zeros_like(d_keys)
            d_values[...] = jnp.zeros_like(d_values)
            for start in range(0, length, step):
                stop = start + step
                queries = qkv_ref[m, start:stop, base : base + HD]
                keys = qkv_ref[m, :stop, base + HD : base + 2 * HD]
                values = qkv_ref[m, :stop, base + 2 * HD : base + 3 * HD]
                d_mix = d_mixed[m, start:stop, slot * HD : (slot + 1) * HD]
                mixed = mixed_ref[m, start:stop, slot * HD : (slot + 1) * HD]
                row_term = jnp.sum(d_mix.astype(F32) * mixed.astype(F32), axis=1, keepdims=True)
                attention = probs[start // step][slot]
                d_scores = (attention.astype(F32) * (dot_nt(d_mix, values) - row_term)).astype(BF)
                turned = turn(dot(d_scores, keys) * factor, cos_ref[start:stop, :], -sin_ref[start:stop, :])
                raw[m, start:stop, base : base + HD] = turned.astype(BF)
                d_keys[:stop, :] += dot_tn(d_scores, queries)
                d_values[:stop, :] += dot_tn(attention, d_mix)
            turned = turn(d_keys[...] * factor, cos_ref[...], -sin_ref[...])
            raw[m, :, base + HD : base + 2 * HD] = turned.astype(BF)
            raw[m, :, base + 2 * HD : base + 3 * HD] = d_values[...].astype(BF)

            @pl.when(m == 1)
            def _():
                scatters[0].slot(min(slot, chips - 2))
                if slot == 1:
                    routed[0].middle()
                    routed[1].middle()

        for start in range(0, length, step):
            back = dot_nt(raw[m, start : start + step, :], w_ref[...]).astype(BF)
            first = start // SEQ_DEV
            parts[m, first : first + step // SEQ_DEV] = back.reshape(step // SEQ_DEV, SEQ_DEV, D)
        return carry

    lax.fori_loop(0, MB, body, 0)
    scatters[1].start()
    for turn_ in range(min(slots, chips - 1), chips - 1):
        scatters[0].slot(turn_)
    ticks = [lambda t=t: scatters[1].slot(t) for t in range(chips - 1)]
    for number, left in enumerate(range(0, D, 256)):
        load(number).wait()
        total = dot_tn(normed[number % 2, 0], raw[0]) + dot_tn(normed[number % 2, 1], raw[1])
        if number + 2 < D // 256:
            load(number + 2).start()
        for unit in range(3 * slots):
            sums_ref[unit, left : left + 256, :] = total[:, unit * HD : (unit + 1) * HD].astype(BF)
        if number == 1:
            ticks[0]()
    spread.start()
    results.start()
    for turn_ in range(1, chips - 1):
        weight.slot(turn_)
    weight.finish(result)
    weight_all.low[:, :far] = result[...].astype(BF)
    weight_all.low[:, far:] = jnp.zeros((rows, LANES), BF)
    weight_all.start()
    scatters[0].finish(grad_a_ref)
    spread.middle()
    routed[2].middle()
    routed[3].middle()
    ticks[1]()
    weight_all.middle()
    for copy in result_loads:
        copy.wait()
    ticks[2]()
    results.slot(0)
    spread.hand_out()
    routed[0].finish()
    routed[1].finish()
    results.slot(1)
    scatters[1].finish(grad_b_ref)
    results.slot(2)
    routed[2].finish()
    routed[3].finish()
    weight_all.take()
    w_out_out[...] = weight_all.whole[:, :D]
    small_out[...] = weight_all.whole[:, D:far]
    spread.take()
    for kind, target in enumerate(weight_outs):
        target[...] = spread.of_kind(kind)[...]
    results.finish(layer)
    layer_ref[...] = (layer[...] + hidden_ref[...]).astype(BF)
    weight_all.finish()
    spread.finish()
    for m in range(MB):
        for away in range(1, devices):
            for slot in range(slots):

                @pl.when(slot_lives(slot, (me + away) % devices, devices))
                def _():
                    exchange(m, away, slot).wait_send()


def middle_rows(
    back_a_ref, back_b_ref, named_ref, hidden_ref, grad_ref, two_ref, router_ref, gain_ref, w_out_ref,
    grad_hidden_ref, mix_ref, d_mixed_ref, small_ref,
    experts,
):
    size = SEQ_DEV
    lane = lax.broadcasted_iota(jnp.int32, (MB * size, LANES), 1)
    named = named_ref[...].astype(F32)
    logits = jnp.where(named > 0.0, dot(two_ref[...], router_ref[...]), -1e30)
    powers = jnp.where(named > 0.0, jnp.exp(logits - jnp.max(logits, axis=1, keepdims=True)), 0.0)
    gates = powers / jnp.sum(powers, axis=1, keepdims=True)
    tail = jnp.concatenate([back_a_ref[:, D:], back_b_ref[:, D:]], axis=0)
    tail = jnp.where(lane < experts, tail + pltpu.roll(tail, LANES - experts, 1), 0.0)
    grad_logits = gates * (tail - jnp.sum(gates * tail, axis=1, keepdims=True))
    grad_logits = grad_logits.astype(BF)
    grad_two = jnp.concatenate([back_a_ref[:, :D], back_b_ref[:, :D]], axis=0)
    grad_two += dot_nt(grad_logits, router_ref[...])
    back, terms = norm_back(hidden_ref[...], gain_ref[1:2, :], grad_two)
    grad_hidden = grad_ref[...].astype(F32) + back
    grad_hidden_ref[...] = grad_hidden
    mix_ref[...] = grad_hidden.astype(BF)
    d_mixed_ref[...] = dot_nt(mix_ref[...], w_out_ref[...]).astype(BF)
    high = terms.astype(BF)
    low = (terms - high.astype(F32)).astype(BF)
    chosen = jnp.where(lane == experts, 1.0, 0.0).astype(BF)
    total = dot_tn(two_ref[...], grad_logits) + dot_tn(high, chosen) + dot_tn(low, chosen)
    small_ref[...] = total.astype(BF)


def last_rows(
    tokens_ref, normed_a_ref, normed_b_ref, grad_hidden_ref, gain_ref, gain_rows_ref, weight_lows, small_ref, layer_refs,
    shared_lows, gate_ref, up_ref, down_ref, w_refs,
    grad_tokens_ref, weight_outs, router_ref, gain_one_ref, gain_two_ref, layer_out, shared_outs, gate_out, up_out, down_out,
    w_rows, w_sem,
    experts,
):
    gate_out[...] = gate_ref[...].astype(F32)
    up_out[...] = up_ref[...].astype(F32)
    down_out[...] = down_ref[...].astype(F32)

    @pl.when(pl.program_id(0) == 0)
    def _():
        small_outputs(
            tokens_ref, normed_a_ref, normed_b_ref, grad_hidden_ref, gain_ref, gain_rows_ref, weight_lows, small_ref,
            layer_refs, shared_lows, w_refs, grad_tokens_ref, weight_outs, router_ref, gain_one_ref, gain_two_ref,
            layer_out, shared_outs, w_rows, w_sem, experts,
        )


def small_outputs(
    tokens_ref, normed_a_ref, normed_b_ref, grad_hidden_ref, gain_ref, gain_rows_ref, weight_lows, small_ref, layer_refs,
    shared_lows, w_refs, grad_tokens_ref, weight_outs, router_ref, gain_one_ref, gain_two_ref, layer_out, shared_outs,
    w_rows, w_sem,
    experts,
):
    rows = D // lax.axis_size("exp")
    start = pl.ds(pl.multiple_of(lax.axis_index("exp") * rows, 32), rows)
    loads = [
        pltpu.make_async_copy(w_refs[k].at[start], w_rows.at[k], w_sem.at[k]) for k in range(3)
    ]
    for copy in loads:
        copy.start()
    for low, out in zip(shared_lows, shared_outs):
        out[...] = low[...].astype(F32)
    for m in range(MB):
        layer_out[m] = layer_refs[m][...]
    for m, normed_ref in enumerate((normed_a_ref, normed_b_ref)):
        part = slice(m * SEQ_DEV, (m + 1) * SEQ_DEV)
        back, _ = norm_back(tokens_ref[part, :].astype(F32), gain_ref[0:1, :], normed_ref[...])
        grad_tokens_ref[part, :] = (grad_hidden_ref[part, :] + back).astype(BF)
    product = jnp.zeros((rows, D), F32)
    for k, (low, out) in enumerate(zip(weight_lows, weight_outs)):
        grad = low[...].astype(F32)
        out[...] = grad
        if k < 3:
            loads[k].wait()
            product += w_rows[k].astype(F32) * grad
    ones = jnp.ones((8, D), BF)
    high = product.astype(BF)
    low = (product - high.astype(F32)).astype(BF)
    gain_one_ref[...] = (dot_nt(ones, high) + dot_nt(ones, low))[0:1, :] / gain_rows_ref[...]
    small = small_ref[...]
    router_ref[...] = small[:, :experts].astype(F32)
    column = lax.broadcasted_iota(jnp.int32, (8, LANES), 1)
    gain_two_ref[...] = dot_nt(jnp.where(column == experts, 1.0, 0.0).astype(BF), small)[0:1, :]


def taking(us):
    return pl.CostEstimate(flops=int(us * 1.0e9), bytes_accessed=2**20, transcendentals=0)


def like(*shape, dtype=BF):
    return jax.ShapeDtypeStruct(shape, dtype)


IN_VMEM = pl.BlockSpec(memory_space=pltpu.VMEM)
ANYWHERE = pl.BlockSpec(memory_space=pl.ANY)


def experts_on_lines(two_own, hidden_one, grad_own, grad_a, named, experts, router, owners, routed, shared):
    devices = lax.axis_size("exp")
    chips = devices // 2
    length = SEQ_DEV * devices
    wide = EXP_DEV * FF + LANES
    block_back = (devices, SEQ_DEV, D + LANES)
    sems = [gather_sems(chips)] * MB + [scatter_sems(chips), gather_sems(chips)]

    def call_rows(*operands):
        def kernel(own_ref, grad_own_ref, grad_ref, named_ref, router_ref, owner_ref, *refs):
            expert_rows(
                chips, experts, own_ref, grad_own_ref, grad_ref, named_ref, router_ref, owner_ref,
                refs[:3], refs[3:6], *refs[6:],
            )

        return pl.pallas_call(
            kernel,
            out_shape=(
                like(MB, devices, SEQ_DEV, D),
                like(MB, devices, SEQ_DEV, D),
                like(MB * length, wide),
                like(MB * length, wide),
                like(MB * length, wide),
                like(MB, devices, SEQ_DEV, D),
                like(*block_back),
                like(SEQ_DEV, D + LANES, dtype=F32),
            ),
            in_specs=[IN_VMEM, ANYWHERE, ANYWHERE] + [IN_VMEM] * 3 + [ANYWHERE] * 6,
            out_specs=(ANYWHERE,) * 7 + (IN_VMEM,),
            scratch_shapes=[
                pltpu.VMEM((3, D, wide), BF),
                pltpu.VMEM((MB, devices, SEQ_DEV, D), BF),
                pltpu.VMEM((MB, devices, SEQ_DEV, D), BF),
                pltpu.VMEM((2, 3, 2 * SEQ_DEV, wide), BF),
                pltpu.VMEM((2, 2, SEQ_DEV, D), BF),
                pltpu.VMEM((MB, *block_back), BF),
                pltpu.VMEM((chips, SEQ_DEV, D + LANES), BF),
                pltpu.VMEM((chips + 1, SEQ_DEV, D + LANES), BF),
                pltpu.SemaphoreType.DMA((3, EXP_DEV + 1)),
                pltpu.SemaphoreType.DMA((4,)),
                pltpu.SemaphoreType.DMA((2, 3)),
                pltpu.SemaphoreType.DMA((4, chips)),
            ]
            + [sem for group in sems for sem in group],
            compiler_params=pltpu.CompilerParams(
                collective_id=1, has_side_effects=True, vmem_limit_bytes=VMEM_BYTES
            ),
            cost_estimate=taking(100),
            name="expert_rows",
        )(*operands)

    rows, grads, hidden, d_gate, d_up, out_parts, back_b, back_sum_a = call_rows(
        two_own, grad_own, grad_a, named, router, owners, *routed, *shared
    )
    flat = MB * length


    def call_sums(*operands):
        def kernel(*refs):
            expert_sums(chips, *refs[:16], refs[16:19], *refs[19:])

        half = D // 2
        by_rows = pl.BlockSpec((flat, half), lambda k, d: (0, d))
        by_grads = pl.BlockSpec((flat, half), lambda k, d: (0, d))

        def for_gate(k, d):
            return (0, (k + 4) // 5)

        def for_up(k, d):
            return (0, k // 3)

        def for_down(k, d):
            return (0, k // 5)

        last = pl.BlockSpec(
            (flat, LANES), lambda k, d: (0, EXP_DEV * FF // LANES), pipeline_mode=pl.Buffered(1)
        )

        def whole(*shape):
            return pl.BlockSpec(shape, lambda k, d: (0,) * len(shape))

        return pl.pallas_call(
            kernel,
            grid=(3 * EXP_DEV, 2),
            out_shape=(like(EXP_DEV, D, FF),) * 3
            + (like(SEQ_DEV, D + LANES, dtype=F32), like(SEQ_DEV, D))
            + (like(D // devices, FF),) * 3
            + (like(EXP_DEV, D // 4, FF),),
            in_specs=[by_rows, by_grads]
            + [pl.BlockSpec((flat, FF), for_down, pipeline_mode=pl.Buffered(1))]
            + [pl.BlockSpec((flat, FF), use) for use in (for_gate, for_up)]
            + [last] * 3
            + [ANYWHERE] * 2
            + [pl.BlockSpec((SEQ_DEV, D), lambda k, d: (0, 0), pipeline_mode=pl.Buffered(1))],
            out_specs=(ANYWHERE,) * 3
            + (whole(SEQ_DEV, D + LANES), whole(SEQ_DEV, D))
            + (whole(D // devices, FF),) * 3
            + (ANYWHERE,),
            scratch_shapes=[
                pltpu.VMEM((chips, SEQ_DEV, D + LANES), BF),
                pltpu.VMEM((chips, SEQ_DEV, D + LANES), BF),
                pltpu.VMEM((chips + 1, SEQ_DEV, D + LANES), BF),
                pltpu.VMEM((chips, SEQ_DEV, D), BF),
                pltpu.VMEM((chips, SEQ_DEV, D), BF),
                pltpu.VMEM((chips + 1, SEQ_DEV, D), BF),
                pltpu.VMEM((SEQ_DEV, D), F32),
                pltpu.SemaphoreType.DMA((2, chips)),
                pltpu.VMEM((2, half, FF), BF),
                pltpu.SemaphoreType.DMA((2,)),
                pltpu.VMEM((3, D, HD), BF),
                pltpu.VMEM((3, 1, D, HD), BF),
                pltpu.VMEM((1, D, HD), BF),
                pltpu.VMEM((4, D // devices, FF), BF),
            ]
            + scatter_sems(chips)
            + spread_sems(devices, 4, 1)
            + scatter_sems(chips)
            + seq_scratch(2),
            compiler_params=pltpu.CompilerParams(
                collective_id=2, has_side_effects=True, vmem_limit_bytes=VMEM_BYTES
            ),
            cost_estimate=taking(60),
            name="expert_sums",
        )(*operands)

    gate_sum, up_sum, down_sum, back_sum_b, layer_a, *shared_grads, gate_rows = call_sums(
        rows.reshape(flat, D), grads.reshape(flat, D), hidden, d_gate, d_up, hidden, d_gate, d_up, back_b,
        out_parts, hidden_one[0],
    )
    backs = (back_sum_a, back_sum_b)
    return (
        layer_a,
        out_parts,
        backs,
        gate_rows,
        (gate_sum, up_sum, down_sum),
        shared_grads,
    )


def named_softmax(logits, named):
    chosen = jnp.where(named, logits, -jnp.inf)
    powers = jnp.where(named, jnp.exp(chosen - jnp.max(chosen, axis=-1, keepdims=True)), 0.0)
    return powers / jnp.sum(powers, axis=-1, keepdims=True)


def on_device_plain(
    tokens,
    cotangent,
    expert_ids,
    owner_table,
    w_query,
    w_key,
    w_value,
    w_out,
    gain_one,
    gain_two,
    w_router,
    shared_gate,
    shared_up,
    shared_down,
    routed_gate,
    routed_up,
    routed_down,
):
    devices = lax.axis_size("exp")
    groups = lax.axis_size("seq")
    me = lax.axis_index("exp")
    experts = owner_table.shape[0]
    length = SEQ_DEV * devices
    rows_out = D // devices
    slots = -(-HEADS // devices)
    wide = slots * HD
    share = FF // devices
    used = EXP_DEV * FF + share
    padded = -(-used // LANES) * LANES

    head_of = [jnp.minimum(me + slot * devices, HEADS - 1) for slot in range(slots)]
    slot_live = jnp.concatenate(
        [
            jnp.full((HD,), jnp.where(me + slot * devices < HEADS, 1.0, 0.0), F32)
            for slot in range(slots)
        ]
    )

    w_qkv = jnp.concatenate(
        [
            lax.dynamic_slice(weight, (0, head * HD), (D, HD))
            for head in head_of
            for weight in (w_query, w_key, w_value)
        ],
        axis=1,
    )
    w_out_heads = jnp.concatenate(
        [lax.dynamic_slice(w_out, (head * HD, 0), (HD, D)) for head in head_of], axis=0
    )
    cos_table, sin_table = angle_tables(jnp.arange(length).astype(F32))
    sin_table = jnp.where(jnp.arange(HD) < HD // 2, -sin_table, sin_table)
    params = pltpu.CompilerParams(vmem_limit_bytes=VMEM_BYTES)

    forward = pl.pallas_call(
        functools.partial(attend_forward, slots),
        out_shape=(
            like(length, D),
            like(length, 3 * wide),
            like(length, wide),
            like(slots, length, 1, dtype=F32),
        ),
        in_specs=[IN_VMEM] * 5,
        out_specs=(IN_VMEM,) * 4,
        compiler_params=params,
        name="attend_forward",
    )
    backward = pl.pallas_call(
        functools.partial(attend_backward, slots),
        out_shape=(like(wide, D, dtype=F32), like(D, 3 * wide, dtype=F32), like(length, D)),
        in_specs=[IN_VMEM] * 10,
        out_specs=(IN_VMEM,) * 3,
        scratch_shapes=[
            pltpu.VMEM((length, 3 * wide), BF),
            pltpu.VMEM((length, wide), BF),
            pltpu.VMEM((length, HD), F32),
            pltpu.VMEM((length, HD), F32),
        ],
        compiler_params=params,
        name="attend_backward",
    )

    def joined(routed, shared):
        own = lax.dynamic_slice(shared, (0, me * share), (D, share))
        blank = jnp.zeros((D, padded - used), BF)
        return jnp.concatenate([routed[i] for i in range(EXP_DEV)] + [own, blank], axis=1)

    gate_all = joined(routed_gate, shared_gate)
    up_all = joined(routed_up, shared_up)
    down_all = joined(routed_down, shared_down)

    expert_at = jnp.sum(
        (owner_table[:, None] == jnp.arange(experts)[None, :]) * jnp.arange(experts)[:, None],
        axis=0,
    )
    router_rows = jnp.take(w_router, expert_at, axis=1)
    ids_all = lax.all_gather(expert_ids[:, 0], "exp", axis=1, tiled=True)

    first = []
    for micro_batch in range(MB):
        rows_all = gather_exp(tokens[micro_batch, 0])
        normed, qkv, mixed, lse = forward(rows_all, gain_one[None], cos_table, sin_table, w_qkv)
        sent = lax.all_to_all(
            mixed.reshape(devices, SEQ_DEV, wide), "exp", split_axis=0, concat_axis=0, tiled=True
        )
        own_mixed = (
            sent.reshape(devices, SEQ_DEV, slots, HD)
            .transpose(1, 2, 0, 3)
            .reshape(SEQ_DEV, slots * devices * HD)[:, :D]
        )
        rows_in = tokens[micro_batch, 0].astype(F32)
        hidden_one = rows_in + dot(own_mixed, w_out)
        two_low = norm_rows(hidden_one, gain_two).astype(BF)
        two_all = gather_exp(two_low)
        grad_all = gather_exp(cotangent[micro_batch, 0])
        first.append(
            (normed, qkv, mixed, lse, rows_in, hidden_one, two_all, grad_all)
        )

    column = jnp.arange(padded)
    second = []
    for micro_batch in range(MB):
        two_all, grad_all = first[micro_batch][6:]
        logits = dot(two_all, router_rows)
        named = jnp.any(ids_all[micro_batch][:, :, None] == expert_at[None, None, :], axis=1)
        chosen = jnp.where(named, logits, -jnp.inf)
        powers = jnp.where(named, jnp.exp(chosen - jnp.max(chosen, axis=-1, keepdims=True)), 0.0)
        gates = powers / jnp.sum(powers, axis=-1, keepdims=True)
        own_gates = lax.dynamic_slice(gates, (0, me * EXP_DEV), (length, EXP_DEV))
        weight = jnp.where(
            column[None, :] < FF,
            own_gates[:, :1],
            jnp.where(column[None, :] < 2 * FF, own_gates[:, 1:], 1.0),
        )
        gate_part = dot(two_all, gate_all)
        up_part = dot(two_all, up_all)
        down_part = dot(grad_all, down_all)
        sigmoid = jax.nn.sigmoid(gate_part)
        act = gate_part * sigmoid
        hidden = act * up_part
        products = hidden * down_part
        own_grads = jnp.stack(
            [jnp.sum(products[:, i * FF : (i + 1) * FF], axis=1) for i in range(EXP_DEV)], axis=1
        )
        hidden_low = (weight * hidden).astype(BF)
        weighted = weight * down_part
        d_gate = (weighted * up_part * (sigmoid + act * (1.0 - sigmoid))).astype(BF)
        d_up = (weighted * act).astype(BF)
        out_part = scatter_exp(dot_nt(hidden_low, down_all))
        back_part = scatter_exp(dot_nt(d_gate, gate_all) + dot_nt(d_up, up_all))
        gate_grads = lax.all_gather(own_grads, "exp", axis=1, tiled=True)
        grad_logits = (
            gates * (gate_grads - jnp.sum(gates * gate_grads, axis=-1, keepdims=True))
        ).astype(BF)
        second.append((hidden_low, d_gate, d_up, out_part, back_part, grad_logits))

    two_both = jnp.concatenate([f[6] for f in first])
    grad_both = jnp.concatenate([f[7] for f in first])
    gate_sum = dot_tn(two_both, jnp.concatenate([s[1] for s in second]))
    up_sum = dot_tn(two_both, jnp.concatenate([s[2] for s in second]))
    down_sum = dot_tn(grad_both, jnp.concatenate([s[0] for s in second]))

    def routed_sum(total):
        parts = jnp.stack([total[:, i * FF : (i + 1) * FF] for i in range(EXP_DEV)])
        return lax.psum_scatter(
            parts.astype(BF), "seq", scatter_dimension=1, tiled=True
        ).astype(F32)

    def shared_part(total):
        return total[:, EXP_DEV * FF : used]

    outputs_list = []
    grads_list = []
    small = jnp.zeros((D, experts + 2), F32)
    qkv_sum = jnp.zeros((D, 3 * wide), F32)
    out_sum = jnp.zeros((wide, D), F32)
    for micro_batch in range(MB):
        normed, qkv, mixed, lse, rows_in, hidden_one, two_all, _ = first[micro_batch]
        _, _, _, out_part, back_part, grad_logits = second[micro_batch]
        outputs_list.append((hidden_one + out_part).astype(BF))
        own_logits = lax.dynamic_slice(grad_logits, (me * SEQ_DEV, 0), (SEQ_DEV, experts))
        grad_two = back_part + dot_nt(own_logits, router_rows)
        back, gain_terms = norm_back(hidden_one, gain_two, grad_two)
        grad_hidden = cotangent[micro_batch, 0].astype(F32) + back
        own_two = lax.dynamic_slice(two_all, (me * SEQ_DEV, 0), (SEQ_DEV, D))
        router_part = dot_tn(own_two, own_logits)
        mix_all = gather_exp(grad_hidden.astype(BF))
        out_one, qkv_one, grad_part = backward(
            mix_all, normed, qkv, mixed, lse, cos_table, sin_table, w_qkv, w_out_heads, slot_live[None]
        )
        out_sum = out_sum + out_one
        qkv_sum = qkv_sum + qkv_one
        grad_normed = scatter_exp(grad_part)
        back_one, gain_one_terms = norm_back(rows_in, gain_one, grad_normed)
        grads_list.append((grad_hidden + back_one).astype(BF))
        small = small + jnp.concatenate(
            [
                router_part,
                jnp.sum(gain_one_terms, axis=0)[:, None],
                jnp.sum(gain_terms, axis=0)[:, None],
            ],
            axis=1,
        )

    def to_rows(columns):
        parts = columns.astype(BF).reshape(devices, rows_out, columns.shape[1])
        parts = lax.psum_scatter(parts, "seq", scatter_dimension=1, tiled=True)
        return lax.all_to_all(parts, "exp", split_axis=0, concat_axis=0, tiled=True)

    def to_all(rows):
        return lax.all_gather(rows, "seq", axis=0, tiled=True).astype(F32)

    piece = rows_out // groups
    shared_cols = jnp.concatenate([shared_part(t) for t in (gate_sum, up_sum, down_sum)], axis=1)
    shared_rows = to_rows(shared_cols).reshape(devices, piece, 3, share)
    shared_full = to_all(shared_rows.transpose(1, 2, 0, 3).reshape(piece, 3 * FF))
    qkv_rows = to_rows(qkv_sum).reshape(devices, piece, slots, 3, HD)
    qkv_rows = qkv_rows.transpose(1, 3, 2, 0, 4).reshape(piece, 3, slots * devices * HD)
    qkv_full = to_all(qkv_rows[:, :, :D].reshape(piece, 3 * D))
    out_part = lax.psum_scatter(out_sum.astype(BF), "seq", scatter_dimension=1, tiled=True)
    spread = jnp.zeros((slots * devices * HD, D // groups), BF)
    for slot in range(slots):
        spread = lax.dynamic_update_slice(
            spread, out_part[slot * HD : (slot + 1) * HD], ((me + slot * devices) * HD, 0)
        )
    out_rows = lax.psum_scatter(spread[:D], "exp", scatter_dimension=0, tiled=True)
    out_full = lax.all_gather(out_rows, "seq", axis=1, tiled=True).astype(F32)
    small_rows = lax.psum_scatter(
        lax.psum(small, "seq"), "exp", scatter_dimension=0, tiled=True
    )
    place_of = jnp.take(small_rows, owner_table, axis=1)
    return (
        jnp.stack(outputs_list)[:, None],
        jnp.stack(grads_list)[:, None],
        qkv_full[:, :D],
        qkv_full[:, D : 2 * D],
        qkv_full[:, 2 * D :],
        out_full,
        small_rows[:, experts],
        small_rows[:, experts + 1],
        place_of,
        shared_full[:, :FF],
        shared_full[:, FF : 2 * FF],
        shared_full[:, 2 * FF :],
        routed_sum(gate_sum),
        routed_sum(up_sum),
        routed_sum(down_sum),
    )


def on_device_lines(
    tokens,
    cotangent,
    expert_ids,
    owner_table,
    w_query,
    w_key,
    w_value,
    w_out,
    gain_one,
    gain_two,
    w_router,
    shared_gate,
    shared_up,
    shared_down,
    routed_gate,
    routed_up,
    routed_down,
):
    devices = lax.axis_size("exp")
    groups = lax.axis_size("seq")
    me = lax.axis_index("exp")
    chips = devices // 2
    experts = owner_table.shape[0]
    length = SEQ_DEV * devices
    rows_out = D // devices
    slots = -(-HEADS // devices)
    wide = slots * HD
    own = MB * SEQ_DEV

    cos_table, sin_table = turn_tables(length)

    router = jnp.pad(w_router, ((0, 0), (0, LANES - experts)))
    owners = jnp.pad(owner_table, (0, LANES - experts), constant_values=-1)[None]
    gains = jnp.stack([gain_one, gain_two])
    named_own = jnp.any(
        expert_ids.reshape(own, TOP)[:, :, None] == jnp.arange(LANES)[None, None, :], axis=1
    ).astype(BF)
    tokens_own = tokens.reshape(MB, SEQ_DEV, D)
    grad_own = cotangent.reshape(MB, SEQ_DEV, D)

    def call_forward(*operands):
        def kernel(*refs):
            heads_forward(chips, slots, *refs[:6], refs[6:9], *refs[9:])

        return pl.pallas_call(
            kernel,
            out_shape=(
                like(MB, length, D),
                like(MB, length, 3 * wide),
                like(MB, length, wide),
                like(MB, SEQ_DEV, D),
                like(MB, SEQ_DEV, D, dtype=F32),
                like(MB, SEQ_DEV, D),
                like(D, 3 * wide),
                like(devices, SEQ_DEV, D),
                like(devices, own, LANES),
            ),
            in_specs=[IN_VMEM, ANYWHERE] + [IN_VMEM] * 4 + [ANYWHERE] * 3 + [IN_VMEM],
            out_specs=(IN_VMEM,) * 7 + (ANYWHERE, IN_VMEM),
            scratch_shapes=[
                pltpu.VMEM((MB, devices, SEQ_DEV, D), BF),
                pltpu.SemaphoreType.DMA((3 * slots,)),
                pltpu.SemaphoreType.DMA((4,)),
                pltpu.SemaphoreType.DMA((MB, devices, slots)),
                pltpu.SemaphoreType.DMA((MB, devices, slots)),
            ]
            + gather_sems(chips) * 4,
            compiler_params=pltpu.CompilerParams(
                collective_id=5, has_side_effects=True, vmem_limit_bytes=VMEM_BYTES
            ),
            cost_estimate=taking(70),
            name="heads_forward",
        )(*operands)

    normed, qkv, mixed, own_mixed, hidden_one, two_low, w_qkv, grad_a, named_all = call_forward(
        tokens_own, grad_own, named_own, gains, cos_table, sin_table,
        w_query, w_key, w_value, w_out,
    )
    hidden_rows = hidden_one
    own_mixed, hidden_one = own_mixed.reshape(own, D), hidden_one.reshape(own, D)
    two_low = two_low.reshape(own, D)

    layer_a, out_parts, backs, gate_full, routed_sums, shared_lows = experts_on_lines(
        two_low.reshape(MB, SEQ_DEV, D),
        hidden_rows,
        grad_own,
        grad_a,
        named_all.reshape(devices, MB * SEQ_DEV, LANES),
        experts,
        router,
        owners,
        (routed_gate, routed_up, routed_down),
        (shared_gate, shared_up, shared_down),
    )
    def call_middle(*operands):
        def kernel(*refs):
            middle_rows(*refs, experts)

        return pl.pallas_call(
            kernel,
            out_shape=(like(own, D, dtype=F32), like(own, D), like(own, D), like(D, LANES)),
            in_specs=[IN_VMEM] * 9,
            out_specs=(IN_VMEM,) * 4,
            compiler_params=pltpu.CompilerParams(vmem_limit_bytes=VMEM_BYTES),
            cost_estimate=taking(5),
            name="middle_rows",
        )(*operands)

    grad_hidden, grad_mix, d_mixed, small = call_middle(
        *backs, named_own, hidden_one, cotangent.reshape(own, D), two_low, router, gains, w_out
    )
    quarter = like(EXP_DEV, D // groups, FF)
    far = D + LANES
    jobs = 4
    slot_shape = (jobs, 2, D // groups, FF)

    def backward_kernel(*refs):
        heads_backward(
            chips, slots, *refs[:16], refs[16:19], *refs[19:24], refs[24:27], *refs[27:36],
            refs[36 : 36 + length // BLOCK], *refs[36 + length // BLOCK :],
        )

    normed_a, normed_b, *backward_out = pl.pallas_call(
        backward_kernel,
        out_shape=(like(SEQ_DEV, D, dtype=F32),) * 2
        + (like(rows_out, D),) * 4
        + (like(rows_out, LANES), like(SEQ_DEV, D), quarter, quarter)
        + (like(*slot_shape), like(*slot_shape), like(jobs, D // groups, FF)),
        in_specs=[IN_VMEM] * 10 + [ANYWHERE] * 4,
        out_specs=(IN_VMEM,) * 8 + (ANYWHERE,) * 5,
        scratch_shapes=[
            pltpu.VMEM((3 * slots, D, HD), BF),
            pltpu.VMEM((groups - 1, slots, D, HD), BF),
            pltpu.VMEM((slots, D, HD), BF),
            pltpu.VMEM((groups, rows_out, D), BF),
            pltpu.VMEM((chips, SEQ_DEV, D), BF),
            pltpu.VMEM((chips, SEQ_DEV, D), BF),
            pltpu.VMEM((chips + 1, SEQ_DEV, D), BF),
            pltpu.VMEM((SEQ_DEV, D), F32),
            pltpu.VMEM((MB, length, wide), BF),
        ]
        + [pltpu.VMEM((slots, BLOCK, stop), BF) for stop in range(BLOCK, length + 1, BLOCK)]
        + [
            pltpu.VMEM((MB, length, 3 * wide), BF),
            pltpu.VMEM((MB, devices, SEQ_DEV, D), BF),
            pltpu.VMEM((length, HD), F32),
            pltpu.VMEM((length, HD), F32),
            pltpu.VMEM((MB, chips, SEQ_DEV, D), BF),
            pltpu.VMEM((MB, chips + 1, SEQ_DEV, D), BF),
            pltpu.VMEM((D, far), BF),
            pltpu.VMEM((chips, rows_out, far), BF),
            pltpu.VMEM((chips + 1, rows_out, far), BF),
            pltpu.VMEM((rows_out, far), F32),
            pltpu.VMEM((2, MB, length, 256), BF),
            pltpu.SemaphoreType.DMA((2,)),
            pltpu.SemaphoreType.DMA((chips,)),
            pltpu.SemaphoreType.DMA((MB, slots)),
            pltpu.SemaphoreType.DMA((MB, devices, slots)),
            pltpu.SemaphoreType.DMA((MB, devices, slots)),
        ]
        + scatter_sems(chips) * (MB + 1)
        + spread_sems(devices, groups, slots)
        + scatter_sems(chips)
        + far_sum_scratch(jobs)
        + seq_all_scratch(rows_out, (far + LANES) // groups),
        compiler_params=pltpu.CompilerParams(
            collective_id=3, has_side_effects=True, vmem_limit_bytes=VMEM_BYTES
        ),
        cost_estimate=taking(140),
        name="heads_backward",
    )(
        d_mixed.reshape(MB, SEQ_DEV, D), qkv, mixed, cos_table, sin_table, w_qkv, own_mixed,
        grad_mix, small, hidden_rows[1], normed, *routed_sums[1:], out_parts,
    )
    gain_rows = lax.dynamic_slice(gain_one, (me * rows_out,), (rows_out,))[None]

    def call_last(*operands):
        def kernel(*refs):
            last_rows(
                *refs[:6], refs[6:10], refs[10], refs[11:13], refs[13:16], *refs[16:19],
                refs[19:22], refs[22], refs[23:27], *refs[27:31], refs[31:34], *refs[34:], experts,
            )

        full = like(EXP_DEV, D // groups, FF, dtype=F32)
        by_expert = pl.BlockSpec((1, D // groups, FF), lambda e: (e, 0, 0))
        return pl.pallas_call(
            kernel,
            out_shape=(like(own, D),)
            + (like(rows_out, D, dtype=F32),) * 4
            + (like(rows_out, experts, dtype=F32),)
            + (like(1, rows_out, dtype=F32),) * 2
            + (like(MB, SEQ_DEV, D),)
            + (like(rows_out, FF, dtype=F32),) * 3
            + (full,) * 3,
            grid=(EXP_DEV,),
            in_specs=[IN_VMEM] * 16 + [by_expert] * 3 + [ANYWHERE] * 3,
            out_specs=(IN_VMEM,) * 12 + (by_expert,) * 3,
            scratch_shapes=[pltpu.VMEM((3, rows_out, D), BF), pltpu.SemaphoreType.DMA((3,))],
            compiler_params=pltpu.CompilerParams(vmem_limit_bytes=VMEM_BYTES),
            cost_estimate=taking(6),
            name="last_rows",
        )(*operands)

    last_out = call_last(
        tokens.reshape(own, D), normed_a, normed_b, grad_hidden, gains, gain_rows,
        *backward_out[:5], layer_a, backward_out[5], *shared_lows, gate_full, *backward_out[6:8],
        w_query, w_key, w_value,
    )
    grad_tokens, attn, router_grad = last_out[0], last_out[1:5], last_out[5]
    gain_one_grad, gain_two_grad, layer_out = last_out[6:9]
    far_grads = last_out[9:]
    whole = (MB, 1, SEQ_DEV, D)
    return (
        layer_out.reshape(whole),
        grad_tokens.reshape(whole),
        *attn,
        gain_one_grad[0],
        gain_two_grad[0],
        router_grad,
        *far_grads,
    )


def solution(mesh):
    rows = P(None, "seq", "exp", None)
    placed = (rows,) * 3 + (P(),) * 11 + (P("exp", None, None),) * 3
    wide = P("exp", None)
    on_lines = mesh.shape["exp"] == 8 and mesh.shape["seq"] == 4
    on_device = on_device_lines if on_lines else on_device_plain
    return jax.shard_map(
        on_device,
        mesh=mesh,
        in_specs=placed,
        out_specs=(rows, rows, wide, wide, wide, wide, P("exp"), P("exp"))
        + (wide,) * 4
        + (P("exp", "seq", None),) * 3,
        check_vma=False,
    )
```
